32 devices in a mesh: seq: 4 (over y, x), fsdp: 8 (over z, core).
Axes of the slice: x: 2, y: 2, z: 4, core: 2. Of those that a mesh axis runs over, the one named last changes fastest.
Arguments:
- tokens: bfloat16 [8, 512, 2048], P('fsdp', 'seq'), may hold values from -6 to 6
- layer_vectors: bfloat16 [8, 512, 256], P('fsdp', 'seq'), may hold values from -6 to 6
- doc_lengths: int32 [8, 3], P('fsdp'), may hold values from 1 to 385, 512 in all within a row
- cotangent: bfloat16 [8, 512, 2048], P('fsdp', 'seq'), may hold values from -6 to 6
- tile_owner: int32 [3712], replicated, may hold values from 0 to 3711, as said below
- tile_master: float32 [3712, 128, 128], P(('seq', 'fsdp'))
- tile_first: float32 [3712, 128, 128], P(('seq', 'fsdp'))
- tile_second: float32 [3712, 128, 128], P(('seq', 'fsdp'))
- left_basis: float32 [3712, 128, 128], P(('seq', 'fsdp')), may hold values from -1 to 1
- right_basis: float32 [3712, 128, 128], P(('seq', 'fsdp')), may hold values from -1 to 1
- small_master: float32 [80, 128, 128], P('seq')
- small_first: float32 [80, 128, 128], P('seq')
- small_second: float32 [80, 128, 128], P('seq')
- small_left: float32 [80, 128, 128], P('seq'), may hold values from -1 to 1
- small_right: float32 [80, 128, 128], P('seq'), may hold values from -1 to 1
- gains: float32 [12800], P('seq'), may hold values from 0.25 to 1.75
- gain_first: float32 [12800], P('seq')
- gain_second: float32 [12800], P('seq')
Outputs:
- output: bfloat16 [8, 512, 2048], P('fsdp', 'seq')
- input_grad: float32 [8, 512, 2048], P('fsdp', 'seq')
- tile_weight_new: float32 [3712, 128, 128], P(('seq', 'fsdp'))
- tile_first_new: float32 [3712, 128, 128], P(('seq', 'fsdp'))
- tile_second_new: float32 [3712, 128, 128], P(('seq', 'fsdp'))
- small_weight_new: float32 [80, 128, 128], P('seq')
- small_first_new: float32 [80, 128, 128], P('seq')
- small_second_new: float32 [80, 128, 128], P('seq')
- gain_new: float32 [12800], P('seq')
- gain_first_new: float32 [12800], P('seq')
- gain_second_new: float32 [12800], P('seq')
The draws below stay inside these ranges and needn't reach their ends.
Inputs may be any that keep to these rules, and one draw needn't show every extreme that they name: `doc_lengths`: each pack's 3 document lengths sum to 512; one of them is exactly 385. A permutation: slot s of the tile arrays holds tile tile_owner[s] of the weight table.
All inputs are finite; a program needn't handle non-finite values.
Results may differ from the reference program's by a relative error of at most 0.028.
Values may be sent and summed in bfloat16 or wider, within the bound.
No kernel may reach another device: no remote copies, remote signals or barrier semaphores. Data moves between devices by JAX's collectives and lax.ppermute only.
A program may use at most 1.125 GiB of HBM per device.

```python
import math
import jax
import jax.numpy as jnp
import numpy as np
from jax import lax

D = 2048
HEADS = 8
KV_HEADS = 2
HEAD_DIM = 256
FF = 8192
RANK = 64
PLD = 256
TILE = 128
DOCS = 3
STEP = 5
TOK_DEV = 128
LEN = 512
PACKS = 8
TOKENS = 4096
KB = 29696
SW = 640
TILES = 3712
SMALL_TILES = 80
NG = 12800
N_SEQ = 4


def owner_list(key):
    return jax.random.permutation(key, TILES).astype(jnp.int32)


def column_scale(key, scale_query, scale_out, scale_ffn, scale_down):
    owners = owner_list(key)
    column_count = KB // TILE
    start = owners % column_count * TILE
    out_col = HEADS * HEAD_DIM + 2 * KV_HEADS * HEAD_DIM
    ffn_col = out_col + HEADS * HEAD_DIM
    down_col = ffn_col + 2 * FF
    chosen = jnp.where(start < out_col, scale_query, jnp.where(start < ffn_col, scale_out, jnp.where(start < down_col, scale_ffn, scale_down)))
    return chosen.astype(jnp.float32)[:, None, None]


def small_scale(values):
    small_columns = SW // TILE
    slot = jnp.arange(SMALL_TILES) % small_columns
    column = slot[:, None] * TILE + jnp.arange(TILE)[None, :]
    chosen = jnp.where(column < RANK, values[0], jnp.where(column < 2 * RANK, values[1], jnp.where(column < 2 * RANK + PLD, values[2], values[3])))
    return chosen.astype(jnp.float32)[:, None, :]


def cosine_basis(key, count):
    first_key, second_key = jax.random.split(key)
    orders = jax.vmap(lambda item: jax.random.permutation(item, TILE))(jax.random.split(first_key, count))
    signs = (2 * jax.random.randint(second_key, (count, 1, TILE), 0, 2) - 1).astype(jnp.float32)
    row_number = jnp.arange(TILE)
    phase = (2 * row_number[None, :, None] + 1) * orders[:, None, :] % (4 * TILE)
    angle = phase.astype(jnp.float32) * (math.pi / (2 * TILE))
    weight = jnp.where(orders[:, None, :] == 0, math.sqrt(1.0 / TILE), math.sqrt(2.0 / TILE)).astype(jnp.float32)
    return (jnp.cos(angle) * weight * signs).astype(jnp.float32)


def draw_tile_owner(key, part):
    return owner_list(key)


def draw_tile_master(key, part):
    scales = column_scale(key, D ** (-0.5), (HEADS * HEAD_DIM) ** (-0.5), D ** (-0.5), FF ** (-0.5))
    key = jax.random.fold_in(key, 1)
    return jax.random.truncated_normal(key, -4.0, 4.0, (TILES, TILE, TILE), jnp.float32) * scales


def draw_tile_first(key, part):
    root = math.sqrt(TOKENS)
    scales = column_scale(key, 1.5 * root, root, 0.5 * root, root)
    key = jax.random.fold_in(key, 2)
    return jax.random.truncated_normal(key, -4.0, 4.0, (TILES, TILE, TILE), jnp.float32) * scales


def draw_tile_second(key, part):
    root = math.sqrt(TOKENS)
    scales = column_scale(key, 1.5 * root, root, 0.5 * root, root)
    key = jax.random.fold_in(key, 3)
    factor = jnp.exp(jax.random.uniform(key, (TILES, TILE, TILE), jnp.float32, 0.0, math.log(4.0)))
    return factor * scales * scales


def draw_left_basis(key, part):
    key = jax.random.fold_in(key, 4)
    return cosine_basis(key, TILES)


def draw_right_basis(key, part):
    key = jax.random.fold_in(key, 5)
    return cosine_basis(key, TILES)


def draw_small_master(key, part):
    key = jax.random.fold_in(key, 6)
    scales = small_scale([D ** (-0.5), RANK ** (-0.5), D ** (-0.5), PLD ** (-0.5)])
    return jax.random.truncated_normal(key, -4.0, 4.0, (SMALL_TILES, TILE, TILE), jnp.float32) * scales


def draw_small_first(key, part):
    key = jax.random.fold_in(key, 7)
    root = math.sqrt(TOKENS)
    scales = small_scale([4.0 * root, 0.7 * root, 4.5 * root, root])
    return jax.random.truncated_normal(key, -4.0, 4.0, (SMALL_TILES, TILE, TILE), jnp.float32) * scales


def draw_small_second(key, part):
    key = jax.random.fold_in(key, 8)
    root = math.sqrt(TOKENS)
    scales = small_scale([4.0 * root, 0.7 * root, 4.5 * root, root])
    factor = jnp.exp(jax.random.uniform(key, (SMALL_TILES, TILE, TILE), jnp.float32, 0.0, math.log(4.0)))
    return factor * scales * scales


def draw_small_left(key, part):
    key = jax.random.fold_in(key, 9)
    return cosine_basis(key, SMALL_TILES)


def draw_small_right(key, part):
    key = jax.random.fold_in(key, 10)
    return cosine_basis(key, SMALL_TILES)


def draw_gain_first(key, part):
    key = jax.random.fold_in(key, 11)
    return jax.random.truncated_normal(key, -4.0, 4.0, (NG,), jnp.float32) * math.sqrt(TOKENS)


def draw_gain_second(key, part):
    key = jax.random.fold_in(key, 12)
    factor = jnp.exp(jax.random.uniform(key, (NG,), jnp.float32, 0.0, math.log(4.0)))
    return factor * float(TOKENS)


def shard_levels(stream_key, shape, shards, low, largest):
    def one(axis_at, shards_of):
        heights = jax.random.uniform(jax.random.fold_in(jax.random.fold_in(stream_key, 6), axis_at), (shards_of,), jnp.float32, low / len(shards), largest / len(shards))
        return jnp.repeat(jnp.exp(heights), shape[axis_at] // shards_of).reshape((-1,) + (1,) * (len(shape) - axis_at - 1))

    level = one(*shards[0])
    for cut in shards[1:]:
        level = level * one(*cut)
    return level


def split_up(number_of, total, reach, slope):
    portions = [(1 << 20) // math.isqrt(standing ** slope) + 1 for standing in range(2, number_of + 1)]
    rest, holding = total - reach - (number_of - 1), [1] * (number_of - 1)
    while rest > 0:
        movable = [i for i in range(number_of - 1) if holding[i] < reach]
        mass, remaining = sum([portions[i] for i in movable]), rest
        for i in movable:
            extra = min(reach - holding[i], max(1, remaining * portions[i] // mass), rest)
            holding[i] = holding[i] + extra
            rest = rest - extra
    return np.array([reach] + holding)


def uneven_parts(own_key, count, total, most, skew):
    if count == 2:
        one = jax.random.randint(own_key, (), max(1, total - most), min(most, total - 1) + 1)
        return jnp.stack([one, total - one])
    sizes = jnp.asarray(split_up(count, total, most, skew), jnp.int32)
    twos = (count - 1) // 2
    donor, sink = sizes[1:1 + 2 * twos:2], sizes[2:2 + 2 * twos:2]
    slack = jnp.minimum(donor - 1, most - sink)
    moved = jax.random.randint(jax.random.fold_in(own_key, 1), (twos,), 0, 1 << 20) % (slack + 1)
    sizes = sizes.at[1:1 + 2 * twos:2].set(donor - moved).at[2:2 + 2 * twos:2].set(sink + moved)
    return sizes[jax.random.permutation(jax.random.fold_in(own_key, 2), count)]


def scatter_about(own_key, dims, spread, reach, pieces=(), held_as=jnp.bfloat16):
    entries = spread * jax.random.normal(own_key, dims, jnp.float32)
    if pieces:
        entries = entries * shard_levels(own_key, dims, pieces, -0.22, 0.18)
    return jnp.clip(entries, -reach, reach).astype(held_as)


def setup_inputs(seed: int = 0) -> dict:
    streams_of = jax.random.split(jax.random.key(seed), 19)
    return {
        "tokens": scatter_about(streams_of[0], (PACKS, LEN, D), 1.0, 6.0, ((0, 8), (1, 4))),
        "layer_vectors": scatter_about(streams_of[1], (PACKS, LEN, PLD), 1.0, 6.0, ((0, 8), (1, 4))),
        "doc_lengths": jax.vmap(lambda own: uneven_parts(own, DOCS, LEN, LEN - TOK_DEV + 1, 2))(jax.random.split(streams_of[2], PACKS)).reshape((PACKS, DOCS)).astype(jnp.int32),
        "cotangent": scatter_about(streams_of[3], (PACKS, LEN, D), 1.0, 6.0, ((0, 8), (1, 4))),
        "tile_owner": draw_tile_owner(jax.random.fold_in(streams_of[18], 71), 0),
        "tile_master": draw_tile_master(jax.random.fold_in(streams_of[18], 71), 0),
        "tile_first": draw_tile_first(jax.random.fold_in(streams_of[18], 71), 0),
        "tile_second": draw_tile_second(jax.random.fold_in(streams_of[18], 71), 0),
        "left_basis": draw_left_basis(jax.random.fold_in(streams_of[18], 71), 0),
        "right_basis": draw_right_basis(jax.random.fold_in(streams_of[18], 71), 0),
        "small_master": draw_small_master(jax.random.fold_in(streams_of[18], 71), 0),
        "small_first": draw_small_first(jax.random.fold_in(streams_of[18], 71), 0),
        "small_second": draw_small_second(jax.random.fold_in(streams_of[18], 71), 0),
        "small_left": draw_small_left(jax.random.fold_in(streams_of[18], 71), 0),
        "small_right": draw_small_right(jax.random.fold_in(streams_of[18], 71), 0),
        "gains": jnp.clip(1.0 + 0.15 * jax.random.normal(streams_of[15], (NG,), jnp.float32), 0.25, 1.75),
        "gain_first": draw_gain_first(jax.random.fold_in(streams_of[18], 71), 0),
        "gain_second": draw_gain_second(jax.random.fold_in(streams_of[18], 71), 0),
    }


EPS = 1e-06
SCALE = 0.0625
THETA = 1000000.0
ROOT_HALF = 0.7071067811865476
BETA_ONE = 0.5
BETA_TWO = 0.5
ADAM_EPS = 1e-08
RATE_TILE = 0.02
RATE_SMALL = 0.04
RATE_GAIN = 0.3
DECAY = 0.01
NEGATIVE = -1e+30
HIGHEST = lax.Precision.HIGHEST

@jax.custom_vjp
def low(v):
    return lax.optimization_barrier(v.astype(jnp.bfloat16)).astype(jnp.float32)

@jax.custom_vjp
def low_back(v):
    return v

def low_keep(v):
    return (low(v), None)

def low_pass(kept, grad):
    return (grad,)

def back_keep(v):
    return (v, None)

def back_low(kept, grad):
    return (low(grad),)
low.defvjp(low_keep, low_pass)
low_back.defvjp(back_keep, back_low)

def product(left, right):
    return jnp.dot(left, right, precision=HIGHEST, preferred_element_type=jnp.float32)

def rms_norm(value, gain):
    return value * lax.rsqrt(lax.optimization_barrier(jnp.mean(value * value, axis=-1, keepdims=True)) + EPS) * gain

def rotary(value, position):
    half = value.shape[-1] // 2
    freq = THETA ** (-2.0 * jnp.arange(half).astype(jnp.float32) / value.shape[-1])
    angle = position.astype(jnp.float32)[:, None] * freq[None, :]
    cosine = jnp.cos(angle)[:, None, :]
    sine = jnp.sin(angle)[:, None, :]
    first = value[..., :half]
    second = value[..., half:]
    return jnp.concatenate([first * cosine - second * sine, second * cosine + first * sine], axis=-1)

def documents(lengths, length):
    places = jnp.arange(length).astype(jnp.int32)
    ends = jnp.cumsum(lengths).astype(jnp.int32)
    passed = places[:, None] >= ends[None, :]
    segment = lax.optimization_barrier(jnp.sum(passed.astype(jnp.int32), axis=1)).astype(jnp.int32)
    before = lax.optimization_barrier(jnp.sum(jnp.where(passed, lengths[None, :], 0), axis=1)).astype(jnp.int32)
    return (segment, (places - before).astype(jnp.int32))

def assemble(tiles, row_blocks):
    size = tiles.shape[1]
    column_blocks = tiles.shape[0] // row_blocks
    return tiles.reshape(row_blocks, column_blocks, size, size).transpose(0, 2, 1, 3).reshape(row_blocks * size, column_blocks * size)

def split_tiles(matrix, size):
    row_blocks = matrix.shape[0] // size
    column_blocks = matrix.shape[1] // size
    return matrix.reshape(row_blocks, size, column_blocks, size).transpose(0, 2, 1, 3).reshape(row_blocks * column_blocks, size, size)

def rotate_update(grad, master, first, second, left, right, rate):
    turned = jnp.einsum('bki,bkj->bij', left, jnp.einsum('bkl,blj->bkj', grad, right, precision=HIGHEST), precision=HIGHEST)
    first_new = BETA_ONE * first + (1.0 - BETA_ONE) * turned
    second_new = BETA_TWO * second + (1.0 - BETA_TWO) * turned * turned
    correct_one = 1.0 - BETA_ONE ** STEP
    correct_two = 1.0 - BETA_TWO ** STEP
    direction = first_new / correct_one / (jnp.sqrt(second_new / correct_two) + ADAM_EPS)
    back = jnp.einsum('bik,bkj->bij', left, jnp.einsum('bkl,bjl->bkj', direction, right, precision=HIGHEST), precision=HIGHEST)
    return (master - rate * (back + DECAY * master), first_new, second_new)

def layer(stream, vectors, table, small, gain_low, segment, position):
    width = stream.shape[1]
    length = stream.shape[0]
    query_width = HEADS * HEAD_DIM
    key_width = KV_HEADS * HEAD_DIM
    out_start = query_width + 2 * key_width
    ffn_start = out_start + query_width
    down_start = ffn_start + 2 * FF
    w_query = table[:, :query_width]
    w_key = table[:, query_width:query_width + key_width]
    w_value = table[:, query_width + key_width:out_start]
    w_out = table[:, out_start:ffn_start]
    w_gate = table[:, ffn_start:ffn_start + FF]
    w_up = table[:, ffn_start + FF:down_start]
    w_down = table[:, down_start:down_start + FF]
    laurel_left = small[:, :RANK]
    laurel_right = small[:, RANK:2 * RANK]
    vector_gate = small[:, 2 * RANK:2 * RANK + PLD]
    vector_proj = small[:, 2 * RANK + PLD:]
    gain_in = gain_low[0:width]
    gain_attn = gain_low[width:2 * width]
    gain_laurel = gain_low[2 * width:3 * width]
    gain_pre = gain_low[3 * width:4 * width]
    gain_post = gain_low[4 * width:5 * width]
    gain_vec = gain_low[5 * width:6 * width]
    gain_query = gain_low[6 * width:6 * width + HEAD_DIM]
    gain_key = gain_low[6 * width + HEAD_DIM:6 * width + 2 * HEAD_DIM]
    normed = rms_norm(stream, gain_in)
    normed_low = low(normed)
    query_pre = low_back(product(normed_low, w_query))
    key_pre = low_back(product(normed_low, w_key))
    value_pre = low_back(product(normed_low, w_value))
    query_rot = rotary(rms_norm(query_pre.reshape(length, HEADS, HEAD_DIM), gain_query), position)
    key_rot = rotary(rms_norm(key_pre.reshape(length, KV_HEADS, HEAD_DIM), gain_key), position)
    query_send = low_back(low(query_rot))
    per_device = HEADS // N_SEQ
    group = HEADS // KV_HEADS
    picks = [copy * per_device // group for copy in range(N_SEQ)]
    keys_low = low(key_rot)
    values_low = low(value_pre.reshape(length, KV_HEADS, HEAD_DIM))
    key_copies = low_back(jnp.stack([keys_low[:, pick] for pick in picks], axis=1))
    value_copies = low_back(jnp.stack([values_low[:, pick] for pick in picks], axis=1))
    key_heads = jnp.stack([key_copies[:, head // per_device] for head in range(HEADS)], axis=1)
    value_heads = jnp.stack([value_copies[:, head // per_device] for head in range(HEADS)], axis=1)
    block = min(512, length)
    count = length // block
    places = jnp.arange(length).astype(jnp.int32)
    starts = (jnp.arange(count) * block).astype(jnp.int32)

    def attend(args):
        query, first = args
        row_places = first + jnp.arange(block).astype(jnp.int32)
        row_segment = lax.dynamic_slice_in_dim(segment, first, block)
        allow = (row_segment[:, None] == segment[None, :]) & (places[None, :] <= row_places[:, None])
        raw = low_back(jnp.einsum('qhd,khd->qhk', query, key_heads, precision=HIGHEST)) * SCALE
        prob = jax.nn.softmax(jnp.where(allow[:, None, :], raw, NEGATIVE), axis=-1)
        return jnp.einsum('qhk,khd->qhd', low(prob), value_heads, precision=HIGHEST)
    attended = lax.map(jax.checkpoint(attend), (query_send.reshape(count, block, HEADS, HEAD_DIM), starts))
    attended = low(low_back(attended.reshape(length, query_width)))
    attn_pre = low_back(product(attended, w_out.T))
    first_sum = stream + rms_norm(attn_pre, gain_attn)
    left_pre = low_back(product(normed_low, laurel_left))
    left_low = low(left_pre)
    right_pre = low_back(product(left_low, laurel_right.T))
    second_sum = (first_sum + normed + rms_norm(right_pre, gain_laurel)) * ROOT_HALF
    feed_low = low(rms_norm(second_sum, gain_pre))
    gate_pre = low_back(product(feed_low, w_gate))
    up_pre = low_back(product(feed_low, w_up))
    hidden_low = low(jax.nn.gelu(gate_pre, approximate=True) * up_pre)
    down_pre = low_back(product(hidden_low, w_down.T))
    third_sum = second_sum + rms_norm(down_pre, gain_post)
    third_low = low(third_sum)
    vector_pre = low_back(product(third_low, vector_gate))
    vector_low = low(jax.nn.gelu(vector_pre, approximate=True) * vectors)
    proj_pre = low_back(product(vector_low, vector_proj.T))
    return third_sum + rms_norm(proj_pre, gain_vec)

def reference(tokens, layer_vectors, doc_lengths, cotangent, tile_owner, tile_master, tile_first, tile_second, left_basis, right_basis, small_master, small_first, small_second, small_left, small_right, gains, gain_first, gain_second):
    row_blocks = D // TILE
    placed = jnp.zeros_like(tile_master).at[tile_owner].set(low(tile_master))
    table = assemble(placed, row_blocks)
    small = assemble(low(small_master), row_blocks)
    gain_low = low(gains)

    def one_pack(carry, inputs):
        table_sum, small_sum, gain_sum = carry
        stream, vectors, lengths, grad_out = inputs
        segment, position = documents(lengths, LEN)

        def forward(stream_in, table_in, small_in, gain_in):
            return layer(stream_in, vectors, table_in, small_in, gain_in, segment, position)
        result, pull = jax.vjp(forward, stream, table, small, gain_low)
        grad_stream, grad_table, grad_small, grad_gain = pull(grad_out)
        return ((table_sum + grad_table, small_sum + grad_small, gain_sum + grad_gain), (result.astype(jnp.bfloat16), grad_stream))
    start = (jnp.zeros(table.shape, jnp.float32), jnp.zeros(small.shape, jnp.float32), jnp.zeros(gain_low.shape, jnp.float32))
    (grad_table, grad_small, grad_gain), (outputs, input_grad) = lax.scan(one_pack, start, (tokens.astype(jnp.float32), layer_vectors.astype(jnp.float32), doc_lengths, cotangent.astype(jnp.float32)))
    tile_grad = split_tiles(grad_table, TILE)[tile_owner]
    small_grad = split_tiles(grad_small, TILE)
    tile_new, tile_first_new, tile_second_new = rotate_update(tile_grad, tile_master, tile_first, tile_second, left_basis, right_basis, RATE_TILE)
    small_new, small_first_new, small_second_new = rotate_update(small_grad, small_master, small_first, small_second, small_left, small_right, RATE_SMALL)
    gain_first_new = BETA_ONE * gain_first + (1.0 - BETA_ONE) * grad_gain
    gain_second_new = BETA_TWO * gain_second + (1.0 - BETA_TWO) * grad_gain * grad_gain
    correct_one = 1.0 - BETA_ONE ** STEP
    correct_two = 1.0 - BETA_TWO ** STEP
    gain_new = gains - RATE_GAIN * (gain_first_new / correct_one) / (jnp.sqrt(gain_second_new / correct_two) + ADAM_EPS)
    return (outputs, input_grad, tile_new, tile_first_new, tile_second_new, small_new, small_first_new, small_second_new, gain_new, gain_first_new, gain_second_new)
```

```python
import math

import jax
import jax.numpy as jnp
from jax import lax
from jax.experimental import pallas as pl
from jax.experimental.pallas import tpu as pltpu
from jax.sharding import PartitionSpec as P

HEADS = 8
KV_HEADS = 2
HEAD_DIM = 256
FF = 8192
RANK = 64
PLD = 256
STEP = 5


EPS = 1e-06
SCALE = 0.0625
THETA = 1000000.0
ROOT_HALF = 0.7071067811865476
BETA_ONE = 0.5
BETA_TWO = 0.5
ADAM_EPS = 1e-08
RATE_TILE = 0.02
RATE_SMALL = 0.04
RATE_GAIN = 0.3
DECAY = 0.01
NEGATIVE = -1e30
HIGHEST = lax.Precision.HIGHEST


def rms_norm(value, gain):
    return value * lax.rsqrt(jnp.mean(value * value, axis=-1, keepdims=True) + EPS) * gain


def rotary(value, position):
    half = value.shape[-1] // 2
    freq = THETA ** (-2.0 * jnp.arange(half).astype(jnp.float32) / value.shape[-1])
    angle = position.astype(jnp.float32)[:, None] * freq[None, :]
    cosine = jnp.cos(angle)[:, None, :]
    sine = jnp.sin(angle)[:, None, :]
    first = value[..., :half]
    second = value[..., half:]
    return jnp.concatenate(
        [first * cosine - second * sine, second * cosine + first * sine], axis=-1
    )


def documents(lengths, length):
    places = jnp.arange(length)
    ends = jnp.cumsum(lengths)
    passed = places[:, None] >= ends[None, :]
    segment = jnp.sum(passed.astype(jnp.int32), axis=1)
    before = jnp.sum(jnp.where(passed, lengths[None, :], 0), axis=1)
    return (segment, places - before)


def matmul(left, right):
    return jnp.dot(left, right, preferred_element_type=jnp.float32)


def matmul_flip(left, right):
    return lax.dot_general(
        left, right, (((1,), (1,)), ((), ())), preferred_element_type=jnp.float32
    )


def matmul_outer(left, right):
    return lax.dot_general(
        left, right, (((0,), (0,)), ((), ())), preferred_element_type=jnp.float32
    )


def assemble(tiles, row_blocks):
    size = tiles.shape[1]
    column_blocks = tiles.shape[0] // row_blocks
    return (
        tiles.reshape(row_blocks, column_blocks, size, size)
        .transpose(0, 2, 1, 3)
        .reshape(row_blocks * size, column_blocks * size)
    )


def split_tiles(matrix, size):
    row_blocks = matrix.shape[0] // size
    column_blocks = matrix.shape[1] // size
    return (
        matrix.reshape(row_blocks, size, column_blocks, size)
        .transpose(0, 2, 1, 3)
        .reshape(row_blocks * column_blocks, size, size)
    )


def gelu_product(first, second):
    return jax.nn.gelu(first, approximate=True) * second


def rotate_update(grad, master, first, second, left, right, rate):
    turned = jnp.einsum(
        "bki,bkj->bij",
        left,
        jnp.einsum("bkl,blj->bkj", grad, right, precision=HIGHEST),
        precision=HIGHEST,
    )
    first_new = BETA_ONE * first + (1.0 - BETA_ONE) * turned
    second_new = BETA_TWO * second + (1.0 - BETA_TWO) * turned * turned
    correct_one = 1.0 - BETA_ONE**STEP
    correct_two = 1.0 - BETA_TWO**STEP
    direction = first_new / correct_one / (jnp.sqrt(second_new / correct_two) + ADAM_EPS)
    back = jnp.einsum(
        "bik,bkj->bij",
        left,
        jnp.einsum("bkl,bjl->bkj", direction, right, precision=HIGHEST),
        precision=HIGHEST,
    )
    return (master - rate * (back + DECAY * master), first_new, second_new)


def room(count, share):
    mean = count * share
    return math.ceil(mean + 3.6 * math.sqrt(mean * (1.0 - share)) + 3.0)


def count_earlier(group, valid):
    size = group.shape[-1]
    order = jnp.arange(size)
    same = (group[..., :, None] == group[..., None, :]) & valid[..., None, :]
    same = same & (order[None, :] < order[:, None])
    return jnp.sum(same.astype(jnp.int32), axis=-1)


def pick(match, value):
    return jnp.sum(jnp.where(match, value, 0), axis=-1)


def tile_kernel_call(kernel, index, arrays, out_shape):
    return pl.pallas_call(
        kernel,
        out_shape=out_shape,
        in_specs=[pl.BlockSpec(memory_space=pltpu.SMEM)]
        + [pl.BlockSpec(memory_space=pl.ANY)] * len(arrays),
        out_specs=jax.tree.map(lambda _: pl.BlockSpec(memory_space=pl.ANY), out_shape),
        scratch_shapes=[pltpu.SemaphoreType.DMA],
    )(index, *arrays)


def gather_tiles(arrays, index):
    tile = arrays[0].shape[-1]
    count = index.shape[0]

    def kernel(index_ref, *refs):
        sources, out, sem = refs[:-2], refs[-2], refs[-1]

        def step(i, carry):
            place = index_ref[i]
            start = 0
            for ref in sources:
                size = ref.shape[0]

                @pl.when((place >= start) & (place < start + size))
                def _(ref=ref, start=start):
                    pltpu.make_async_copy(ref.at[place - start], out.at[i], sem).start()

                start = start + size
            return carry

        lax.fori_loop(0, count, step, 0)
        pltpu.make_async_copy(out, out, sem).wait()

    total = sum(array.shape[0] for array in arrays)
    index = jnp.clip(index, 0, total - 1)
    out_shape = jax.ShapeDtypeStruct((count, tile, tile), arrays[0].dtype)
    return tile_kernel_call(kernel, index, arrays, out_shape)


def join_tiles(tiles, index, row_blocks, first_columns, second_columns):
    tile = tiles.shape[-1]
    first_count = row_blocks * first_columns

    def kernel(index_ref, source, first, second, sem):
        for out, start, columns in ((first, 0, first_columns), (second, first_count, second_columns)):

            def step(row, carry, out=out, start=start, columns=columns):
                for column in range(columns):
                    place = index_ref[start + row * columns + column]
                    pltpu.make_async_copy(
                        source.at[place],
                        out.at[pl.ds(row * tile, tile), pl.ds(column * tile, tile)],
                        sem,
                    ).start()
                return carry

            lax.fori_loop(0, row_blocks, step, 0)
        pltpu.make_async_copy(first, first, sem).wait()
        pltpu.make_async_copy(second, second, sem).wait()

    index = jnp.clip(index, 0, tiles.shape[0] - 1)
    out_shape = (
        jax.ShapeDtypeStruct((row_blocks * tile, first_columns * tile), tiles.dtype),
        jax.ShapeDtypeStruct((row_blocks * tile, second_columns * tile), tiles.dtype),
    )
    return tile_kernel_call(kernel, index, [tiles], out_shape)


def cut_tiles(first, second, index, tile):
    row_blocks = first.shape[0] // tile
    first_columns = first.shape[1] // tile
    second_columns = second.shape[1] // tile
    first_count = row_blocks * first_columns
    count = index.shape[0]

    def kernel(index_ref, first_ref, second_ref, out, sem):
        def step(i, carry):
            place = index_ref[i]

            def send(ref, local, columns):
                row = pl.multiple_of((local // columns) * tile, tile)
                column = pl.multiple_of((local % columns) * tile, tile)
                pltpu.make_async_copy(
                    ref.at[pl.ds(row, tile), pl.ds(column, tile)], out.at[i], sem
                ).start()

            @pl.when(place < first_count)
            def _():
                send(first_ref, place, first_columns)

            @pl.when(place >= first_count)
            def _():
                send(second_ref, place - first_count, second_columns)

            return carry

        lax.fori_loop(0, count, step, 0)
        pltpu.make_async_copy(out, out, sem).wait()

    index = jnp.clip(index, 0, first_count + row_blocks * second_columns - 1)
    out_shape = jax.ShapeDtypeStruct((count, tile, tile), first.dtype)
    return tile_kernel_call(kernel, index, [first, second], out_shape)


def seq_swap(value, flip):
    size = lax.axis_size("seq")
    return lax.ppermute(value, "seq", [(i, i ^ flip) for i in range(size)])


def core_swap(value):
    size = lax.axis_size("fsdp")
    return lax.ppermute(value, "fsdp", [(i, i ^ 1) for i in range(size)])


def chip_shift(value, offset):
    size = lax.axis_size("fsdp")
    chips = size // 2
    return lax.ppermute(
        value, "fsdp", [(i, (i // 2 + offset) % chips * 2 + i % 2) for i in range(size)]
    )


def seq_gather(value):
    size = lax.axis_size("seq")
    return jnp.concatenate([value] + [seq_swap(value, flip) for flip in range(1, size)], axis=0)


def seq_exchange(value):
    size = lax.axis_size("seq")
    parts = [value[0]] + [seq_swap(value[flip], flip) for flip in range(1, size)]
    return jnp.stack(parts, axis=0)


def seq_sum(value):
    size = lax.axis_size("seq")
    rows = value.shape[0] // size
    parts = value.reshape(size, rows, value.shape[1])
    low = parts.astype(jnp.bfloat16)
    total = parts[0]
    for flip in range(1, size):
        total = total + seq_swap(low[flip], flip).astype(jnp.float32)
    return total


def chip_exchange(value):
    chips = value.shape[0]
    parts = [value[0]] + [chip_shift(value[offset], offset) for offset in range(1, chips)]
    return jnp.stack(parts, axis=0)


def on_device(
    tokens,
    layer_vectors,
    doc_lengths,
    cotangent,
    tile_owner,
    tile_master,
    tile_first,
    tile_second,
    left_basis,
    right_basis,
    small_master,
    small_first,
    small_second,
    small_left,
    small_right,
    gains,
    gain_first,
    gain_second,
):
    bf16 = jnp.bfloat16
    f32 = jnp.float32
    tile = tile_master.shape[1]
    width = tokens.shape[2]
    row_blocks = width // tile
    rows = tokens.shape[1]
    seq_size = lax.axis_size("seq")
    fsdp_size = lax.axis_size("fsdp")
    chips = fsdp_size // 2
    mine = tile_master.shape[0]
    tiles = tile_owner.shape[0]
    length = rows * seq_size
    per_device = HEADS // seq_size
    per_key = seq_size // KV_HEADS
    query_width = HEADS * HEAD_DIM
    key_width = KV_HEADS * HEAD_DIM
    my_seq = lax.axis_index("seq")
    my_fsdp = lax.axis_index("fsdp")
    my_chip = my_fsdp // 2
    my_core = my_fsdp % 2
    flips = jnp.arange(seq_size)
    shifts = jnp.arange(chips)

    query_blocks = query_width // tile
    key_blocks = key_width // tile
    ffn_blocks = FF // tile
    query_each = query_blocks // seq_size
    head_blocks = HEAD_DIM // tile
    ffn_each = ffn_blocks // fsdp_size
    columns = tiles // row_blocks
    attn_first = query_each + head_blocks
    attn_count = row_blocks * (attn_first + query_each)
    ffn_first = 2 * ffn_each
    ffn_count = row_blocks * 3 * ffn_each
    attn_share = (2 * query_blocks + 2 * key_blocks) / columns
    ffn_share = 3 * ffn_blocks / columns
    attn_room = room(mine, attn_share / seq_size)
    attn_hold = room(attn_count, 1.0 / fsdp_size)
    ffn_room = (room(2 * mine, ffn_share / chips) + 1) // 2
    ffn_hold = room(ffn_count, 1.0 / seq_size)

    def tile_places(owner):
        row = owner // columns
        column = owner % columns
        key_at = column - query_blocks
        value_at = key_at - key_blocks
        out_at = value_at - key_blocks
        ffn_at = out_at - query_blocks
        is_attn = ffn_at < 0
        kind = ffn_at // ffn_blocks
        ffn_column = ffn_at % ffn_blocks
        ffn_to = jnp.where(is_attn, -1, ffn_column // ffn_each)
        ffn_local = ffn_column % ffn_each
        ffn_place = jnp.where(
            kind == 2,
            row_blocks * ffn_first + row * ffn_each + ffn_local,
            row * ffn_first + kind * ffn_each + ffn_local,
        )
        attn_to = jnp.where(
            key_at < 0,
            column // query_each,
            jnp.where(
                value_at < 0,
                key_at // head_blocks * per_key,
                jnp.where(
                    out_at < 0,
                    value_at // head_blocks * per_key + per_key - 1,
                    out_at // query_each,
                ),
            ),
        )
        attn_place = jnp.where(
            key_at < 0,
            row * attn_first + column % query_each,
            jnp.where(
                out_at < 0,
                row * attn_first + query_each + key_at % head_blocks,
                row_blocks * attn_first + row * query_each + out_at % query_each,
            ),
        )
        attn_to = jnp.where(is_attn, attn_to, -1)
        return (ffn_to, ffn_place, attn_to, attn_place)

    owners = tile_owner.reshape(seq_size, fsdp_size, mine)
    ffn_to, ffn_place, attn_to, attn_place = tile_places(owners)
    slot_seq = jnp.arange(seq_size)[:, None, None]
    slot_fsdp = jnp.arange(fsdp_size)[None, :, None]
    slot_chip = slot_fsdp // 2
    ffn_chip = jnp.where(ffn_to < 0, -1, ffn_to // 2)
    chip_view = ffn_chip.reshape(seq_size, chips, 2 * mine)
    chip_rank = count_earlier(chip_view, chip_view >= 0).reshape(owners.shape)
    seq_view = ffn_to.reshape(seq_size, fsdp_size * mine)
    ffn_rank = count_earlier(seq_view, seq_view >= 0).reshape(owners.shape)
    attn_rank = count_earlier(attn_to, attn_to >= 0)
    fsdp_view = attn_to.transpose(1, 0, 2).reshape(fsdp_size, seq_size * mine)
    attn_order = (
        count_earlier(fsdp_view, fsdp_view >= 0)
        .reshape(fsdp_size, seq_size, mine)
        .transpose(1, 0, 2)
    )
    fits = jnp.all(
        jnp.where(
            ffn_to < 0,
            (attn_rank < attn_room) & (attn_order < attn_hold),
            (chip_rank < 2 * ffn_room) & (ffn_rank < ffn_hold),
        )
    )
    half = chips * ffn_room
    rank_core = chip_rank // ffn_room
    rank_local = chip_rank % ffn_room
    out_place = (
        jnp.where(rank_core == my_core, 0, half)
        + (my_chip - slot_chip) % chips * ffn_room
        + rank_local
    )
    back_place = (
        jnp.where(rank_core == my_core, 0, half) + (my_chip - ffn_chip) % chips * ffn_room + rank_local
    )
    my_chip_slots = lax.dynamic_slice(
        jnp.stack([ffn_chip, chip_rank]), (0, my_seq, 2 * my_chip, 0), (2, 1, 2, mine)
    ).reshape(2, 2 * mine)
    my_slots = lax.dynamic_slice(
        jnp.stack([ffn_to, attn_to, attn_rank, back_place]),
        (0, my_seq, my_fsdp, 0),
        (4, 1, 1, mine),
    ).reshape(4, mine)
    seq_slots = lax.dynamic_slice(
        jnp.stack([ffn_to, ffn_rank, ffn_place, out_place, chip_rank, jnp.broadcast_to(slot_chip, owners.shape)]),
        (0, my_seq, 0, 0),
        (6, 1, fsdp_size, mine),
    ).reshape(6, fsdp_size * mine)
    fsdp_slots = lax.dynamic_slice(
        jnp.stack([attn_to, attn_order, attn_rank, jnp.broadcast_to(slot_seq, owners.shape)]),
        (0, 0, my_fsdp, 0),
        (4, seq_size, 1, mine),
    ).reshape(4, seq_size * mine)

    local_slots = jnp.arange(mine)
    attn_pack = pick(
        (my_slots[1][None, None, :] == (my_seq ^ flips)[:, None, None])
        & (my_slots[2][None, None, :] == jnp.arange(attn_room)[None, :, None]),
        local_slots,
    )
    attn_keep = pick(
        (fsdp_slots[0][None, :] == my_seq)
        & (fsdp_slots[1][None, :] == jnp.arange(attn_hold)[:, None]),
        (fsdp_slots[3] ^ my_seq) * attn_room + fsdp_slots[2],
    )
    attn_join = pick(
        (attn_to.reshape(1, -1) == my_seq)
        & (attn_place.reshape(1, -1) == jnp.arange(attn_count)[:, None]),
        (slot_fsdp * attn_hold + attn_order).reshape(1, -1),
    )
    ffn_pack = pick(
        (my_chip_slots[0][None, None, :] == ((my_chip + shifts) % chips)[:, None, None])
        & (
            my_chip_slots[1][None, None, :]
            == (my_core * ffn_room + jnp.arange(ffn_room))[None, :, None]
        ),
        jnp.arange(2 * mine) ^ 0,
    )
    ffn_pack = jnp.where(
        ffn_pack // mine == my_core, ffn_pack % mine, mine + ffn_pack % mine
    )
    ffn_keep = pick(
        (seq_slots[0][None, :] == my_fsdp) & (seq_slots[1][None, :] == jnp.arange(ffn_hold)[:, None]),
        seq_slots[3][None, :],
    )
    ffn_join = pick(
        (ffn_to.reshape(1, -1) == my_fsdp)
        & (ffn_place.reshape(1, -1) == jnp.arange(ffn_count)[:, None]),
        (slot_seq * ffn_hold + ffn_rank).reshape(1, -1),
    )
    master_low = tile_master.astype(bf16)
    attn_sent = gather_tiles([master_low], attn_pack.reshape(-1))
    attn_got = seq_exchange(attn_sent.reshape(seq_size, attn_room, tile, tile))
    attn_kept = gather_tiles([attn_got.reshape(-1, tile, tile)], attn_keep)
    attn_all = lax.all_gather(attn_kept, "fsdp", axis=0, tiled=True)
    w_first, w_out = join_tiles(attn_all, attn_join, row_blocks, attn_first, query_each)

    master_other = core_swap(master_low)
    ffn_sent = gather_tiles([master_low, master_other], ffn_pack.reshape(-1))
    ffn_got = chip_exchange(ffn_sent.reshape(chips, ffn_room, tile, tile)).reshape(-1, tile, tile)
    ffn_other = core_swap(ffn_got)
    ffn_kept = gather_tiles([ffn_got, ffn_other], ffn_keep)
    ffn_all = lax.all_gather(ffn_kept, "seq", axis=0, tiled=True)
    w_both, w_down = join_tiles(ffn_all, ffn_join, row_blocks, ffn_first, ffn_each)

    my_columns = jnp.arange(tiles)
    def slow_fetch(_, kept):
        whole = lax.all_gather(master_low, ("seq", "fsdp"), axis=0, tiled=True)
        slots = my_columns.reshape(1, -1)
        attn_slots = pick(
            (attn_to.reshape(1, -1) == my_seq)
            & (attn_place.reshape(1, -1) == jnp.arange(attn_count)[:, None]),
            slots,
        )
        ffn_slots = pick(
            (ffn_to.reshape(1, -1) == my_fsdp)
            & (ffn_place.reshape(1, -1) == jnp.arange(ffn_count)[:, None]),
            slots,
        )
        return join_tiles(whole, attn_slots, row_blocks, attn_first, query_each) + join_tiles(
            whole, ffn_slots, row_blocks, ffn_first, ffn_each
        )

    slow_steps = jnp.where(fits, 0, 1)
    w_first, w_out, w_both, w_down = lax.fori_loop(
        0, slow_steps, slow_fetch, (w_first, w_out, w_both, w_down)
    )

    small_got, gain_got = (
        lax.all_gather(small_master.astype(bf16), "seq", axis=0, tiled=True),
        lax.all_gather(gains.astype(bf16), "seq", axis=0, tiled=True),
    )
    small_table = assemble(small_got, row_blocks)
    gain_full = gain_got.astype(f32)
    gain_in = gain_full[0:width]
    gain_attn = gain_full[width : 2 * width]
    gain_laurel = gain_full[2 * width : 3 * width]
    gain_pre = gain_full[3 * width : 4 * width]
    gain_post = gain_full[4 * width : 5 * width]
    gain_vec = gain_full[5 * width : 6 * width]
    gain_query = gain_full[6 * width : 6 * width + HEAD_DIM]
    gain_key = gain_full[6 * width + HEAD_DIM : 6 * width + 2 * HEAD_DIM]
    laurel_left = small_table[:, :RANK]
    laurel_right = small_table[:, RANK : 2 * RANK]
    vector_gate_w = small_table[:, 2 * RANK : 2 * RANK + PLD]
    vector_proj_w = small_table[:, 2 * RANK + PLD :]

    pack_tokens = seq_gather(tokens[0])
    segment, position = documents(doc_lengths[0], length)
    places = ((my_seq ^ flips)[:, None] * rows + jnp.arange(rows)[None, :]).reshape(-1)

    def reorder(values):
        blocks = values.reshape(seq_size, rows)
        return jnp.concatenate(
            [lax.dynamic_index_in_dim(blocks, my_seq ^ i, 0, False) for i in range(seq_size)]
        )

    pack_segment = reorder(segment)
    pack_position = reorder(position)
    stream = tokens[0].astype(f32)
    vectors = layer_vectors[0].astype(f32)
    normed, normed_pull = jax.vjp(rms_norm, stream, gain_in)
    normed_low = normed.astype(bf16)
    pack_normed = rms_norm(pack_tokens.astype(f32), gain_in).astype(bf16)
    first_pre = matmul(pack_normed, w_first)
    is_key = my_seq % per_key == 0

    def shape_query(query_in, query_gain):
        return rotary(
            rms_norm(query_in.reshape(length, per_device, HEAD_DIM), query_gain), pack_position
        )

    def shape_key(key_in, key_gain):
        return rotary(rms_norm(key_in.reshape(length, 1, HEAD_DIM), key_gain), pack_position)

    query_pre = first_pre[:, : per_device * HEAD_DIM]
    other_pre = first_pre[:, per_device * HEAD_DIM :]
    query_rot, query_pull = jax.vjp(shape_query, query_pre, gain_query)
    key_rot, key_pull = jax.vjp(shape_key, other_pre, gain_key)
    query_heads = query_rot.astype(bf16)
    other_low = jnp.where(is_key, key_rot[:, 0, :], other_pre).astype(bf16)
    partner_low = seq_swap(other_low, 1).reshape(seq_size // 2, 2, rows, HEAD_DIM)
    partner_low = partner_low[:, ::-1].reshape(length, HEAD_DIM)
    key_single = jnp.where(is_key, other_low, partner_low)
    value_single = jnp.where(is_key, partner_low, other_low)

    allow = (pack_segment[:, None] == pack_segment[None, :]) & (
        places[None, :] <= places[:, None]
    )
    raw = (
        jnp.einsum("qhd,kd->qhk", query_heads, key_single, preferred_element_type=f32) * SCALE
    )
    scores = jnp.where(allow[:, None, :], raw, NEGATIVE)
    powers = jnp.exp(scores - jnp.max(scores, axis=-1, keepdims=True))
    prob = powers / jnp.sum(powers, axis=-1, keepdims=True)
    prob_low = prob.astype(bf16)
    attended_low = (
        jnp.einsum("qhk,kd->qhd", prob_low, value_single, preferred_element_type=f32)
        .astype(bf16)
        .reshape(length, per_device * HEAD_DIM)
    )
    attn_pre = seq_sum(matmul_flip(attended_low, w_out))
    attn_normed, attn_pull = jax.vjp(rms_norm, attn_pre, gain_attn)
    first_sum = stream + attn_normed
    left_pre = matmul(normed_low, laurel_left)
    left_low = left_pre.astype(bf16)
    right_pre = matmul_flip(left_low, laurel_right)
    laurel_normed, laurel_pull = jax.vjp(rms_norm, right_pre, gain_laurel)
    second_sum = (first_sum + normed + laurel_normed) * ROOT_HALF
    feed_normed, feed_pull = jax.vjp(rms_norm, second_sum, gain_pre)
    feed_low = lax.all_gather(feed_normed.astype(bf16), "fsdp", axis=0, tiled=True)
    both_pre = matmul(feed_low, w_both)
    ffn_width = w_down.shape[1]
    hidden, hidden_pull = jax.vjp(gelu_product, both_pre[:, :ffn_width], both_pre[:, ffn_width:])
    hidden_low = hidden.astype(bf16)
    down_pre = lax.psum_scatter(
        matmul_flip(hidden_low, w_down).astype(bf16), "fsdp", scatter_dimension=0, tiled=True
    ).astype(f32)
    down_normed, down_pull = jax.vjp(rms_norm, down_pre, gain_post)
    third_sum = second_sum + down_normed
    third_low = third_sum.astype(bf16)
    vector_pre = matmul(third_low, vector_gate_w)
    vector_gated, vector_pull = jax.vjp(lambda inner: gelu_product(inner, vectors), vector_pre)
    vector_low = vector_gated.astype(bf16)
    proj_pre = matmul_flip(vector_low, vector_proj_w)
    proj_normed, proj_pull = jax.vjp(rms_norm, proj_pre, gain_vec)
    result = third_sum + proj_normed
    output = result.astype(bf16)[None]

    grad_out = cotangent[0].astype(f32)
    grad_proj, grad_gain_vec = proj_pull(grad_out)
    proj_grad_low = grad_proj.astype(bf16)
    (grad_vector_pre,) = vector_pull(matmul(proj_grad_low, vector_proj_w))
    vector_grad_low = grad_vector_pre.astype(bf16)
    grad_third = grad_out + matmul_flip(vector_grad_low, vector_gate_w)
    grad_down, grad_gain_post = down_pull(grad_third)
    down_grad_low = lax.all_gather(grad_down.astype(bf16), "fsdp", axis=0, tiled=True)
    grad_gate, grad_up = hidden_pull(matmul(down_grad_low, w_down))
    both_grad_low = jnp.concatenate([grad_gate, grad_up], axis=1).astype(bf16)
    grad_feed = lax.psum_scatter(
        matmul_flip(both_grad_low, w_both).astype(bf16), "fsdp", scatter_dimension=0, tiled=True
    ).astype(f32)
    both_grad_w = matmul_outer(feed_low, both_grad_low).astype(bf16)
    down_grad_w = matmul_outer(down_grad_low, hidden_low).astype(bf16)

    grad_second_norm, grad_gain_pre = feed_pull(grad_feed)
    half_grad = (grad_third + grad_second_norm) * ROOT_HALF
    grad_right, grad_gain_laurel = laurel_pull(half_grad)
    right_grad_low = grad_right.astype(bf16)
    left_grad_low = matmul(right_grad_low, laurel_right).astype(bf16)
    grad_attn, grad_gain_attn = attn_pull(half_grad)
    attn_grad_low = seq_gather(grad_attn.astype(bf16))
    grad_attended = (
        matmul(attn_grad_low, w_out).astype(bf16).reshape(length, per_device, HEAD_DIM)
    )
    out_grad_w = matmul_outer(attn_grad_low, attended_low).astype(bf16)
    value_grad = jnp.einsum("qhk,qhd->kd", prob_low, grad_attended, preferred_element_type=f32)
    grad_prob = jnp.einsum("qhd,kd->qhk", grad_attended, value_single, preferred_element_type=f32)
    inner = jnp.sum(prob * grad_prob, axis=-1, keepdims=True)
    grad_score = (prob * (grad_prob - inner)).astype(bf16)
    grad_query = (
        jnp.einsum("qhk,kd->qhd", grad_score, key_single, preferred_element_type=f32) * SCALE
    ).astype(bf16)
    key_grad = (
        jnp.einsum("qhk,qhd->kd", grad_score, query_heads, preferred_element_type=f32) * SCALE
    ).astype(bf16)
    value_grad = value_grad.astype(bf16)
    partner_grad = seq_swap(jnp.where(is_key, value_grad, key_grad), 1)
    partner_grad = partner_grad.reshape(seq_size // 2, 2, rows, HEAD_DIM)[:, ::-1]
    other_grad = jnp.where(is_key, key_grad, value_grad).astype(f32) + partner_grad.reshape(
        length, HEAD_DIM
    ).astype(f32)
    grad_query_pre, grad_gain_query = query_pull(grad_query.astype(f32))
    grad_key_pre, grad_gain_key = key_pull(other_grad[:, None, :])
    grad_gain_key = jnp.where(is_key, grad_gain_key, 0.0)
    first_grad_low = jnp.concatenate(
        [grad_query_pre, jnp.where(is_key, grad_key_pre, other_grad)], axis=1
    ).astype(bf16)
    first_grad_w = matmul_outer(pack_normed, first_grad_low).astype(bf16)
    grad_normed = (
        half_grad
        + matmul_flip(left_grad_low, laurel_left)
        + seq_sum(matmul_flip(first_grad_low, w_first))
    )
    grad_stream_norm, grad_gain_in = normed_pull(grad_normed)
    input_grad = (half_grad + grad_stream_norm)[None]

    ffn_cut = pick(
        (ffn_to.reshape(seq_size, 1, -1) == my_fsdp)
        & (ffn_rank.reshape(seq_size, 1, -1) == jnp.arange(ffn_hold)[None, :, None]),
        ffn_place.reshape(seq_size, 1, -1),
    )
    ffn_back = pick(
        (seq_slots[5][None, None, :] == ((my_chip + shifts) % chips)[:, None, None])
        & (seq_slots[0][None, None, :] // 2 == my_chip)
        & (seq_slots[0][None, None, :] >= 0)
        & (seq_slots[4][None, None, :] == (my_core * ffn_room + jnp.arange(ffn_room))[None, :, None]),
        jnp.where(seq_slots[0] == my_fsdp, 0, ffn_hold) + seq_slots[1],
    )
    ffn_parts = cut_tiles(both_grad_w, down_grad_w, ffn_cut.reshape(-1), tile)
    ffn_sum = lax.psum_scatter(ffn_parts, "seq", scatter_dimension=0, tiled=True)
    ffn_sum_other = core_swap(ffn_sum)
    ffn_return = gather_tiles([ffn_sum, ffn_sum_other], ffn_back.reshape(-1))
    ffn_returned = chip_exchange(ffn_return.reshape(chips, ffn_room, tile, tile))
    ffn_returned = ffn_returned.reshape(-1, tile, tile)
    ffn_returned_other = core_swap(ffn_returned)

    attn_cut = pick(
        (attn_to.transpose(1, 0, 2).reshape(fsdp_size, 1, -1) == my_seq)
        & (
            attn_order.transpose(1, 0, 2).reshape(fsdp_size, 1, -1)
            == jnp.arange(attn_hold)[None, :, None]
        ),
        attn_place.transpose(1, 0, 2).reshape(fsdp_size, 1, -1),
    )
    attn_back = pick(
        (fsdp_slots[3][None, None, :] == (my_seq ^ flips)[:, None, None])
        & (fsdp_slots[0][None, None, :] == my_seq)
        & (fsdp_slots[2][None, None, :] == jnp.arange(attn_room)[None, :, None]),
        fsdp_slots[1],
    )
    attn_parts = cut_tiles(first_grad_w, out_grad_w, attn_cut.reshape(-1), tile)
    attn_sum = lax.psum_scatter(attn_parts, "fsdp", scatter_dimension=0, tiled=True)
    attn_return = gather_tiles([attn_sum], attn_back.reshape(-1))
    attn_returned = seq_exchange(attn_return.reshape(seq_size, attn_room, tile, tile))
    slot_grad = jnp.where(
        my_slots[0] >= 0,
        my_slots[3],
        2 * half + (my_slots[1] ^ my_seq) * attn_room + my_slots[2],
    )
    tile_grad_low = gather_tiles(
        [ffn_returned, ffn_returned_other, attn_returned.reshape(-1, tile, tile)], slot_grad
    )

    def slow_return(_, kept):
        ffn_parts = split_tiles(both_grad_w, tile), split_tiles(down_grad_w, tile)
        attn_parts = split_tiles(first_grad_w, tile), split_tiles(out_grad_w, tile)
        parts = jnp.concatenate(ffn_parts + attn_parts + (jnp.zeros((1, tile, tile), bf16),))
        index = jnp.where(
            ffn_to == my_fsdp,
            ffn_place,
            jnp.where(attn_to == my_seq, ffn_count + attn_place, ffn_count + attn_count),
        )
        spread = gather_tiles([parts], index.reshape(-1))
        return lax.psum_scatter(spread, ("seq", "fsdp"), scatter_dimension=0, tiled=True)

    tile_grad = lax.fori_loop(0, slow_steps, slow_return, tile_grad_low).astype(f32)

    small_full = jnp.concatenate(
        [
            matmul_outer(normed_low, left_grad_low),
            matmul_outer(right_grad_low, left_low),
            matmul_outer(third_low, vector_grad_low),
            matmul_outer(proj_grad_low, vector_low),
        ],
        axis=1,
    )
    small_tiles_grad = split_tiles(small_full, tile)
    gain_grad = jnp.concatenate(
        [
            grad_gain_in,
            grad_gain_attn,
            grad_gain_laurel,
            grad_gain_pre,
            grad_gain_post,
            grad_gain_vec,
            grad_gain_query,
            grad_gain_key,
        ]
    )
    small_part = lax.psum_scatter(
        small_tiles_grad.astype(bf16), "seq", scatter_dimension=0, tiled=True
    )
    small_grad = lax.psum(small_part, "fsdp").astype(f32)
    whole_gain = lax.psum(gain_grad.astype(bf16), "fsdp")
    gain_grad_mine = lax.psum_scatter(whole_gain, "seq", scatter_dimension=0, tiled=True).astype(f32)
    tile_new, tile_first_new, tile_second_new = rotate_update(
        tile_grad, tile_master, tile_first, tile_second, left_basis, right_basis, RATE_TILE
    )
    small_new, small_first_new, small_second_new = rotate_update(
        small_grad, small_master, small_first, small_second, small_left, small_right, RATE_SMALL
    )
    gain_first_new = BETA_ONE * gain_first + (1.0 - BETA_ONE) * gain_grad_mine
    gain_second_new = BETA_TWO * gain_second + (1.0 - BETA_TWO) * gain_grad_mine * gain_grad_mine
    correct_one = 1.0 - BETA_ONE**STEP
    correct_two = 1.0 - BETA_TWO**STEP
    gain_new = gains - RATE_GAIN * (gain_first_new / correct_one) / (
        jnp.sqrt(gain_second_new / correct_two) + ADAM_EPS
    )
    return (
        output,
        input_grad,
        tile_new,
        tile_first_new,
        tile_second_new,
        small_new,
        small_first_new,
        small_second_new,
        gain_new,
        gain_first_new,
        gain_second_new,
    )


def solution(mesh):
    return jax.shard_map(
        on_device,
        mesh=mesh,
        in_specs=(
            P("fsdp", "seq", None),
            P("fsdp", "seq", None),
            P("fsdp", None),
            P("fsdp", "seq", None),
            P(),
            P(("seq", "fsdp"), None, None),
            P(("seq", "fsdp"), None, None),
            P(("seq", "fsdp"), None, None),
            P(("seq", "fsdp"), None, None),
            P(("seq", "fsdp"), None, None),
            P("seq", None, None),
            P("seq", None, None),
            P("seq", None, None),
            P("seq", None, None),
            P("seq", None, None),
            P("seq"),
            P("seq"),
            P("seq"),
        ),
        out_specs=(
            P("fsdp", "seq", None),
            P("fsdp", "seq", None),
            P(("seq", "fsdp"), None, None),
            P(("seq", "fsdp"), None, None),
            P(("seq", "fsdp"), None, None),
            P("seq", None, None),
            P("seq", None, None),
            P("seq", None, None),
            P("seq"),
            P("seq"),
            P("seq"),
        ),
        check_vma=False,
    )
```

```python
import math

import jax
import jax.numpy as jnp
from jax import lax
from jax.experimental import pallas as pl
from jax.experimental.pallas import tpu as pltpu
from jax.sharding import PartitionSpec as P

HEADS = 8
KV_HEADS = 2
HEAD_DIM = 256
FF = 8192
RANK = 64
PLD = 256
STEP = 5


EPS = 1e-06
SCALE = 0.0625
THETA = 1000000.0
ROOT_HALF = 0.7071067811865476
BETA_ONE = 0.5
BETA_TWO = 0.5
ADAM_EPS = 1e-08
RATE_TILE = 0.02
RATE_SMALL = 0.04
RATE_GAIN = 0.3
DECAY = 0.01
NEGATIVE = -1e30
VMEM_BYTES = 32 * 1024 * 1024


def rms_norm(value, gain):
    return value * lax.rsqrt(jnp.mean(value * value, axis=-1, keepdims=True) + EPS) * gain


def rotary(value, position):
    half = value.shape[-1] // 2
    freq = THETA ** (-2.0 * jnp.arange(half).astype(jnp.float32) / value.shape[-1])
    angle = position.astype(jnp.float32)[:, None] * freq[None, :]
    cosine = jnp.cos(angle)[:, None, :]
    sine = jnp.sin(angle)[:, None, :]
    first = value[..., :half]
    second = value[..., half:]
    return jnp.concatenate(
        [first * cosine - second * sine, second * cosine + first * sine], axis=-1
    )


def documents(lengths, length):
    places = jnp.arange(length)
    ends = jnp.cumsum(lengths)
    passed = places[:, None] >= ends[None, :]
    segment = jnp.sum(passed.astype(jnp.int32), axis=1)
    before = jnp.sum(jnp.where(passed, lengths[None, :], 0), axis=1)
    return (segment, places - before)


def matmul(left, right):
    return jnp.dot(left, right, preferred_element_type=jnp.float32)


def matmul_flip(left, right):
    return lax.dot_general(
        left, right, (((1,), (1,)), ((), ())), preferred_element_type=jnp.float32
    )


def matmul_outer(left, right):
    return lax.dot_general(
        left, right, (((0,), (0,)), ((), ())), preferred_element_type=jnp.float32
    )


def assemble(tiles, row_blocks):
    size = tiles.shape[1]
    column_blocks = tiles.shape[0] // row_blocks
    return (
        tiles.reshape(row_blocks, column_blocks, size, size)
        .transpose(0, 2, 1, 3)
        .reshape(row_blocks * size, column_blocks * size)
    )


def split_tiles(matrix, size):
    row_blocks = matrix.shape[0] // size
    column_blocks = matrix.shape[1] // size
    return (
        matrix.reshape(row_blocks, size, column_blocks, size)
        .transpose(0, 2, 1, 3)
        .reshape(row_blocks * column_blocks, size, size)
    )


def gelu_product(first, second):
    return jax.nn.gelu(first, approximate=True) * second


def room(count, share):
    mean = count * share
    return math.ceil(mean + 3.6 * math.sqrt(mean * (1.0 - share)) + 3.0)


def count_earlier(group, valid):
    size = group.shape[-1]
    order = jnp.arange(size)
    same = (group[..., :, None] == group[..., None, :]) & valid[..., None, :]
    same = same & (order[None, :] < order[:, None])
    return jnp.sum(same.astype(jnp.int32), axis=-1)


def pick(match, value):
    return jnp.sum(jnp.where(match, value, 0), axis=-1)


def steps_of(count):
    for steps in range(4, 65):
        if count % steps == 0 and 16 <= count // steps <= 160:
            return steps
    return 2 if count % 2 == 0 else 1


def tile_kernel_call(kernel, index, arrays, out_shape, out_specs, steps):
    return pl.pallas_call(
        kernel,
        grid=(steps,),
        out_shape=out_shape,
        in_specs=[pl.BlockSpec(memory_space=pltpu.SMEM)]
        + [pl.BlockSpec(memory_space=pl.ANY)] * len(arrays),
        out_specs=out_specs,
        scratch_shapes=[pltpu.SemaphoreType.DMA],
        compiler_params=pltpu.CompilerParams(vmem_limit_bytes=VMEM_BYTES),
    )(index, *arrays)


def start_copy(sources, place, target, sem):
    start = 0
    for ref in sources:
        size = ref.shape[0]

        @pl.when((place >= start) & (place < start + size))
        def _(ref=ref, start=start):
            pltpu.make_async_copy(ref.at[place - start], target, sem).start()

        start = start + size


def gather_tiles(arrays, index):
    tile = arrays[0].shape[-1]
    count = index.shape[0]
    steps = steps_of(count)
    each = count // steps

    def kernel(index_ref, *refs):
        sources, out, sem = refs[:-2], refs[-2], refs[-1]
        base = pl.program_id(0) * each

        def step(i, carry):
            start_copy(sources, index_ref[base + i], out.at[i], sem)
            return carry

        lax.fori_loop(0, each, step, 0)
        pltpu.make_async_copy(out, out, sem).wait()

    total = sum(array.shape[0] for array in arrays)
    return tile_kernel_call(
        kernel,
        jnp.clip(index, 0, total - 1),
        arrays,
        jax.ShapeDtypeStruct((count, tile, tile), arrays[0].dtype),
        pl.BlockSpec((each, tile, tile), lambda i: (i, 0, 0)),
        steps,
    )


def join_tiles(arrays, index, row_blocks, first_columns, second_columns):
    tile = arrays[0].shape[-1]
    first_count = row_blocks * first_columns
    steps = 4
    each = row_blocks // steps

    def kernel(index_ref, *refs):
        sources, first, second, sem = refs[:-3], refs[-3], refs[-2], refs[-1]
        base = pl.program_id(0) * each
        for out, start, columns in ((first, 0, first_columns), (second, first_count, second_columns)):

            def step(i, carry, out=out, start=start, columns=columns):
                row = i // columns
                column = i - row * columns
                target = out.at[
                    pl.ds(pl.multiple_of(row * tile, tile), tile),
                    pl.ds(pl.multiple_of(column * tile, tile), tile),
                ]
                start_copy(sources, index_ref[start + base * columns + i], target, sem)
                return carry

            lax.fori_loop(0, each * columns, step, 0)
        pltpu.make_async_copy(first, first, sem).wait()
        pltpu.make_async_copy(second, second, sem).wait()

    total = sum(array.shape[0] for array in arrays)
    out_shape = tuple(
        jax.ShapeDtypeStruct((row_blocks * tile, count * tile), arrays[0].dtype)
        for count in (first_columns, second_columns)
    )
    out_specs = tuple(
        pl.BlockSpec((each * tile, count * tile), lambda i: (i, 0))
        for count in (first_columns, second_columns)
    )
    return tile_kernel_call(
        kernel, jnp.clip(index, 0, total - 1), arrays, out_shape, out_specs, steps
    )


def cut_tiles(first, second, index, tile):
    row_blocks = first.shape[0] // tile
    first_columns = first.shape[1] // tile
    second_columns = second.shape[1] // tile
    first_count = row_blocks * first_columns
    count = index.shape[0]
    steps = steps_of(count)
    each = count // steps

    def kernel(index_ref, first_ref, second_ref, out, sem):
        base = pl.program_id(0) * each

        def step(i, carry):
            place = index_ref[base + i]

            def send(ref, local, columns):
                row = pl.multiple_of((local // columns) * tile, tile)
                column = pl.multiple_of((local % columns) * tile, tile)
                pltpu.make_async_copy(
                    ref.at[pl.ds(row, tile), pl.ds(column, tile)], out.at[i], sem
                ).start()

            @pl.when(place < first_count)
            def _():
                send(first_ref, place, first_columns)

            @pl.when(place >= first_count)
            def _():
                send(second_ref, place - first_count, second_columns)

            return carry

        lax.fori_loop(0, each, step, 0)
        pltpu.make_async_copy(out, out, sem).wait()

    return tile_kernel_call(
        kernel,
        jnp.clip(index, 0, first_count + row_blocks * second_columns - 1),
        [first, second],
        jax.ShapeDtypeStruct((count, tile, tile), first.dtype),
        pl.BlockSpec((each, tile, tile), lambda i: (i, 0, 0)),
        steps,
    )


def split_low(value):
    high = value.astype(jnp.bfloat16)
    return high, (value - high.astype(jnp.float32)).astype(jnp.bfloat16)


def rotate_update(grads, index, master, first, second, left, right, rate):
    count, tile, _ = master.shape
    each = 4 if count % 4 == 0 else 1
    correct_one = 1.0 - BETA_ONE**STEP
    correct_two = 1.0 - BETA_TWO**STEP

    def product(one, two, dims):
        return lax.dot_general(one, two, (dims, ((), ())), preferred_element_type=jnp.float32)

    def kernel(index_ref, *refs):
        sources, refs = refs[: len(grads)], refs[len(grads) :]
        master_ref, first_ref, second_ref, left_ref, right_ref = refs[:5]
        master_out, first_out, second_out, held, sem = refs[5:]
        base = pl.program_id(0) * each

        @pl.when(pl.program_id(0) == 0)
        def _():
            def step(i, carry):
                start_copy(sources, index_ref[i], held.at[i], sem)
                return carry

            lax.fori_loop(0, count, step, 0)
            pltpu.make_async_copy(held, held, sem).wait()

        for i in range(each):
            grad = held[base + i]
            left_high, left_low = split_low(left_ref[i])
            right_high, right_low = split_low(right_ref[i])
            half_turned = product(
                jnp.concatenate([grad, grad], axis=1),
                jnp.concatenate([right_high, right_low], axis=0),
                ((1,), (0,)),
            )
            high, low = split_low(half_turned)
            turned = product(
                jnp.concatenate([left_high, left_high, left_low], axis=0),
                jnp.concatenate([high, low, high], axis=0),
                ((0,), (0,)),
            )
            first_new = BETA_ONE * first_ref[i] + (1.0 - BETA_ONE) * turned
            second_new = BETA_TWO * second_ref[i] + (1.0 - BETA_TWO) * turned * turned
            direction = first_new / correct_one / (jnp.sqrt(second_new / correct_two) + ADAM_EPS)
            high, low = split_low(direction)
            half_back = product(
                jnp.concatenate([high, low, high], axis=1),
                jnp.concatenate([right_high, right_high, right_low], axis=1),
                ((1,), (1,)),
            )
            high, low = split_low(half_back)
            back = product(
                jnp.concatenate([left_high, left_high, left_low], axis=1),
                jnp.concatenate([high, low, high], axis=0),
                ((1,), (0,)),
            )
            weight = master_ref[i]
            master_out[i] = weight - rate * (back + DECAY * weight)
            first_out[i] = first_new
            second_out[i] = second_new

    spec = pl.BlockSpec((each, tile, tile), lambda i: (i, 0, 0))
    shape = jax.ShapeDtypeStruct(master.shape, jnp.float32)
    total = sum(array.shape[0] for array in grads)
    return pl.pallas_call(
        kernel,
        grid=(count // each,),
        out_shape=(shape, shape, shape),
        in_specs=[pl.BlockSpec(memory_space=pltpu.SMEM)]
        + [pl.BlockSpec(memory_space=pl.ANY)] * len(grads)
        + [spec] * 5,
        out_specs=(spec, spec, spec),
        scratch_shapes=[
            pltpu.VMEM((count, tile, tile), jnp.bfloat16),
            pltpu.SemaphoreType.DMA,
        ],
        compiler_params=pltpu.CompilerParams(vmem_limit_bytes=VMEM_BYTES),
    )(jnp.clip(index, 0, total - 1), *grads, master, first, second, left, right)


def seq_swap(value, flip):
    size = lax.axis_size("seq")
    return lax.ppermute(value, "seq", [(i, i ^ flip) for i in range(size)])


def core_swap(value):
    size = lax.axis_size("fsdp")
    return lax.ppermute(value, "fsdp", [(i, i ^ 1) for i in range(size)])


def chip_shift(value, offset):
    size = lax.axis_size("fsdp")
    chips = size // 2
    return lax.ppermute(
        value, "fsdp", [(i, (i // 2 + offset) % chips * 2 + i % 2) for i in range(size)]
    )


def seq_gather(value):
    size = lax.axis_size("seq")
    return jnp.concatenate([value] + [seq_swap(value, flip) for flip in range(1, size)], axis=0)


def seq_ordered(value):
    size = lax.axis_size("seq")
    parts = jnp.stack([value] + [seq_swap(value, flip) for flip in range(1, size)], axis=0)
    return parts[lax.axis_index("seq") ^ jnp.arange(size)]


def seq_exchange(values):
    return [values[0]] + [seq_swap(values[flip], flip) for flip in range(1, len(values))]


def seq_sum(value, wire, ordered=False):
    size = lax.axis_size("seq")
    parts = value.reshape((size, value.shape[0] // size) + value.shape[1:])
    if ordered:
        parts = parts[lax.axis_index("seq") ^ jnp.arange(size)]
    total = parts[0]
    for flip in range(1, size):
        total = total + seq_swap(parts[flip].astype(wire), flip).astype(jnp.float32)
    return total


def chip_exchange(values):
    return [values[0]] + [chip_shift(values[offset], offset) for offset in range(1, len(values))]


def fsdp_sum(value):
    size = lax.axis_size("fsdp")
    chips = size // 2
    chip = lax.axis_index("fsdp") // 2
    even = lax.axis_index("fsdp") % 2 == 0
    shares = value.reshape((chips, 2, value.shape[0] // size) + value.shape[1:])
    kept = jnp.where(even, shares[:, 0], shares[:, 1])
    given = jnp.where(even, shares[:, 1], shares[:, 0])
    kept = kept + core_swap(given.astype(jnp.bfloat16)).astype(jnp.float32)
    kept = kept[(chip + jnp.arange(chips)) % chips]
    total = kept[0]
    for offset in range(1, chips):
        total = total + chip_shift(kept[offset].astype(jnp.bfloat16), offset).astype(jnp.float32)
    total = total.astype(jnp.bfloat16)
    parts = jnp.stack([total] + [chip_shift(total, offset) for offset in range(1, chips)])
    parts = parts[(chip - jnp.arange(chips)) % chips]
    other = core_swap(parts)
    both = jnp.where(even, jnp.stack([parts, other], axis=1), jnp.stack([other, parts], axis=1))
    return both.reshape(value.shape)


def on_device(
    tokens,
    layer_vectors,
    doc_lengths,
    cotangent,
    tile_owner,
    tile_master,
    tile_first,
    tile_second,
    left_basis,
    right_basis,
    small_master,
    small_first,
    small_second,
    small_left,
    small_right,
    gains,
    gain_first,
    gain_second,
):
    bf16 = jnp.bfloat16
    f32 = jnp.float32
    tile = tile_master.shape[1]
    width = tokens.shape[2]
    row_blocks = width // tile
    rows = tokens.shape[1]
    seq_size = lax.axis_size("seq")
    fsdp_size = lax.axis_size("fsdp")
    chips = fsdp_size // 2
    mine = tile_master.shape[0]
    tiles = tile_owner.shape[0]
    length = rows * seq_size
    per_device = HEADS // seq_size
    per_key = seq_size // KV_HEADS
    query_width = HEADS * HEAD_DIM
    key_width = KV_HEADS * HEAD_DIM
    my_seq = lax.axis_index("seq")
    my_fsdp = lax.axis_index("fsdp")
    my_chip = my_fsdp // 2
    my_core = my_fsdp % 2
    flips = jnp.arange(seq_size)
    shifts = jnp.arange(chips)

    query_blocks = query_width // tile
    key_blocks = key_width // tile
    ffn_blocks = FF // tile
    query_each = query_blocks // seq_size
    head_blocks = HEAD_DIM // tile
    ffn_each = ffn_blocks // fsdp_size
    columns = tiles // row_blocks
    attn_first = query_each + head_blocks
    attn_count = row_blocks * (attn_first + query_each)
    ffn_first = 2 * ffn_each
    ffn_count = row_blocks * 3 * ffn_each
    attn_share = (2 * query_blocks + 2 * key_blocks) / columns
    ffn_share = 3 * ffn_blocks / columns
    attn_room = room(mine, attn_share / seq_size)
    attn_hold = room(attn_count, 1.0 / fsdp_size)
    ffn_room = (room(2 * mine, ffn_share / chips) + 1) // 2
    ffn_half = (room(ffn_count, 1.0 / seq_size) + 3) // 4 * 2
    ffn_hold = 2 * ffn_half

    def tile_places(owner):
        row = owner // columns
        column = owner % columns
        key_at = column - query_blocks
        value_at = key_at - key_blocks
        out_at = value_at - key_blocks
        ffn_at = out_at - query_blocks
        is_attn = ffn_at < 0
        kind = ffn_at // ffn_blocks
        ffn_column = ffn_at % ffn_blocks
        ffn_to = jnp.where(is_attn, -1, ffn_column // ffn_each)
        ffn_local = ffn_column % ffn_each
        ffn_place = jnp.where(
            kind == 2,
            row_blocks * ffn_first + row * ffn_each + ffn_local,
            row * ffn_first + kind * ffn_each + ffn_local,
        )
        attn_to = jnp.where(
            key_at < 0,
            column // query_each,
            jnp.where(
                value_at < 0,
                key_at // head_blocks * per_key,
                jnp.where(
                    out_at < 0,
                    value_at // head_blocks * per_key + per_key - 1,
                    out_at // query_each,
                ),
            ),
        )
        attn_place = jnp.where(
            key_at < 0,
            row * attn_first + column % query_each,
            jnp.where(
                out_at < 0,
                row * attn_first + query_each + key_at % head_blocks,
                row_blocks * attn_first + row * query_each + out_at % query_each,
            ),
        )
        attn_to = jnp.where(is_attn, attn_to, -1)
        return (ffn_to, ffn_place, attn_to, attn_place)

    owners = tile_owner.reshape(seq_size, fsdp_size, mine)
    ffn_to, ffn_place, attn_to, attn_place = tile_places(owners)
    slot_seq = jnp.arange(seq_size)[:, None, None]
    slot_fsdp = jnp.arange(fsdp_size)[None, :, None]
    slot_chip = slot_fsdp // 2
    ffn_chip = jnp.where(ffn_to < 0, -1, ffn_to // 2)
    chip_view = ffn_chip.reshape(seq_size, chips, 2 * mine)
    chip_rank = count_earlier(chip_view, chip_view >= 0).reshape(owners.shape)
    seq_view = ffn_to.reshape(seq_size, fsdp_size * mine)
    ffn_rank = count_earlier(seq_view, seq_view >= 0).reshape(owners.shape)
    attn_rank = count_earlier(attn_to, attn_to >= 0)
    fsdp_view = attn_to.transpose(1, 0, 2).reshape(fsdp_size, seq_size * mine)
    attn_order = (
        count_earlier(fsdp_view, fsdp_view >= 0)
        .reshape(fsdp_size, seq_size, mine)
        .transpose(1, 0, 2)
    )
    fits = jnp.all(
        jnp.where(
            ffn_to < 0,
            (attn_rank < attn_room) & (attn_order < attn_hold),
            (chip_rank < 2 * ffn_room) & (ffn_rank < ffn_hold),
        )
    )
    half = chips * ffn_room
    rank_core = chip_rank // ffn_room
    rank_local = chip_rank % ffn_room
    out_place = (
        jnp.where(rank_core == my_core, 0, half)
        + (my_chip - slot_chip) % chips * ffn_room
        + rank_local
    )
    back_place = (
        jnp.where(rank_core == my_core, 0, half) + (my_chip - ffn_chip) % chips * ffn_room + rank_local
    )
    my_chip_slots = lax.dynamic_slice(
        jnp.stack([ffn_chip, chip_rank]), (0, my_seq, 2 * my_chip, 0), (2, 1, 2, mine)
    ).reshape(2, 2 * mine)
    my_slots = lax.dynamic_slice(
        jnp.stack([ffn_to, attn_to, attn_rank, back_place]),
        (0, my_seq, my_fsdp, 0),
        (4, 1, 1, mine),
    ).reshape(4, mine)
    seq_slots = lax.dynamic_slice(
        jnp.stack([ffn_to, ffn_rank, ffn_place, out_place, chip_rank, jnp.broadcast_to(slot_chip, owners.shape)]),
        (0, my_seq, 0, 0),
        (6, 1, fsdp_size, mine),
    ).reshape(6, fsdp_size * mine)
    fsdp_slots = lax.dynamic_slice(
        jnp.stack([attn_to, attn_order, attn_rank, jnp.broadcast_to(slot_seq, owners.shape)]),
        (0, 0, my_fsdp, 0),
        (4, seq_size, 1, mine),
    ).reshape(4, seq_size * mine)

    local_slots = jnp.arange(mine)
    attn_pack = pick(
        (my_slots[1][None, None, :] == (my_seq ^ flips)[:, None, None])
        & (my_slots[2][None, None, :] == jnp.arange(attn_room)[None, :, None]),
        local_slots,
    )
    attn_keep = pick(
        (fsdp_slots[0][None, :] == my_seq)
        & (fsdp_slots[1][None, :] == jnp.arange(attn_hold)[:, None]),
        (fsdp_slots[3] ^ my_seq) * attn_room + fsdp_slots[2],
    )
    attn_join = pick(
        (attn_to.reshape(1, -1) == my_seq)
        & (attn_place.reshape(1, -1) == jnp.arange(attn_count)[:, None]),
        (slot_fsdp * attn_hold + attn_order).reshape(1, -1),
    )
    ffn_pack = pick(
        (my_chip_slots[0][None, None, :] == ((my_chip + shifts) % chips)[:, None, None])
        & (
            my_chip_slots[1][None, None, :]
            == (my_core * ffn_room + jnp.arange(ffn_room))[None, :, None]
        ),
        jnp.arange(2 * mine),
    )
    ffn_pack = jnp.where(
        ffn_pack // mine == my_core, ffn_pack % mine, mine + ffn_pack % mine
    )
    ffn_keep = pick(
        (seq_slots[0][None, :] == my_fsdp) & (seq_slots[1][None, :] == jnp.arange(ffn_hold)[:, None]),
        seq_slots[3][None, :],
    )
    ffn_join = pick(
        (ffn_to.reshape(1, -1) == my_fsdp)
        & (ffn_place.reshape(1, -1) == jnp.arange(ffn_count)[:, None]),
        ((slot_seq ^ my_seq) * ffn_hold + ffn_rank).reshape(1, -1),
    )
    master_low = tile_master.astype(bf16)
    attn_sent = gather_tiles([master_low], attn_pack.reshape(-1)).reshape(seq_size, attn_room, tile, tile)
    attn_got = seq_exchange([attn_sent[i] for i in range(seq_size)])
    attn_kept = gather_tiles(attn_got, attn_keep)

    master_other = core_swap(master_low)
    ffn_sent = [gather_tiles([master_low, master_other], ffn_pack[i]) for i in range(chips)]
    ffn_got = chip_exchange(ffn_sent)
    ffn_other = [core_swap(value) for value in ffn_got]
    kept_one = gather_tiles(ffn_got + ffn_other, ffn_keep[:ffn_half])
    kept_two = gather_tiles(ffn_got + ffn_other, ffn_keep[ffn_half:])
    attn_all = lax.all_gather(attn_kept, "fsdp", axis=0, tiled=True)
    w_first, w_out = join_tiles([attn_all], attn_join, row_blocks, attn_first, query_each)
    one_x, two_y = seq_swap(kept_one, 1), seq_swap(kept_two, 2)
    two_x, one_y = seq_swap(kept_two, 1), seq_swap(kept_one, 2)
    one_xy, two_xy = seq_swap(one_x, 2), seq_swap(two_y, 1)
    ffn_all = [kept_one, kept_two, one_x, two_x, one_y, two_y, one_xy, two_xy]
    w_both, w_down = join_tiles(ffn_all, ffn_join, row_blocks, ffn_first, ffn_each)

    my_columns = jnp.arange(tiles)
    def slow_fetch(_, kept):
        whole = lax.all_gather(master_low, ("seq", "fsdp"), axis=0, tiled=True)
        slots = my_columns.reshape(1, -1)
        attn_slots = pick(
            (attn_to.reshape(1, -1) == my_seq)
            & (attn_place.reshape(1, -1) == jnp.arange(attn_count)[:, None]),
            slots,
        )
        ffn_slots = pick(
            (ffn_to.reshape(1, -1) == my_fsdp)
            & (ffn_place.reshape(1, -1) == jnp.arange(ffn_count)[:, None]),
            slots,
        )
        return join_tiles([whole], attn_slots, row_blocks, attn_first, query_each) + join_tiles(
            [whole], ffn_slots, row_blocks, ffn_first, ffn_each
        )

    slow_steps = jnp.where(fits, 0, 1)
    w_first, w_out, w_both, w_down = lax.fori_loop(
        0, slow_steps, slow_fetch, (w_first, w_out, w_both, w_down)
    )

    small_got = seq_ordered(small_master.astype(bf16))
    small_table = assemble(small_got.reshape((-1,) + small_master.shape[1:]), row_blocks)
    gain_full = seq_ordered(gains.astype(bf16)).reshape(-1).astype(f32)
    gain_in = gain_full[0:width]
    gain_attn = gain_full[width : 2 * width]
    gain_laurel = gain_full[2 * width : 3 * width]
    gain_pre = gain_full[3 * width : 4 * width]
    gain_post = gain_full[4 * width : 5 * width]
    gain_vec = gain_full[5 * width : 6 * width]
    gain_query = gain_full[6 * width : 6 * width + HEAD_DIM]
    gain_key = gain_full[6 * width + HEAD_DIM : 6 * width + 2 * HEAD_DIM]
    laurel_left = small_table[:, :RANK]
    laurel_right = small_table[:, RANK : 2 * RANK]
    vector_gate_w = small_table[:, 2 * RANK : 2 * RANK + PLD]
    vector_proj_w = small_table[:, 2 * RANK + PLD :]

    pack_tokens = seq_gather(tokens[0])
    segment, position = documents(doc_lengths[0], length)
    places = ((my_seq ^ flips)[:, None] * rows + jnp.arange(rows)[None, :]).reshape(-1)

    def reorder(values):
        blocks = values.reshape(seq_size, rows)
        return jnp.concatenate(
            [lax.dynamic_index_in_dim(blocks, my_seq ^ i, 0, False) for i in range(seq_size)]
        )

    pack_segment = reorder(segment)
    pack_position = reorder(position)
    stream = tokens[0].astype(f32)
    vectors = layer_vectors[0].astype(f32)
    normed, normed_pull = jax.vjp(rms_norm, stream, gain_in)
    normed_low = normed.astype(bf16)
    pack_normed = rms_norm(pack_tokens.astype(f32), gain_in).astype(bf16)
    first_pre = matmul(pack_normed, w_first)
    is_key = my_seq % per_key == 0

    def shape_query(query_in, query_gain):
        return rotary(
            rms_norm(query_in.reshape(length, per_device, HEAD_DIM), query_gain), pack_position
        )

    def shape_key(key_in, key_gain):
        return rotary(rms_norm(key_in.reshape(length, 1, HEAD_DIM), key_gain), pack_position)

    query_pre = first_pre[:, : per_device * HEAD_DIM]
    other_pre = first_pre[:, per_device * HEAD_DIM :]
    query_rot, query_pull = jax.vjp(shape_query, query_pre, gain_query)
    key_rot, key_pull = jax.vjp(shape_key, other_pre, gain_key)
    query_heads = query_rot.astype(bf16)
    other_low = jnp.where(is_key, key_rot[:, 0, :], other_pre).astype(bf16)
    partner_low = seq_swap(other_low, 1).reshape(seq_size // 2, 2, rows, HEAD_DIM)
    partner_low = partner_low[:, ::-1].reshape(length, HEAD_DIM)
    key_single = jnp.where(is_key, other_low, partner_low)
    value_single = jnp.where(is_key, partner_low, other_low)

    allow = (pack_segment[:, None] == pack_segment[None, :]) & (
        places[None, :] <= places[:, None]
    )
    raw = (
        jnp.einsum("qhd,kd->qhk", query_heads, key_single, preferred_element_type=f32) * SCALE
    )
    scores = jnp.where(allow[:, None, :], raw, NEGATIVE)
    powers = jnp.exp(scores - jnp.max(scores, axis=-1, keepdims=True))
    prob = powers / jnp.sum(powers, axis=-1, keepdims=True)
    prob_low = prob.astype(bf16)
    attended_low = (
        jnp.einsum("qhk,kd->qhd", prob_low, value_single, preferred_element_type=f32)
        .astype(bf16)
        .reshape(length, per_device * HEAD_DIM)
    )
    attn_pre = seq_sum(matmul_flip(attended_low, w_out), bf16)
    attn_normed, attn_pull = jax.vjp(rms_norm, attn_pre, gain_attn)
    first_sum = stream + attn_normed
    left_pre = matmul(normed_low, laurel_left)
    left_low = left_pre.astype(bf16)
    right_pre = matmul_flip(left_low, laurel_right)
    laurel_normed, laurel_pull = jax.vjp(rms_norm, right_pre, gain_laurel)
    second_sum = (first_sum + normed + laurel_normed) * ROOT_HALF
    feed_normed, feed_pull = jax.vjp(rms_norm, second_sum, gain_pre)
    feed_low = lax.all_gather(feed_normed.astype(bf16), "fsdp", axis=0, tiled=True)
    both_pre = matmul(feed_low, w_both)
    ffn_width = w_down.shape[1]
    hidden, hidden_pull = jax.vjp(gelu_product, both_pre[:, :ffn_width], both_pre[:, ffn_width:])
    hidden_low = hidden.astype(bf16)
    down_pre = lax.psum_scatter(
        matmul_flip(hidden_low, w_down).astype(bf16), "fsdp", scatter_dimension=0, tiled=True
    ).astype(f32)
    down_normed, down_pull = jax.vjp(rms_norm, down_pre, gain_post)
    third_sum = second_sum + down_normed
    third_low = third_sum.astype(bf16)
    vector_pre = matmul(third_low, vector_gate_w)
    vector_gated, vector_pull = jax.vjp(lambda inner: gelu_product(inner, vectors), vector_pre)
    vector_low = vector_gated.astype(bf16)
    proj_pre = matmul_flip(vector_low, vector_proj_w)
    proj_normed, proj_pull = jax.vjp(rms_norm, proj_pre, gain_vec)
    result = third_sum + proj_normed
    output = result.astype(bf16)[None]

    grad_out = cotangent[0].astype(f32)
    grad_proj, grad_gain_vec = proj_pull(grad_out)
    proj_grad_low = grad_proj.astype(bf16)
    (grad_vector_pre,) = vector_pull(matmul(proj_grad_low, vector_proj_w))
    vector_grad_low = grad_vector_pre.astype(bf16)
    grad_third = grad_out + matmul_flip(vector_grad_low, vector_gate_w)
    grad_down, grad_gain_post = down_pull(grad_third)
    down_grad_low = lax.all_gather(grad_down.astype(bf16), "fsdp", axis=0, tiled=True)
    grad_gate, grad_up = hidden_pull(matmul(down_grad_low, w_down))
    both_grad_low = jnp.concatenate([grad_gate, grad_up], axis=1).astype(bf16)
    grad_feed = lax.psum_scatter(
        matmul_flip(both_grad_low, w_both).astype(bf16), "fsdp", scatter_dimension=0, tiled=True
    ).astype(f32)
    both_grad_w = matmul_outer(feed_low, both_grad_low).astype(bf16)
    down_grad_w = matmul_outer(down_grad_low, hidden_low).astype(bf16)

    grad_second_norm, grad_gain_pre = feed_pull(grad_feed)
    half_grad = (grad_third + grad_second_norm) * ROOT_HALF
    grad_right, grad_gain_laurel = laurel_pull(half_grad)
    right_grad_low = grad_right.astype(bf16)
    left_grad_low = matmul(right_grad_low, laurel_right).astype(bf16)
    grad_attn, grad_gain_attn = attn_pull(half_grad)
    attn_grad_low = seq_gather(grad_attn.astype(bf16))
    grad_attended = (
        matmul(attn_grad_low, w_out).astype(bf16).reshape(length, per_device, HEAD_DIM)
    )
    out_grad_w = matmul_outer(attn_grad_low, attended_low).astype(bf16)
    value_grad = jnp.einsum("qhk,qhd->kd", prob_low, grad_attended, preferred_element_type=f32)
    grad_prob = jnp.einsum("qhd,kd->qhk", grad_attended, value_single, preferred_element_type=f32)
    inner = jnp.sum(prob * grad_prob, axis=-1, keepdims=True)
    grad_score = (prob * (grad_prob - inner)).astype(bf16)
    grad_query = (
        jnp.einsum("qhk,kd->qhd", grad_score, key_single, preferred_element_type=f32) * SCALE
    ).astype(bf16)
    key_grad = (
        jnp.einsum("qhk,qhd->kd", grad_score, query_heads, preferred_element_type=f32) * SCALE
    ).astype(bf16)
    value_grad = value_grad.astype(bf16)
    partner_grad = seq_swap(jnp.where(is_key, value_grad, key_grad), 1)
    partner_grad = partner_grad.reshape(seq_size // 2, 2, rows, HEAD_DIM)[:, ::-1]
    other_grad = jnp.where(is_key, key_grad, value_grad).astype(f32) + partner_grad.reshape(
        length, HEAD_DIM
    ).astype(f32)
    grad_query_pre, grad_gain_query = query_pull(grad_query.astype(f32))
    grad_key_pre, grad_gain_key = key_pull(other_grad[:, None, :])
    grad_gain_key = jnp.where(is_key, grad_gain_key, 0.0)
    first_grad_low = jnp.concatenate(
        [grad_query_pre, jnp.where(is_key, grad_key_pre, other_grad)], axis=1
    ).astype(bf16)
    first_grad_w = matmul_outer(pack_normed, first_grad_low).astype(bf16)
    grad_normed = (
        half_grad
        + matmul_flip(left_grad_low, laurel_left)
        + seq_sum(matmul_flip(first_grad_low, w_first), bf16)
    )
    grad_stream_norm, grad_gain_in = normed_pull(grad_normed)
    input_grad = (half_grad + grad_stream_norm)[None]

    flip_to = ffn_to.reshape(seq_size, 1, -1)[my_seq ^ flips]
    flip_rank = ffn_rank.reshape(seq_size, 1, -1)[my_seq ^ flips]
    flip_place = ffn_place.reshape(seq_size, 1, -1)[my_seq ^ flips]
    ffn_cut = pick(
        (flip_to == my_fsdp) & (flip_rank == jnp.arange(ffn_hold)[None, :, None]), flip_place
    )
    ffn_back = pick(
        (seq_slots[5][None, None, :] == ((my_chip + shifts) % chips)[:, None, None])
        & (seq_slots[0][None, None, :] // 2 == my_chip)
        & (seq_slots[0][None, None, :] >= 0)
        & (seq_slots[4][None, None, :] == (my_core * ffn_room + jnp.arange(ffn_room))[None, :, None]),
        jnp.where(seq_slots[0] == my_fsdp, 0, ffn_hold) + seq_slots[1],
    )

    def ffn_parts(flips_of, half):
        index = ffn_cut[:, half * ffn_half : (half + 1) * ffn_half][jnp.array(flips_of)]
        return cut_tiles(both_grad_w, down_grad_w, index.reshape(-1), tile)

    def added(one, two):
        return one.astype(f32) + two.astype(f32)

    one_sum = added(ffn_parts([0, 2], 0), seq_swap(ffn_parts([1, 3], 0), 1))
    two_sum = added(ffn_parts([0, 1], 1), seq_swap(ffn_parts([2, 3], 1), 2))
    one_sum = added(one_sum[:ffn_half], seq_swap(one_sum[ffn_half:].astype(bf16), 2)).astype(bf16)
    two_sum = added(two_sum[:ffn_half], seq_swap(two_sum[ffn_half:].astype(bf16), 1)).astype(bf16)
    ffn_sums = [one_sum, two_sum, core_swap(one_sum), core_swap(two_sum)]
    ffn_returned = chip_exchange([gather_tiles(ffn_sums, ffn_back[i]) for i in range(chips)])
    ffn_returned = ffn_returned + [core_swap(value) for value in ffn_returned]

    attn_cut = pick(
        (attn_to.transpose(1, 0, 2).reshape(fsdp_size, 1, -1) == my_seq)
        & (
            attn_order.transpose(1, 0, 2).reshape(fsdp_size, 1, -1)
            == jnp.arange(attn_hold)[None, :, None]
        ),
        attn_place.transpose(1, 0, 2).reshape(fsdp_size, 1, -1),
    )
    attn_back = pick(
        (fsdp_slots[3][None, None, :] == (my_seq ^ flips)[:, None, None])
        & (fsdp_slots[0][None, None, :] == my_seq)
        & (fsdp_slots[2][None, None, :] == jnp.arange(attn_room)[None, :, None]),
        fsdp_slots[1],
    )
    attn_parts = cut_tiles(first_grad_w, out_grad_w, attn_cut.reshape(-1), tile)
    attn_sum = lax.psum_scatter(attn_parts, "fsdp", scatter_dimension=0, tiled=True)
    attn_returned = seq_exchange([gather_tiles([attn_sum], attn_back[i]) for i in range(seq_size)])
    slot_grad = jnp.where(
        my_slots[0] >= 0,
        my_slots[3],
        2 * half + (my_slots[1] ^ my_seq) * attn_room + my_slots[2],
    )

    def slow_return(_, kept):
        own_ffn = split_tiles(both_grad_w, tile), split_tiles(down_grad_w, tile)
        own_attn = split_tiles(first_grad_w, tile), split_tiles(out_grad_w, tile)
        parts = jnp.concatenate(own_ffn + own_attn + (jnp.zeros((1, tile, tile), bf16),))
        index = jnp.where(
            ffn_to == my_fsdp,
            ffn_place,
            jnp.where(attn_to == my_seq, ffn_count + attn_place, ffn_count + attn_count),
        )
        spread = gather_tiles([parts], index.reshape(-1))
        return lax.psum_scatter(spread, ("seq", "fsdp"), scatter_dimension=0, tiled=True)

    tile_grads = ffn_returned + attn_returned
    slow_start = 2 * half + seq_size * attn_room
    slow_grads = lax.fori_loop(0, slow_steps, slow_return, jnp.zeros((mine, tile, tile), bf16))
    tile_grads = tile_grads + [slow_grads]
    slot_grad = jnp.where(fits, slot_grad, slow_start + local_slots)

    small_full = jnp.concatenate(
        [
            matmul_outer(normed_low, left_grad_low),
            matmul_outer(right_grad_low, left_low),
            matmul_outer(third_low, vector_grad_low),
            matmul_outer(proj_grad_low, vector_low),
        ],
        axis=1,
    )
    small_tiles_grad = split_tiles(small_full, tile)
    gain_grad = jnp.concatenate(
        [
            grad_gain_in,
            grad_gain_attn,
            grad_gain_laurel,
            grad_gain_pre,
            grad_gain_post,
            grad_gain_vec,
            grad_gain_query,
            grad_gain_key,
        ]
    )
    small_part = seq_sum(small_tiles_grad, bf16, True)
    small_grad = fsdp_sum(small_part.reshape(-1, tile)).reshape(small_part.shape)
    gain_part = seq_sum(gain_grad, f32, True)
    gain_part = gain_part + core_swap(gain_part)
    gain_grad_mine = gain_part
    for offset in range(1, chips):
        gain_grad_mine = gain_grad_mine + chip_shift(gain_part, offset)
    tile_new, tile_first_new, tile_second_new = rotate_update(
        tile_grads, slot_grad, tile_master, tile_first, tile_second, left_basis, right_basis, RATE_TILE
    )
    small_new, small_first_new, small_second_new = rotate_update(
        [small_grad],
        jnp.arange(small_master.shape[0]),
        small_master,
        small_first,
        small_second,
        small_left,
        small_right,
        RATE_SMALL,
    )
    gain_first_new = BETA_ONE * gain_first + (1.0 - BETA_ONE) * gain_grad_mine
    gain_second_new = BETA_TWO * gain_second + (1.0 - BETA_TWO) * gain_grad_mine * gain_grad_mine
    correct_one = 1.0 - BETA_ONE**STEP
    correct_two = 1.0 - BETA_TWO**STEP
    gain_new = gains - RATE_GAIN * (gain_first_new / correct_one) / (
        jnp.sqrt(gain_second_new / correct_two) + ADAM_EPS
    )
    return (
        output,
        input_grad,
        tile_new,
        tile_first_new,
        tile_second_new,
        small_new,
        small_first_new,
        small_second_new,
        gain_new,
        gain_first_new,
        gain_second_new,
    )


def solution(mesh):
    return jax.shard_map(
        on_device,
        mesh=mesh,
        in_specs=(
            P("fsdp", "seq", None),
            P("fsdp", "seq", None),
            P("fsdp", None),
            P("fsdp", "seq", None),
            P(),
            P(("seq", "fsdp"), None, None),
            P(("seq", "fsdp"), None, None),
            P(("seq", "fsdp"), None, None),
            P(("seq", "fsdp"), None, None),
            P(("seq", "fsdp"), None, None),
            P("seq", None, None),
            P("seq", None, None),
            P("seq", None, None),
            P("seq", None, None),
            P("seq", None, None),
            P("seq"),
            P("seq"),
            P("seq"),
        ),
        out_specs=(
            P("fsdp", "seq", None),
            P("fsdp", "seq", None),
            P(("seq", "fsdp"), None, None),
            P(("seq", "fsdp"), None, None),
            P(("seq", "fsdp"), None, None),
            P("seq", None, None),
            P("seq", None, None),
            P("seq", None, None),
            P("seq"),
            P("seq"),
            P("seq"),
        ),
        check_vma=False,
    )
```

```python
import math

import jax
import jax.numpy as jnp
from jax import lax
from jax.experimental import pallas as pl
from jax.experimental.pallas import tpu as pltpu
from jax.sharding import PartitionSpec as P

HEADS = 8
KV_HEADS = 2
HEAD_DIM = 256
FF = 8192
RANK = 64
PLD = 256
STEP = 5


EPS = 1e-06
SCALE = 0.0625
THETA = 1000000.0
ROOT_HALF = 0.7071067811865476
BETA_ONE = 0.5
BETA_TWO = 0.5
ADAM_EPS = 1e-08
RATE_TILE = 0.02
RATE_SMALL = 0.04
RATE_GAIN = 0.3
DECAY = 0.01
NEGATIVE = -1e30
VMEM_BYTES = 32 * 1024 * 1024


def rms_norm(value, gain):
    return value * lax.rsqrt(jnp.mean(value * value, axis=-1, keepdims=True) + EPS) * gain


def rotary(value, position):
    half = value.shape[-1] // 2
    freq = THETA ** (-2.0 * jnp.arange(half).astype(jnp.float32) / value.shape[-1])
    angle = position.astype(jnp.float32)[:, None] * freq[None, :]
    cosine = jnp.cos(angle)[:, None, :]
    sine = jnp.sin(angle)[:, None, :]
    first = value[..., :half]
    second = value[..., half:]
    return jnp.concatenate(
        [first * cosine - second * sine, second * cosine + first * sine], axis=-1
    )


def documents(lengths, length):
    places = jnp.arange(length)
    ends = jnp.cumsum(lengths)
    passed = places[:, None] >= ends[None, :]
    segment = jnp.sum(passed.astype(jnp.int32), axis=1)
    before = jnp.sum(jnp.where(passed, lengths[None, :], 0), axis=1)
    return (segment, places - before)


def matmul(left, right):
    return jnp.dot(left, right, preferred_element_type=jnp.float32)


def matmul_flip(left, right):
    return lax.dot_general(
        left, right, (((1,), (1,)), ((), ())), preferred_element_type=jnp.float32
    )


def matmul_outer(left, right):
    return lax.dot_general(
        left, right, (((0,), (0,)), ((), ())), preferred_element_type=jnp.float32
    )


def assemble(tiles, row_blocks):
    size = tiles.shape[1]
    column_blocks = tiles.shape[0] // row_blocks
    return (
        tiles.reshape(row_blocks, column_blocks, size, size)
        .transpose(0, 2, 1, 3)
        .reshape(row_blocks * size, column_blocks * size)
    )


def split_tiles(matrix, size):
    row_blocks = matrix.shape[0] // size
    column_blocks = matrix.shape[1] // size
    return (
        matrix.reshape(row_blocks, size, column_blocks, size)
        .transpose(0, 2, 1, 3)
        .reshape(row_blocks * column_blocks, size, size)
    )


def gelu_product(first, second):
    return jax.nn.gelu(first, approximate=True) * second


def room(count, share):
    mean = count * share
    return math.ceil(mean + 3.6 * math.sqrt(mean * (1.0 - share)) + 3.0)


def count_earlier(group, valid):
    size = group.shape[-1]
    order = jnp.arange(size)
    same = (group[..., :, None] == group[..., None, :]) & valid[..., None, :]
    same = same & (order[None, :] < order[:, None])
    return jnp.sum(same.astype(jnp.int32), axis=-1)


def pick(match, value):
    return jnp.sum(jnp.where(match, value, 0), axis=-1)


def steps_of(count):
    for steps in range(4, 65):
        if count % steps == 0 and 16 <= count // steps <= 160:
            return steps
    return 2 if count % 2 == 0 else 1


def tile_kernel_call(kernel, index, arrays, out_shape, out_specs, steps):
    return pl.pallas_call(
        kernel,
        grid=(steps,),
        out_shape=out_shape,
        in_specs=[pl.BlockSpec(memory_space=pltpu.SMEM)]
        + [pl.BlockSpec(memory_space=pl.ANY)] * len(arrays),
        out_specs=out_specs,
        scratch_shapes=[pltpu.SemaphoreType.DMA],
        compiler_params=pltpu.CompilerParams(vmem_limit_bytes=VMEM_BYTES),
    )(index, *arrays)


def start_copy(sources, place, target, sem):
    start = 0
    for ref in sources:
        size = ref.shape[0]

        @pl.when((place >= start) & (place < start + size))
        def _(ref=ref, start=start):
            pltpu.make_async_copy(ref.at[place - start], target, sem).start()

        start = start + size


def gather_tiles(arrays, index):
    tile = arrays[0].shape[-1]
    count = index.shape[0]
    steps = steps_of(count)
    each = count // steps

    def kernel(index_ref, *refs):
        sources, out, sem = refs[:-2], refs[-2], refs[-1]
        base = pl.program_id(0) * each

        def step(i, carry):
            start_copy(sources, index_ref[base + i], out.at[i], sem)
            return carry

        lax.fori_loop(0, each, step, 0)
        pltpu.make_async_copy(out, out, sem).wait()

    total = sum(array.shape[0] for array in arrays)
    return tile_kernel_call(
        kernel,
        jnp.clip(index, 0, total - 1),
        arrays,
        jax.ShapeDtypeStruct((count, tile, tile), arrays[0].dtype),
        pl.BlockSpec((each, tile, tile), lambda i: (i, 0, 0)),
        steps,
    )


def join_tiles(arrays, index, row_blocks, first_columns, second_columns):
    tile = arrays[0].shape[-1]
    first_count = row_blocks * first_columns
    steps = 4
    each = row_blocks // steps

    def kernel(index_ref, *refs):
        sources, first, second, sem = refs[:-3], refs[-3], refs[-2], refs[-1]
        base = pl.program_id(0) * each
        for out, start, columns in ((first, 0, first_columns), (second, first_count, second_columns)):

            def step(i, carry, out=out, start=start, columns=columns):
                row = i // columns
                column = i - row * columns
                target = out.at[
                    pl.ds(pl.multiple_of(row * tile, tile), tile),
                    pl.ds(pl.multiple_of(column * tile, tile), tile),
                ]
                start_copy(sources, index_ref[start + base * columns + i], target, sem)
                return carry

            lax.fori_loop(0, each * columns, step, 0)
        pltpu.make_async_copy(first, first, sem).wait()
        pltpu.make_async_copy(second, second, sem).wait()

    total = sum(array.shape[0] for array in arrays)
    out_shape = tuple(
        jax.ShapeDtypeStruct((row_blocks * tile, count * tile), arrays[0].dtype)
        for count in (first_columns, second_columns)
    )
    out_specs = tuple(
        pl.BlockSpec((each * tile, count * tile), lambda i: (i, 0))
        for count in (first_columns, second_columns)
    )
    return tile_kernel_call(
        kernel, jnp.clip(index, 0, total - 1), arrays, out_shape, out_specs, steps
    )


def cut_tiles(first, second, index, tile):
    row_blocks = first.shape[0] // tile
    first_columns = first.shape[1] // tile
    second_columns = second.shape[1] // tile
    first_count = row_blocks * first_columns
    count = index.shape[0]
    steps = steps_of(count)
    each = count // steps

    def kernel(index_ref, first_ref, second_ref, out, sem):
        base = pl.program_id(0) * each

        def step(i, carry):
            place = index_ref[base + i]

            def send(ref, local, columns):
                row = pl.multiple_of((local // columns) * tile, tile)
                column = pl.multiple_of((local % columns) * tile, tile)
                pltpu.make_async_copy(
                    ref.at[pl.ds(row, tile), pl.ds(column, tile)], out.at[i], sem
                ).start()

            @pl.when(place < first_count)
            def _():
                send(first_ref, place, first_columns)

            @pl.when(place >= first_count)
            def _():
                send(second_ref, place - first_count, second_columns)

            return carry

        lax.fori_loop(0, each, step, 0)
        pltpu.make_async_copy(out, out, sem).wait()

    return tile_kernel_call(
        kernel,
        jnp.clip(index, 0, first_count + row_blocks * second_columns - 1),
        [first, second],
        jax.ShapeDtypeStruct((count, tile, tile), first.dtype),
        pl.BlockSpec((each, tile, tile), lambda i: (i, 0, 0)),
        steps,
    )


def split_low(value):
    high = value.astype(jnp.bfloat16)
    return high, (value - high.astype(jnp.float32)).astype(jnp.bfloat16)


def rotate_update(grads, index, master, first, second, left, right, rate):
    count, tile, _ = master.shape
    each = 4 if count % 4 == 0 else 1
    correct_one = 1.0 - BETA_ONE**STEP
    correct_two = 1.0 - BETA_TWO**STEP

    def product(one, two, dims):
        return lax.dot_general(one, two, (dims, ((), ())), preferred_element_type=jnp.float32)

    def kernel(index_ref, *refs):
        sources, refs = refs[: len(grads)], refs[len(grads) :]
        master_ref, first_ref, second_ref, left_ref, right_ref = refs[:5]
        master_out, first_out, second_out, held, sems = refs[5:]
        now = pl.program_id(0)

        @pl.when(now == 0)
        def _():
            def step(i, carry):
                start_copy(sources, index_ref[i], held.at[i], sems.at[i // each])
                return carry

            lax.fori_loop(0, count, step, 0)

        block = held.at[pl.ds(now * each, each)]
        pltpu.make_async_copy(block, block, sems.at[now]).wait()
        lefts, rights, turns = [], [], []
        for i in range(each):
            grad = held[now * each + i]
            lefts.append(split_low(left_ref[i]))
            rights.append(split_low(right_ref[i]))
            half_turned = product(
                jnp.concatenate([grad, grad], axis=1),
                jnp.concatenate(rights[i], axis=0),
                ((1,), (0,)),
            )
            turns.append(split_low(half_turned))
        for i in range(each):
            (left_high, left_low), (high, low) = lefts[i], turns[i]
            turns[i] = product(
                jnp.concatenate([left_high, left_high, left_low], axis=0),
                jnp.concatenate([high, low, high], axis=0),
                ((0,), (0,)),
            )
        for i in range(each):
            right_high, right_low = rights[i]
            first_new = BETA_ONE * first_ref[i] + (1.0 - BETA_ONE) * turns[i]
            second_new = BETA_TWO * second_ref[i] + (1.0 - BETA_TWO) * turns[i] * turns[i]
            first_out[i] = first_new
            second_out[i] = second_new
            high, low = split_low(
                first_new / correct_one / (jnp.sqrt(second_new / correct_two) + ADAM_EPS)
            )
            half_back = product(
                jnp.concatenate([high, low, high], axis=1),
                jnp.concatenate([right_high, right_high, right_low], axis=1),
                ((1,), (1,)),
            )
            turns[i] = split_low(half_back)
        for i in range(each):
            (left_high, left_low), (high, low) = lefts[i], turns[i]
            back = product(
                jnp.concatenate([left_high, left_high, left_low], axis=1),
                jnp.concatenate([high, low, high], axis=0),
                ((1,), (0,)),
            )
            weight = master_ref[i]
            master_out[i] = weight - rate * (back + DECAY * weight)

    spec = pl.BlockSpec((each, tile, tile), lambda i: (i, 0, 0))
    shape = jax.ShapeDtypeStruct(master.shape, jnp.float32)
    total = sum(array.shape[0] for array in grads)
    return pl.pallas_call(
        kernel,
        grid=(count // each,),
        out_shape=(shape, shape, shape),
        in_specs=[pl.BlockSpec(memory_space=pltpu.SMEM)]
        + [pl.BlockSpec(memory_space=pl.ANY)] * len(grads)
        + [spec] * 5,
        out_specs=(spec, spec, spec),
        scratch_shapes=[
            pltpu.VMEM((count, tile, tile), jnp.bfloat16),
            pltpu.SemaphoreType.DMA((count // each,)),
        ],
        compiler_params=pltpu.CompilerParams(vmem_limit_bytes=VMEM_BYTES),
    )(jnp.clip(index, 0, total - 1), *grads, master, first, second, left, right)


def seq_swap(value, flip):
    size = lax.axis_size("seq")
    return lax.ppermute(value, "seq", [(i, i ^ flip) for i in range(size)])


def core_swap(value):
    size = lax.axis_size("fsdp")
    return lax.ppermute(value, "fsdp", [(i, i ^ 1) for i in range(size)])


def chip_shift(value, offset):
    size = lax.axis_size("fsdp")
    chips = size // 2
    return lax.ppermute(
        value, "fsdp", [(i, (i // 2 + offset) % chips * 2 + i % 2) for i in range(size)]
    )


def seq_gather(value):
    size = lax.axis_size("seq")
    return jnp.concatenate([value] + [seq_swap(value, flip) for flip in range(1, size)], axis=0)


def seq_ordered(value):
    size = lax.axis_size("seq")
    parts = jnp.stack([value] + [seq_swap(value, flip) for flip in range(1, size)], axis=0)
    return parts[lax.axis_index("seq") ^ jnp.arange(size)]


def seq_exchange(values):
    return [values[0]] + [seq_swap(values[flip], flip) for flip in range(1, len(values))]


def seq_sum(value, wire, ordered=False):
    size = lax.axis_size("seq")
    parts = value.reshape((size, value.shape[0] // size) + value.shape[1:])
    if ordered:
        parts = parts[lax.axis_index("seq") ^ jnp.arange(size)]
    total = parts[0]
    for flip in range(1, size):
        total = total + seq_swap(parts[flip].astype(wire), flip).astype(jnp.float32)
    return total


def chip_exchange(values):
    return [values[0]] + [chip_shift(values[offset], offset) for offset in range(1, len(values))]


def fsdp_sum(value):
    size = lax.axis_size("fsdp")
    chips = size // 2
    chip = lax.axis_index("fsdp") // 2
    even = lax.axis_index("fsdp") % 2 == 0
    shares = value.reshape((chips, 2, value.shape[0] // size) + value.shape[1:])
    kept = jnp.where(even, shares[:, 0], shares[:, 1])
    given = jnp.where(even, shares[:, 1], shares[:, 0])
    kept = kept + core_swap(given.astype(jnp.bfloat16)).astype(jnp.float32)
    kept = kept[(chip + jnp.arange(chips)) % chips]
    total = kept[0]
    for offset in range(1, chips):
        total = total + chip_shift(kept[offset].astype(jnp.bfloat16), offset).astype(jnp.float32)
    total = total.astype(jnp.bfloat16)
    parts = jnp.stack([total] + [chip_shift(total, offset) for offset in range(1, chips)])
    parts = parts[(chip - jnp.arange(chips)) % chips]
    other = core_swap(parts)
    both = jnp.where(even, jnp.stack([parts, other], axis=1), jnp.stack([other, parts], axis=1))
    return both.reshape(value.shape)


def on_device(
    tokens,
    layer_vectors,
    doc_lengths,
    cotangent,
    tile_owner,
    tile_master,
    tile_first,
    tile_second,
    left_basis,
    right_basis,
    small_master,
    small_first,
    small_second,
    small_left,
    small_right,
    gains,
    gain_first,
    gain_second,
):
    bf16 = jnp.bfloat16
    f32 = jnp.float32
    tile = tile_master.shape[1]
    width = tokens.shape[2]
    row_blocks = width // tile
    rows = tokens.shape[1]
    seq_size = lax.axis_size("seq")
    fsdp_size = lax.axis_size("fsdp")
    chips = fsdp_size // 2
    mine = tile_master.shape[0]
    tiles = tile_owner.shape[0]
    length = rows * seq_size
    per_device = HEADS // seq_size
    per_key = seq_size // KV_HEADS
    query_width = HEADS * HEAD_DIM
    key_width = KV_HEADS * HEAD_DIM
    my_seq = lax.axis_index("seq")
    my_fsdp = lax.axis_index("fsdp")
    my_chip = my_fsdp // 2
    my_core = my_fsdp % 2
    flips = jnp.arange(seq_size)
    shifts = jnp.arange(chips)

    query_blocks = query_width // tile
    key_blocks = key_width // tile
    ffn_blocks = FF // tile
    query_each = query_blocks // seq_size
    head_blocks = HEAD_DIM // tile
    ffn_each = ffn_blocks // fsdp_size
    columns = tiles // row_blocks
    attn_first = query_each + head_blocks
    attn_count = row_blocks * (attn_first + query_each)
    ffn_first = 2 * ffn_each
    ffn_count = row_blocks * 3 * ffn_each
    attn_share = (2 * query_blocks + 2 * key_blocks) / columns
    ffn_share = 3 * ffn_blocks / columns
    attn_room = (room(2 * mine, attn_share / seq_size) + 1) // 2
    attn_hold = (room(attn_count, 1.0 / chips) + 1) // 2 + 1
    ffn_room = (room(2 * mine, ffn_share / chips) + 1) // 2
    ffn_half = (room(ffn_count, 1.0 / seq_size) + 3) // 4 * 2
    ffn_hold = 2 * ffn_half

    def tile_places(owner):
        row = owner // columns
        column = owner % columns
        key_at = column - query_blocks
        value_at = key_at - key_blocks
        out_at = value_at - key_blocks
        ffn_at = out_at - query_blocks
        is_attn = ffn_at < 0
        kind = ffn_at // ffn_blocks
        ffn_column = ffn_at % ffn_blocks
        ffn_to = jnp.where(is_attn, -1, ffn_column // ffn_each)
        ffn_local = ffn_column % ffn_each
        ffn_place = jnp.where(
            kind == 2,
            row_blocks * ffn_first + row * ffn_each + ffn_local,
            row * ffn_first + kind * ffn_each + ffn_local,
        )
        attn_to = jnp.where(
            key_at < 0,
            column // query_each,
            jnp.where(
                value_at < 0,
                key_at // head_blocks * per_key,
                jnp.where(
                    out_at < 0,
                    value_at // head_blocks * per_key + per_key - 1,
                    out_at // query_each,
                ),
            ),
        )
        attn_place = jnp.where(
            key_at < 0,
            row * attn_first + column % query_each,
            jnp.where(
                out_at < 0,
                row * attn_first + query_each + key_at % head_blocks,
                row_blocks * attn_first + row * query_each + out_at % query_each,
            ),
        )
        attn_to = jnp.where(is_attn, attn_to, -1)
        return (ffn_to, ffn_place, attn_to, attn_place)

    owners = tile_owner.reshape(seq_size, fsdp_size, mine)
    ffn_to, ffn_place, attn_to, attn_place = tile_places(owners)
    slot_seq = jnp.arange(seq_size)[:, None, None]
    slot_fsdp = jnp.arange(fsdp_size)[None, :, None]
    slot_chip = slot_fsdp // 2
    ffn_chip = jnp.where(ffn_to < 0, -1, ffn_to // 2)
    chip_view = ffn_chip.reshape(seq_size, chips, 2 * mine)
    chip_rank = count_earlier(chip_view, chip_view >= 0).reshape(owners.shape)
    seq_view = ffn_to.reshape(seq_size, fsdp_size * mine)
    ffn_rank = count_earlier(seq_view, seq_view >= 0).reshape(owners.shape)
    attn_view = attn_to.reshape(seq_size, chips, 2 * mine)
    attn_rank = count_earlier(attn_view, attn_view >= 0).reshape(owners.shape)
    attn_core = (attn_rank + slot_seq) % 2
    attn_rank = attn_rank // 2
    attn_key = jnp.where(attn_to < 0, -1, 2 * attn_to + attn_core)

    def by_chip(value):
        value = value.reshape(seq_size, chips, 2 * mine).transpose(1, 0, 2)
        return value.reshape(chips, seq_size * 2 * mine)

    attn_key_chip = by_chip(attn_key)
    attn_order_chip = count_earlier(attn_key_chip, attn_key_chip >= 0)
    attn_order = (
        attn_order_chip.reshape(chips, seq_size, 2 * mine).transpose(1, 0, 2).reshape(owners.shape)
    )
    fits = jnp.all(
        jnp.where(
            ffn_to < 0,
            (attn_rank < attn_room) & (attn_order < attn_hold),
            (chip_rank < 2 * ffn_room) & (ffn_rank < ffn_hold),
        )
    )
    half = chips * ffn_room
    rank_core = chip_rank // ffn_room
    rank_local = chip_rank % ffn_room
    out_place = (
        jnp.where(rank_core == my_core, 0, half)
        + (my_chip - slot_chip) % chips * ffn_room
        + rank_local
    )
    back_place = (
        jnp.where(rank_core == my_core, 0, half) + (my_chip - ffn_chip) % chips * ffn_room + rank_local
    )
    attn_back_place = (
        jnp.where(attn_core == my_core, 0, seq_size * attn_room)
        + (attn_to ^ my_seq) * attn_room
        + attn_rank
    )
    chip_slots = lax.dynamic_slice(
        jnp.stack([ffn_chip, chip_rank, attn_key, attn_rank]),
        (0, my_seq, 2 * my_chip, 0),
        (4, 1, 2, mine),
    ).reshape(4, 1, 1, 2 * mine)
    my_slots = lax.dynamic_slice(
        jnp.stack([ffn_to, back_place, attn_back_place]), (0, my_seq, my_fsdp, 0), (3, 1, 1, mine)
    ).reshape(3, mine)
    seq_slots = lax.dynamic_slice(
        jnp.stack(
            [
                ffn_to,
                ffn_rank,
                ffn_place,
                out_place,
                chip_rank,
                jnp.broadcast_to(slot_chip, owners.shape),
            ]
        ),
        (0, my_seq, 0, 0),
        (6, 1, fsdp_size, mine),
    ).reshape(6, fsdp_size * mine)
    column_slots = lax.dynamic_slice(
        jnp.stack([attn_key, attn_order, attn_rank, jnp.broadcast_to(slot_seq, owners.shape)]),
        (0, 0, 2 * my_chip, 0),
        (4, seq_size, 2, mine),
    ).reshape(4, 2 * seq_size * mine)
    my_key = 2 * my_seq + my_core

    local_slots = jnp.arange(mine)
    both_slots = jnp.arange(2 * mine)
    both_slots = jnp.where(
        both_slots // mine == my_core, both_slots % mine, mine + both_slots % mine
    )
    attn_pack = pick(
        (chip_slots[2] == (2 * (my_seq ^ flips) + my_core)[:, None, None])
        & (chip_slots[3] == jnp.arange(attn_room)[None, :, None]),
        both_slots,
    )
    attn_keep = pick(
        (column_slots[0][None, :] == my_key)
        & (column_slots[1][None, :] == jnp.arange(attn_hold)[:, None]),
        (column_slots[3] ^ my_seq) * attn_room + column_slots[2],
    )
    attn_join = pick(
        (attn_to.reshape(1, -1) == my_seq)
        & (attn_place.reshape(1, -1) == jnp.arange(attn_count)[:, None]),
        ((2 * slot_chip + attn_core) * attn_hold + attn_order).reshape(1, -1),
    )
    ffn_pack = pick(
        (chip_slots[0] == ((my_chip + shifts) % chips)[:, None, None])
        & (chip_slots[1] == (my_core * ffn_room + jnp.arange(ffn_room))[None, :, None]),
        both_slots,
    )
    ffn_keep = pick(
        (seq_slots[0][None, :] == my_fsdp) & (seq_slots[1][None, :] == jnp.arange(ffn_hold)[:, None]),
        seq_slots[3][None, :],
    )
    ffn_join = pick(
        (ffn_to.reshape(1, -1) == my_fsdp)
        & (ffn_place.reshape(1, -1) == jnp.arange(ffn_count)[:, None]),
        (slot_seq * ffn_hold + ffn_rank).reshape(1, -1),
    )
    master_low = tile_master.astype(bf16)
    masters = [master_low, core_swap(master_low)]
    attn_sent = gather_tiles(masters, attn_pack.reshape(-1))
    attn_sent = attn_sent.reshape(seq_size, attn_room, tile, tile)
    attn_got = seq_exchange([attn_sent[i] for i in range(seq_size)])
    attn_kept = gather_tiles(attn_got, attn_keep)
    attn_all = lax.all_gather(attn_kept, "fsdp", axis=0, tiled=True)

    ffn_got = chip_exchange([gather_tiles(masters, ffn_pack[i]) for i in range(chips)])
    pack_tokens = seq_gather(tokens[0])
    gain_full = seq_ordered(gains.astype(bf16))
    small_got = seq_ordered(small_master.astype(bf16))
    ffn_got, pack_tokens, gain_full, small_got = lax.optimization_barrier(
        (ffn_got, pack_tokens, gain_full, small_got)
    )
    ffn_other = [core_swap(value) for value in ffn_got]
    ffn_kept = gather_tiles(ffn_got + ffn_other, ffn_keep)
    ffn_all = lax.all_gather(ffn_kept, "seq", axis=0, tiled=True)
    w_first, w_out = join_tiles([attn_all], attn_join, row_blocks, attn_first, query_each)

    def slow_fetch(to, me, place, columns_of):
        def fetch(_, kept):
            whole = lax.all_gather(master_low, ("seq", "fsdp"), axis=0, tiled=True)
            count = row_blocks * sum(columns_of)
            index = pick(
                (to.reshape(1, -1) == me) & (place.reshape(1, -1) == jnp.arange(count)[:, None]),
                jnp.arange(tiles)[None, :],
            )
            return join_tiles([whole], index, row_blocks, *columns_of)

        return fetch

    slow_steps = jnp.where(fits, 0, 1)
    w_first, w_out = lax.fori_loop(
        0, slow_steps, slow_fetch(attn_to, my_seq, attn_place, (attn_first, query_each)), (w_first, w_out)
    )

    small_table = assemble(small_got.reshape((-1,) + small_master.shape[1:]), row_blocks)
    gain_full = gain_full.reshape(-1).astype(f32)
    gain_in = gain_full[0:width]
    gain_attn = gain_full[width : 2 * width]
    gain_laurel = gain_full[2 * width : 3 * width]
    gain_pre = gain_full[3 * width : 4 * width]
    gain_post = gain_full[4 * width : 5 * width]
    gain_vec = gain_full[5 * width : 6 * width]
    gain_query = gain_full[6 * width : 6 * width + HEAD_DIM]
    gain_key = gain_full[6 * width + HEAD_DIM : 6 * width + 2 * HEAD_DIM]
    laurel_left = small_table[:, :RANK]
    laurel_right = small_table[:, RANK : 2 * RANK]
    vector_gate_w = small_table[:, 2 * RANK : 2 * RANK + PLD]
    vector_proj_w = small_table[:, 2 * RANK + PLD :]

    segment, position = documents(doc_lengths[0], length)
    places = ((my_seq ^ flips)[:, None] * rows + jnp.arange(rows)[None, :]).reshape(-1)

    def reorder(values):
        blocks = values.reshape(seq_size, rows)
        return jnp.concatenate(
            [lax.dynamic_index_in_dim(blocks, my_seq ^ i, 0, False) for i in range(seq_size)]
        )

    pack_segment = reorder(segment)
    pack_position = reorder(position)
    stream = tokens[0].astype(f32)
    vectors = layer_vectors[0].astype(f32)
    normed, normed_pull = jax.vjp(rms_norm, stream, gain_in)
    normed_low = normed.astype(bf16)
    pack_normed = rms_norm(pack_tokens.astype(f32), gain_in).astype(bf16)
    first_pre = matmul(pack_normed, w_first)
    is_key = my_seq % per_key == 0

    def shape_query(query_in, query_gain):
        return rotary(
            rms_norm(query_in.reshape(length, per_device, HEAD_DIM), query_gain), pack_position
        )

    def shape_key(key_in, key_gain):
        return rotary(rms_norm(key_in.reshape(length, 1, HEAD_DIM), key_gain), pack_position)

    query_pre = first_pre[:, : per_device * HEAD_DIM]
    other_pre = first_pre[:, per_device * HEAD_DIM :]
    query_rot, query_pull = jax.vjp(shape_query, query_pre, gain_query)
    key_rot, key_pull = jax.vjp(shape_key, other_pre, gain_key)
    query_heads = query_rot.astype(bf16)
    other_low = jnp.where(is_key, key_rot[:, 0, :], other_pre).astype(bf16)
    partner_low = seq_swap(other_low, 1).reshape(seq_size // 2, 2, rows, HEAD_DIM)
    partner_low = partner_low[:, ::-1].reshape(length, HEAD_DIM)
    key_single = jnp.where(is_key, other_low, partner_low)
    value_single = jnp.where(is_key, partner_low, other_low)

    allow = (pack_segment[:, None] == pack_segment[None, :]) & (
        places[None, :] <= places[:, None]
    )
    raw = (
        jnp.einsum("qhd,kd->qhk", query_heads, key_single, preferred_element_type=f32) * SCALE
    )
    scores = jnp.where(allow[:, None, :], raw, NEGATIVE)
    powers = jnp.exp(scores - jnp.max(scores, axis=-1, keepdims=True))
    prob = powers / jnp.sum(powers, axis=-1, keepdims=True)
    prob_low = prob.astype(bf16)
    attended_low = (
        jnp.einsum("qhk,kd->qhd", prob_low, value_single, preferred_element_type=f32)
        .astype(bf16)
        .reshape(length, per_device * HEAD_DIM)
    )
    attn_pre = seq_sum(matmul_flip(attended_low, w_out), bf16)
    attn_normed, attn_pull = jax.vjp(rms_norm, attn_pre, gain_attn)
    first_sum = stream + attn_normed
    left_pre = matmul(normed_low, laurel_left)
    left_low = left_pre.astype(bf16)
    right_pre = matmul_flip(left_low, laurel_right)
    laurel_normed, laurel_pull = jax.vjp(rms_norm, right_pre, gain_laurel)
    second_sum = (first_sum + normed + laurel_normed) * ROOT_HALF
    feed_normed, feed_pull = jax.vjp(rms_norm, second_sum, gain_pre)
    ffn_all, feed_own = lax.optimization_barrier((ffn_all, feed_normed.astype(bf16)))
    feed_low = lax.all_gather(feed_own, "fsdp", axis=0, tiled=True)
    w_both, w_down = join_tiles([ffn_all], ffn_join, row_blocks, ffn_first, ffn_each)
    w_both, w_down = lax.fori_loop(
        0, slow_steps, slow_fetch(ffn_to, my_fsdp, ffn_place, (ffn_first, ffn_each)), (w_both, w_down)
    )
    both_pre = matmul(feed_low, w_both)
    ffn_width = w_down.shape[1]
    hidden, hidden_pull = jax.vjp(gelu_product, both_pre[:, :ffn_width], both_pre[:, ffn_width:])
    hidden_low = hidden.astype(bf16)
    down_pre = lax.psum_scatter(
        matmul_flip(hidden_low, w_down).astype(bf16), "fsdp", scatter_dimension=0, tiled=True
    ).astype(f32)
    down_normed, down_pull = jax.vjp(rms_norm, down_pre, gain_post)
    third_sum = second_sum + down_normed
    third_low = third_sum.astype(bf16)
    vector_pre = matmul(third_low, vector_gate_w)
    vector_gated, vector_pull = jax.vjp(lambda inner: gelu_product(inner, vectors), vector_pre)
    vector_low = vector_gated.astype(bf16)
    proj_pre = matmul_flip(vector_low, vector_proj_w)
    proj_normed, proj_pull = jax.vjp(rms_norm, proj_pre, gain_vec)
    result = third_sum + proj_normed
    output = result.astype(bf16)[None]

    grad_out = cotangent[0].astype(f32)
    grad_proj, grad_gain_vec = proj_pull(grad_out)
    proj_grad_low = grad_proj.astype(bf16)
    (grad_vector_pre,) = vector_pull(matmul(proj_grad_low, vector_proj_w))
    vector_grad_low = grad_vector_pre.astype(bf16)
    grad_third = grad_out + matmul_flip(vector_grad_low, vector_gate_w)
    grad_down, grad_gain_post = down_pull(grad_third)
    down_grad_low = lax.all_gather(grad_down.astype(bf16), "fsdp", axis=0, tiled=True)
    grad_gate, grad_up = hidden_pull(matmul(down_grad_low, w_down))
    both_grad_low = jnp.concatenate([grad_gate, grad_up], axis=1).astype(bf16)
    grad_feed = lax.psum_scatter(
        matmul_flip(both_grad_low, w_both).astype(bf16), "fsdp", scatter_dimension=0, tiled=True
    ).astype(f32)
    both_grad_w = matmul_outer(feed_low, both_grad_low).astype(bf16)
    down_grad_w = matmul_outer(down_grad_low, hidden_low).astype(bf16)

    flip_to = ffn_to.reshape(seq_size, 1, -1)[my_seq ^ flips]
    flip_rank = ffn_rank.reshape(seq_size, 1, -1)[my_seq ^ flips]
    flip_place = ffn_place.reshape(seq_size, 1, -1)[my_seq ^ flips]
    ffn_cut = pick(
        (flip_to == my_fsdp) & (flip_rank == jnp.arange(ffn_hold)[None, :, None]), flip_place
    )
    ffn_back = pick(
        (seq_slots[5][None, None, :] == ((my_chip + shifts) % chips)[:, None, None])
        & (seq_slots[0][None, None, :] // 2 == my_chip)
        & (seq_slots[0][None, None, :] >= 0)
        & (seq_slots[4][None, None, :] == (my_core * ffn_room + jnp.arange(ffn_room))[None, :, None]),
        jnp.where(seq_slots[0] == my_fsdp, 0, ffn_hold) + seq_slots[1],
    )

    def ffn_parts(flips_of, half):
        index = ffn_cut[:, half * ffn_half : (half + 1) * ffn_half][jnp.array(flips_of)]
        return cut_tiles(both_grad_w, down_grad_w, index.reshape(-1), tile)

    cut_one, cut_two = ffn_parts([1, 3], 0), ffn_parts([2, 3], 1)
    cut_one, cut_two, grad_feed = lax.optimization_barrier((cut_one, cut_two, grad_feed))
    got_one, got_two = seq_swap(cut_one, 1), seq_swap(cut_two, 2)

    grad_second_norm, grad_gain_pre = feed_pull(grad_feed)
    half_grad = (grad_third + grad_second_norm) * ROOT_HALF
    grad_right, grad_gain_laurel = laurel_pull(half_grad)
    right_grad_low = grad_right.astype(bf16)
    left_grad_low = matmul(right_grad_low, laurel_right).astype(bf16)
    grad_attn, grad_gain_attn = attn_pull(half_grad)
    attn_grad_low = seq_gather(grad_attn.astype(bf16))
    grad_attended = (
        matmul(attn_grad_low, w_out).astype(bf16).reshape(length, per_device, HEAD_DIM)
    )
    out_grad_w = matmul_outer(attn_grad_low, attended_low).astype(bf16)
    value_grad = jnp.einsum("qhk,qhd->kd", prob_low, grad_attended, preferred_element_type=f32)
    grad_prob = jnp.einsum("qhd,kd->qhk", grad_attended, value_single, preferred_element_type=f32)
    inner = jnp.sum(prob * grad_prob, axis=-1, keepdims=True)
    grad_score = (prob * (grad_prob - inner)).astype(bf16)
    grad_query = (
        jnp.einsum("qhk,kd->qhd", grad_score, key_single, preferred_element_type=f32) * SCALE
    ).astype(bf16)
    key_grad = (
        jnp.einsum("qhk,qhd->kd", grad_score, query_heads, preferred_element_type=f32) * SCALE
    ).astype(bf16)
    value_grad = value_grad.astype(bf16)
    partner_grad = seq_swap(jnp.where(is_key, value_grad, key_grad), 1)
    partner_grad = partner_grad.reshape(seq_size // 2, 2, rows, HEAD_DIM)[:, ::-1]
    other_grad = jnp.where(is_key, key_grad, value_grad).astype(f32) + partner_grad.reshape(
        length, HEAD_DIM
    ).astype(f32)
    grad_query_pre, grad_gain_query = query_pull(grad_query.astype(f32))
    grad_key_pre, grad_gain_key = key_pull(other_grad[:, None, :])
    grad_gain_key = jnp.where(is_key, grad_gain_key, 0.0)
    first_grad_low = jnp.concatenate(
        [grad_query_pre, jnp.where(is_key, grad_key_pre, other_grad)], axis=1
    ).astype(bf16)
    first_grad_w = matmul_outer(pack_normed, first_grad_low).astype(bf16)
    grad_normed = (
        half_grad
        + matmul_flip(left_grad_low, laurel_left)
        + seq_sum(matmul_flip(first_grad_low, w_first), bf16)
    )
    grad_stream_norm, grad_gain_in = normed_pull(grad_normed)
    input_grad = (half_grad + grad_stream_norm)[None]

    def added(one, two):
        return one.astype(f32) + two.astype(f32)

    one_sum = added(ffn_parts([0, 2], 0), got_one)
    two_sum = added(ffn_parts([0, 1], 1), got_two)
    one_sum = added(one_sum[:ffn_half], seq_swap(one_sum[ffn_half:].astype(bf16), 2)).astype(bf16)
    two_sum = added(two_sum[:ffn_half], seq_swap(two_sum[ffn_half:].astype(bf16), 1)).astype(bf16)
    ffn_sums = [one_sum, two_sum, core_swap(one_sum), core_swap(two_sum)]
    ffn_return = [gather_tiles(ffn_sums, ffn_back[i]) for i in range(chips)]
    ffn_returned = chip_exchange(ffn_return)
    ffn_returned = ffn_returned + [core_swap(value) for value in ffn_returned]

    attn_cut = pick(
        (attn_key_chip[:, None, None, :] == (2 * my_seq + jnp.arange(2))[None, :, None, None])
        & (attn_order_chip[:, None, None, :] == jnp.arange(attn_hold)[None, None, :, None]),
        by_chip(attn_place)[:, None, None, :],
    )
    attn_back = pick(
        (column_slots[3][None, None, :] == (my_seq ^ flips)[:, None, None])
        & (column_slots[0][None, None, :] == my_key)
        & (column_slots[2][None, None, :] == jnp.arange(attn_room)[None, :, None]),
        column_slots[1],
    )
    attn_parts = cut_tiles(first_grad_w, out_grad_w, attn_cut.reshape(-1), tile)
    attn_sum = lax.psum_scatter(attn_parts, "fsdp", scatter_dimension=0, tiled=True)
    attn_returned = seq_exchange([gather_tiles([attn_sum], attn_back[i]) for i in range(seq_size)])
    attn_returned = attn_returned + [core_swap(value) for value in attn_returned]
    slot_grad = jnp.where(my_slots[0] >= 0, my_slots[1], 2 * half + my_slots[2])

    def slow_return(_, kept):
        own_ffn = split_tiles(both_grad_w, tile), split_tiles(down_grad_w, tile)
        own_attn = split_tiles(first_grad_w, tile), split_tiles(out_grad_w, tile)
        parts = jnp.concatenate(own_ffn + own_attn + (jnp.zeros((1, tile, tile), bf16),))
        index = jnp.where(
            ffn_to == my_fsdp,
            ffn_place,
            jnp.where(attn_to == my_seq, ffn_count + attn_place, ffn_count + attn_count),
        )
        spread = gather_tiles([parts], index.reshape(-1))
        return lax.psum_scatter(spread, ("seq", "fsdp"), scatter_dimension=0, tiled=True)

    tile_grads = ffn_returned + attn_returned
    slow_start = 2 * half + 2 * seq_size * attn_room
    slow_grads = lax.fori_loop(0, slow_steps, slow_return, jnp.zeros((mine, tile, tile), bf16))
    tile_grads = tile_grads + [slow_grads]
    slot_grad = jnp.where(fits, slot_grad, slow_start + local_slots)

    small_full = jnp.concatenate(
        [
            matmul_outer(normed_low, left_grad_low),
            matmul_outer(right_grad_low, left_low),
            matmul_outer(third_low, vector_grad_low),
            matmul_outer(proj_grad_low, vector_low),
        ],
        axis=1,
    )
    small_tiles_grad = split_tiles(small_full, tile)
    gain_grad = jnp.concatenate(
        [
            grad_gain_in,
            grad_gain_attn,
            grad_gain_laurel,
            grad_gain_pre,
            grad_gain_post,
            grad_gain_vec,
            grad_gain_query,
            grad_gain_key,
        ]
    )
    small_part = seq_sum(small_tiles_grad, bf16, True)
    small_grad = fsdp_sum(small_part.reshape(-1, tile)).reshape(small_part.shape)
    gain_part = seq_sum(gain_grad, f32, True)
    gain_part = gain_part + core_swap(gain_part)
    gain_grad_mine = gain_part
    for offset in range(1, chips):
        gain_grad_mine = gain_grad_mine + chip_shift(gain_part, offset)
    tile_new, tile_first_new, tile_second_new = rotate_update(
        tile_grads, slot_grad, tile_master, tile_first, tile_second, left_basis, right_basis, RATE_TILE
    )
    small_new, small_first_new, small_second_new = rotate_update(
        [small_grad],
        jnp.arange(small_master.shape[0]),
        small_master,
        small_first,
        small_second,
        small_left,
        small_right,
        RATE_SMALL,
    )
    gain_first_new = BETA_ONE * gain_first + (1.0 - BETA_ONE) * gain_grad_mine
    gain_second_new = BETA_TWO * gain_second + (1.0 - BETA_TWO) * gain_grad_mine * gain_grad_mine
    correct_one = 1.0 - BETA_ONE**STEP
    correct_two = 1.0 - BETA_TWO**STEP
    gain_new = gains - RATE_GAIN * (gain_first_new / correct_one) / (
        jnp.sqrt(gain_second_new / correct_two) + ADAM_EPS
    )
    return (
        output,
        input_grad,
        tile_new,
        tile_first_new,
        tile_second_new,
        small_new,
        small_first_new,
        small_second_new,
        gain_new,
        gain_first_new,
        gain_second_new,
    )


def solution(mesh):
    return jax.shard_map(
        on_device,
        mesh=mesh,
        in_specs=(
            P("fsdp", "seq", None),
            P("fsdp", "seq", None),
            P("fsdp", None),
            P("fsdp", "seq", None),
            P(),
            P(("seq", "fsdp"), None, None),
            P(("seq", "fsdp"), None, None),
            P(("seq", "fsdp"), None, None),
            P(("seq", "fsdp"), None, None),
            P(("seq", "fsdp"), None, None),
            P("seq", None, None),
            P("seq", None, None),
            P("seq", None, None),
            P("seq", None, None),
            P("seq", None, None),
            P("seq"),
            P("seq"),
            P("seq"),
        ),
        out_specs=(
            P("fsdp", "seq", None),
            P("fsdp", "seq", None),
            P(("seq", "fsdp"), None, None),
            P(("seq", "fsdp"), None, None),
            P(("seq", "fsdp"), None, None),
            P("seq", None, None),
            P("seq", None, None),
            P("seq", None, None),
            P("seq"),
            P("seq"),
            P("seq"),
        ),
        check_vma=False,
    )
```

```python
import math

import jax
import jax.numpy as jnp
from jax import lax
from jax.experimental import pallas as pl
from jax.experimental.pallas import tpu as pltpu
from jax.sharding import PartitionSpec as P

HEADS = 8
KV_HEADS = 2
HEAD_DIM = 256
FF = 8192
RANK = 64
PLD = 256
STEP = 5


EPS = 1e-06
SCALE = 0.0625
THETA = 1000000.0
ROOT_HALF = 0.7071067811865476
BETA_ONE = 0.5
BETA_TWO = 0.5
ADAM_EPS = 1e-08
RATE_TILE = 0.02
RATE_SMALL = 0.04
RATE_GAIN = 0.3
DECAY = 0.01
NEGATIVE = -1e30
VMEM_BYTES = 32 * 1024 * 1024


def rms_norm(value, gain):
    return value * lax.rsqrt(jnp.mean(value * value, axis=-1, keepdims=True) + EPS) * gain


def rotary(value, position):
    half = value.shape[-1] // 2
    freq = THETA ** (-2.0 * jnp.arange(half).astype(jnp.float32) / value.shape[-1])
    angle = position.astype(jnp.float32)[:, None] * freq[None, :]
    cosine = jnp.cos(angle)[:, None, :]
    sine = jnp.sin(angle)[:, None, :]
    first = value[..., :half]
    second = value[..., half:]
    return jnp.concatenate(
        [first * cosine - second * sine, second * cosine + first * sine], axis=-1
    )


def documents(lengths, length):
    places = jnp.arange(length)
    ends = jnp.cumsum(lengths)
    passed = places[:, None] >= ends[None, :]
    segment = jnp.sum(passed.astype(jnp.int32), axis=1)
    before = jnp.sum(jnp.where(passed, lengths[None, :], 0), axis=1)
    return (segment, places - before)


def matmul(left, right):
    return jnp.dot(left, right, preferred_element_type=jnp.float32)


def matmul_flip(left, right):
    return lax.dot_general(
        left, right, (((1,), (1,)), ((), ())), preferred_element_type=jnp.float32
    )


def matmul_outer(left, right):
    return lax.dot_general(
        left, right, (((0,), (0,)), ((), ())), preferred_element_type=jnp.float32
    )


def assemble(tiles, row_blocks):
    size = tiles.shape[1]
    column_blocks = tiles.shape[0] // row_blocks
    return (
        tiles.reshape(row_blocks, column_blocks, size, size)
        .transpose(0, 2, 1, 3)
        .reshape(row_blocks * size, column_blocks * size)
    )


def split_tiles(matrix, size):
    row_blocks = matrix.shape[0] // size
    column_blocks = matrix.shape[1] // size
    return (
        matrix.reshape(row_blocks, size, column_blocks, size)
        .transpose(0, 2, 1, 3)
        .reshape(row_blocks * column_blocks, size, size)
    )


def gelu_product(first, second):
    return jax.nn.gelu(first, approximate=True) * second


def room(count, share):
    mean = count * share
    return math.ceil(mean + 3.6 * math.sqrt(mean * (1.0 - share)) + 3.0)


def count_earlier(group, valid):
    size = group.shape[-1]
    order = jnp.arange(size)
    same = (group[..., :, None] == group[..., None, :]) & valid[..., None, :]
    same = same & (order[None, :] < order[:, None])
    return jnp.sum(same.astype(jnp.int32), axis=-1)


def pick(match, value):
    return jnp.sum(jnp.where(match, value, 0), axis=-1)


def steps_of(count):
    for steps in range(4, 65):
        if count % steps == 0 and 16 <= count // steps <= 160:
            return steps
    return 2 if count % 2 == 0 else 1


def tile_kernel_call(kernel, index, arrays, out_shape, out_specs, steps):
    return pl.pallas_call(
        kernel,
        grid=(steps,),
        out_shape=out_shape,
        in_specs=[pl.BlockSpec(memory_space=pltpu.SMEM)]
        + [pl.BlockSpec(memory_space=pl.ANY)] * len(arrays),
        out_specs=out_specs,
        scratch_shapes=[pltpu.SemaphoreType.DMA],
        compiler_params=pltpu.CompilerParams(vmem_limit_bytes=VMEM_BYTES),
    )(index, *arrays)


def start_copy(sources, place, target, sem):
    start = 0
    for ref in sources:
        size = ref.shape[0]

        @pl.when((place >= start) & (place < start + size))
        def _(ref=ref, start=start):
            pltpu.make_async_copy(ref.at[place - start], target, sem).start()

        start = start + size


def gather_tiles(arrays, index):
    tile = arrays[0].shape[-1]
    count = index.shape[0]
    steps = steps_of(count)
    each = count // steps

    def kernel(index_ref, *refs):
        sources, out, sem = refs[:-2], refs[-2], refs[-1]
        base = pl.program_id(0) * each

        def step(i, carry):
            start_copy(sources, index_ref[base + i], out.at[i], sem)
            return carry

        lax.fori_loop(0, each, step, 0)
        pltpu.make_async_copy(out, out, sem).wait()

    total = sum(array.shape[0] for array in arrays)
    return tile_kernel_call(
        kernel,
        jnp.clip(index, 0, total - 1),
        arrays,
        jax.ShapeDtypeStruct((count, tile, tile), arrays[0].dtype),
        pl.BlockSpec((each, tile, tile), lambda i: (i, 0, 0)),
        steps,
    )


def join_tiles(arrays, index, row_blocks, first_columns, second_columns):
    tile = arrays[0].shape[-1]
    first_count = row_blocks * first_columns
    steps = 4
    each = row_blocks // steps

    def kernel(index_ref, *refs):
        sources, first, second, sem = refs[:-3], refs[-3], refs[-2], refs[-1]
        base = pl.program_id(0) * each
        for out, start, columns in ((first, 0, first_columns), (second, first_count, second_columns)):

            def step(i, carry, out=out, start=start, columns=columns):
                row = i // columns
                column = i - row * columns
                target = out.at[
                    pl.ds(pl.multiple_of(row * tile, tile), tile),
                    pl.ds(pl.multiple_of(column * tile, tile), tile),
                ]
                start_copy(sources, index_ref[start + base * columns + i], target, sem)
                return carry

            lax.fori_loop(0, each * columns, step, 0)
        pltpu.make_async_copy(first, first, sem).wait()
        pltpu.make_async_copy(second, second, sem).wait()

    total = sum(array.shape[0] for array in arrays)
    out_shape = tuple(
        jax.ShapeDtypeStruct((row_blocks * tile, count * tile), arrays[0].dtype)
        for count in (first_columns, second_columns)
    )
    out_specs = tuple(
        pl.BlockSpec((each * tile, count * tile), lambda i: (i, 0))
        for count in (first_columns, second_columns)
    )
    return tile_kernel_call(
        kernel, jnp.clip(index, 0, total - 1), arrays, out_shape, out_specs, steps
    )


def cut_tiles(first, second, index, tile):
    row_blocks = first.shape[0] // tile
    first_columns = first.shape[1] // tile
    second_columns = second.shape[1] // tile
    first_count = row_blocks * first_columns
    count = index.shape[0]
    steps = steps_of(count)
    each = count // steps

    def kernel(index_ref, first_ref, second_ref, out, sem):
        base = pl.program_id(0) * each

        def step(i, carry):
            place = index_ref[base + i]

            def send(ref, local, columns):
                row = pl.multiple_of((local // columns) * tile, tile)
                column = pl.multiple_of((local % columns) * tile, tile)
                pltpu.make_async_copy(
                    ref.at[pl.ds(row, tile), pl.ds(column, tile)], out.at[i], sem
                ).start()

            @pl.when(place < first_count)
            def _():
                send(first_ref, place, first_columns)

            @pl.when(place >= first_count)
            def _():
                send(second_ref, place - first_count, second_columns)

            return carry

        lax.fori_loop(0, each, step, 0)
        pltpu.make_async_copy(out, out, sem).wait()

    return tile_kernel_call(
        kernel,
        jnp.clip(index, 0, first_count + row_blocks * second_columns - 1),
        [first, second],
        jax.ShapeDtypeStruct((count, tile, tile), first.dtype),
        pl.BlockSpec((each, tile, tile), lambda i: (i, 0, 0)),
        steps,
    )


def split_low(value):
    high = value.astype(jnp.bfloat16)
    return high, (value - high.astype(jnp.float32)).astype(jnp.bfloat16)


def rotate_update(grads, index, master, first, second, left, right, rate):
    count, tile, _ = master.shape
    each = 4 if count % 4 == 0 else 1
    correct_one = 1.0 - BETA_ONE**STEP
    correct_two = 1.0 - BETA_TWO**STEP

    def product(one, two, dims):
        return lax.dot_general(one, two, (dims, ((), ())), preferred_element_type=jnp.float32)

    def kernel(index_ref, *refs):
        sources, refs = refs[: len(grads)], refs[len(grads) :]
        master_ref, first_ref, second_ref, left_ref, right_ref = refs[:5]
        master_out, first_out, second_out, held, sems = refs[5:]
        now = pl.program_id(0)

        @pl.when(now == 0)
        def _():
            def step(i, carry):
                start_copy(sources, index_ref[i], held.at[i], sems.at[i // each])
                return carry

            lax.fori_loop(0, count, step, 0)

        block = held.at[pl.ds(now * each, each)]
        pltpu.make_async_copy(block, block, sems.at[now]).wait()
        lefts, rights, turns = [], [], []
        for i in range(each):
            grad = held[now * each + i]
            lefts.append(split_low(left_ref[i]))
            rights.append(split_low(right_ref[i]))
            half_turned = product(
                jnp.concatenate([grad, grad], axis=1),
                jnp.concatenate(rights[i], axis=0),
                ((1,), (0,)),
            )
            turns.append(split_low(half_turned))
        for i in range(each):
            (left_high, left_low), (high, low) = lefts[i], turns[i]
            turns[i] = product(
                jnp.concatenate([left_high, left_high, left_low], axis=0),
                jnp.concatenate([high, low, high], axis=0),
                ((0,), (0,)),
            )
        for i in range(each):
            right_high, right_low = rights[i]
            first_new = BETA_ONE * first_ref[i] + (1.0 - BETA_ONE) * turns[i]
            second_new = BETA_TWO * second_ref[i] + (1.0 - BETA_TWO) * turns[i] * turns[i]
            first_out[i] = first_new
            second_out[i] = second_new
            high, low = split_low(
                first_new / correct_one / (jnp.sqrt(second_new / correct_two) + ADAM_EPS)
            )
            half_back = product(
                jnp.concatenate([high, low, high], axis=1),
                jnp.concatenate([right_high, right_high, right_low], axis=1),
                ((1,), (1,)),
            )
            turns[i] = split_low(half_back)
        for i in range(each):
            (left_high, left_low), (high, low) = lefts[i], turns[i]
            back = product(
                jnp.concatenate([left_high, left_high, left_low], axis=1),
                jnp.concatenate([high, low, high], axis=0),
                ((1,), (0,)),
            )
            weight = master_ref[i]
            master_out[i] = weight - rate * (back + DECAY * weight)

    spec = pl.BlockSpec((each, tile, tile), lambda i: (i, 0, 0))
    shape = jax.ShapeDtypeStruct(master.shape, jnp.float32)
    total = sum(array.shape[0] for array in grads)
    return pl.pallas_call(
        kernel,
        grid=(count // each,),
        out_shape=(shape, shape, shape),
        in_specs=[pl.BlockSpec(memory_space=pltpu.SMEM)]
        + [pl.BlockSpec(memory_space=pl.ANY)] * len(grads)
        + [spec] * 5,
        out_specs=(spec, spec, spec),
        scratch_shapes=[
            pltpu.VMEM((count, tile, tile), jnp.bfloat16),
            pltpu.SemaphoreType.DMA((count // each,)),
        ],
        compiler_params=pltpu.CompilerParams(vmem_limit_bytes=VMEM_BYTES),
    )(jnp.clip(index, 0, total - 1), *grads, master, first, second, left, right)


def seq_swap(value, flip):
    size = lax.axis_size("seq")
    return lax.ppermute(value, "seq", [(i, i ^ flip) for i in range(size)])


def core_swap(value):
    size = lax.axis_size("fsdp")
    return lax.ppermute(value, "fsdp", [(i, i ^ 1) for i in range(size)])


def chip_shift(value, offset):
    size = lax.axis_size("fsdp")
    chips = size // 2
    return lax.ppermute(
        value, "fsdp", [(i, (i // 2 + offset) % chips * 2 + i % 2) for i in range(size)]
    )


def seq_gather(value):
    size = lax.axis_size("seq")
    return jnp.concatenate([value] + [seq_swap(value, flip) for flip in range(1, size)], axis=0)


def seq_ordered(value):
    size = lax.axis_size("seq")
    parts = jnp.stack([value] + [seq_swap(value, flip) for flip in range(1, size)], axis=0)
    return parts[lax.axis_index("seq") ^ jnp.arange(size)]


def seq_exchange(values):
    return [values[0]] + [seq_swap(values[flip], flip) for flip in range(1, len(values))]


def seq_sum(value, wire, ordered=False):
    size = lax.axis_size("seq")
    parts = value.reshape((size, value.shape[0] // size) + value.shape[1:])
    if ordered:
        parts = parts[lax.axis_index("seq") ^ jnp.arange(size)]
    total = parts[0]
    for flip in range(1, size):
        total = total + seq_swap(parts[flip].astype(wire), flip).astype(jnp.float32)
    return total


def chip_exchange(values):
    return [values[0]] + [chip_shift(values[offset], offset) for offset in range(1, len(values))]


def fsdp_sum(value):
    size = lax.axis_size("fsdp")
    chips = size // 2
    chip = lax.axis_index("fsdp") // 2
    even = lax.axis_index("fsdp") % 2 == 0
    shares = value.reshape((chips, 2, value.shape[0] // size) + value.shape[1:])
    kept = jnp.where(even, shares[:, 0], shares[:, 1])
    given = jnp.where(even, shares[:, 1], shares[:, 0])
    kept = kept + core_swap(given.astype(jnp.bfloat16)).astype(jnp.float32)
    kept = kept[(chip + jnp.arange(chips)) % chips]
    total = kept[0]
    for offset in range(1, chips):
        total = total + chip_shift(kept[offset].astype(jnp.bfloat16), offset).astype(jnp.float32)
    total = total.astype(jnp.bfloat16)
    parts = jnp.stack([total] + [chip_shift(total, offset) for offset in range(1, chips)])
    parts = parts[(chip - jnp.arange(chips)) % chips]
    other = core_swap(parts)
    both = jnp.where(even, jnp.stack([parts, other], axis=1), jnp.stack([other, parts], axis=1))
    return both.reshape(value.shape)


def on_device(
    tokens,
    layer_vectors,
    doc_lengths,
    cotangent,
    tile_owner,
    tile_master,
    tile_first,
    tile_second,
    left_basis,
    right_basis,
    small_master,
    small_first,
    small_second,
    small_left,
    small_right,
    gains,
    gain_first,
    gain_second,
):
    bf16 = jnp.bfloat16
    f32 = jnp.float32
    tile = tile_master.shape[1]
    width = tokens.shape[2]
    row_blocks = width // tile
    rows = tokens.shape[1]
    seq_size = lax.axis_size("seq")
    fsdp_size = lax.axis_size("fsdp")
    chips = fsdp_size // 2
    mine = tile_master.shape[0]
    tiles = tile_owner.shape[0]
    length = rows * seq_size
    per_device = HEADS // seq_size
    per_key = seq_size // KV_HEADS
    query_width = HEADS * HEAD_DIM
    key_width = KV_HEADS * HEAD_DIM
    my_seq = lax.axis_index("seq")
    my_fsdp = lax.axis_index("fsdp")
    my_chip = my_fsdp // 2
    my_core = my_fsdp % 2
    flips = jnp.arange(seq_size)
    shifts = jnp.arange(chips)

    query_blocks = query_width // tile
    key_blocks = key_width // tile
    ffn_blocks = FF // tile
    query_each = query_blocks // seq_size
    head_blocks = HEAD_DIM // tile
    ffn_each = ffn_blocks // fsdp_size
    columns = tiles // row_blocks
    attn_first = query_each + head_blocks
    attn_count = row_blocks * (attn_first + query_each)
    ffn_first = 2 * ffn_each
    ffn_count = row_blocks * 3 * ffn_each
    attn_share = (2 * query_blocks + 2 * key_blocks) / columns
    ffn_share = 3 * ffn_blocks / columns
    attn_room = (room(2 * mine, attn_share / seq_size) + 1) // 2
    attn_hold = (room(attn_count, 1.0 / chips) + 1) // 2 + 1
    ffn_room = (room(2 * mine, ffn_share / chips) + 1) // 2
    ffn_hold = (room(ffn_count, 1.0 / seq_size) + 3) // 4 * 4

    def tile_places(owner):
        row = owner // columns
        column = owner % columns
        key_at = column - query_blocks
        value_at = key_at - key_blocks
        out_at = value_at - key_blocks
        ffn_at = out_at - query_blocks
        is_attn = ffn_at < 0
        kind = ffn_at // ffn_blocks
        ffn_column = ffn_at % ffn_blocks
        ffn_to = jnp.where(is_attn, -1, ffn_column // ffn_each)
        ffn_local = ffn_column % ffn_each
        ffn_place = jnp.where(
            kind == 2,
            row_blocks * ffn_first + row * ffn_each + ffn_local,
            row * ffn_first + kind * ffn_each + ffn_local,
        )
        attn_to = jnp.where(
            key_at < 0,
            column // query_each,
            jnp.where(
                value_at < 0,
                key_at // head_blocks * per_key,
                jnp.where(
                    out_at < 0,
                    value_at // head_blocks * per_key + per_key - 1,
                    out_at // query_each,
                ),
            ),
        )
        attn_place = jnp.where(
            key_at < 0,
            row * attn_first + column % query_each,
            jnp.where(
                out_at < 0,
                row * attn_first + query_each + key_at % head_blocks,
                row_blocks * attn_first + row * query_each + out_at % query_each,
            ),
        )
        attn_to = jnp.where(is_attn, attn_to, -1)
        return (ffn_to, ffn_place, attn_to, attn_place)

    owners = tile_owner.reshape(seq_size, fsdp_size, mine)
    ffn_to, ffn_place, attn_to, attn_place = tile_places(owners)
    slot_seq = jnp.arange(seq_size)[:, None, None]
    slot_fsdp = jnp.arange(fsdp_size)[None, :, None]
    slot_chip = slot_fsdp // 2
    ffn_chip = jnp.where(ffn_to < 0, -1, ffn_to // 2)
    chip_view = ffn_chip.reshape(seq_size, chips, 2 * mine)
    chip_rank = count_earlier(chip_view, chip_view >= 0).reshape(owners.shape)
    seq_view = ffn_to.reshape(seq_size, fsdp_size * mine)
    ffn_rank = count_earlier(seq_view, seq_view >= 0).reshape(owners.shape)
    attn_view = attn_to.reshape(seq_size, chips, 2 * mine)
    attn_rank = count_earlier(attn_view, attn_view >= 0).reshape(owners.shape)
    attn_core = (attn_rank + slot_seq) % 2
    attn_rank = attn_rank // 2
    attn_key = jnp.where(attn_to < 0, -1, 2 * attn_to + attn_core)

    def by_chip(value):
        value = value.reshape(seq_size, chips, 2 * mine).transpose(1, 0, 2)
        return value.reshape(chips, seq_size * 2 * mine)

    attn_key_chip = by_chip(attn_key)
    attn_order_chip = count_earlier(attn_key_chip, attn_key_chip >= 0)
    attn_order = (
        attn_order_chip.reshape(chips, seq_size, 2 * mine).transpose(1, 0, 2).reshape(owners.shape)
    )
    fits = jnp.all(
        jnp.where(
            ffn_to < 0,
            (attn_rank < attn_room) & (attn_order < attn_hold),
            (chip_rank < 2 * ffn_room) & (ffn_rank < ffn_hold),
        )
    )
    half = chips * ffn_room
    rank_core = chip_rank // ffn_room
    rank_local = chip_rank % ffn_room
    out_place = (
        jnp.where(rank_core == my_core, 0, half)
        + (my_chip - slot_chip) % chips * ffn_room
        + rank_local
    )
    back_place = (
        jnp.where(rank_core == my_core, 0, half) + (my_chip - ffn_chip) % chips * ffn_room + rank_local
    )
    attn_back_place = (
        jnp.where(attn_core == my_core, 0, seq_size * attn_room)
        + (attn_to ^ my_seq) * attn_room
        + attn_rank
    )
    chip_slots = lax.dynamic_slice(
        jnp.stack([ffn_chip, chip_rank, attn_key, attn_rank]),
        (0, my_seq, 2 * my_chip, 0),
        (4, 1, 2, mine),
    ).reshape(4, 1, 1, 2 * mine)
    my_slots = lax.dynamic_slice(
        jnp.stack([ffn_to, back_place, attn_back_place]), (0, my_seq, my_fsdp, 0), (3, 1, 1, mine)
    ).reshape(3, mine)
    seq_slots = lax.dynamic_slice(
        jnp.stack(
            [
                ffn_to,
                ffn_rank,
                ffn_place,
                out_place,
                chip_rank,
                jnp.broadcast_to(slot_chip, owners.shape),
            ]
        ),
        (0, my_seq, 0, 0),
        (6, 1, fsdp_size, mine),
    ).reshape(6, fsdp_size * mine)
    column_slots = lax.dynamic_slice(
        jnp.stack([attn_key, attn_order, attn_rank, jnp.broadcast_to(slot_seq, owners.shape)]),
        (0, 0, 2 * my_chip, 0),
        (4, seq_size, 2, mine),
    ).reshape(4, 2 * seq_size * mine)
    my_key = 2 * my_seq + my_core

    local_slots = jnp.arange(mine)
    both_slots = jnp.arange(2 * mine)
    both_slots = jnp.where(
        both_slots // mine == my_core, both_slots % mine, mine + both_slots % mine
    )
    attn_pack = pick(
        (chip_slots[2] == (2 * (my_seq ^ flips) + my_core)[:, None, None])
        & (chip_slots[3] == jnp.arange(attn_room)[None, :, None]),
        both_slots,
    )
    attn_keep = pick(
        (column_slots[0][None, :] == my_key)
        & (column_slots[1][None, :] == jnp.arange(attn_hold)[:, None]),
        (column_slots[3] ^ my_seq) * attn_room + column_slots[2],
    )
    attn_join = pick(
        (attn_to.reshape(1, -1) == my_seq)
        & (attn_place.reshape(1, -1) == jnp.arange(attn_count)[:, None]),
        ((2 * slot_chip + attn_core) * attn_hold + attn_order).reshape(1, -1),
    )
    ffn_pack = pick(
        (chip_slots[0] == ((my_chip + shifts) % chips)[:, None, None])
        & (chip_slots[1] == (my_core * ffn_room + jnp.arange(ffn_room))[None, :, None]),
        both_slots,
    )
    ffn_keep = pick(
        (seq_slots[0][None, :] == my_fsdp) & (seq_slots[1][None, :] == jnp.arange(ffn_hold)[:, None]),
        seq_slots[3][None, :],
    )
    ffn_join = pick(
        (ffn_to.reshape(1, -1) == my_fsdp)
        & (ffn_place.reshape(1, -1) == jnp.arange(ffn_count)[:, None]),
        (slot_seq * ffn_hold + ffn_rank).reshape(1, -1),
    )
    master_low = tile_master.astype(bf16)
    masters = [master_low, core_swap(master_low)]
    ffn_sent = [gather_tiles(masters, ffn_pack[i]) for i in range(chips)]
    masters, ffn_sent, attn_pack = lax.optimization_barrier((masters, ffn_sent, attn_pack))
    ffn_got = chip_exchange(ffn_sent)
    attn_sent = gather_tiles(masters, attn_pack.reshape(-1))
    attn_sent = attn_sent.reshape(seq_size, attn_room, tile, tile)
    attn_got = seq_exchange([attn_sent[i] for i in range(seq_size)])
    pack_tokens = seq_gather(tokens[0])
    gain_full = seq_ordered(gains.astype(bf16))
    small_got = seq_ordered(small_master.astype(bf16))
    ffn_got, attn_got, pack_tokens, gain_full, small_got = lax.optimization_barrier(
        (ffn_got, attn_got, pack_tokens, gain_full, small_got)
    )
    attn_kept = gather_tiles(attn_got, attn_keep)
    attn_all = lax.all_gather(attn_kept, "fsdp", axis=0, tiled=True)
    ffn_other = [core_swap(value) for value in ffn_got]
    ffn_kept = gather_tiles(ffn_got + ffn_other, ffn_keep)
    ffn_all = lax.all_gather(ffn_kept, "seq", axis=0, tiled=True)
    w_first, w_out = join_tiles([attn_all], attn_join, row_blocks, attn_first, query_each)

    def slow_fetch(to, me, place, columns_of):
        def fetch(_, kept):
            whole = lax.all_gather(master_low, ("seq", "fsdp"), axis=0, tiled=True)
            count = row_blocks * sum(columns_of)
            index = pick(
                (to.reshape(1, -1) == me) & (place.reshape(1, -1) == jnp.arange(count)[:, None]),
                jnp.arange(tiles)[None, :],
            )
            return join_tiles([whole], index, row_blocks, *columns_of)

        return fetch

    slow_steps = jnp.where(fits, 0, 1)
    w_first, w_out = lax.fori_loop(
        0, slow_steps, slow_fetch(attn_to, my_seq, attn_place, (attn_first, query_each)), (w_first, w_out)
    )

    small_table = assemble(small_got.reshape((-1,) + small_master.shape[1:]), row_blocks)
    gain_full = gain_full.reshape(-1).astype(f32)
    gain_in = gain_full[0:width]
    gain_attn = gain_full[width : 2 * width]
    gain_laurel = gain_full[2 * width : 3 * width]
    gain_pre = gain_full[3 * width : 4 * width]
    gain_post = gain_full[4 * width : 5 * width]
    gain_vec = gain_full[5 * width : 6 * width]
    gain_query = gain_full[6 * width : 6 * width + HEAD_DIM]
    gain_key = gain_full[6 * width + HEAD_DIM : 6 * width + 2 * HEAD_DIM]
    laurel_left = small_table[:, :RANK]
    laurel_right = small_table[:, RANK : 2 * RANK]
    vector_gate_w = small_table[:, 2 * RANK : 2 * RANK + PLD]
    vector_proj_w = small_table[:, 2 * RANK + PLD :]

    segment, position = documents(doc_lengths[0], length)
    places = ((my_seq ^ flips)[:, None] * rows + jnp.arange(rows)[None, :]).reshape(-1)

    def reorder(values):
        blocks = values.reshape(seq_size, rows)
        return jnp.concatenate(
            [lax.dynamic_index_in_dim(blocks, my_seq ^ i, 0, False) for i in range(seq_size)]
        )

    pack_segment = reorder(segment)
    pack_position = reorder(position)
    stream = tokens[0].astype(f32)
    vectors = layer_vectors[0].astype(f32)
    normed, normed_pull = jax.vjp(rms_norm, stream, gain_in)
    normed_low = normed.astype(bf16)
    pack_normed = rms_norm(pack_tokens.astype(f32), gain_in).astype(bf16)
    first_pre = matmul(pack_normed, w_first)
    is_key = my_seq % per_key == 0

    def shape_query(query_in, query_gain):
        return rotary(
            rms_norm(query_in.reshape(length, per_device, HEAD_DIM), query_gain), pack_position
        )

    def shape_key(key_in, key_gain):
        return rotary(rms_norm(key_in.reshape(length, 1, HEAD_DIM), key_gain), pack_position)

    query_pre = first_pre[:, : per_device * HEAD_DIM]
    other_pre = first_pre[:, per_device * HEAD_DIM :]
    query_rot, query_pull = jax.vjp(shape_query, query_pre, gain_query)
    key_rot, key_pull = jax.vjp(shape_key, other_pre, gain_key)
    query_heads = query_rot.astype(bf16)
    other_low = jnp.where(is_key, key_rot[:, 0, :], other_pre).astype(bf16)
    partner_low = seq_swap(other_low, 1).reshape(seq_size // 2, 2, rows, HEAD_DIM)
    partner_low = partner_low[:, ::-1].reshape(length, HEAD_DIM)
    key_single = jnp.where(is_key, other_low, partner_low)
    value_single = jnp.where(is_key, partner_low, other_low)

    allow = (pack_segment[:, None] == pack_segment[None, :]) & (
        places[None, :] <= places[:, None]
    )
    raw = (
        jnp.einsum("qhd,kd->qhk", query_heads, key_single, preferred_element_type=f32) * SCALE
    )
    scores = jnp.where(allow[:, None, :], raw, NEGATIVE)
    powers = jnp.exp(scores - jnp.max(scores, axis=-1, keepdims=True))
    prob = powers / jnp.sum(powers, axis=-1, keepdims=True)
    prob_low = prob.astype(bf16)
    attended_low = (
        jnp.einsum("qhk,kd->qhd", prob_low, value_single, preferred_element_type=f32)
        .astype(bf16)
        .reshape(length, per_device * HEAD_DIM)
    )
    attn_pre = seq_sum(matmul_flip(attended_low, w_out), bf16)
    attn_normed, attn_pull = jax.vjp(rms_norm, attn_pre, gain_attn)
    first_sum = stream + attn_normed
    left_pre = matmul(normed_low, laurel_left)
    left_low = left_pre.astype(bf16)
    right_pre = matmul_flip(left_low, laurel_right)
    laurel_normed, laurel_pull = jax.vjp(rms_norm, right_pre, gain_laurel)
    second_sum = (first_sum + normed + laurel_normed) * ROOT_HALF
    feed_normed, feed_pull = jax.vjp(rms_norm, second_sum, gain_pre)
    ffn_all, feed_own = lax.optimization_barrier((ffn_all, feed_normed.astype(bf16)))
    feed_low = lax.all_gather(feed_own, "fsdp", axis=0, tiled=True)
    w_both, w_down = join_tiles([ffn_all], ffn_join, row_blocks, ffn_first, ffn_each)
    w_both, w_down = lax.fori_loop(
        0, slow_steps, slow_fetch(ffn_to, my_fsdp, ffn_place, (ffn_first, ffn_each)), (w_both, w_down)
    )
    both_pre = matmul(feed_low, w_both)
    ffn_width = w_down.shape[1]
    hidden, hidden_pull = jax.vjp(gelu_product, both_pre[:, :ffn_width], both_pre[:, ffn_width:])
    hidden_low = hidden.astype(bf16)
    down_pre = lax.psum_scatter(
        matmul_flip(hidden_low, w_down).astype(bf16), "fsdp", scatter_dimension=0, tiled=True
    ).astype(f32)
    down_normed, down_pull = jax.vjp(rms_norm, down_pre, gain_post)
    third_sum = second_sum + down_normed
    third_low = third_sum.astype(bf16)
    vector_pre = matmul(third_low, vector_gate_w)
    vector_gated, vector_pull = jax.vjp(lambda inner: gelu_product(inner, vectors), vector_pre)
    vector_low = vector_gated.astype(bf16)
    proj_pre = matmul_flip(vector_low, vector_proj_w)
    proj_normed, proj_pull = jax.vjp(rms_norm, proj_pre, gain_vec)
    result = third_sum + proj_normed
    output = result.astype(bf16)[None]

    grad_out = cotangent[0].astype(f32)
    grad_proj, grad_gain_vec = proj_pull(grad_out)
    proj_grad_low = grad_proj.astype(bf16)
    (grad_vector_pre,) = vector_pull(matmul(proj_grad_low, vector_proj_w))
    vector_grad_low = grad_vector_pre.astype(bf16)
    grad_third = grad_out + matmul_flip(vector_grad_low, vector_gate_w)
    grad_down, grad_gain_post = down_pull(grad_third)
    down_grad_low = lax.all_gather(grad_down.astype(bf16), "fsdp", axis=0, tiled=True)
    grad_gate, grad_up = hidden_pull(matmul(down_grad_low, w_down))
    both_grad_low = jnp.concatenate([grad_gate, grad_up], axis=1).astype(bf16)
    grad_feed = lax.psum_scatter(
        matmul_flip(both_grad_low, w_both).astype(bf16), "fsdp", scatter_dimension=0, tiled=True
    ).astype(f32)
    both_grad_w = matmul_outer(feed_low, both_grad_low).astype(bf16)
    down_grad_w = matmul_outer(down_grad_low, hidden_low).astype(bf16)

    ffn_cut = pick(
        (ffn_to.reshape(seq_size, 1, -1) == my_fsdp)
        & (ffn_rank.reshape(seq_size, 1, -1) == jnp.arange(ffn_hold)[None, :, None]),
        ffn_place.reshape(seq_size, 1, -1),
    )
    ffn_parts = cut_tiles(both_grad_w, down_grad_w, ffn_cut.reshape(-1), tile)
    ffn_parts, grad_feed = lax.optimization_barrier((ffn_parts, grad_feed))
    ffn_sum = lax.psum_scatter(ffn_parts, "seq", scatter_dimension=0, tiled=True)

    grad_second_norm, grad_gain_pre = feed_pull(grad_feed)
    half_grad = (grad_third + grad_second_norm) * ROOT_HALF
    grad_right, grad_gain_laurel = laurel_pull(half_grad)
    right_grad_low = grad_right.astype(bf16)
    left_grad_low = matmul(right_grad_low, laurel_right).astype(bf16)
    grad_attn, grad_gain_attn = attn_pull(half_grad)
    attn_grad_low = seq_gather(grad_attn.astype(bf16))
    grad_attended = (
        matmul(attn_grad_low, w_out).astype(bf16).reshape(length, per_device, HEAD_DIM)
    )
    out_grad_w = matmul_outer(attn_grad_low, attended_low).astype(bf16)
    value_grad = jnp.einsum("qhk,qhd->kd", prob_low, grad_attended, preferred_element_type=f32)
    grad_prob = jnp.einsum("qhd,kd->qhk", grad_attended, value_single, preferred_element_type=f32)
    inner = jnp.sum(prob * grad_prob, axis=-1, keepdims=True)
    grad_score = (prob * (grad_prob - inner)).astype(bf16)
    grad_query = (
        jnp.einsum("qhk,kd->qhd", grad_score, key_single, preferred_element_type=f32) * SCALE
    ).astype(bf16)
    key_grad = (
        jnp.einsum("qhk,qhd->kd", grad_score, query_heads, preferred_element_type=f32) * SCALE
    ).astype(bf16)
    value_grad = value_grad.astype(bf16)
    partner_grad = seq_swap(jnp.where(is_key, value_grad, key_grad), 1)
    partner_grad = partner_grad.reshape(seq_size // 2, 2, rows, HEAD_DIM)[:, ::-1]
    other_grad = jnp.where(is_key, key_grad, value_grad).astype(f32) + partner_grad.reshape(
        length, HEAD_DIM
    ).astype(f32)
    grad_query_pre, grad_gain_query = query_pull(grad_query.astype(f32))
    grad_key_pre, grad_gain_key = key_pull(other_grad[:, None, :])
    grad_gain_key = jnp.where(is_key, grad_gain_key, 0.0)
    first_grad_low = jnp.concatenate(
        [grad_query_pre, jnp.where(is_key, grad_key_pre, other_grad)], axis=1
    ).astype(bf16)
    first_grad_w = matmul_outer(pack_normed, first_grad_low).astype(bf16)
    grad_normed = (
        half_grad
        + matmul_flip(left_grad_low, laurel_left)
        + seq_sum(matmul_flip(first_grad_low, w_first), bf16)
    )
    grad_stream_norm, grad_gain_in = normed_pull(grad_normed)
    input_grad = (half_grad + grad_stream_norm)[None]

    small_full = jnp.concatenate(
        [
            matmul_outer(normed_low, left_grad_low),
            matmul_outer(right_grad_low, left_low),
            matmul_outer(third_low, vector_grad_low),
            matmul_outer(proj_grad_low, vector_low),
        ],
        axis=1,
    )
    small_tiles_grad = split_tiles(small_full, tile)
    gain_grad = jnp.concatenate(
        [
            grad_gain_in,
            grad_gain_attn,
            grad_gain_laurel,
            grad_gain_pre,
            grad_gain_post,
            grad_gain_vec,
            grad_gain_query,
            grad_gain_key,
        ]
    )
    small_part = seq_sum(small_tiles_grad, bf16, True)
    small_grad = fsdp_sum(small_part.reshape(-1, tile)).reshape(small_part.shape)
    gain_part = seq_sum(gain_grad, f32, True)
    gain_part = gain_part + core_swap(gain_part)
    gain_grad_mine = gain_part
    for offset in range(1, chips):
        gain_grad_mine = gain_grad_mine + chip_shift(gain_part, offset)

    ffn_back = pick(
        (seq_slots[5][None, None, :] == ((my_chip + shifts) % chips)[:, None, None])
        & (seq_slots[0][None, None, :] // 2 == my_chip)
        & (seq_slots[0][None, None, :] >= 0)
        & (seq_slots[4][None, None, :] == (my_core * ffn_room + jnp.arange(ffn_room))[None, :, None]),
        jnp.where(seq_slots[0] == my_fsdp, 0, ffn_hold) + seq_slots[1],
    )
    ffn_sum, small_grad, gain_grad_mine = lax.optimization_barrier(
        (ffn_sum, small_grad, gain_grad_mine)
    )
    ffn_sums = [ffn_sum, core_swap(ffn_sum)]
    ffn_return = [gather_tiles(ffn_sums, ffn_back[i]) for i in range(chips)]
    ffn_returned = chip_exchange(ffn_return)
    ffn_returned = ffn_returned + [core_swap(value) for value in ffn_returned]

    attn_cut = pick(
        (attn_key_chip[:, None, None, :] == (2 * my_seq + jnp.arange(2))[None, :, None, None])
        & (attn_order_chip[:, None, None, :] == jnp.arange(attn_hold)[None, None, :, None]),
        by_chip(attn_place)[:, None, None, :],
    )
    attn_back = pick(
        (column_slots[3][None, None, :] == (my_seq ^ flips)[:, None, None])
        & (column_slots[0][None, None, :] == my_key)
        & (column_slots[2][None, None, :] == jnp.arange(attn_room)[None, :, None]),
        column_slots[1],
    )
    attn_parts = cut_tiles(first_grad_w, out_grad_w, attn_cut.reshape(-1), tile)
    attn_sum = lax.psum_scatter(attn_parts, "fsdp", scatter_dimension=0, tiled=True)
    attn_returned = seq_exchange([gather_tiles([attn_sum], attn_back[i]) for i in range(seq_size)])
    attn_returned = attn_returned + [core_swap(value) for value in attn_returned]
    slot_grad = jnp.where(my_slots[0] >= 0, my_slots[1], 2 * half + my_slots[2])

    def slow_return(_, kept):
        own_ffn = split_tiles(both_grad_w, tile), split_tiles(down_grad_w, tile)
        own_attn = split_tiles(first_grad_w, tile), split_tiles(out_grad_w, tile)
        parts = jnp.concatenate(own_ffn + own_attn + (jnp.zeros((1, tile, tile), bf16),))
        index = jnp.where(
            ffn_to == my_fsdp,
            ffn_place,
            jnp.where(attn_to == my_seq, ffn_count + attn_place, ffn_count + attn_count),
        )
        spread = gather_tiles([parts], index.reshape(-1))
        return lax.psum_scatter(spread, ("seq", "fsdp"), scatter_dimension=0, tiled=True)

    tile_grads = ffn_returned + attn_returned
    slow_start = 2 * half + 2 * seq_size * attn_room
    slow_grads = lax.fori_loop(0, slow_steps, slow_return, jnp.zeros((mine, tile, tile), bf16))
    tile_grads = tile_grads + [slow_grads]
    slot_grad = jnp.where(fits, slot_grad, slow_start + local_slots)

    tile_new, tile_first_new, tile_second_new = rotate_update(
        tile_grads, slot_grad, tile_master, tile_first, tile_second, left_basis, right_basis, RATE_TILE
    )
    small_new, small_first_new, small_second_new = rotate_update(
        [small_grad],
        jnp.arange(small_master.shape[0]),
        small_master,
        small_first,
        small_second,
        small_left,
        small_right,
        RATE_SMALL,
    )
    gain_first_new = BETA_ONE * gain_first + (1.0 - BETA_ONE) * gain_grad_mine
    gain_second_new = BETA_TWO * gain_second + (1.0 - BETA_TWO) * gain_grad_mine * gain_grad_mine
    correct_one = 1.0 - BETA_ONE**STEP
    correct_two = 1.0 - BETA_TWO**STEP
    gain_new = gains - RATE_GAIN * (gain_first_new / correct_one) / (
        jnp.sqrt(gain_second_new / correct_two) + ADAM_EPS
    )
    return (
        output,
        input_grad,
        tile_new,
        tile_first_new,
        tile_second_new,
        small_new,
        small_first_new,
        small_second_new,
        gain_new,
        gain_first_new,
        gain_second_new,
    )


def solution(mesh):
    return jax.shard_map(
        on_device,
        mesh=mesh,
        in_specs=(
            P("fsdp", "seq", None),
            P("fsdp", "seq", None),
            P("fsdp", None),
            P("fsdp", "seq", None),
            P(),
            P(("seq", "fsdp"), None, None),
            P(("seq", "fsdp"), None, None),
            P(("seq", "fsdp"), None, None),
            P(("seq", "fsdp"), None, None),
            P(("seq", "fsdp"), None, None),
            P("seq", None, None),
            P("seq", None, None),
            P("seq", None, None),
            P("seq", None, None),
            P("seq", None, None),
            P("seq"),
            P("seq"),
            P("seq"),
        ),
        out_specs=(
            P("fsdp", "seq", None),
            P("fsdp", "seq", None),
            P(("seq", "fsdp"), None, None),
            P(("seq", "fsdp"), None, None),
            P(("seq", "fsdp"), None, None),
            P("seq", None, None),
            P("seq", None, None),
            P("seq", None, None),
            P("seq"),
            P("seq"),
            P("seq"),
        ),
        check_vma=False,
    )
```

```python
import math

import jax
import jax.numpy as jnp
from jax import lax
from jax.experimental import pallas as pl
from jax.experimental.pallas import tpu as pltpu
from jax.sharding import PartitionSpec as P

HEADS = 8
KV_HEADS = 2
HEAD_DIM = 256
FF = 8192
RANK = 64
PLD = 256
STEP = 5


EPS = 1e-06
SCALE = 0.0625
THETA = 1000000.0
ROOT_HALF = 0.7071067811865476
BETA_ONE = 0.5
BETA_TWO = 0.5
ADAM_EPS = 1e-08
RATE_TILE = 0.02
RATE_SMALL = 0.04
RATE_GAIN = 0.3
DECAY = 0.01
NEGATIVE = -1e30
VMEM_BYTES = 32 * 1024 * 1024


def rms_norm(value, gain):
    return value * lax.rsqrt(jnp.mean(value * value, axis=-1, keepdims=True) + EPS) * gain


def rotary(value, position):
    half = value.shape[-1] // 2
    freq = THETA ** (-2.0 * jnp.arange(half).astype(jnp.float32) / value.shape[-1])
    angle = position.astype(jnp.float32)[:, None] * freq[None, :]
    cosine = jnp.cos(angle)[:, None, :]
    sine = jnp.sin(angle)[:, None, :]
    first = value[..., :half]
    second = value[..., half:]
    return jnp.concatenate(
        [first * cosine - second * sine, second * cosine + first * sine], axis=-1
    )


def documents(lengths, length):
    places = jnp.arange(length)
    ends = jnp.cumsum(lengths)
    passed = places[:, None] >= ends[None, :]
    segment = jnp.sum(passed.astype(jnp.int32), axis=1)
    before = jnp.sum(jnp.where(passed, lengths[None, :], 0), axis=1)
    return (segment, places - before)


def matmul(left, right):
    return jnp.dot(left, right, preferred_element_type=jnp.float32)


def matmul_flip(left, right):
    return lax.dot_general(
        left, right, (((1,), (1,)), ((), ())), preferred_element_type=jnp.float32
    )


def matmul_outer(left, right):
    return lax.dot_general(
        left, right, (((0,), (0,)), ((), ())), preferred_element_type=jnp.float32
    )


def assemble(tiles, row_blocks):
    size = tiles.shape[1]
    column_blocks = tiles.shape[0] // row_blocks
    return (
        tiles.reshape(row_blocks, column_blocks, size, size)
        .transpose(0, 2, 1, 3)
        .reshape(row_blocks * size, column_blocks * size)
    )


def split_tiles(matrix, size):
    row_blocks = matrix.shape[0] // size
    column_blocks = matrix.shape[1] // size
    return (
        matrix.reshape(row_blocks, size, column_blocks, size)
        .transpose(0, 2, 1, 3)
        .reshape(row_blocks * column_blocks, size, size)
    )


def gelu_product(first, second):
    return jax.nn.gelu(first, approximate=True) * second


def room(count, share):
    mean = count * share
    return math.ceil(mean + 3.6 * math.sqrt(mean * (1.0 - share)) + 3.0)


def count_earlier(group, valid):
    size = group.shape[-1]
    order = jnp.arange(size)
    same = (group[..., :, None] == group[..., None, :]) & valid[..., None, :]
    same = same & (order[None, :] < order[:, None])
    return jnp.sum(same.astype(jnp.int32), axis=-1)


def pick(match, value):
    return jnp.sum(jnp.where(match, value, 0), axis=-1)


def steps_of(count):
    for steps in range(4, 65):
        if count % steps == 0 and 16 <= count // steps <= 160:
            return steps
    return 2 if count % 2 == 0 else 1


def tile_kernel_call(kernel, index, arrays, out_shape, out_specs, steps):
    return pl.pallas_call(
        kernel,
        grid=(steps,),
        out_shape=out_shape,
        in_specs=[pl.BlockSpec(memory_space=pltpu.SMEM)]
        + [pl.BlockSpec(memory_space=pl.ANY)] * len(arrays),
        out_specs=out_specs,
        scratch_shapes=[pltpu.SemaphoreType.DMA],
        compiler_params=pltpu.CompilerParams(vmem_limit_bytes=VMEM_BYTES),
    )(index, *arrays)


def start_copy(sources, place, target, sem):
    start = 0
    for ref in sources:
        size = ref.shape[0]

        @pl.when((place >= start) & (place < start + size))
        def _(ref=ref, start=start):
            pltpu.make_async_copy(ref.at[place - start], target, sem).start()

        start = start + size


def gather_tiles(arrays, index):
    tile = arrays[0].shape[-1]
    count = index.shape[0]
    steps = steps_of(count)
    each = count // steps

    def kernel(index_ref, *refs):
        sources, out, sem = refs[:-2], refs[-2], refs[-1]
        base = pl.program_id(0) * each

        def step(i, carry):
            start_copy(sources, index_ref[base + i], out.at[i], sem)
            return carry

        lax.fori_loop(0, each, step, 0)
        pltpu.make_async_copy(out, out, sem).wait()

    total = sum(array.shape[0] for array in arrays)
    return tile_kernel_call(
        kernel,
        jnp.clip(index, 0, total - 1),
        arrays,
        jax.ShapeDtypeStruct((count, tile, tile), arrays[0].dtype),
        pl.BlockSpec((each, tile, tile), lambda i: (i, 0, 0)),
        steps,
    )


def join_tiles(arrays, index, row_blocks, columns):
    tile = arrays[0].shape[-1]
    steps = 4
    each = row_blocks // steps

    def kernel(index_ref, *refs):
        sources, outs, sem = refs[: len(arrays)], refs[len(arrays) : -1], refs[-1]
        base = pl.program_id(0) * each
        start = 0
        for out, width in zip(outs, columns):

            def step(i, carry, out=out, start=start, width=width):
                row = i // width
                column = i - row * width
                target = out.at[
                    pl.ds(pl.multiple_of(row * tile, tile), tile),
                    pl.ds(pl.multiple_of(column * tile, tile), tile),
                ]
                start_copy(sources, index_ref[start + base * width + i], target, sem)
                return carry

            lax.fori_loop(0, each * width, step, 0)
            start = start + row_blocks * width
        for out in outs:
            pltpu.make_async_copy(out, out, sem).wait()

    total = sum(array.shape[0] for array in arrays)
    out_shape = tuple(
        jax.ShapeDtypeStruct((row_blocks * tile, width * tile), arrays[0].dtype)
        for width in columns
    )
    out_specs = tuple(pl.BlockSpec((each * tile, width * tile), lambda i: (i, 0)) for width in columns)
    return tile_kernel_call(
        kernel, jnp.clip(index, 0, total - 1), arrays, out_shape, out_specs, steps
    )


def cut_tiles(matrices, index, tile):
    row_blocks = matrices[0].shape[0] // tile
    widths = [matrix.shape[1] // tile for matrix in matrices]
    count = index.shape[0]
    steps = steps_of(count)
    each = count // steps

    def kernel(index_ref, *refs):
        sources, out, sem = refs[:-2], refs[-2], refs[-1]
        base = pl.program_id(0) * each

        def step(i, carry):
            place = index_ref[base + i]
            start = 0
            for ref, width in zip(sources, widths):
                size = row_blocks * width

                @pl.when((place >= start) & (place < start + size))
                def _(ref=ref, start=start, width=width):
                    row = (place - start) // width
                    column = place - start - row * width
                    source = ref.at[
                        pl.ds(pl.multiple_of(row * tile, tile), tile),
                        pl.ds(pl.multiple_of(column * tile, tile), tile),
                    ]
                    pltpu.make_async_copy(source, out.at[i], sem).start()

                start = start + size
            return carry

        lax.fori_loop(0, each, step, 0)
        pltpu.make_async_copy(out, out, sem).wait()

    return tile_kernel_call(
        kernel,
        jnp.clip(index, 0, row_blocks * sum(widths) - 1),
        matrices,
        jax.ShapeDtypeStruct((count, tile, tile), matrices[0].dtype),
        pl.BlockSpec((each, tile, tile), lambda i: (i, 0, 0)),
        steps,
    )


def split_low(value):
    high = value.astype(jnp.bfloat16)
    return high, (value - high.astype(jnp.float32)).astype(jnp.bfloat16)


def rotate_update(grads, index, master, first, second, left, right, rate):
    count, tile, _ = master.shape
    each = 4 if count % 4 == 0 else 1
    correct_one = 1.0 - BETA_ONE**STEP
    correct_two = 1.0 - BETA_TWO**STEP

    def product(one, two, dims):
        return lax.dot_general(one, two, (dims, ((), ())), preferred_element_type=jnp.float32)

    def kernel(index_ref, *refs):
        sources, refs = refs[: len(grads)], refs[len(grads) :]
        master_ref, first_ref, second_ref, left_ref, right_ref = refs[:5]
        master_out, first_out, second_out, held, sems = refs[5:]
        now = pl.program_id(0)

        @pl.when(now == 0)
        def _():
            def step(i, carry):
                start_copy(sources, index_ref[i], held.at[i], sems.at[i // each])
                return carry

            lax.fori_loop(0, count, step, 0)

        block = held.at[pl.ds(now * each, each)]
        pltpu.make_async_copy(block, block, sems.at[now]).wait()
        lefts, rights, turns = [], [], []
        for i in range(each):
            grad = held[now * each + i]
            lefts.append(split_low(left_ref[i]))
            rights.append(split_low(right_ref[i]))
            half_turned = product(
                jnp.concatenate([grad, grad], axis=1),
                jnp.concatenate(rights[i], axis=0),
                ((1,), (0,)),
            )
            turns.append(split_low(half_turned))
        for i in range(each):
            (left_high, left_low), (high, low) = lefts[i], turns[i]
            turns[i] = product(
                jnp.concatenate([left_high, left_high, left_low], axis=0),
                jnp.concatenate([high, low, high], axis=0),
                ((0,), (0,)),
            )
        for i in range(each):
            right_high, right_low = rights[i]
            first_new = BETA_ONE * first_ref[i] + (1.0 - BETA_ONE) * turns[i]
            second_new = BETA_TWO * second_ref[i] + (1.0 - BETA_TWO) * turns[i] * turns[i]
            first_out[i] = first_new
            second_out[i] = second_new
            high, low = split_low(
                first_new / correct_one / (jnp.sqrt(second_new / correct_two) + ADAM_EPS)
            )
            half_back = product(
                jnp.concatenate([high, low, high], axis=1),
                jnp.concatenate([right_high, right_high, right_low], axis=1),
                ((1,), (1,)),
            )
            turns[i] = split_low(half_back)
        for i in range(each):
            (left_high, left_low), (high, low) = lefts[i], turns[i]
            back = product(
                jnp.concatenate([left_high, left_high, left_low], axis=1),
                jnp.concatenate([high, low, high], axis=0),
                ((1,), (0,)),
            )
            weight = master_ref[i]
            master_out[i] = weight - rate * (back + DECAY * weight)

    spec = pl.BlockSpec((each, tile, tile), lambda i: (i, 0, 0))
    shape = jax.ShapeDtypeStruct(master.shape, jnp.float32)
    total = sum(array.shape[0] for array in grads)
    return pl.pallas_call(
        kernel,
        grid=(count // each,),
        out_shape=(shape, shape, shape),
        in_specs=[pl.BlockSpec(memory_space=pltpu.SMEM)]
        + [pl.BlockSpec(memory_space=pl.ANY)] * len(grads)
        + [spec] * 5,
        out_specs=(spec, spec, spec),
        scratch_shapes=[
            pltpu.VMEM((count, tile, tile), jnp.bfloat16),
            pltpu.SemaphoreType.DMA((count // each,)),
        ],
        compiler_params=pltpu.CompilerParams(vmem_limit_bytes=VMEM_BYTES),
    )(jnp.clip(index, 0, total - 1), *grads, master, first, second, left, right)


def seq_swap(value, flip):
    size = lax.axis_size("seq")
    return lax.ppermute(value, "seq", [(i, i ^ flip) for i in range(size)])


def core_swap(value):
    size = lax.axis_size("fsdp")
    return lax.ppermute(value, "fsdp", [(i, i ^ 1) for i in range(size)])


def chip_shift(value, offset):
    size = lax.axis_size("fsdp")
    chips = size // 2
    return lax.ppermute(
        value, "fsdp", [(i, (i // 2 + offset) % chips * 2 + i % 2) for i in range(size)]
    )


def seq_gather(value):
    size = lax.axis_size("seq")
    return jnp.concatenate([value] + [seq_swap(value, flip) for flip in range(1, size)], axis=0)


def seq_ordered(value):
    size = lax.axis_size("seq")
    parts = jnp.stack([value] + [seq_swap(value, flip) for flip in range(1, size)], axis=0)
    return parts[lax.axis_index("seq") ^ jnp.arange(size)]


def seq_exchange(values):
    return [values[0]] + [seq_swap(values[flip], flip) for flip in range(1, len(values))]


def seq_sum(value, wire, ordered=False):
    size = lax.axis_size("seq")
    parts = value.reshape((size, value.shape[0] // size) + value.shape[1:])
    if ordered:
        parts = parts[lax.axis_index("seq") ^ jnp.arange(size)]
    total = parts[0]
    for flip in range(1, size):
        total = total + seq_swap(parts[flip].astype(wire), flip).astype(jnp.float32)
    return total


def chip_exchange(values):
    return [values[0]] + [chip_shift(values[offset], offset) for offset in range(1, len(values))]


def core_pair(value):
    other = core_swap(value)
    even = lax.axis_index("fsdp") % 2 == 0
    return jnp.where(even, jnp.stack([value, other]), jnp.stack([other, value]))


def small_sum(value):
    seq_size = lax.axis_size("seq")
    chips = lax.axis_size("fsdp") // 2
    chip = lax.axis_index("fsdp") // 2
    even = lax.axis_index("fsdp") % 2 == 0
    low = value.astype(jnp.bfloat16)
    parts = low.reshape((seq_size, 2, low.shape[0] // (2 * seq_size)) + low.shape[1:])
    kept = jnp.where(even, parts[:, 0], parts[:, 1]).astype(jnp.float32)
    given = jnp.where(even, parts[:, 1], parts[:, 0])
    kept = kept + core_swap(given).astype(jnp.float32)
    kept = seq_sum(kept.reshape((-1,) + low.shape[1:]), jnp.bfloat16, True)
    kept = kept.reshape((chips, kept.shape[0] // chips) + kept.shape[1:])
    kept = kept[(chip + jnp.arange(chips)) % chips]
    total = kept[0]
    for offset in range(1, chips):
        total = total + chip_shift(kept[offset].astype(jnp.bfloat16), offset).astype(jnp.float32)
    total = total.astype(jnp.bfloat16)
    parts = jnp.stack([total] + [chip_shift(total, offset) for offset in range(1, chips)])
    parts = parts[(chip - jnp.arange(chips)) % chips]
    return core_pair(parts).reshape((value.shape[0] // seq_size,) + value.shape[1:])


def on_device(
    tokens,
    layer_vectors,
    doc_lengths,
    cotangent,
    tile_owner,
    tile_master,
    tile_first,
    tile_second,
    left_basis,
    right_basis,
    small_master,
    small_first,
    small_second,
    small_left,
    small_right,
    gains,
    gain_first,
    gain_second,
):
    bf16 = jnp.bfloat16
    f32 = jnp.float32
    tile = tile_master.shape[1]
    width = tokens.shape[2]
    row_blocks = width // tile
    rows = tokens.shape[1]
    seq_size = lax.axis_size("seq")
    fsdp_size = lax.axis_size("fsdp")
    chips = fsdp_size // 2
    mine = tile_master.shape[0]
    tiles = tile_owner.shape[0]
    length = rows * seq_size
    per_device = HEADS // seq_size
    per_key = seq_size // KV_HEADS
    query_width = HEADS * HEAD_DIM
    key_width = KV_HEADS * HEAD_DIM
    my_seq = lax.axis_index("seq")
    my_fsdp = lax.axis_index("fsdp")
    my_chip = my_fsdp // 2
    my_core = my_fsdp % 2
    flips = jnp.arange(seq_size)
    shifts = jnp.arange(chips)

    query_blocks = query_width // tile
    key_blocks = key_width // tile
    ffn_blocks = FF // tile
    query_each = query_blocks // seq_size
    head_blocks = HEAD_DIM // tile
    ffn_each = ffn_blocks // fsdp_size
    columns = tiles // row_blocks
    attn_first = query_each + head_blocks
    attn_count = row_blocks * (attn_first + query_each)
    ffn_first = 2 * ffn_each
    ffn_count = row_blocks * 3 * ffn_each
    attn_share = (2 * query_blocks + 2 * key_blocks) / columns
    ffn_share = 3 * ffn_blocks / columns
    attn_room = (room(2 * mine, attn_share / seq_size) + 1) // 2
    attn_hold = (room(attn_count, 1.0 / chips) + 1) // 2 + 1
    ffn_rooms, ffn_holds = [], []
    both_count = row_blocks * ffn_first
    for part in (2.0 / 3.0, 1.0 / 3.0):
        ffn_rooms.append((room(2 * mine, ffn_share * part / chips) + 1) // 2)
        ffn_holds.append((room(ffn_count * part, 1.0 / seq_size) + 3) // 4 * 4)

    def tile_places(owner):
        row = owner // columns
        column = owner % columns
        key_at = column - query_blocks
        value_at = key_at - key_blocks
        out_at = value_at - key_blocks
        ffn_at = out_at - query_blocks
        is_attn = ffn_at < 0
        kind = ffn_at // ffn_blocks
        ffn_column = ffn_at % ffn_blocks
        ffn_to = jnp.where(is_attn, -1, ffn_column // ffn_each)
        ffn_local = ffn_column % ffn_each
        ffn_place = jnp.where(
            kind == 2, row * ffn_each + ffn_local, row * ffn_first + kind * ffn_each + ffn_local
        )
        is_down = (kind == 2).astype(jnp.int32)
        attn_to = jnp.where(
            key_at < 0,
            column // query_each,
            jnp.where(
                value_at < 0,
                key_at // head_blocks * per_key,
                jnp.where(
                    out_at < 0,
                    value_at // head_blocks * per_key + per_key - 1,
                    out_at // query_each,
                ),
            ),
        )
        attn_place = jnp.where(
            key_at < 0,
            row * attn_first + column % query_each,
            jnp.where(
                out_at < 0,
                row * attn_first + query_each + key_at % head_blocks,
                row_blocks * attn_first + row * query_each + out_at % query_each,
            ),
        )
        attn_to = jnp.where(is_attn, attn_to, -1)
        return (ffn_to, is_down, ffn_place, attn_to, attn_place)

    owners = tile_owner.reshape(seq_size, fsdp_size, mine)
    ffn_to, is_down, ffn_place, attn_to, attn_place = tile_places(owners)
    slot_seq = jnp.arange(seq_size)[:, None, None]
    slot_fsdp = jnp.arange(fsdp_size)[None, :, None]
    slot_chip = slot_fsdp // 2
    ffn_chip = jnp.where(ffn_to < 0, -1, ffn_to // 2)
    ffn_key = jnp.where(ffn_to < 0, -1, 2 * ffn_to + is_down)
    chip_key = jnp.where(ffn_to < 0, -1, 2 * ffn_chip + is_down)
    ffn_room = jnp.where(is_down == 1, ffn_rooms[1], ffn_rooms[0])
    ffn_hold = jnp.where(is_down == 1, ffn_holds[1], ffn_holds[0])
    chip_view = chip_key.reshape(seq_size, chips, 2 * mine)
    chip_rank = count_earlier(chip_view, chip_view >= 0).reshape(owners.shape)
    seq_view = ffn_key.reshape(seq_size, fsdp_size * mine)
    ffn_rank = count_earlier(seq_view, seq_view >= 0).reshape(owners.shape)
    attn_view = attn_to.reshape(seq_size, chips, 2 * mine)
    attn_rank = count_earlier(attn_view, attn_view >= 0).reshape(owners.shape)
    attn_core = (attn_rank + slot_seq) % 2
    attn_rank = attn_rank // 2
    attn_key = jnp.where(attn_to < 0, -1, 2 * attn_to + attn_core)

    def by_chip(value):
        value = value.reshape(seq_size, chips, 2 * mine).transpose(1, 0, 2)
        return value.reshape(chips, seq_size * 2 * mine)

    attn_key_chip = by_chip(attn_key)
    attn_order_chip = count_earlier(attn_key_chip, attn_key_chip >= 0)
    attn_order = (
        attn_order_chip.reshape(chips, seq_size, 2 * mine).transpose(1, 0, 2).reshape(owners.shape)
    )
    fits = jnp.all(
        jnp.where(
            ffn_to < 0,
            (attn_rank < attn_room) & (attn_order < attn_hold),
            (chip_rank < 2 * ffn_room) & (ffn_rank < ffn_hold),
        )
    )
    rank_core = (chip_rank >= ffn_room).astype(jnp.int32)
    rank_local = chip_rank - rank_core * ffn_room
    core_start = jnp.where(rank_core == my_core, 0, chips * ffn_room) + rank_local
    out_place = core_start + (my_chip - slot_chip) % chips * ffn_room
    down_start = 2 * chips * ffn_rooms[0]
    attn_start = down_start + 2 * chips * ffn_rooms[1]
    back_place = core_start + (my_chip - ffn_chip) % chips * ffn_room + is_down * down_start
    attn_back_place = (
        attn_start
        + jnp.where(attn_core == my_core, 0, seq_size * attn_room)
        + (attn_to ^ my_seq) * attn_room
        + attn_rank
    )
    chip_slots = lax.dynamic_slice(
        jnp.stack([chip_key, chip_rank, attn_key, attn_rank]),
        (0, my_seq, 2 * my_chip, 0),
        (4, 1, 2, mine),
    ).reshape(4, 1, 1, 2 * mine)
    my_slots = lax.dynamic_slice(
        jnp.stack([ffn_to, back_place, attn_back_place]), (0, my_seq, my_fsdp, 0), (3, 1, 1, mine)
    ).reshape(3, mine)
    seq_slots = lax.dynamic_slice(
        jnp.stack(
            [
                ffn_key,
                ffn_rank,
                chip_key,
                out_place,
                chip_rank,
                jnp.broadcast_to(slot_chip, owners.shape),
            ]
        ),
        (0, my_seq, 0, 0),
        (6, 1, fsdp_size, mine),
    ).reshape(6, fsdp_size * mine)
    column_slots = lax.dynamic_slice(
        jnp.stack([attn_key, attn_order, attn_rank, jnp.broadcast_to(slot_seq, owners.shape)]),
        (0, 0, 2 * my_chip, 0),
        (4, seq_size, 2, mine),
    ).reshape(4, 2 * seq_size * mine)
    my_key = 2 * my_seq + my_core

    local_slots = jnp.arange(mine)
    both_slots = jnp.arange(2 * mine)
    both_slots = jnp.where(
        both_slots // mine == my_core, both_slots % mine, mine + both_slots % mine
    )
    attn_pack = pick(
        (chip_slots[2] == (2 * (my_seq ^ flips) + my_core)[:, None, None])
        & (chip_slots[3] == jnp.arange(attn_room)[None, :, None]),
        both_slots,
    )
    attn_keep = pick(
        (column_slots[0][None, :] == my_key)
        & (column_slots[1][None, :] == jnp.arange(attn_hold)[:, None]),
        (column_slots[3] ^ my_seq) * attn_room + column_slots[2],
    )
    attn_join = pick(
        (attn_to.reshape(1, -1) == my_seq)
        & (attn_place.reshape(1, -1) == jnp.arange(attn_count)[:, None]),
        ((2 * slot_chip + attn_core) * attn_hold + attn_order).reshape(1, -1),
    )
    def ffn_tables(kind):
        room_now, hold_now = ffn_rooms[kind], ffn_holds[kind]
        ranks = my_core * room_now + jnp.arange(room_now)
        pack = pick(
            (chip_slots[0] == (2 * ((my_chip + shifts) % chips) + kind)[:, None, None])
            & (chip_slots[1] == ranks[None, :, None]),
            both_slots,
        )
        keep = pick(
            (seq_slots[0][None, :] == 2 * my_fsdp + kind)
            & (seq_slots[1][None, :] == jnp.arange(hold_now)[:, None]),
            seq_slots[3][None, :],
        )
        half_now = hold_now // 2
        piece = 2 * (slot_seq ^ my_seq) * half_now + ffn_rank
        count = both_count if kind == 0 else ffn_count - both_count
        join = pick(
            (ffn_key.reshape(1, -1) == 2 * my_fsdp + kind)
            & (ffn_place.reshape(1, -1) == jnp.arange(count)[:, None]),
            piece.reshape(1, -1),
        )
        cut = pick(
            (ffn_key.reshape(seq_size, 1, -1) == 2 * my_fsdp + kind)
            & (ffn_rank.reshape(seq_size, 1, -1) == jnp.arange(hold_now)[None, :, None]),
            ffn_place.reshape(seq_size, 1, -1),
        )
        back = pick(
            (seq_slots[5][None, None, :] == ((my_chip + shifts) % chips)[:, None, None])
            & (seq_slots[2][None, None, :] == 2 * my_chip + kind)
            & (seq_slots[4][None, None, :] == ranks[None, :, None]),
            jnp.where(seq_slots[0] == 2 * my_fsdp + kind, 0, hold_now) + seq_slots[1],
        )
        return (pack, keep, join, cut, back)

    both_pack, both_keep, both_join, both_cut, both_back = ffn_tables(0)
    down_pack, down_keep, down_join, down_cut, down_back = ffn_tables(1)

    def seq_first(kept):
        half_now = kept.shape[0] // 2
        one, two = kept[:half_now], kept[half_now:]
        return [one, two, seq_swap(one, 1), seq_swap(two, 1), seq_swap(one, 2), seq_swap(two, 2)]

    def seq_second(pieces):
        return pieces + [seq_swap(pieces[2], 2), seq_swap(pieces[5], 1)]

    master_low = tile_master.astype(bf16)
    masters = [master_low, core_swap(master_low)]
    both_sent = [gather_tiles(masters, both_pack[i]) for i in range(chips)]
    masters, both_sent = lax.optimization_barrier((masters, both_sent))
    both_got = chip_exchange(both_sent)
    attn_sent = gather_tiles(masters, attn_pack.reshape(-1))
    attn_sent = attn_sent.reshape(seq_size, attn_room, tile, tile)
    attn_got = seq_exchange([attn_sent[i] for i in range(seq_size)])
    down_sent = [gather_tiles(masters, down_pack[i]) for i in range(chips)]
    pack_tokens = seq_gather(tokens[0])
    gain_full = seq_ordered(gains.astype(bf16))
    both_got, attn_got, down_sent, pack_tokens, gain_full = lax.optimization_barrier(
        (both_got, attn_got, down_sent, pack_tokens, gain_full)
    )
    attn_kept = gather_tiles(attn_got, attn_keep)
    attn_all = lax.all_gather(attn_kept, "fsdp", axis=0, tiled=True)
    both_kept = gather_tiles(both_got + [core_swap(value) for value in both_got], both_keep)
    down_got = chip_exchange(down_sent)
    down_got = down_got + [core_swap(value) for value in down_got]
    both_all = seq_second(seq_first(both_kept))
    small_rows = small_master.shape[0] // 2
    small_half = lax.dynamic_slice_in_dim(small_master, my_core * small_rows, small_rows)
    small_got = seq_ordered(small_half.astype(bf16))
    attn_all, both_all, down_got, small_got = lax.optimization_barrier(
        (attn_all, both_all, down_got, small_got)
    )
    w_first, w_out = join_tiles([attn_all], attn_join, row_blocks, (attn_first, query_each))
    (w_both,) = join_tiles(both_all, both_join, row_blocks, (ffn_first,))
    down_pieces = seq_first(gather_tiles(down_got, down_keep))

    def slow_fetch(to, me, place, columns_of):
        def fetch(_, kept):
            whole = lax.all_gather(master_low, ("seq", "fsdp"), axis=0, tiled=True)
            count = row_blocks * sum(columns_of)
            index = pick(
                (to.reshape(1, -1) == me) & (place.reshape(1, -1) == jnp.arange(count)[:, None]),
                jnp.arange(tiles)[None, :],
            )
            return join_tiles([whole], index, row_blocks, columns_of)

        return fetch

    slow_steps = jnp.where(fits, 0, 1)
    w_first, w_out = lax.fori_loop(
        0,
        slow_steps,
        slow_fetch(attn_to, my_seq, attn_place, (attn_first, query_each)),
        (w_first, w_out),
    )
    small_got = core_pair(small_got).transpose(1, 0, 2, 3, 4)
    small_table = assemble(small_got.reshape((-1,) + small_master.shape[1:]), row_blocks)
    gain_full = gain_full.reshape(-1).astype(f32)
    gain_in = gain_full[0:width]
    gain_attn = gain_full[width : 2 * width]
    gain_laurel = gain_full[2 * width : 3 * width]
    gain_pre = gain_full[3 * width : 4 * width]
    gain_post = gain_full[4 * width : 5 * width]
    gain_vec = gain_full[5 * width : 6 * width]
    gain_query = gain_full[6 * width : 6 * width + HEAD_DIM]
    gain_key = gain_full[6 * width + HEAD_DIM : 6 * width + 2 * HEAD_DIM]
    laurel_left = small_table[:, :RANK]
    laurel_right = small_table[:, RANK : 2 * RANK]
    vector_gate_w = small_table[:, 2 * RANK : 2 * RANK + PLD]
    vector_proj_w = small_table[:, 2 * RANK + PLD :]

    segment, position = documents(doc_lengths[0], length)
    places = ((my_seq ^ flips)[:, None] * rows + jnp.arange(rows)[None, :]).reshape(-1)

    def reorder(values):
        blocks = values.reshape(seq_size, rows)
        return jnp.concatenate(
            [lax.dynamic_index_in_dim(blocks, my_seq ^ i, 0, False) for i in range(seq_size)]
        )

    pack_segment = reorder(segment)
    pack_position = reorder(position)
    stream = tokens[0].astype(f32)
    vectors = layer_vectors[0].astype(f32)
    normed, normed_pull = jax.vjp(rms_norm, stream, gain_in)
    normed_low = normed.astype(bf16)
    pack_normed = rms_norm(pack_tokens.astype(f32), gain_in).astype(bf16)
    first_pre = matmul(pack_normed, w_first)
    is_key = my_seq % per_key == 0

    def shape_query(query_in, query_gain):
        return rotary(
            rms_norm(query_in.reshape(length, per_device, HEAD_DIM), query_gain), pack_position
        )

    def shape_key(key_in, key_gain):
        return rotary(rms_norm(key_in.reshape(length, 1, HEAD_DIM), key_gain), pack_position)

    query_pre = first_pre[:, : per_device * HEAD_DIM]
    other_pre = first_pre[:, per_device * HEAD_DIM :]
    query_rot, query_pull = jax.vjp(shape_query, query_pre, gain_query)
    key_rot, key_pull = jax.vjp(shape_key, other_pre, gain_key)
    query_heads = query_rot.astype(bf16)
    other_low = jnp.where(is_key, key_rot[:, 0, :], other_pre).astype(bf16)
    partner_low = seq_swap(other_low, 1).reshape(seq_size // 2, 2, rows, HEAD_DIM)
    partner_low = partner_low[:, ::-1].reshape(length, HEAD_DIM)
    key_single = jnp.where(is_key, other_low, partner_low)
    value_single = jnp.where(is_key, partner_low, other_low)

    allow = (pack_segment[:, None] == pack_segment[None, :]) & (
        places[None, :] <= places[:, None]
    )
    raw = (
        jnp.einsum("qhd,kd->qhk", query_heads, key_single, preferred_element_type=f32) * SCALE
    )
    scores = jnp.where(allow[:, None, :], raw, NEGATIVE)
    powers = jnp.exp(scores - jnp.max(scores, axis=-1, keepdims=True))
    prob = powers / jnp.sum(powers, axis=-1, keepdims=True)
    prob_low = prob.astype(bf16)
    attended_low = (
        jnp.einsum("qhk,kd->qhd", prob_low, value_single, preferred_element_type=f32)
        .astype(bf16)
        .reshape(length, per_device * HEAD_DIM)
    )
    attn_pre = seq_sum(matmul_flip(attended_low, w_out), bf16)
    attn_normed, attn_pull = jax.vjp(rms_norm, attn_pre, gain_attn)
    first_sum = stream + attn_normed
    left_pre = matmul(normed_low, laurel_left)
    left_low = left_pre.astype(bf16)
    right_pre = matmul_flip(left_low, laurel_right)
    laurel_normed, laurel_pull = jax.vjp(rms_norm, right_pre, gain_laurel)
    second_sum = (first_sum + normed + laurel_normed) * ROOT_HALF
    feed_normed, feed_pull = jax.vjp(rms_norm, second_sum, gain_pre)
    down_pieces, feed_own = lax.optimization_barrier((down_pieces, feed_normed.astype(bf16)))
    feed_low = lax.all_gather(feed_own, "fsdp", axis=0, tiled=True)
    (w_down,) = join_tiles(seq_second(down_pieces), down_join, row_blocks, (ffn_each,))
    (w_both,) = lax.fori_loop(
        0, slow_steps, slow_fetch(ffn_key, 2 * my_fsdp, ffn_place, (ffn_first,)), (w_both,)
    )
    (w_down,) = lax.fori_loop(
        0, slow_steps, slow_fetch(ffn_key, 2 * my_fsdp + 1, ffn_place, (ffn_each,)), (w_down,)
    )
    both_pre = matmul(feed_low, w_both)
    ffn_width = w_down.shape[1]
    hidden, hidden_pull = jax.vjp(gelu_product, both_pre[:, :ffn_width], both_pre[:, ffn_width:])
    hidden_low = hidden.astype(bf16)
    down_pre = lax.psum_scatter(
        matmul_flip(hidden_low, w_down).astype(bf16), "fsdp", scatter_dimension=0, tiled=True
    ).astype(f32)
    down_normed, down_pull = jax.vjp(rms_norm, down_pre, gain_post)
    third_sum = second_sum + down_normed
    third_low = third_sum.astype(bf16)
    vector_pre = matmul(third_low, vector_gate_w)
    vector_gated, vector_pull = jax.vjp(lambda inner: gelu_product(inner, vectors), vector_pre)
    vector_low = vector_gated.astype(bf16)
    proj_pre = matmul_flip(vector_low, vector_proj_w)
    proj_normed, proj_pull = jax.vjp(rms_norm, proj_pre, gain_vec)
    result = third_sum + proj_normed
    output = result.astype(bf16)[None]

    grad_out = cotangent[0].astype(f32)
    grad_proj, grad_gain_vec = proj_pull(grad_out)
    proj_grad_low = grad_proj.astype(bf16)
    (grad_vector_pre,) = vector_pull(matmul(proj_grad_low, vector_proj_w))
    vector_grad_low = grad_vector_pre.astype(bf16)
    grad_third = grad_out + matmul_flip(vector_grad_low, vector_gate_w)
    grad_down, grad_gain_post = down_pull(grad_third)
    down_grad_low = lax.all_gather(grad_down.astype(bf16), "fsdp", axis=0, tiled=True)

    def added(one, two):
        return one.astype(f32) + two.astype(f32)

    def cut_parts(matrices, cut, flips_of, half):
        half_now = cut.shape[1] // 2
        index = cut[my_seq ^ jnp.array(flips_of), half * half_now : (half + 1) * half_now]
        return cut_tiles(matrices, index.reshape(-1), tile)

    down_grad_w = matmul_outer(down_grad_low, hidden_low).astype(bf16)
    down_parts = (
        cut_parts([down_grad_w], down_cut, [1, 3], 0),
        cut_parts([down_grad_w], down_cut, [2, 3], 1),
        cut_parts([down_grad_w], down_cut, [0, 2], 0),
        cut_parts([down_grad_w], down_cut, [0, 1], 1),
    )
    down_grad_low, hidden_low, down_parts = lax.optimization_barrier(
        (down_grad_low, hidden_low, down_parts)
    )
    down_one = added(down_parts[2], seq_swap(down_parts[0], 1))
    down_two = added(down_parts[3], seq_swap(down_parts[1], 2))
    grad_gate, grad_up = hidden_pull(matmul(down_grad_low, w_down))
    both_grad_low = jnp.concatenate([grad_gate, grad_up], axis=1).astype(bf16)
    grad_feed = lax.psum_scatter(
        matmul_flip(both_grad_low, w_both).astype(bf16), "fsdp", scatter_dimension=0, tiled=True
    ).astype(f32)
    both_grad_w = matmul_outer(feed_low, both_grad_low).astype(bf16)
    both_parts = cut_tiles([both_grad_w], both_cut.reshape(-1), tile)
    both_parts, down_one, down_two, grad_feed = lax.optimization_barrier(
        (both_parts, down_one, down_two, grad_feed)
    )
    both_sum = lax.psum_scatter(both_parts, "seq", scatter_dimension=0, tiled=True)
    down_half = down_one.shape[0] // 2
    down_one = added(down_one[:down_half], seq_swap(down_one[down_half:].astype(bf16), 2))
    down_two = added(down_two[:down_half], seq_swap(down_two[down_half:].astype(bf16), 1))
    down_sums = [down_one.astype(bf16), down_two.astype(bf16)]
    down_sums = down_sums + [core_swap(value) for value in down_sums]
    down_returned = chip_exchange([gather_tiles(down_sums, down_back[i]) for i in range(chips)])
    down_returned = down_returned + [core_swap(value) for value in down_returned]

    grad_second_norm, grad_gain_pre = feed_pull(grad_feed)
    half_grad = (grad_third + grad_second_norm) * ROOT_HALF
    grad_right, grad_gain_laurel = laurel_pull(half_grad)
    right_grad_low = grad_right.astype(bf16)
    left_grad_low = matmul(right_grad_low, laurel_right).astype(bf16)
    grad_attn, grad_gain_attn = attn_pull(half_grad)
    attn_grad_low = seq_gather(grad_attn.astype(bf16))
    grad_attended = (
        matmul(attn_grad_low, w_out).astype(bf16).reshape(length, per_device, HEAD_DIM)
    )
    out_grad_w = matmul_outer(attn_grad_low, attended_low).astype(bf16)
    value_grad = jnp.einsum("qhk,qhd->kd", prob_low, grad_attended, preferred_element_type=f32)
    grad_prob = jnp.einsum("qhd,kd->qhk", grad_attended, value_single, preferred_element_type=f32)
    inner = jnp.sum(prob * grad_prob, axis=-1, keepdims=True)
    grad_score = (prob * (grad_prob - inner)).astype(bf16)
    grad_query = (
        jnp.einsum("qhk,kd->qhd", grad_score, key_single, preferred_element_type=f32) * SCALE
    ).astype(bf16)
    key_grad = (
        jnp.einsum("qhk,qhd->kd", grad_score, query_heads, preferred_element_type=f32) * SCALE
    ).astype(bf16)
    value_grad = value_grad.astype(bf16)
    partner_grad = seq_swap(jnp.where(is_key, value_grad, key_grad), 1)
    partner_grad = partner_grad.reshape(seq_size // 2, 2, rows, HEAD_DIM)[:, ::-1]
    other_grad = jnp.where(is_key, key_grad, value_grad).astype(f32) + partner_grad.reshape(
        length, HEAD_DIM
    ).astype(f32)
    grad_query_pre, grad_gain_query = query_pull(grad_query.astype(f32))
    grad_key_pre, grad_gain_key = key_pull(other_grad[:, None, :])
    grad_gain_key = jnp.where(is_key, grad_gain_key, 0.0)
    first_grad_low = jnp.concatenate(
        [grad_query_pre, jnp.where(is_key, grad_key_pre, other_grad)], axis=1
    ).astype(bf16)
    first_grad_w = matmul_outer(pack_normed, first_grad_low).astype(bf16)
    grad_normed = (
        half_grad
        + matmul_flip(left_grad_low, laurel_left)
        + seq_sum(matmul_flip(first_grad_low, w_first), bf16)
    )
    grad_stream_norm, grad_gain_in = normed_pull(grad_normed)
    input_grad = (half_grad + grad_stream_norm)[None]

    small_full = jnp.concatenate(
        [
            matmul_outer(normed_low, left_grad_low),
            matmul_outer(right_grad_low, left_low),
            matmul_outer(third_low, vector_grad_low),
            matmul_outer(proj_grad_low, vector_low),
        ],
        axis=1,
    )
    small_grad = small_sum(split_tiles(small_full, tile).reshape(-1, tile))
    small_grad = small_grad.reshape(small_master.shape)
    gain_grad = jnp.concatenate(
        [
            grad_gain_in,
            grad_gain_attn,
            grad_gain_laurel,
            grad_gain_pre,
            grad_gain_post,
            grad_gain_vec,
            grad_gain_query,
            grad_gain_key,
        ]
    )
    gain_part = seq_sum(gain_grad, f32, True)
    gain_part = gain_part + core_swap(gain_part)

    near = (my_chip + shifts) % chips
    near_key = attn_key_chip[near][:, None, :]
    near_order = attn_order_chip[near][:, None, :]
    near_place = by_chip(attn_place)[near][:, None, :]

    def attn_cut(core):
        index = pick(
            (near_key == 2 * my_seq + core)
            & (near_order == jnp.arange(attn_hold)[None, :, None]),
            near_place,
        )
        return cut_tiles([first_grad_w, out_grad_w], index.reshape(-1), tile)

    attn_given, attn_own = attn_cut(1 - my_core), attn_cut(my_core)
    attn_given, attn_own, small_grad, down_returned = lax.optimization_barrier(
        (attn_given, attn_own, small_grad, down_returned)
    )
    attn_own = added(attn_own, core_swap(attn_given)).reshape(chips, attn_hold, tile, tile)
    attn_sum = attn_own[0]
    for offset in range(1, chips):
        attn_sum = attn_sum + chip_shift(attn_own[offset].astype(bf16), offset).astype(f32)
    attn_back = pick(
        (column_slots[3][None, None, :] == (my_seq ^ flips)[:, None, None])
        & (column_slots[0][None, None, :] == my_key)
        & (column_slots[2][None, None, :] == jnp.arange(attn_room)[None, :, None]),
        column_slots[1],
    )
    attn_sum = attn_sum.astype(bf16)
    attn_returned = seq_exchange([gather_tiles([attn_sum], attn_back[i]) for i in range(seq_size)])
    attn_returned = attn_returned + [core_swap(value) for value in attn_returned]

    both_sums = [both_sum, core_swap(both_sum)]
    both_return = [gather_tiles(both_sums, both_back[i]) for i in range(chips)]
    both_return, gain_part = lax.optimization_barrier((both_return, gain_part))
    both_returned = chip_exchange(both_return)
    both_returned = both_returned + [core_swap(value) for value in both_returned]
    gain_grad_mine = gain_part
    for offset in range(1, chips):
        gain_grad_mine = gain_grad_mine + chip_shift(gain_part, offset)
    slot_grad = jnp.where(my_slots[0] >= 0, my_slots[1], my_slots[2])

    def slow_return(_, kept):
        parts = jnp.concatenate(
            [
                split_tiles(value, tile)
                for value in (both_grad_w, down_grad_w, first_grad_w, out_grad_w)
            ]
            + [jnp.zeros((1, tile, tile), bf16)]
        )
        index = jnp.where(
            ffn_to == my_fsdp,
            is_down * both_count + ffn_place,
            jnp.where(attn_to == my_seq, ffn_count + attn_place, ffn_count + attn_count),
        )
        spread = gather_tiles([parts], index.reshape(-1))
        return lax.psum_scatter(spread, ("seq", "fsdp"), scatter_dimension=0, tiled=True)

    tile_grads = both_returned + down_returned + attn_returned
    slow_start = attn_start + 2 * seq_size * attn_room
    slow_grads = lax.fori_loop(0, slow_steps, slow_return, jnp.zeros((mine, tile, tile), bf16))
    tile_grads = tile_grads + [slow_grads]
    slot_grad = jnp.where(fits, slot_grad, slow_start + local_slots)

    tile_new, tile_first_new, tile_second_new = rotate_update(
        tile_grads, slot_grad, tile_master, tile_first, tile_second, left_basis, right_basis, RATE_TILE
    )
    small_new, small_first_new, small_second_new = rotate_update(
        [small_grad],
        jnp.arange(small_master.shape[0]),
        small_master,
        small_first,
        small_second,
        small_left,
        small_right,
        RATE_SMALL,
    )
    gain_first_new = BETA_ONE * gain_first + (1.0 - BETA_ONE) * gain_grad_mine
    gain_second_new = BETA_TWO * gain_second + (1.0 - BETA_TWO) * gain_grad_mine * gain_grad_mine
    correct_one = 1.0 - BETA_ONE**STEP
    correct_two = 1.0 - BETA_TWO**STEP
    gain_new = gains - RATE_GAIN * (gain_first_new / correct_one) / (
        jnp.sqrt(gain_second_new / correct_two) + ADAM_EPS
    )
    return (
        output,
        input_grad,
        tile_new,
        tile_first_new,
        tile_second_new,
        small_new,
        small_first_new,
        small_second_new,
        gain_new,
        gain_first_new,
        gain_second_new,
    )


def solution(mesh):
    return jax.shard_map(
        on_device,
        mesh=mesh,
        in_specs=(
            P("fsdp", "seq", None),
            P("fsdp", "seq", None),
            P("fsdp", None),
            P("fsdp", "seq", None),
            P(),
            P(("seq", "fsdp"), None, None),
            P(("seq", "fsdp"), None, None),
            P(("seq", "fsdp"), None, None),
            P(("seq", "fsdp"), None, None),
            P(("seq", "fsdp"), None, None),
            P("seq", None, None),
            P("seq", None, None),
            P("seq", None, None),
            P("seq", None, None),
            P("seq", None, None),
            P("seq"),
            P("seq"),
            P("seq"),
        ),
        out_specs=(
            P("fsdp", "seq", None),
            P("fsdp", "seq", None),
            P(("seq", "fsdp"), None, None),
            P(("seq", "fsdp"), None, None),
            P(("seq", "fsdp"), None, None),
            P("seq", None, None),
            P("seq", None, None),
            P("seq", None, None),
            P("seq"),
            P("seq"),
            P("seq"),
        ),
        check_vma=False,
    )
```

```python
import math

import jax
import jax.numpy as jnp
from jax import lax
from jax.experimental import pallas as pl
from jax.experimental.pallas import tpu as pltpu
from jax.sharding import PartitionSpec as P

HEADS = 8
KV_HEADS = 2
HEAD_DIM = 256
FF = 8192
RANK = 64
PLD = 256
STEP = 5


EPS = 1e-06
SCALE = 0.0625
THETA = 1000000.0
ROOT_HALF = 0.7071067811865476
BETA_ONE = 0.5
BETA_TWO = 0.5
ADAM_EPS = 1e-08
RATE_TILE = 0.02
RATE_SMALL = 0.04
RATE_GAIN = 0.3
DECAY = 0.01
NEGATIVE = -1e30
VMEM_BYTES = 32 * 1024 * 1024


def rms_norm(value, gain):
    return value * lax.rsqrt(jnp.mean(value * value, axis=-1, keepdims=True) + EPS) * gain


def rotary(value, position):
    half = value.shape[-1] // 2
    freq = THETA ** (-2.0 * jnp.arange(half).astype(jnp.float32) / value.shape[-1])
    angle = position.astype(jnp.float32)[:, None] * freq[None, :]
    cosine = jnp.cos(angle)[:, None, :]
    sine = jnp.sin(angle)[:, None, :]
    first = value[..., :half]
    second = value[..., half:]
    return jnp.concatenate(
        [first * cosine - second * sine, second * cosine + first * sine], axis=-1
    )


def documents(lengths, length):
    places = jnp.arange(length)
    ends = jnp.cumsum(lengths)
    passed = places[:, None] >= ends[None, :]
    segment = jnp.sum(passed.astype(jnp.int32), axis=1)
    before = jnp.sum(jnp.where(passed, lengths[None, :], 0), axis=1)
    return (segment, places - before)


def matmul(left, right):
    return jnp.dot(left, right, preferred_element_type=jnp.float32)


def matmul_flip(left, right):
    return lax.dot_general(
        left, right, (((1,), (1,)), ((), ())), preferred_element_type=jnp.float32
    )


def matmul_outer(left, right):
    return lax.dot_general(
        left, right, (((0,), (0,)), ((), ())), preferred_element_type=jnp.float32
    )


def assemble(tiles, row_blocks):
    size = tiles.shape[1]
    column_blocks = tiles.shape[0] // row_blocks
    return (
        tiles.reshape(row_blocks, column_blocks, size, size)
        .transpose(0, 2, 1, 3)
        .reshape(row_blocks * size, column_blocks * size)
    )


def split_tiles(matrix, size):
    row_blocks = matrix.shape[0] // size
    column_blocks = matrix.shape[1] // size
    return (
        matrix.reshape(row_blocks, size, column_blocks, size)
        .transpose(0, 2, 1, 3)
        .reshape(row_blocks * column_blocks, size, size)
    )


def gelu_product(first, second):
    return jax.nn.gelu(first, approximate=True) * second


def room(count, share):
    mean = count * share
    return math.ceil(mean + 3.6 * math.sqrt(mean * (1.0 - share)) + 3.0)


def count_earlier(group, valid):
    size = group.shape[-1]
    order = jnp.arange(size)
    same = (group[..., :, None] == group[..., None, :]) & valid[..., None, :]
    same = same & (order[None, :] < order[:, None])
    return jnp.sum(same.astype(jnp.int32), axis=-1)


def pick(match, value):
    return jnp.sum(jnp.where(match, value, 0), axis=-1)


def steps_of(count):
    for steps in range(4, 65):
        if count % steps == 0 and 16 <= count // steps <= 160:
            return steps
    return 2 if count % 2 == 0 else 1


def tile_kernel_call(kernel, index, arrays, out_shape, out_specs, steps):
    moved = sum(math.prod(one.shape) * 2 for one in jax.tree.leaves(out_shape))
    return pl.pallas_call(
        kernel,
        grid=(steps,),
        cost_estimate=pl.CostEstimate(flops=0, transcendentals=0, bytes_accessed=2 * moved),
        out_shape=out_shape,
        in_specs=[pl.BlockSpec(memory_space=pltpu.SMEM)]
        + [pl.BlockSpec(memory_space=pl.ANY)] * len(arrays),
        out_specs=out_specs,
        scratch_shapes=[pltpu.SemaphoreType.DMA],
        compiler_params=pltpu.CompilerParams(vmem_limit_bytes=VMEM_BYTES),
    )(index, *arrays)


def start_copy(sources, place, target, sem):
    start = 0
    for ref in sources:
        size = ref.shape[0]

        @pl.when((place >= start) & (place < start + size))
        def _(ref=ref, start=start):
            pltpu.make_async_copy(ref.at[place - start], target, sem).start()

        start = start + size


def gather_tiles(arrays, index):
    tile = arrays[0].shape[-1]
    count = index.shape[0]
    steps = steps_of(count)
    each = count // steps

    def kernel(index_ref, *refs):
        sources, out, sem = refs[:-2], refs[-2], refs[-1]
        base = pl.program_id(0) * each

        def step(i, carry):
            start_copy(sources, index_ref[base + i], out.at[i], sem)
            return carry

        lax.fori_loop(0, each, step, 0)
        pltpu.make_async_copy(out, out, sem).wait()

    total = sum(array.shape[0] for array in arrays)
    return tile_kernel_call(
        kernel,
        jnp.clip(index, 0, total - 1),
        arrays,
        jax.ShapeDtypeStruct((count, tile, tile), arrays[0].dtype),
        pl.BlockSpec((each, tile, tile), lambda i: (i, 0, 0)),
        steps,
    )


def join_tiles(arrays, index, row_blocks, columns):
    tile = arrays[0].shape[-1]
    steps = 4
    each = row_blocks // steps

    def kernel(index_ref, *refs):
        sources, outs, sem = refs[: len(arrays)], refs[len(arrays) : -1], refs[-1]
        base = pl.program_id(0) * each
        start = 0
        for out, width in zip(outs, columns):

            def step(i, carry, out=out, start=start, width=width):
                row = i // width
                column = i - row * width
                target = out.at[
                    pl.ds(pl.multiple_of(row * tile, tile), tile),
                    pl.ds(pl.multiple_of(column * tile, tile), tile),
                ]
                start_copy(sources, index_ref[start + base * width + i], target, sem)
                return carry

            lax.fori_loop(0, each * width, step, 0)
            start = start + row_blocks * width
        for out in outs:
            pltpu.make_async_copy(out, out, sem).wait()

    total = sum(array.shape[0] for array in arrays)
    out_shape = tuple(
        jax.ShapeDtypeStruct((row_blocks * tile, width * tile), arrays[0].dtype)
        for width in columns
    )
    out_specs = tuple(pl.BlockSpec((each * tile, width * tile), lambda i: (i, 0)) for width in columns)
    return tile_kernel_call(
        kernel, jnp.clip(index, 0, total - 1), arrays, out_shape, out_specs, steps
    )


def cut_tiles(matrices, index, tile):
    row_blocks = matrices[0].shape[0] // tile
    widths = [matrix.shape[1] // tile for matrix in matrices]
    count = index.shape[0]
    steps = steps_of(count)
    each = count // steps

    def kernel(index_ref, *refs):
        sources, out, sem = refs[:-2], refs[-2], refs[-1]
        base = pl.program_id(0) * each

        def step(i, carry):
            place = index_ref[base + i]
            start = 0
            for ref, width in zip(sources, widths):
                size = row_blocks * width

                @pl.when((place >= start) & (place < start + size))
                def _(ref=ref, start=start, width=width):
                    row = (place - start) // width
                    column = place - start - row * width
                    source = ref.at[
                        pl.ds(pl.multiple_of(row * tile, tile), tile),
                        pl.ds(pl.multiple_of(column * tile, tile), tile),
                    ]
                    pltpu.make_async_copy(source, out.at[i], sem).start()

                start = start + size
            return carry

        lax.fori_loop(0, each, step, 0)
        pltpu.make_async_copy(out, out, sem).wait()

    return tile_kernel_call(
        kernel,
        jnp.clip(index, 0, row_blocks * sum(widths) - 1),
        matrices,
        jax.ShapeDtypeStruct((count, tile, tile), matrices[0].dtype),
        pl.BlockSpec((each, tile, tile), lambda i: (i, 0, 0)),
        steps,
    )


def split_low(value):
    high = value.astype(jnp.bfloat16)
    return high, (value - high.astype(jnp.float32)).astype(jnp.bfloat16)


def rotate_update(grads, index, master, first, second, left, right, rate):
    count, tile, _ = master.shape
    each = 4 if count % 4 == 0 else 1
    correct_one = 1.0 - BETA_ONE**STEP
    correct_two = 1.0 - BETA_TWO**STEP

    def product(one, two, dims):
        return lax.dot_general(one, two, (dims, ((), ())), preferred_element_type=jnp.float32)

    def kernel(index_ref, *refs):
        sources, refs = refs[: len(grads)], refs[len(grads) :]
        master_ref, first_ref, second_ref, left_ref, right_ref = refs[:5]
        master_out, first_out, second_out, held, sems = refs[5:]
        now = pl.program_id(0)

        @pl.when(now == 0)
        def _():
            def step(i, carry):
                start_copy(sources, index_ref[i], held.at[i], sems.at[i // each])
                return carry

            lax.fori_loop(0, count, step, 0)

        block = held.at[pl.ds(now * each, each)]
        pltpu.make_async_copy(block, block, sems.at[now]).wait()
        lefts, rights, turns = [], [], []
        for i in range(each):
            grad = held[now * each + i]
            lefts.append(split_low(left_ref[i]))
            rights.append(split_low(right_ref[i]))
            half_turned = product(
                jnp.concatenate([grad, grad], axis=1),
                jnp.concatenate(rights[i], axis=0),
                ((1,), (0,)),
            )
            turns.append(split_low(half_turned))
        for i in range(each):
            (left_high, left_low), (high, low) = lefts[i], turns[i]
            turns[i] = product(
                jnp.concatenate([left_high, left_high, left_low], axis=0),
                jnp.concatenate([high, low, high], axis=0),
                ((0,), (0,)),
            )
        for i in range(each):
            right_high, right_low = rights[i]
            first_new = BETA_ONE * first_ref[i] + (1.0 - BETA_ONE) * turns[i]
            second_new = BETA_TWO * second_ref[i] + (1.0 - BETA_TWO) * turns[i] * turns[i]
            first_out[i] = first_new
            second_out[i] = second_new
            high, low = split_low(
                first_new / correct_one / (jnp.sqrt(second_new / correct_two) + ADAM_EPS)
            )
            half_back = product(
                jnp.concatenate([high, low, high], axis=1),
                jnp.concatenate([right_high, right_high, right_low], axis=1),
                ((1,), (1,)),
            )
            turns[i] = split_low(half_back)
        for i in range(each):
            (left_high, left_low), (high, low) = lefts[i], turns[i]
            back = product(
                jnp.concatenate([left_high, left_high, left_low], axis=1),
                jnp.concatenate([high, low, high], axis=0),
                ((1,), (0,)),
            )
            weight = master_ref[i]
            master_out[i] = weight - rate * (back + DECAY * weight)

    spec = pl.BlockSpec((each, tile, tile), lambda i: (i, 0, 0))
    shape = jax.ShapeDtypeStruct(master.shape, jnp.float32)
    total = sum(array.shape[0] for array in grads)
    return pl.pallas_call(
        kernel,
        grid=(count // each,),
        out_shape=(shape, shape, shape),
        in_specs=[pl.BlockSpec(memory_space=pltpu.SMEM)]
        + [pl.BlockSpec(memory_space=pl.ANY)] * len(grads)
        + [spec] * 5,
        out_specs=(spec, spec, spec),
        scratch_shapes=[
            pltpu.VMEM((count, tile, tile), jnp.bfloat16),
            pltpu.SemaphoreType.DMA((count // each,)),
        ],
        compiler_params=pltpu.CompilerParams(vmem_limit_bytes=VMEM_BYTES),
    )(jnp.clip(index, 0, total - 1), *grads, master, first, second, left, right)


def seq_swap(value, flip):
    size = lax.axis_size("seq")
    return lax.ppermute(value, "seq", [(i, i ^ flip) for i in range(size)])


def core_swap(value):
    size = lax.axis_size("fsdp")
    return lax.ppermute(value, "fsdp", [(i, i ^ 1) for i in range(size)])


def chip_shift(value, offset):
    size = lax.axis_size("fsdp")
    chips = size // 2
    return lax.ppermute(
        value, "fsdp", [(i, (i // 2 + offset) % chips * 2 + i % 2) for i in range(size)]
    )


def seq_gather(value):
    size = lax.axis_size("seq")
    return jnp.concatenate([value] + [seq_swap(value, flip) for flip in range(1, size)], axis=0)


def seq_ordered(value):
    size = lax.axis_size("seq")
    parts = jnp.stack([value] + [seq_swap(value, flip) for flip in range(1, size)], axis=0)
    return parts[lax.axis_index("seq") ^ jnp.arange(size)]


def seq_exchange(values):
    return [values[0]] + [seq_swap(values[flip], flip) for flip in range(1, len(values))]


def seq_sum(value, wire, ordered=False):
    size = lax.axis_size("seq")
    parts = value.reshape((size, value.shape[0] // size) + value.shape[1:])
    if ordered:
        parts = parts[lax.axis_index("seq") ^ jnp.arange(size)]
    total = parts[0]
    for flip in range(1, size):
        total = total + seq_swap(parts[flip].astype(wire), flip).astype(jnp.float32)
    return total


def chip_exchange(values):
    return [values[0]] + [chip_shift(values[offset], offset) for offset in range(1, len(values))]


def core_pair(value):
    other = core_swap(value)
    even = lax.axis_index("fsdp") % 2 == 0
    return jnp.where(even, jnp.stack([value, other]), jnp.stack([other, value]))


def small_sum(value):
    seq_size = lax.axis_size("seq")
    even = lax.axis_index("fsdp") % 2 == 0
    low = value.astype(jnp.bfloat16)
    parts = low.reshape((seq_size, 2, low.shape[0] // (2 * seq_size)) + low.shape[1:])
    kept = jnp.where(even, parts[:, 0], parts[:, 1]).astype(jnp.float32)
    given = jnp.where(even, parts[:, 1], parts[:, 0])
    kept = kept + core_swap(given).astype(jnp.float32)
    return seq_sum(kept.reshape((-1,) + low.shape[1:]), jnp.bfloat16, True).astype(jnp.bfloat16)


def small_all(kept):
    even = lax.axis_index("fsdp") % 2 == 0
    empty = jnp.zeros_like(kept)
    both = jnp.where(even, jnp.stack([kept, empty]), jnp.stack([empty, kept]))
    return lax.psum(both, "fsdp").reshape((2 * kept.shape[0],) + kept.shape[1:])


def on_device(
    tokens,
    layer_vectors,
    doc_lengths,
    cotangent,
    tile_owner,
    tile_master,
    tile_first,
    tile_second,
    left_basis,
    right_basis,
    small_master,
    small_first,
    small_second,
    small_left,
    small_right,
    gains,
    gain_first,
    gain_second,
):
    bf16 = jnp.bfloat16
    f32 = jnp.float32
    tile = tile_master.shape[1]
    width = tokens.shape[2]
    row_blocks = width // tile
    rows = tokens.shape[1]
    seq_size = lax.axis_size("seq")
    fsdp_size = lax.axis_size("fsdp")
    chips = fsdp_size // 2
    mine = tile_master.shape[0]
    tiles = tile_owner.shape[0]
    length = rows * seq_size
    per_device = HEADS // seq_size
    per_key = seq_size // KV_HEADS
    query_width = HEADS * HEAD_DIM
    key_width = KV_HEADS * HEAD_DIM
    my_seq = lax.axis_index("seq")
    my_fsdp = lax.axis_index("fsdp")
    my_chip = my_fsdp // 2
    my_core = my_fsdp % 2
    flips = jnp.arange(seq_size)
    shifts = jnp.arange(chips)

    query_blocks = query_width // tile
    key_blocks = key_width // tile
    ffn_blocks = FF // tile
    query_each = query_blocks // seq_size
    head_blocks = HEAD_DIM // tile
    ffn_each = ffn_blocks // fsdp_size
    columns = tiles // row_blocks
    attn_first = query_each + head_blocks
    attn_count = row_blocks * (attn_first + query_each)
    ffn_first = 2 * ffn_each
    ffn_count = row_blocks * 3 * ffn_each
    attn_share = (2 * query_blocks + 2 * key_blocks) / columns
    ffn_share = 3 * ffn_blocks / columns
    attn_room = (room(2 * mine, attn_share / seq_size) + 1) // 2
    attn_hold = (room(attn_count, 1.0 / chips) + 1) // 2 + 1
    ffn_room = (room(2 * mine, ffn_share / chips) + 1) // 2
    ffn_hold = (room(ffn_count, 1.0 / seq_size) + 3) // 4 * 4
    ffn_half = ffn_hold // 2

    def tile_places(owner):
        row = owner // columns
        column = owner % columns
        key_at = column - query_blocks
        value_at = key_at - key_blocks
        out_at = value_at - key_blocks
        ffn_at = out_at - query_blocks
        is_attn = ffn_at < 0
        kind = ffn_at // ffn_blocks
        ffn_column = ffn_at % ffn_blocks
        ffn_to = jnp.where(is_attn, -1, ffn_column // ffn_each)
        ffn_local = ffn_column % ffn_each
        ffn_place = jnp.where(
            kind == 2,
            row_blocks * ffn_first + row * ffn_each + ffn_local,
            row * ffn_first + kind * ffn_each + ffn_local,
        )
        attn_to = jnp.where(
            key_at < 0,
            column // query_each,
            jnp.where(
                value_at < 0,
                key_at // head_blocks * per_key,
                jnp.where(
                    out_at < 0,
                    value_at // head_blocks * per_key + per_key - 1,
                    out_at // query_each,
                ),
            ),
        )
        attn_place = jnp.where(
            key_at < 0,
            row * attn_first + column % query_each,
            jnp.where(
                out_at < 0,
                row * attn_first + query_each + key_at % head_blocks,
                row_blocks * attn_first + row * query_each + out_at % query_each,
            ),
        )
        attn_to = jnp.where(is_attn, attn_to, -1)
        return (ffn_to, ffn_place, attn_to, attn_place)

    owners = tile_owner.reshape(seq_size, fsdp_size, mine)
    ffn_to, ffn_place, attn_to, attn_place = tile_places(owners)
    slot_seq = jnp.arange(seq_size)[:, None, None]
    slot_fsdp = jnp.arange(fsdp_size)[None, :, None]
    slot_chip = slot_fsdp // 2
    ffn_chip = jnp.where(ffn_to < 0, -1, ffn_to // 2)
    chip_view = ffn_chip.reshape(seq_size, chips, 2 * mine)
    chip_rank = count_earlier(chip_view, chip_view >= 0).reshape(owners.shape)
    seq_view = ffn_to.reshape(seq_size, fsdp_size * mine)
    ffn_rank = count_earlier(seq_view, seq_view >= 0).reshape(owners.shape)
    attn_view = attn_to.reshape(seq_size, chips, 2 * mine)
    attn_rank = count_earlier(attn_view, attn_view >= 0).reshape(owners.shape)
    attn_core = (attn_rank + slot_seq) % 2
    attn_rank = attn_rank // 2
    attn_key = jnp.where(attn_to < 0, -1, 2 * attn_to + attn_core)

    def by_chip(value):
        value = value.reshape(seq_size, chips, 2 * mine).transpose(1, 0, 2)
        return value.reshape(chips, seq_size * 2 * mine)

    attn_key_chip = by_chip(attn_key)
    attn_order_chip = count_earlier(attn_key_chip, attn_key_chip >= 0)
    attn_order = (
        attn_order_chip.reshape(chips, seq_size, 2 * mine).transpose(1, 0, 2).reshape(owners.shape)
    )
    fits = jnp.all(
        jnp.where(
            ffn_to < 0,
            (attn_rank < attn_room) & (attn_order < attn_hold),
            (chip_rank < 2 * ffn_room) & (ffn_rank < ffn_hold),
        )
    )
    half = chips * ffn_room
    rank_core = chip_rank // ffn_room
    rank_local = chip_rank % ffn_room
    out_place = (
        jnp.where(rank_core == my_core, 0, half)
        + (my_chip - slot_chip) % chips * ffn_room
        + rank_local
    )
    back_place = (
        jnp.where(rank_core == my_core, 0, half) + (my_chip - ffn_chip) % chips * ffn_room + rank_local
    )
    attn_back_place = (
        jnp.where(attn_core == my_core, 0, seq_size * attn_room)
        + (attn_to ^ my_seq) * attn_room
        + attn_rank
    )
    chip_slots = lax.dynamic_slice(
        jnp.stack([ffn_chip, chip_rank, attn_key, attn_rank]),
        (0, my_seq, 2 * my_chip, 0),
        (4, 1, 2, mine),
    ).reshape(4, 1, 1, 2 * mine)
    my_slots = lax.dynamic_slice(
        jnp.stack([ffn_to, back_place, attn_back_place]), (0, my_seq, my_fsdp, 0), (3, 1, 1, mine)
    ).reshape(3, mine)
    seq_slots = lax.dynamic_slice(
        jnp.stack(
            [
                ffn_to,
                ffn_rank,
                ffn_place,
                out_place,
                chip_rank,
                jnp.broadcast_to(slot_chip, owners.shape),
            ]
        ),
        (0, my_seq, 0, 0),
        (6, 1, fsdp_size, mine),
    ).reshape(6, fsdp_size * mine)
    column_slots = lax.dynamic_slice(
        jnp.stack([attn_key, attn_order, attn_rank, jnp.broadcast_to(slot_seq, owners.shape)]),
        (0, 0, 2 * my_chip, 0),
        (4, seq_size, 2, mine),
    ).reshape(4, 2 * seq_size * mine)
    my_key = 2 * my_seq + my_core

    local_slots = jnp.arange(mine)
    both_slots = jnp.arange(2 * mine)
    both_slots = jnp.where(
        both_slots // mine == my_core, both_slots % mine, mine + both_slots % mine
    )
    attn_pack = pick(
        (chip_slots[2] == (2 * (my_seq ^ flips) + my_core)[:, None, None])
        & (chip_slots[3] == jnp.arange(attn_room)[None, :, None]),
        both_slots,
    )
    attn_keep = pick(
        (column_slots[0][None, :] == my_key)
        & (column_slots[1][None, :] == jnp.arange(attn_hold)[:, None]),
        (column_slots[3] ^ my_seq) * attn_room + column_slots[2],
    )
    attn_join = pick(
        (attn_to.reshape(1, -1) == my_seq)
        & (attn_place.reshape(1, -1) == jnp.arange(attn_count)[:, None]),
        (
            jnp.where(attn_core == my_core, 0, chips * attn_hold)
            + (my_chip - slot_chip) % chips * attn_hold
            + attn_order
        ).reshape(1, -1),
    )
    ffn_pack = pick(
        (chip_slots[0] == ((my_chip + shifts) % chips)[:, None, None])
        & (chip_slots[1] == (my_core * ffn_room + jnp.arange(ffn_room))[None, :, None]),
        both_slots,
    )
    ffn_keep = pick(
        (seq_slots[0][None, :] == my_fsdp) & (seq_slots[1][None, :] == jnp.arange(ffn_hold)[:, None]),
        seq_slots[3][None, :],
    )
    ffn_join = pick(
        (ffn_to.reshape(1, -1) == my_fsdp)
        & (ffn_place.reshape(1, -1) == jnp.arange(ffn_count)[:, None]),
        (
            ffn_rank // ffn_half * (seq_size * ffn_half) + slot_seq * ffn_half + ffn_rank % ffn_half
        ).reshape(1, -1),
    )
    master_low = tile_master.astype(bf16)
    masters = [master_low, core_swap(master_low)]
    ffn_sent = [gather_tiles(masters, ffn_pack[i]) for i in range(chips)]
    masters, ffn_sent, attn_pack = lax.optimization_barrier((masters, ffn_sent, attn_pack))
    ffn_got = chip_exchange(ffn_sent)
    attn_sent = gather_tiles(masters, attn_pack.reshape(-1))
    attn_sent = attn_sent.reshape(seq_size, attn_room, tile, tile)
    attn_got = seq_exchange([attn_sent[i] for i in range(seq_size)])
    pack_tokens = seq_gather(tokens[0])
    gain_full = seq_ordered(gains.astype(bf16))
    small_rows = small_master.shape[0] // 2
    small_half = lax.dynamic_slice_in_dim(small_master, my_core * small_rows, small_rows)
    small_got = core_pair(seq_ordered(small_half.astype(bf16))).transpose(1, 0, 2, 3, 4)
    ffn_got, attn_got, pack_tokens, gain_full, small_got = lax.optimization_barrier(
        (ffn_got, attn_got, pack_tokens, gain_full, small_got)
    )
    attn_kept = gather_tiles(attn_got, attn_keep)
    ffn_other = [core_swap(value) for value in ffn_got]
    ffn_kept = [
        gather_tiles(ffn_got + ffn_other, ffn_keep[:ffn_half]),
        gather_tiles(ffn_got + ffn_other, ffn_keep[ffn_half:]),
    ]
    ffn_kept, attn_kept = lax.optimization_barrier((ffn_kept, attn_kept))
    ffn_all = [lax.all_gather(value, "seq", axis=0, tiled=True) for value in ffn_kept]
    attn_all = [attn_kept] + [chip_shift(attn_kept, offset) for offset in range(1, chips)]
    attn_all = attn_all + [core_swap(value) for value in attn_all]
    attn_all, ffn_all[0] = lax.optimization_barrier((attn_all, ffn_all[0]))
    w_first, w_out = join_tiles(attn_all, attn_join, row_blocks, (attn_first, query_each))

    def slow_fetch(to, me, place, columns_of):
        def fetch(_, kept):
            whole = lax.all_gather(master_low, ("seq", "fsdp"), axis=0, tiled=True)
            count = row_blocks * sum(columns_of)
            index = pick(
                (to.reshape(1, -1) == me) & (place.reshape(1, -1) == jnp.arange(count)[:, None]),
                jnp.arange(tiles)[None, :],
            )
            return join_tiles([whole], index, row_blocks, columns_of)

        return fetch

    slow_steps = jnp.where(fits, 0, 1)
    w_first, w_out = lax.fori_loop(
        0, slow_steps, slow_fetch(attn_to, my_seq, attn_place, (attn_first, query_each)), (w_first, w_out)
    )

    small_table = assemble(small_got.reshape((-1,) + small_master.shape[1:]), row_blocks)
    gain_full = gain_full.reshape(-1).astype(f32)
    gain_in = gain_full[0:width]
    gain_attn = gain_full[width : 2 * width]
    gain_laurel = gain_full[2 * width : 3 * width]
    gain_pre = gain_full[3 * width : 4 * width]
    gain_post = gain_full[4 * width : 5 * width]
    gain_vec = gain_full[5 * width : 6 * width]
    gain_query = gain_full[6 * width : 6 * width + HEAD_DIM]
    gain_key = gain_full[6 * width + HEAD_DIM : 6 * width + 2 * HEAD_DIM]
    laurel_left = small_table[:, :RANK]
    laurel_right = small_table[:, RANK : 2 * RANK]
    vector_gate_w = small_table[:, 2 * RANK : 2 * RANK + PLD]
    vector_proj_w = small_table[:, 2 * RANK + PLD :]

    segment, position = documents(doc_lengths[0], length)
    places = ((my_seq ^ flips)[:, None] * rows + jnp.arange(rows)[None, :]).reshape(-1)

    def reorder(values):
        blocks = values.reshape(seq_size, rows)
        return jnp.concatenate(
            [lax.dynamic_index_in_dim(blocks, my_seq ^ i, 0, False) for i in range(seq_size)]
        )

    pack_segment = reorder(segment)
    pack_position = reorder(position)
    stream = tokens[0].astype(f32)
    vectors = layer_vectors[0].astype(f32)
    normed, normed_pull = jax.vjp(rms_norm, stream, gain_in)
    normed_low = normed.astype(bf16)
    pack_normed = rms_norm(pack_tokens.astype(f32), gain_in).astype(bf16)
    first_pre = matmul(pack_normed, w_first)
    is_key = my_seq % per_key == 0

    def shape_query(query_in, query_gain):
        return rotary(
            rms_norm(query_in.reshape(length, per_device, HEAD_DIM), query_gain), pack_position
        )

    def shape_key(key_in, key_gain):
        return rotary(rms_norm(key_in.reshape(length, 1, HEAD_DIM), key_gain), pack_position)

    query_pre = first_pre[:, : per_device * HEAD_DIM]
    other_pre = first_pre[:, per_device * HEAD_DIM :]
    query_rot, query_pull = jax.vjp(shape_query, query_pre, gain_query)
    key_rot, key_pull = jax.vjp(shape_key, other_pre, gain_key)
    query_heads = query_rot.astype(bf16)
    other_low = jnp.where(is_key, key_rot[:, 0, :], other_pre).astype(bf16)
    partner_low = seq_swap(other_low, 1).reshape(seq_size // 2, 2, rows, HEAD_DIM)
    partner_low = partner_low[:, ::-1].reshape(length, HEAD_DIM)
    key_single = jnp.where(is_key, other_low, partner_low)
    value_single = jnp.where(is_key, partner_low, other_low)

    allow = (pack_segment[:, None] == pack_segment[None, :]) & (
        places[None, :] <= places[:, None]
    )
    raw = (
        jnp.einsum("qhd,kd->qhk", query_heads, key_single, preferred_element_type=f32) * SCALE
    )
    scores = jnp.where(allow[:, None, :], raw, NEGATIVE)
    powers = jnp.exp(scores - jnp.max(scores, axis=-1, keepdims=True))
    prob = powers / jnp.sum(powers, axis=-1, keepdims=True)
    prob_low = prob.astype(bf16)
    attended_low = (
        jnp.einsum("qhk,kd->qhd", prob_low, value_single, preferred_element_type=f32)
        .astype(bf16)
        .reshape(length, per_device * HEAD_DIM)
    )
    attn_pre = seq_sum(matmul_flip(attended_low, w_out), bf16)
    attn_normed, attn_pull = jax.vjp(rms_norm, attn_pre, gain_attn)
    first_sum = stream + attn_normed
    left_pre = matmul(normed_low, laurel_left)
    left_low = left_pre.astype(bf16)
    right_pre = matmul_flip(left_low, laurel_right)
    laurel_normed, laurel_pull = jax.vjp(rms_norm, right_pre, gain_laurel)
    second_sum = (first_sum + normed + laurel_normed) * ROOT_HALF
    feed_normed, feed_pull = jax.vjp(rms_norm, second_sum, gain_pre)
    feed_own = feed_normed.astype(bf16)
    ffn_all, _ = lax.optimization_barrier((ffn_all, feed_own))
    feed_low = lax.all_gather(feed_own, "fsdp", axis=0, tiled=True)
    w_both, w_down = join_tiles(ffn_all, ffn_join, row_blocks, (ffn_first, ffn_each))
    w_both, w_down = lax.fori_loop(
        0, slow_steps, slow_fetch(ffn_to, my_fsdp, ffn_place, (ffn_first, ffn_each)), (w_both, w_down)
    )
    both_pre = matmul(feed_low, w_both)
    ffn_width = w_down.shape[1]
    hidden, hidden_pull = jax.vjp(gelu_product, both_pre[:, :ffn_width], both_pre[:, ffn_width:])
    hidden_low = hidden.astype(bf16)
    down_pre = lax.psum_scatter(
        matmul_flip(hidden_low, w_down).astype(bf16), "fsdp", scatter_dimension=0, tiled=True
    ).astype(f32)
    down_normed, down_pull = jax.vjp(rms_norm, down_pre, gain_post)
    third_sum = second_sum + down_normed
    third_low = third_sum.astype(bf16)
    vector_pre = matmul(third_low, vector_gate_w)
    vector_gated, vector_pull = jax.vjp(lambda inner: gelu_product(inner, vectors), vector_pre)
    vector_low = vector_gated.astype(bf16)
    proj_pre = matmul_flip(vector_low, vector_proj_w)
    proj_normed, proj_pull = jax.vjp(rms_norm, proj_pre, gain_vec)
    result = third_sum + proj_normed
    output = result.astype(bf16)[None]

    grad_out = cotangent[0].astype(f32)
    grad_proj, grad_gain_vec = proj_pull(grad_out)
    proj_grad_low = grad_proj.astype(bf16)
    (grad_vector_pre,) = vector_pull(matmul(proj_grad_low, vector_proj_w))
    vector_grad_low = grad_vector_pre.astype(bf16)
    grad_third = grad_out + matmul_flip(vector_grad_low, vector_gate_w)
    grad_down, grad_gain_post = down_pull(grad_third)
    down_grad_low = lax.all_gather(grad_down.astype(bf16), "fsdp", axis=0, tiled=True)
    grad_gate, grad_up = hidden_pull(matmul(down_grad_low, w_down))
    both_grad_low = jnp.concatenate([grad_gate, grad_up], axis=1).astype(bf16)
    grad_feed = lax.psum_scatter(
        matmul_flip(both_grad_low, w_both).astype(bf16), "fsdp", scatter_dimension=0, tiled=True
    ).astype(f32)
    both_grad_w = matmul_outer(feed_low, both_grad_low).astype(bf16)
    down_grad_w = matmul_outer(down_grad_low, hidden_low).astype(bf16)

    ffn_cut = pick(
        (ffn_to.reshape(seq_size, 1, -1) == my_fsdp)
        & (ffn_rank.reshape(seq_size, 1, -1) == jnp.arange(ffn_hold)[None, :, None]),
        ffn_place.reshape(seq_size, 1, -1),
    )
    ffn_parts = cut_tiles([both_grad_w, down_grad_w], ffn_cut.reshape(-1), tile)
    ffn_parts, grad_feed = lax.optimization_barrier((ffn_parts, grad_feed))
    ffn_sum = lax.psum_scatter(ffn_parts, "seq", scatter_dimension=0, tiled=True)

    grad_second_norm, grad_gain_pre = feed_pull(grad_feed)
    half_grad = (grad_third + grad_second_norm) * ROOT_HALF
    grad_right, grad_gain_laurel = laurel_pull(half_grad)
    right_grad_low = grad_right.astype(bf16)
    left_grad_low = matmul(right_grad_low, laurel_right).astype(bf16)
    grad_attn, grad_gain_attn = attn_pull(half_grad)
    attn_grad_low = seq_gather(grad_attn.astype(bf16))
    grad_attended = (
        matmul(attn_grad_low, w_out).astype(bf16).reshape(length, per_device, HEAD_DIM)
    )
    out_grad_w = matmul_outer(attn_grad_low, attended_low).astype(bf16)
    value_grad = jnp.einsum("qhk,qhd->kd", prob_low, grad_attended, preferred_element_type=f32)
    grad_prob = jnp.einsum("qhd,kd->qhk", grad_attended, value_single, preferred_element_type=f32)
    inner = jnp.sum(prob * grad_prob, axis=-1, keepdims=True)
    grad_score = (prob * (grad_prob - inner)).astype(bf16)
    grad_query = (
        jnp.einsum("qhk,kd->qhd", grad_score, key_single, preferred_element_type=f32) * SCALE
    ).astype(bf16)
    key_grad = (
        jnp.einsum("qhk,qhd->kd", grad_score, query_heads, preferred_element_type=f32) * SCALE
    ).astype(bf16)
    value_grad = value_grad.astype(bf16)
    partner_grad = seq_swap(jnp.where(is_key, value_grad, key_grad), 1)
    partner_grad = partner_grad.reshape(seq_size // 2, 2, rows, HEAD_DIM)[:, ::-1]
    other_grad = jnp.where(is_key, key_grad, value_grad).astype(f32) + partner_grad.reshape(
        length, HEAD_DIM
    ).astype(f32)
    grad_query_pre, grad_gain_query = query_pull(grad_query.astype(f32))
    grad_key_pre, grad_gain_key = key_pull(other_grad[:, None, :])
    grad_gain_key = jnp.where(is_key, grad_gain_key, 0.0)
    first_grad_low = jnp.concatenate(
        [grad_query_pre, jnp.where(is_key, grad_key_pre, other_grad)], axis=1
    ).astype(bf16)
    first_grad_w = matmul_outer(pack_normed, first_grad_low).astype(bf16)
    grad_normed = (
        half_grad
        + matmul_flip(left_grad_low, laurel_left)
        + seq_sum(matmul_flip(first_grad_low, w_first), bf16)
    )
    grad_stream_norm, grad_gain_in = normed_pull(grad_normed)
    input_grad = (half_grad + grad_stream_norm)[None]

    small_full = jnp.concatenate(
        [
            matmul_outer(normed_low, left_grad_low),
            matmul_outer(right_grad_low, left_low),
            matmul_outer(third_low, vector_grad_low),
            matmul_outer(proj_grad_low, vector_low),
        ],
        axis=1,
    )
    gain_grad = jnp.concatenate(
        [
            grad_gain_in,
            grad_gain_attn,
            grad_gain_laurel,
            grad_gain_pre,
            grad_gain_post,
            grad_gain_vec,
            grad_gain_query,
            grad_gain_key,
        ]
    )
    small_part = small_sum(split_tiles(small_full, tile).reshape(-1, tile))
    gain_part = seq_sum(gain_grad, f32, True)
    gain_part = gain_part + core_swap(gain_part)
    ffn_back = pick(
        (seq_slots[5][None, None, :] == ((my_chip + shifts) % chips)[:, None, None])
        & (seq_slots[0][None, None, :] // 2 == my_chip)
        & (seq_slots[0][None, None, :] >= 0)
        & (seq_slots[4][None, None, :] == (my_core * ffn_room + jnp.arange(ffn_room))[None, :, None]),
        jnp.where(seq_slots[0] == my_fsdp, 0, ffn_hold) + seq_slots[1],
    )
    near = (my_chip + shifts) % chips
    near_key = attn_key_chip[near][:, None, :]
    near_order = attn_order_chip[near][:, None, :]
    near_place = by_chip(attn_place)[near][:, None, :]

    def attn_cut(core):
        index = pick(
            (near_key == 2 * my_seq + core)
            & (near_order == jnp.arange(attn_hold)[None, :, None]),
            near_place,
        )
        return cut_tiles([first_grad_w, out_grad_w], index.reshape(-1), tile)

    attn_given, attn_own = attn_cut(1 - my_core), attn_cut(my_core)
    def added(one, two):
        return one.astype(f32) + two.astype(f32)

    attn_own = added(attn_own, core_swap(attn_given)).reshape(chips, attn_hold, tile, tile)
    attn_sum = attn_own[0]
    for offset in range(1, chips):
        attn_sum = attn_sum + chip_shift(attn_own[offset].astype(bf16), offset).astype(f32)
    attn_sum = attn_sum.astype(bf16)
    attn_back = pick(
        (column_slots[3][None, None, :] == (my_seq ^ flips)[:, None, None])
        & (column_slots[0][None, None, :] == my_key)
        & (column_slots[2][None, None, :] == jnp.arange(attn_room)[None, :, None]),
        column_slots[1],
    )
    ffn_sum, attn_sum, small_part, gain_part = lax.optimization_barrier(
        (ffn_sum, attn_sum, small_part, gain_part)
    )
    ffn_sums = [ffn_sum, core_swap(ffn_sum)]
    ffn_return = [gather_tiles(ffn_sums, ffn_back[i]) for i in range(chips)]
    ffn_return, gain_part, small_part = lax.optimization_barrier((ffn_return, gain_part, small_part))
    small_grad = small_all(small_part).reshape(small_master.shape)
    ffn_returned = chip_exchange(ffn_return)
    ffn_returned = ffn_returned + [core_swap(value) for value in ffn_returned]
    gain_grad_mine = gain_part
    for offset in range(1, chips):
        gain_grad_mine = gain_grad_mine + chip_shift(gain_part, offset)
    attn_returned = seq_exchange([gather_tiles([attn_sum], attn_back[i]) for i in range(seq_size)])
    attn_returned = attn_returned + [core_swap(value) for value in attn_returned]
    slot_grad = jnp.where(my_slots[0] >= 0, my_slots[1], 2 * half + my_slots[2])

    def slow_return(_, kept):
        own_ffn = split_tiles(both_grad_w, tile), split_tiles(down_grad_w, tile)
        own_attn = split_tiles(first_grad_w, tile), split_tiles(out_grad_w, tile)
        parts = jnp.concatenate(own_ffn + own_attn + (jnp.zeros((1, tile, tile), bf16),))
        index = jnp.where(
            ffn_to == my_fsdp,
            ffn_place,
            jnp.where(attn_to == my_seq, ffn_count + attn_place, ffn_count + attn_count),
        )
        spread = gather_tiles([parts], index.reshape(-1))
        return lax.psum_scatter(spread, ("seq", "fsdp"), scatter_dimension=0, tiled=True)

    tile_grads = ffn_returned + attn_returned
    slow_start = 2 * half + 2 * seq_size * attn_room
    slow_grads = lax.fori_loop(0, slow_steps, slow_return, jnp.zeros((mine, tile, tile), bf16))
    tile_grads = tile_grads + [slow_grads]
    slot_grad = jnp.where(fits, slot_grad, slow_start + local_slots)

    tile_new, tile_first_new, tile_second_new = rotate_update(
        tile_grads, slot_grad, tile_master, tile_first, tile_second, left_basis, right_basis, RATE_TILE
    )
    small_new, small_first_new, small_second_new = rotate_update(
        [small_grad],
        jnp.arange(small_master.shape[0]),
        small_master,
        small_first,
        small_second,
        small_left,
        small_right,
        RATE_SMALL,
    )
    gain_first_new = BETA_ONE * gain_first + (1.0 - BETA_ONE) * gain_grad_mine
    gain_second_new = BETA_TWO * gain_second + (1.0 - BETA_TWO) * gain_grad_mine * gain_grad_mine
    correct_one = 1.0 - BETA_ONE**STEP
    correct_two = 1.0 - BETA_TWO**STEP
    gain_new = gains - RATE_GAIN * (gain_first_new / correct_one) / (
        jnp.sqrt(gain_second_new / correct_two) + ADAM_EPS
    )
    return (
        output,
        input_grad,
        tile_new,
        tile_first_new,
        tile_second_new,
        small_new,
        small_first_new,
        small_second_new,
        gain_new,
        gain_first_new,
        gain_second_new,
    )


def solution(mesh):
    return jax.shard_map(
        on_device,
        mesh=mesh,
        in_specs=(
            P("fsdp", "seq", None),
            P("fsdp", "seq", None),
            P("fsdp", None),
            P("fsdp", "seq", None),
            P(),
            P(("seq", "fsdp"), None, None),
            P(("seq", "fsdp"), None, None),
            P(("seq", "fsdp"), None, None),
            P(("seq", "fsdp"), None, None),
            P(("seq", "fsdp"), None, None),
            P("seq", None, None),
            P("seq", None, None),
            P("seq", None, None),
            P("seq", None, None),
            P("seq", None, None),
            P("seq"),
            P("seq"),
            P("seq"),
        ),
        out_specs=(
            P("fsdp", "seq", None),
            P("fsdp", "seq", None),
            P(("seq", "fsdp"), None, None),
            P(("seq", "fsdp"), None, None),
            P(("seq", "fsdp"), None, None),
            P("seq", None, None),
            P("seq", None, None),
            P("seq", None, None),
            P("seq"),
            P("seq"),
            P("seq"),
        ),
        check_vma=False,
    )
```

```python
import math

import jax
import jax.numpy as jnp
from jax import lax
from jax.experimental import pallas as pl
from jax.experimental.pallas import tpu as pltpu
from jax.sharding import PartitionSpec as P

HEADS = 8
KV_HEADS = 2
HEAD_DIM = 256
FF = 8192
RANK = 64
PLD = 256
STEP = 5


EPS = 1e-06
SCALE = 0.0625
THETA = 1000000.0
ROOT_HALF = 0.7071067811865476
BETA_ONE = 0.5
BETA_TWO = 0.5
ADAM_EPS = 1e-08
RATE_TILE = 0.02
RATE_SMALL = 0.04
RATE_GAIN = 0.3
DECAY = 0.01
NEGATIVE = -1e30
VMEM_BYTES = 32 * 1024 * 1024


def rms_norm(value, gain):
    return value * lax.rsqrt(jnp.mean(value * value, axis=-1, keepdims=True) + EPS) * gain


def rotary(value, position):
    half = value.shape[-1] // 2
    freq = THETA ** (-2.0 * jnp.arange(half).astype(jnp.float32) / value.shape[-1])
    angle = position.astype(jnp.float32)[:, None] * freq[None, :]
    cosine = jnp.cos(angle)[:, None, :]
    sine = jnp.sin(angle)[:, None, :]
    first = value[..., :half]
    second = value[..., half:]
    return jnp.concatenate(
        [first * cosine - second * sine, second * cosine + first * sine], axis=-1
    )


def documents(lengths, length):
    places = jnp.arange(length)
    ends = jnp.cumsum(lengths)
    passed = places[:, None] >= ends[None, :]
    segment = jnp.sum(passed.astype(jnp.int32), axis=1)
    before = jnp.sum(jnp.where(passed, lengths[None, :], 0), axis=1)
    return (segment, places - before)


def matmul(left, right):
    return jnp.dot(left, right, preferred_element_type=jnp.float32)


def matmul_flip(left, right):
    return lax.dot_general(
        left, right, (((1,), (1,)), ((), ())), preferred_element_type=jnp.float32
    )


def matmul_outer(left, right):
    return lax.dot_general(
        left, right, (((0,), (0,)), ((), ())), preferred_element_type=jnp.float32
    )


def assemble(tiles, row_blocks):
    size = tiles.shape[1]
    column_blocks = tiles.shape[0] // row_blocks
    return (
        tiles.reshape(row_blocks, column_blocks, size, size)
        .transpose(0, 2, 1, 3)
        .reshape(row_blocks * size, column_blocks * size)
    )


def split_tiles(matrix, size):
    row_blocks = matrix.shape[0] // size
    column_blocks = matrix.shape[1] // size
    return (
        matrix.reshape(row_blocks, size, column_blocks, size)
        .transpose(0, 2, 1, 3)
        .reshape(row_blocks * column_blocks, size, size)
    )


def gelu_product(first, second):
    return jax.nn.gelu(first, approximate=True) * second


def room(count, share):
    mean = count * share
    return math.ceil(mean + 3.6 * math.sqrt(mean * (1.0 - share)) + 3.0)


def count_earlier(group, valid):
    size = group.shape[-1]
    order = jnp.arange(size)
    same = (group[..., :, None] == group[..., None, :]) & valid[..., None, :]
    same = same & (order[None, :] < order[:, None])
    return jnp.sum(same.astype(jnp.int32), axis=-1)


def pick(match, value):
    return jnp.sum(jnp.where(match, value, 0), axis=-1)


def steps_of(count):
    for steps in range(4, 65):
        if count % steps == 0 and 16 <= count // steps <= 160:
            return steps
    return 2 if count % 2 == 0 else 1


def tile_kernel_call(kernel, index, arrays, out_shape, out_specs, steps):
    moved = sum(math.prod(one.shape) * 2 for one in jax.tree.leaves(out_shape))
    return pl.pallas_call(
        kernel,
        grid=(steps,),
        cost_estimate=pl.CostEstimate(flops=0, transcendentals=0, bytes_accessed=2 * moved),
        out_shape=out_shape,
        in_specs=[pl.BlockSpec(memory_space=pltpu.SMEM)]
        + [pl.BlockSpec(memory_space=pl.ANY)] * len(arrays),
        out_specs=out_specs,
        scratch_shapes=[pltpu.SemaphoreType.DMA],
        compiler_params=pltpu.CompilerParams(vmem_limit_bytes=VMEM_BYTES),
    )(index, *arrays)


def start_copy(sources, place, target, sem):
    start = 0
    for ref in sources:
        size = ref.shape[0]

        @pl.when((place >= start) & (place < start + size))
        def _(ref=ref, start=start):
            pltpu.make_async_copy(ref.at[place - start], target, sem).start()

        start = start + size


def gather_tiles(arrays, index):
    tile = arrays[0].shape[-1]
    count = index.shape[0]
    steps = steps_of(count)
    each = count // steps

    def kernel(index_ref, *refs):
        sources, out, sem = refs[:-2], refs[-2], refs[-1]
        base = pl.program_id(0) * each

        def step(i, carry):
            start_copy(sources, index_ref[base + i], out.at[i], sem)
            return carry

        lax.fori_loop(0, each, step, 0)
        pltpu.make_async_copy(out, out, sem).wait()

    total = sum(array.shape[0] for array in arrays)
    return tile_kernel_call(
        kernel,
        jnp.clip(index, 0, total - 1),
        arrays,
        jax.ShapeDtypeStruct((count, tile, tile), arrays[0].dtype),
        pl.BlockSpec((each, tile, tile), lambda i: (i, 0, 0)),
        steps,
    )


def join_tiles(arrays, index, row_blocks, columns):
    tile = arrays[0].shape[-1]
    steps = 4
    each = row_blocks // steps

    def kernel(index_ref, *refs):
        sources, outs, sem = refs[: len(arrays)], refs[len(arrays) : -1], refs[-1]
        base = pl.program_id(0) * each
        start = 0
        for out, width in zip(outs, columns):

            def step(i, carry, out=out, start=start, width=width):
                row = i // width
                column = i - row * width
                target = out.at[
                    pl.ds(pl.multiple_of(row * tile, tile), tile),
                    pl.ds(pl.multiple_of(column * tile, tile), tile),
                ]
                start_copy(sources, index_ref[start + base * width + i], target, sem)
                return carry

            lax.fori_loop(0, each * width, step, 0)
            start = start + row_blocks * width
        for out in outs:
            pltpu.make_async_copy(out, out, sem).wait()

    total = sum(array.shape[0] for array in arrays)
    out_shape = tuple(
        jax.ShapeDtypeStruct((row_blocks * tile, width * tile), arrays[0].dtype)
        for width in columns
    )
    out_specs = tuple(pl.BlockSpec((each * tile, width * tile), lambda i: (i, 0)) for width in columns)
    return tile_kernel_call(
        kernel, jnp.clip(index, 0, total - 1), arrays, out_shape, out_specs, steps
    )


def cut_tiles(matrices, index, tile):
    row_blocks = matrices[0].shape[0] // tile
    widths = [matrix.shape[1] // tile for matrix in matrices]
    count = index.shape[0]
    steps = steps_of(count)
    each = count // steps

    def kernel(index_ref, *refs):
        sources, out, sem = refs[:-2], refs[-2], refs[-1]
        base = pl.program_id(0) * each

        def step(i, carry):
            place = index_ref[base + i]
            start = 0
            for ref, width in zip(sources, widths):
                size = row_blocks * width

                @pl.when((place >= start) & (place < start + size))
                def _(ref=ref, start=start, width=width):
                    row = (place - start) // width
                    column = place - start - row * width
                    source = ref.at[
                        pl.ds(pl.multiple_of(row * tile, tile), tile),
                        pl.ds(pl.multiple_of(column * tile, tile), tile),
                    ]
                    pltpu.make_async_copy(source, out.at[i], sem).start()

                start = start + size
            return carry

        lax.fori_loop(0, each, step, 0)
        pltpu.make_async_copy(out, out, sem).wait()

    return tile_kernel_call(
        kernel,
        jnp.clip(index, 0, row_blocks * sum(widths) - 1),
        matrices,
        jax.ShapeDtypeStruct((count, tile, tile), matrices[0].dtype),
        pl.BlockSpec((each, tile, tile), lambda i: (i, 0, 0)),
        steps,
    )


def split_low(value):
    high = value.astype(jnp.bfloat16)
    return high, (value - high.astype(jnp.float32)).astype(jnp.bfloat16)


def rotate_update(grads, index, master, first, second, left, right, rate):
    count, tile, _ = master.shape
    each = 4 if count % 4 == 0 else 1
    correct_one = 1.0 - BETA_ONE**STEP
    correct_two = 1.0 - BETA_TWO**STEP

    def product(one, two, dims):
        return lax.dot_general(one, two, (dims, ((), ())), preferred_element_type=jnp.float32)

    def kernel(index_ref, *refs):
        sources, refs = refs[: len(grads)], refs[len(grads) :]
        master_ref, first_ref, second_ref, left_ref, right_ref = refs[:5]
        master_out, first_out, second_out, held, sems = refs[5:]
        now = pl.program_id(0)

        @pl.when(now == 0)
        def _():
            def step(i, carry):
                start_copy(sources, index_ref[i], held.at[i], sems.at[i // each])
                return carry

            lax.fori_loop(0, count, step, 0)

        block = held.at[pl.ds(now * each, each)]
        pltpu.make_async_copy(block, block, sems.at[now]).wait()
        lefts, rights, turns = [], [], []
        for i in range(each):
            grad = held[now * each + i]
            lefts.append(split_low(left_ref[i]))
            rights.append(split_low(right_ref[i]))
            half_turned = product(
                jnp.concatenate([grad, grad], axis=1),
                jnp.concatenate(rights[i], axis=0),
                ((1,), (0,)),
            )
            turns.append(split_low(half_turned))
        for i in range(each):
            (left_high, left_low), (high, low) = lefts[i], turns[i]
            turns[i] = product(
                jnp.concatenate([left_high, left_high, left_low], axis=0),
                jnp.concatenate([high, low, high], axis=0),
                ((0,), (0,)),
            )
        for i in range(each):
            right_high, right_low = rights[i]
            first_new = BETA_ONE * first_ref[i] + (1.0 - BETA_ONE) * turns[i]
            second_new = BETA_TWO * second_ref[i] + (1.0 - BETA_TWO) * turns[i] * turns[i]
            first_out[i] = first_new
            second_out[i] = second_new
            high, low = split_low(
                first_new / correct_one / (jnp.sqrt(second_new / correct_two) + ADAM_EPS)
            )
            half_back = product(
                jnp.concatenate([high, low, high], axis=1),
                jnp.concatenate([right_high, right_high, right_low], axis=1),
                ((1,), (1,)),
            )
            turns[i] = split_low(half_back)
        for i in range(each):
            (left_high, left_low), (high, low) = lefts[i], turns[i]
            back = product(
                jnp.concatenate([left_high, left_high, left_low], axis=1),
                jnp.concatenate([high, low, high], axis=0),
                ((1,), (0,)),
            )
            weight = master_ref[i]
            master_out[i] = weight - rate * (back + DECAY * weight)

    spec = pl.BlockSpec((each, tile, tile), lambda i: (i, 0, 0))
    shape = jax.ShapeDtypeStruct(master.shape, jnp.float32)
    total = sum(array.shape[0] for array in grads)
    return pl.pallas_call(
        kernel,
        grid=(count // each,),
        out_shape=(shape, shape, shape),
        in_specs=[pl.BlockSpec(memory_space=pltpu.SMEM)]
        + [pl.BlockSpec(memory_space=pl.ANY)] * len(grads)
        + [spec] * 5,
        out_specs=(spec, spec, spec),
        scratch_shapes=[
            pltpu.VMEM((count, tile, tile), jnp.bfloat16),
            pltpu.SemaphoreType.DMA((count // each,)),
        ],
        compiler_params=pltpu.CompilerParams(vmem_limit_bytes=VMEM_BYTES),
    )(jnp.clip(index, 0, total - 1), *grads, master, first, second, left, right)


def seq_swap(value, flip):
    size = lax.axis_size("seq")
    return lax.ppermute(value, "seq", [(i, i ^ flip) for i in range(size)])


def core_swap(value):
    size = lax.axis_size("fsdp")
    return lax.ppermute(value, "fsdp", [(i, i ^ 1) for i in range(size)])


def chip_shift(value, offset):
    size = lax.axis_size("fsdp")
    chips = size // 2
    return lax.ppermute(
        value, "fsdp", [(i, (i // 2 + offset) % chips * 2 + i % 2) for i in range(size)]
    )


def seq_gather(value):
    size = lax.axis_size("seq")
    return jnp.concatenate([value] + [seq_swap(value, flip) for flip in range(1, size)], axis=0)


def seq_ordered(value):
    size = lax.axis_size("seq")
    parts = jnp.stack([value] + [seq_swap(value, flip) for flip in range(1, size)], axis=0)
    return parts[lax.axis_index("seq") ^ jnp.arange(size)]


def seq_exchange(values):
    return [values[0]] + [seq_swap(values[flip], flip) for flip in range(1, len(values))]


def seq_sum(value, wire, ordered=False):
    size = lax.axis_size("seq")
    parts = value.reshape((size, value.shape[0] // size) + value.shape[1:])
    if ordered:
        parts = parts[lax.axis_index("seq") ^ jnp.arange(size)]
    total = parts[0]
    for flip in range(1, size):
        total = total + seq_swap(parts[flip].astype(wire), flip).astype(jnp.float32)
    return total


def chip_exchange(values):
    return [values[0]] + [chip_shift(values[offset], offset) for offset in range(1, len(values))]


def core_pair(value):
    other = core_swap(value)
    even = lax.axis_index("fsdp") % 2 == 0
    return jnp.where(even, jnp.stack([value, other]), jnp.stack([other, value]))


def small_sum(value):
    seq_size = lax.axis_size("seq")
    chips = lax.axis_size("fsdp") // 2
    chip = lax.axis_index("fsdp") // 2
    even = lax.axis_index("fsdp") % 2 == 0
    low = value.astype(jnp.bfloat16)
    parts = low.reshape((seq_size, 2, low.shape[0] // (2 * seq_size)) + low.shape[1:])
    kept = jnp.where(even, parts[:, 0], parts[:, 1]).astype(jnp.float32)
    given = jnp.where(even, parts[:, 1], parts[:, 0])
    kept = kept + core_swap(given).astype(jnp.float32)
    kept = seq_sum(kept.reshape((-1,) + low.shape[1:]), jnp.bfloat16, True)
    kept = kept.reshape((chips, kept.shape[0] // chips) + kept.shape[1:])
    kept = kept[(chip + jnp.arange(chips)) % chips]
    total = kept[0]
    for offset in range(1, chips):
        total = total + chip_shift(kept[offset].astype(jnp.bfloat16), offset).astype(jnp.float32)
    total = total.astype(jnp.bfloat16)
    parts = jnp.stack([total] + [chip_shift(total, offset) for offset in range(1, chips)])
    parts = parts[(chip - jnp.arange(chips)) % chips]
    return core_pair(parts).reshape((value.shape[0] // seq_size,) + value.shape[1:])


def turn(value, cosine, sine):
    half = value.shape[-1] // 2
    first, second = value[..., :half], value[..., half:]
    return jnp.concatenate(
        [first * cosine - second * sine, second * cosine + first * sine], axis=-1
    )


def added(one, two):
    return one.astype(jnp.float32) + two.astype(jnp.float32)


def on_device(
    tokens,
    layer_vectors,
    doc_lengths,
    cotangent,
    tile_owner,
    tile_master,
    tile_first,
    tile_second,
    left_basis,
    right_basis,
    small_master,
    small_first,
    small_second,
    small_left,
    small_right,
    gains,
    gain_first,
    gain_second,
):
    bf16 = jnp.bfloat16
    f32 = jnp.float32
    tile = tile_master.shape[1]
    width = tokens.shape[2]
    row_blocks = width // tile
    rows = tokens.shape[1]
    seq_size = lax.axis_size("seq")
    fsdp_size = lax.axis_size("fsdp")
    chips = fsdp_size // 2
    mine = tile_master.shape[0]
    tiles = tile_owner.shape[0]
    length = rows * seq_size
    per_device = HEADS // seq_size
    per_key = seq_size // KV_HEADS
    query_width = HEADS * HEAD_DIM
    key_width = KV_HEADS * HEAD_DIM
    my_seq = lax.axis_index("seq")
    my_fsdp = lax.axis_index("fsdp")
    my_chip = my_fsdp // 2
    my_core = my_fsdp % 2
    flips = jnp.arange(seq_size)
    shifts = jnp.arange(chips)

    query_blocks = query_width // tile
    key_blocks = key_width // tile
    ffn_blocks = FF // tile
    query_each = query_blocks // seq_size
    head_blocks = HEAD_DIM // tile
    ffn_each = ffn_blocks // fsdp_size
    columns = tiles // row_blocks
    attn_first = query_each + head_blocks
    attn_count = row_blocks * (attn_first + query_each)
    ffn_first = 2 * ffn_each
    ffn_count = row_blocks * 3 * ffn_each
    attn_share = (2 * query_blocks + 2 * key_blocks) / columns
    ffn_share = 3 * ffn_blocks / columns
    attn_room = (room(2 * mine, attn_share / seq_size) + 1) // 2
    attn_hold = (room(attn_count, 1.0 / chips) + 1) // 2 + 1
    ffn_room = (room(2 * mine, ffn_share / chips) + 1) // 2
    both_count = row_blocks * ffn_first
    both_hold, down_hold = (
        (room(count, 1.0 / seq_size) + 3) // 4 * 4 for count in (both_count, ffn_count - both_count)
    )

    def tile_places(owner):
        row = owner // columns
        column = owner % columns
        key_at = column - query_blocks
        value_at = key_at - key_blocks
        out_at = value_at - key_blocks
        ffn_at = out_at - query_blocks
        is_attn = ffn_at < 0
        kind = ffn_at // ffn_blocks
        ffn_column = ffn_at % ffn_blocks
        ffn_to = jnp.where(is_attn, -1, ffn_column // ffn_each)
        ffn_local = ffn_column % ffn_each
        ffn_place = jnp.where(
            kind == 2, row * ffn_each + ffn_local, row * ffn_first + kind * ffn_each + ffn_local
        )
        is_down = (kind == 2).astype(jnp.int32)
        attn_to = jnp.where(
            key_at < 0,
            column // query_each,
            jnp.where(
                value_at < 0,
                key_at // head_blocks * per_key,
                jnp.where(
                    out_at < 0,
                    value_at // head_blocks * per_key + per_key - 1,
                    out_at // query_each,
                ),
            ),
        )
        attn_place = jnp.where(
            key_at < 0,
            row * attn_first + column % query_each,
            jnp.where(
                out_at < 0,
                row * attn_first + query_each + key_at % head_blocks,
                row_blocks * attn_first + row * query_each + out_at % query_each,
            ),
        )
        attn_to = jnp.where(is_attn, attn_to, -1)
        return (ffn_to, is_down, ffn_place, attn_to, attn_place)

    owners = tile_owner.reshape(seq_size, fsdp_size, mine)
    slot_seq = jnp.arange(seq_size)[:, None, None]
    slot_fsdp = jnp.arange(fsdp_size)[None, :, None]
    slot_chip = slot_fsdp // 2
    local_slots = jnp.arange(mine)
    both_slots = jnp.arange(2 * mine)
    both_slots = jnp.where(
        both_slots // mine == my_core, both_slots % mine, mine + both_slots % mine
    )

    ffn_to = tile_places(owners)[0]
    ffn_chip = jnp.where(ffn_to < 0, -1, ffn_to // 2)
    chip_view = ffn_chip.reshape(seq_size, chips, 2 * mine)
    chip_rank = count_earlier(chip_view, chip_view >= 0).reshape(owners.shape)
    ffn_slots = lax.dynamic_slice(
        jnp.stack([ffn_chip, chip_rank]), (0, my_seq, 2 * my_chip, 0), (2, 1, 2, mine)
    ).reshape(2, 1, 1, 2 * mine)
    ffn_pack = pick(
        (ffn_slots[0] == ((my_chip + shifts) % chips)[:, None, None])
        & (ffn_slots[1] == (my_core * ffn_room + jnp.arange(ffn_room))[None, :, None]),
        both_slots,
    )
    master_low = tile_master.astype(bf16)
    masters = [master_low, core_swap(master_low)]
    ffn_sent = [gather_tiles(masters, ffn_pack[i]) for i in range(chips)]
    small_rows = small_master.shape[0] // 2
    small_half = lax.dynamic_slice_in_dim(small_master, my_core * small_rows, small_rows)
    masters, ffn_sent, chip_rank, owners, own_tokens, own_gains, small_half = (
        lax.optimization_barrier(
            (
                masters,
                ffn_sent,
                chip_rank,
                owners,
                tokens[0],
                gains.astype(bf16),
                small_half.astype(bf16),
            )
        )
    )
    ffn_got = chip_exchange(ffn_sent)

    ffn_to, is_down, ffn_place, attn_to, attn_place = tile_places(owners)
    ffn_chip = jnp.where(ffn_to < 0, -1, ffn_to // 2)
    ffn_key = jnp.where(ffn_to < 0, -1, 2 * ffn_to + is_down)
    ffn_hold = jnp.where(is_down == 1, down_hold, both_hold)
    seq_view = ffn_key.reshape(seq_size, fsdp_size * mine)
    ffn_rank = count_earlier(seq_view, seq_view >= 0).reshape(owners.shape)
    attn_view = attn_to.reshape(seq_size, chips, 2 * mine)
    attn_rank = count_earlier(attn_view, attn_view >= 0).reshape(owners.shape)
    attn_core = (attn_rank + slot_seq) % 2
    attn_rank = attn_rank // 2
    attn_key = jnp.where(attn_to < 0, -1, 2 * attn_to + attn_core)

    def by_chip(value):
        value = value.reshape(seq_size, chips, 2 * mine).transpose(1, 0, 2)
        return value.reshape(chips, seq_size * 2 * mine)

    attn_key_chip = by_chip(attn_key)
    attn_order_chip = count_earlier(attn_key_chip, attn_key_chip >= 0)
    attn_order = (
        attn_order_chip.reshape(chips, seq_size, 2 * mine).transpose(1, 0, 2).reshape(owners.shape)
    )
    fits = jnp.all(
        jnp.where(
            ffn_to < 0,
            (attn_rank < attn_room) & (attn_order < attn_hold),
            (chip_rank < 2 * ffn_room) & (ffn_rank < ffn_hold),
        )
    )
    half = chips * ffn_room
    rank_core = chip_rank // ffn_room
    rank_local = chip_rank % ffn_room
    out_place = (
        jnp.where(rank_core == my_core, 0, half)
        + (my_chip - slot_chip) % chips * ffn_room
        + rank_local
    )
    back_place = (
        jnp.where(rank_core == my_core, 0, half) + (my_chip - ffn_chip) % chips * ffn_room + rank_local
    )
    attn_back_place = (
        jnp.where(attn_core == my_core, 0, seq_size * attn_room)
        + (attn_to ^ my_seq) * attn_room
        + attn_rank
    )
    chip_slots = lax.dynamic_slice(
        jnp.stack([attn_key, attn_rank]), (0, my_seq, 2 * my_chip, 0), (2, 1, 2, mine)
    ).reshape(2, 1, 1, 2 * mine)
    my_slots = lax.dynamic_slice(
        jnp.stack([ffn_to, back_place, attn_back_place]), (0, my_seq, my_fsdp, 0), (3, 1, 1, mine)
    ).reshape(3, mine)
    seq_slots = lax.dynamic_slice(
        jnp.stack(
            [
                ffn_key,
                ffn_rank,
                ffn_chip,
                out_place,
                chip_rank,
                jnp.broadcast_to(slot_chip, owners.shape),
            ]
        ),
        (0, my_seq, 0, 0),
        (6, 1, fsdp_size, mine),
    ).reshape(6, fsdp_size * mine)
    column_slots = lax.dynamic_slice(
        jnp.stack([attn_key, attn_order, attn_rank, jnp.broadcast_to(slot_seq, owners.shape)]),
        (0, 0, 2 * my_chip, 0),
        (4, seq_size, 2, mine),
    ).reshape(4, 2 * seq_size * mine)
    my_key = 2 * my_seq + my_core

    attn_message = attn_room + row_blocks * rows // tile + small_rows + -(-own_gains.shape[0] // tile**2)
    attn_pack = pick(
        (chip_slots[0] == (2 * (my_seq ^ flips) + my_core)[:, None, None])
        & (chip_slots[1] == jnp.arange(attn_room)[None, :, None]),
        both_slots,
    )
    attn_keep = pick(
        (column_slots[0][None, :] == my_key)
        & (column_slots[1][None, :] == jnp.arange(attn_hold)[:, None]),
        jnp.where(
            column_slots[3] == my_seq,
            0,
            attn_room + ((column_slots[3] ^ my_seq) - 1) * attn_message,
        )
        + column_slots[2],
    )
    attn_join = pick(
        (attn_to.reshape(1, -1) == my_seq)
        & (attn_place.reshape(1, -1) == jnp.arange(attn_count)[:, None]),
        (
            jnp.where(attn_core == my_core, 0, chips * attn_hold)
            + (my_chip - slot_chip) % chips * attn_hold
            + attn_order
        ).reshape(1, -1),
    )
    def ffn_tables(kind, hold, count):
        key = 2 * my_fsdp + kind
        keep = pick(
            (seq_slots[0][None, :] == key) & (seq_slots[1][None, :] == jnp.arange(hold)[:, None]),
            seq_slots[3][None, :],
        )
        join = pick(
            (ffn_key.reshape(1, -1) == key)
            & (ffn_place.reshape(1, -1) == jnp.arange(count)[:, None]),
            (slot_seq * hold + ffn_rank).reshape(1, -1),
        )
        cut = pick(
            (ffn_key.reshape(seq_size, 1, -1) == key)
            & (ffn_rank.reshape(seq_size, 1, -1) == jnp.arange(hold)[None, :, None]),
            ffn_place.reshape(seq_size, 1, -1),
        )
        return (keep, join, cut)

    both_keep, both_join, both_cut = ffn_tables(0, both_hold, both_count)
    down_keep, down_join, down_cut = ffn_tables(1, down_hold, ffn_count - both_count)
    ffn_back = pick(
        (seq_slots[5][None, None, :] == ((my_chip + shifts) % chips)[:, None, None])
        & (seq_slots[2][None, None, :] == my_chip)
        & (seq_slots[4][None, None, :] == (my_core * ffn_room + jnp.arange(ffn_room))[None, :, None]),
        jnp.where(seq_slots[0] % 2 == 1, 2 * both_hold, 0)
        + jnp.where(
            seq_slots[0] // 2 == my_fsdp, 0, jnp.where(seq_slots[0] % 2 == 1, down_hold, both_hold)
        )
        + seq_slots[1],
    )

    attn_sent = gather_tiles(masters, attn_pack.reshape(-1))
    attn_sent = attn_sent.reshape(seq_size, attn_room, tile, tile)
    token_tiles = own_tokens.reshape(rows, row_blocks, tile).transpose(1, 0, 2)
    token_tiles = token_tiles.reshape(-1, tile, tile)
    gain_rows = own_gains.reshape(-1, tile)
    gain_tiles = jnp.pad(gain_rows, ((0, -gain_rows.shape[0] % tile), (0, 0))).reshape(-1, tile, tile)
    common = jnp.concatenate([token_tiles, small_half, gain_tiles])
    attn_got = [attn_sent[0]] + [
        seq_swap(jnp.concatenate([attn_sent[flip], common]), flip) for flip in range(1, seq_size)
    ]
    segment, position = documents(doc_lengths[0], length)
    places = ((my_seq ^ flips)[:, None] * rows + jnp.arange(rows)[None, :]).reshape(-1)

    def reorder(values):
        blocks = values.reshape(seq_size, rows)
        return jnp.concatenate(
            [lax.dynamic_index_in_dim(blocks, my_seq ^ i, 0, False) for i in range(seq_size)]
        )

    pack_segment = reorder(segment)
    allow = (pack_segment[:, None] == pack_segment[None, :]) & (
        places[None, :] <= places[:, None]
    )
    turns = jnp.arange(HEAD_DIM // 2).astype(f32)
    angle = reorder(position).astype(f32)[:, None] * (THETA ** (-2.0 * turns / HEAD_DIM))[None, :]
    cosine, sine = jnp.cos(angle)[:, None, :], jnp.sin(angle)[:, None, :]
    ready = (allow, cosine, sine, attn_join, both_join)
    ffn_got, attn_got, common, ready = lax.optimization_barrier((ffn_got, attn_got, common, ready))
    allow, cosine, sine, attn_join, both_join = ready
    parts = [common] + [value[attn_room:] for value in attn_got[1:]]
    token_end = token_tiles.shape[0]
    small_end = token_end + small_rows

    def seq_order(value):
        return value[my_seq ^ flips]

    pack_tokens = jnp.concatenate(
        [
            part[:token_end].reshape(row_blocks, rows, tile).transpose(1, 0, 2).reshape(rows, width)
            for part in parts
        ]
    )
    gain_full = seq_order(
        jnp.stack([part[small_end:].reshape(-1, tile)[: gain_rows.shape[0]] for part in parts])
    )
    gain_full = gain_full.reshape(-1).astype(f32)
    gain_in = gain_full[0:width]
    small_got = core_pair(seq_order(jnp.stack([part[token_end:small_end] for part in parts])))
    small_got = small_got.transpose(1, 0, 2, 3, 4)
    small_table = assemble(small_got.reshape((-1,) + small_master.shape[1:]), row_blocks)
    pack_normed = rms_norm(pack_tokens.astype(f32), gain_in).astype(bf16)
    attn_kept = gather_tiles(attn_got, attn_keep)
    ffn_got = ffn_got + [core_swap(value) for value in ffn_got]
    both_kept, down_kept = gather_tiles(ffn_got, both_keep), gather_tiles(ffn_got, down_keep)
    both_kept, down_kept, attn_kept = lax.optimization_barrier((both_kept, down_kept, attn_kept))
    both_all = lax.all_gather(both_kept, "seq", axis=0, tiled=True)
    down_all = lax.all_gather(down_kept, "seq", axis=0, tiled=True)
    attn_all = [attn_kept] + [chip_shift(attn_kept, offset) for offset in range(1, chips)]
    attn_all = attn_all + [core_swap(value) for value in attn_all]

    attn_all, both_all, pack_normed, gain_full = lax.optimization_barrier(
        (attn_all, both_all, pack_normed, gain_full)
    )
    gain_in = gain_full[0:width]

    def fetch(arrays, index, to, me, place, columns_of):
        def fast():
            return join_tiles(arrays, index, row_blocks, columns_of)

        def slow():
            whole = lax.all_gather(master_low, ("seq", "fsdp"), axis=0, tiled=True)
            count = row_blocks * sum(columns_of)
            slots = pick(
                (to.reshape(1, -1) == me) & (place.reshape(1, -1) == jnp.arange(count)[:, None]),
                jnp.arange(tiles)[None, :],
            )
            return join_tiles([whole], slots, row_blocks, columns_of)

        return lax.cond(fits, fast, slow)

    w_first, w_out = fetch(
        attn_all, attn_join, attn_to, my_seq, attn_place, (attn_first, query_each)
    )
    gain_attn = gain_full[width : 2 * width]
    gain_laurel = gain_full[2 * width : 3 * width]
    gain_pre = gain_full[3 * width : 4 * width]
    gain_post = gain_full[4 * width : 5 * width]
    gain_vec = gain_full[5 * width : 6 * width]
    gain_query = gain_full[6 * width : 6 * width + HEAD_DIM]
    gain_key = gain_full[6 * width + HEAD_DIM : 6 * width + 2 * HEAD_DIM]
    stream = own_tokens.astype(f32)
    vectors = layer_vectors[0].astype(f32)
    normed, normed_pull = jax.vjp(rms_norm, stream, gain_in)
    normed_low = normed.astype(bf16)
    first_pre = matmul(pack_normed, w_first)
    is_key = my_seq % per_key == 0

    def shape_query(query_in, query_gain):
        value = rms_norm(query_in.reshape(length, per_device, HEAD_DIM), query_gain)
        return turn(value, cosine, sine)

    def shape_key(key_in, key_gain):
        return turn(rms_norm(key_in.reshape(length, 1, HEAD_DIM), key_gain), cosine, sine)

    query_pre = first_pre[:, : per_device * HEAD_DIM]
    other_pre = first_pre[:, per_device * HEAD_DIM :]
    query_rot, query_pull = jax.vjp(shape_query, query_pre, gain_query)
    key_rot, key_pull = jax.vjp(shape_key, other_pre, gain_key)
    query_heads = query_rot.astype(bf16)
    other_low = jnp.where(is_key, key_rot[:, 0, :], other_pre).astype(bf16)
    partner_low = seq_swap(other_low, 1).reshape(seq_size // 2, 2, rows, HEAD_DIM)
    partner_low = partner_low[:, ::-1].reshape(length, HEAD_DIM)
    key_single = jnp.where(is_key, other_low, partner_low)
    value_single = jnp.where(is_key, partner_low, other_low)

    raw = (
        jnp.einsum("qhd,kd->qhk", query_heads, key_single, preferred_element_type=f32) * SCALE
    )
    scores = jnp.where(allow[:, None, :], raw, NEGATIVE)
    powers = jnp.exp(scores - jnp.max(scores, axis=-1, keepdims=True))
    prob = powers / jnp.sum(powers, axis=-1, keepdims=True)
    prob_low = prob.astype(bf16)
    attended_low = (
        jnp.einsum("qhk,kd->qhd", prob_low, value_single, preferred_element_type=f32)
        .astype(bf16)
        .reshape(length, per_device * HEAD_DIM)
    )
    (w_both,) = fetch([both_all], both_join, ffn_key, 2 * my_fsdp, ffn_place, (ffn_first,))
    attn_pre = seq_sum(matmul_flip(attended_low, w_out), bf16)
    attn_pre, w_both, small_table = lax.optimization_barrier((attn_pre, w_both, small_table))
    laurel_left = small_table[:, :RANK]
    laurel_right = small_table[:, RANK : 2 * RANK]
    vector_gate_w = small_table[:, 2 * RANK : 2 * RANK + PLD]
    vector_proj_w = small_table[:, 2 * RANK + PLD :]

    attn_normed, attn_pull = jax.vjp(rms_norm, attn_pre, gain_attn)
    first_sum = stream + attn_normed
    left_pre = matmul(normed_low, laurel_left)
    left_low = left_pre.astype(bf16)
    right_pre = matmul_flip(left_low, laurel_right)
    laurel_normed, laurel_pull = jax.vjp(rms_norm, right_pre, gain_laurel)
    second_sum = (first_sum + normed + laurel_normed) * ROOT_HALF
    feed_normed, feed_pull = jax.vjp(rms_norm, second_sum, gain_pre)
    feed_own = feed_normed.astype(bf16)
    down_all, _ = lax.optimization_barrier((down_all, feed_own))
    feed_low = lax.all_gather(feed_own, "fsdp", axis=0, tiled=True)
    (w_down,) = fetch([down_all], down_join, ffn_key, 2 * my_fsdp + 1, ffn_place, (ffn_each,))
    both_pre = matmul(feed_low, w_both)
    ffn_width = w_down.shape[1]
    hidden, hidden_pull = jax.vjp(gelu_product, both_pre[:, :ffn_width], both_pre[:, ffn_width:])
    hidden_low = hidden.astype(bf16)
    down_pre = lax.psum_scatter(
        matmul_flip(hidden_low, w_down).astype(bf16), "fsdp", scatter_dimension=0, tiled=True
    ).astype(f32)
    down_normed, down_pull = jax.vjp(rms_norm, down_pre, gain_post)
    third_sum = second_sum + down_normed
    third_low = third_sum.astype(bf16)
    vector_pre = matmul(third_low, vector_gate_w)
    vector_gated, vector_pull = jax.vjp(lambda inner: gelu_product(inner, vectors), vector_pre)
    vector_low = vector_gated.astype(bf16)
    proj_pre = matmul_flip(vector_low, vector_proj_w)
    proj_normed, proj_pull = jax.vjp(rms_norm, proj_pre, gain_vec)
    result = third_sum + proj_normed
    output = result.astype(bf16)[None]

    grad_out = cotangent[0].astype(f32)
    grad_proj, grad_gain_vec = proj_pull(grad_out)
    proj_grad_low = grad_proj.astype(bf16)
    (grad_vector_pre,) = vector_pull(matmul(proj_grad_low, vector_proj_w))
    vector_grad_low = grad_vector_pre.astype(bf16)
    grad_third = grad_out + matmul_flip(vector_grad_low, vector_gate_w)
    grad_down, grad_gain_post = down_pull(grad_third)
    down_grad_low = lax.all_gather(grad_down.astype(bf16), "fsdp", axis=0, tiled=True)
    grad_gate, grad_up = hidden_pull(matmul(down_grad_low, w_down))
    both_grad_low = jnp.concatenate([grad_gate, grad_up], axis=1).astype(bf16)

    def cut_parts(flips_of, half):
        half_now = down_hold // 2
        index = down_cut[my_seq ^ jnp.array(flips_of), half * half_now : (half + 1) * half_now]
        return cut_tiles([down_grad_w], index.reshape(-1), tile)

    early_full = jnp.concatenate(
        [matmul_outer(third_low, vector_grad_low), matmul_outer(proj_grad_low, vector_low)], axis=1
    )
    small_early = small_sum(split_tiles(early_full, tile).reshape(-1, tile))
    down_grad_w = matmul_outer(down_grad_low, hidden_low).astype(bf16)
    down_cuts = cut_parts([1, 3], 0), cut_parts([2, 3], 1)
    both_grad_low, down_cuts, small_early = lax.optimization_barrier(
        (both_grad_low, down_cuts, small_early)
    )
    grad_feed = lax.psum_scatter(
        matmul_flip(both_grad_low, w_both).astype(bf16), "fsdp", scatter_dimension=0, tiled=True
    ).astype(f32)
    down_one = added(cut_parts([0, 2], 0), seq_swap(down_cuts[0], 1))
    down_two = added(cut_parts([0, 1], 1), seq_swap(down_cuts[1], 2))
    both_grad_w = matmul_outer(feed_low, both_grad_low).astype(bf16)
    both_parts = cut_tiles([both_grad_w], both_cut.reshape(-1), tile)
    both_parts, down_one, down_two, grad_feed = lax.optimization_barrier(
        (both_parts, down_one, down_two, grad_feed)
    )
    both_sum = lax.psum_scatter(both_parts, "seq", scatter_dimension=0, tiled=True)
    down_half = down_one.shape[0] // 2
    down_one = added(down_one[:down_half], seq_swap(down_one[down_half:].astype(bf16), 2))
    down_two = added(down_two[:down_half], seq_swap(down_two[down_half:].astype(bf16), 1))
    down_sum = jnp.concatenate([down_one, down_two]).astype(bf16)

    grad_second_norm, grad_gain_pre = feed_pull(grad_feed)
    half_grad = (grad_third + grad_second_norm) * ROOT_HALF
    grad_right, grad_gain_laurel = laurel_pull(half_grad)
    right_grad_low = grad_right.astype(bf16)
    left_grad_low = matmul(right_grad_low, laurel_right).astype(bf16)
    grad_attn, grad_gain_attn = attn_pull(half_grad)
    attn_grad_low = seq_gather(grad_attn.astype(bf16))
    grad_attended = (
        matmul(attn_grad_low, w_out).astype(bf16).reshape(length, per_device, HEAD_DIM)
    )
    out_grad_w = matmul_outer(attn_grad_low, attended_low).astype(bf16)
    value_grad = jnp.einsum("qhk,qhd->kd", prob_low, grad_attended, preferred_element_type=f32)
    grad_prob = jnp.einsum("qhd,kd->qhk", grad_attended, value_single, preferred_element_type=f32)
    inner = jnp.sum(prob * grad_prob, axis=-1, keepdims=True)
    grad_score = (prob * (grad_prob - inner)).astype(bf16)
    grad_query = (
        jnp.einsum("qhk,kd->qhd", grad_score, key_single, preferred_element_type=f32) * SCALE
    ).astype(bf16)
    key_grad = (
        jnp.einsum("qhk,qhd->kd", grad_score, query_heads, preferred_element_type=f32) * SCALE
    ).astype(bf16)
    value_grad = value_grad.astype(bf16)
    partner_grad = seq_swap(jnp.where(is_key, value_grad, key_grad), 1)
    partner_grad = partner_grad.reshape(seq_size // 2, 2, rows, HEAD_DIM)[:, ::-1]
    other_grad = jnp.where(is_key, key_grad, value_grad).astype(f32) + partner_grad.reshape(
        length, HEAD_DIM
    ).astype(f32)
    grad_query_pre, grad_gain_query = query_pull(grad_query.astype(f32))
    grad_key_pre, grad_gain_key = key_pull(other_grad[:, None, :])
    grad_gain_key = jnp.where(is_key, grad_gain_key, 0.0)
    first_grad_low = jnp.concatenate(
        [grad_query_pre, jnp.where(is_key, grad_key_pre, other_grad)], axis=1
    ).astype(bf16)
    first_grad_w = matmul_outer(pack_normed, first_grad_low).astype(bf16)
    near = (my_chip + shifts) % chips
    near_key = attn_key_chip[near][:, None, :]
    near_order = attn_order_chip[near][:, None, :]
    near_place = by_chip(attn_place)[near][:, None, :]

    def attn_cut(core):
        index = pick(
            (near_key == 2 * my_seq + core)
            & (near_order == jnp.arange(attn_hold)[None, :, None]),
            near_place,
        )
        return cut_tiles([first_grad_w, out_grad_w], index.reshape(-1), tile)

    attn_given, attn_own = attn_cut(1 - my_core), attn_cut(my_core)
    attn_parts = added(attn_own, core_swap(attn_given)).reshape(chips, attn_hold, tile, tile)
    attn_sum = attn_parts[0]
    attn_parts = [attn_parts[offset].astype(bf16) for offset in range(1, chips)]
    normed_sum = seq_sum(matmul_flip(first_grad_low, w_first), bf16)
    attn_sum, attn_parts, normed_sum = lax.optimization_barrier((attn_sum, attn_parts, normed_sum))
    for offset in range(1, chips):
        attn_sum = attn_sum + chip_shift(attn_parts[offset - 1], offset).astype(f32)
    attn_sum = attn_sum.astype(bf16)
    attn_back = pick(
        (column_slots[3][None, None, :] == (my_seq ^ flips)[:, None, None])
        & (column_slots[0][None, None, :] == my_key)
        & (column_slots[2][None, None, :] == jnp.arange(attn_room)[None, :, None]),
        column_slots[1],
    )

    grad_normed = half_grad + matmul_flip(left_grad_low, laurel_left) + normed_sum
    grad_stream_norm, grad_gain_in = normed_pull(grad_normed)
    input_grad = (half_grad + grad_stream_norm)[None]
    gain_grad = jnp.concatenate(
        [
            grad_gain_in,
            grad_gain_attn,
            grad_gain_laurel,
            grad_gain_pre,
            grad_gain_post,
            grad_gain_vec,
            grad_gain_query,
            grad_gain_key,
        ]
    )
    late_full = jnp.concatenate(
        [matmul_outer(normed_low, left_grad_low), matmul_outer(right_grad_low, left_low)], axis=1
    )
    late = jnp.concatenate(
        [late_full.reshape(seq_size, -1), gain_grad.reshape(seq_size, -1)], axis=1
    ).reshape(seq_size, -1, tile)
    late = seq_sum(late.reshape(-1, tile), bf16, True)

    ffn_sums = [both_sum, core_swap(both_sum), down_sum, core_swap(down_sum)]
    ffn_return = [gather_tiles(ffn_sums, ffn_back[i]) for i in range(chips)]
    ffn_return, attn_sum, late, input_grad = lax.optimization_barrier(
        (ffn_return, attn_sum, late, input_grad)
    )
    ffn_returned = chip_exchange(ffn_return)
    ffn_returned = ffn_returned + [core_swap(value) for value in ffn_returned]
    late = late + core_swap(late.astype(bf16)).astype(f32)
    late_low = late.astype(bf16)
    for offset in range(1, chips):
        late = late + chip_shift(late_low, offset).astype(f32)
    late_rows = late_full.shape[0] // seq_size
    late_tiles = late[:late_rows].reshape(-1, 1, tile, tile)
    gain_grad_mine = late[late_rows:].reshape(-1)
    small_grad = jnp.concatenate(
        [
            late_tiles.astype(bf16),
            small_early.reshape(late_tiles.shape[0], -1, tile, tile),
        ],
        axis=1,
    ).reshape(small_master.shape)
    attn_returned = seq_exchange([gather_tiles([attn_sum], attn_back[i]) for i in range(seq_size)])
    attn_returned = attn_returned + [core_swap(value) for value in attn_returned]
    slot_grad = jnp.where(my_slots[0] >= 0, my_slots[1], 2 * half + my_slots[2])

    def slow_return(_, kept):
        own_ffn = split_tiles(both_grad_w, tile), split_tiles(down_grad_w, tile)
        own_attn = split_tiles(first_grad_w, tile), split_tiles(out_grad_w, tile)
        parts = jnp.concatenate(own_ffn + own_attn + (jnp.zeros((1, tile, tile), bf16),))
        index = jnp.where(
            ffn_to == my_fsdp,
            is_down * both_count + ffn_place,
            jnp.where(attn_to == my_seq, ffn_count + attn_place, ffn_count + attn_count),
        )
        spread = gather_tiles([parts], index.reshape(-1))
        return lax.psum_scatter(spread, ("seq", "fsdp"), scatter_dimension=0, tiled=True)

    tile_grads = ffn_returned + attn_returned
    slow_start = 2 * half + 2 * seq_size * attn_room
    slow_steps = jnp.where(fits, 0, 1)
    slow_grads = lax.fori_loop(0, slow_steps, slow_return, jnp.zeros((mine, tile, tile), bf16))
    tile_grads = tile_grads + [slow_grads]
    slot_grad = jnp.where(fits, slot_grad, slow_start + local_slots)

    tile_new, tile_first_new, tile_second_new = rotate_update(
        tile_grads, slot_grad, tile_master, tile_first, tile_second, left_basis, right_basis, RATE_TILE
    )
    small_new, small_first_new, small_second_new = rotate_update(
        [small_grad],
        jnp.arange(small_master.shape[0]),
        small_master,
        small_first,
        small_second,
        small_left,
        small_right,
        RATE_SMALL,
    )
    gain_first_new = BETA_ONE * gain_first + (1.0 - BETA_ONE) * gain_grad_mine
    gain_second_new = BETA_TWO * gain_second + (1.0 - BETA_TWO) * gain_grad_mine * gain_grad_mine
    correct_one = 1.0 - BETA_ONE**STEP
    correct_two = 1.0 - BETA_TWO**STEP
    gain_new = gains - RATE_GAIN * (gain_first_new / correct_one) / (
        jnp.sqrt(gain_second_new / correct_two) + ADAM_EPS
    )
    return (
        output,
        input_grad,
        tile_new,
        tile_first_new,
        tile_second_new,
        small_new,
        small_first_new,
        small_second_new,
        gain_new,
        gain_first_new,
        gain_second_new,
    )


def solution(mesh):
    return jax.shard_map(
        on_device,
        mesh=mesh,
        in_specs=(
            P("fsdp", "seq", None),
            P("fsdp", "seq", None),
            P("fsdp", None),
            P("fsdp", "seq", None),
            P(),
            P(("seq", "fsdp"), None, None),
            P(("seq", "fsdp"), None, None),
            P(("seq", "fsdp"), None, None),
            P(("seq", "fsdp"), None, None),
            P(("seq", "fsdp"), None, None),
            P("seq", None, None),
            P("seq", None, None),
            P("seq", None, None),
            P("seq", None, None),
            P("seq", None, None),
            P("seq"),
            P("seq"),
            P("seq"),
        ),
        out_specs=(
            P("fsdp", "seq", None),
            P("fsdp", "seq", None),
            P(("seq", "fsdp"), None, None),
            P(("seq", "fsdp"), None, None),
            P(("seq", "fsdp"), None, None),
            P("seq", None, None),
            P("seq", None, None),
            P("seq", None, None),
            P("seq"),
            P("seq"),
            P("seq"),
        ),
        check_vma=False,
    )
```

```python
import math

import jax
import jax.numpy as jnp
from jax import lax
from jax.experimental import pallas as pl
from jax.experimental.pallas import tpu as pltpu
from jax.sharding import PartitionSpec as P

HEADS = 8
KV_HEADS = 2
HEAD_DIM = 256
FF = 8192
RANK = 64
PLD = 256
STEP = 5


EPS = 1e-06
SCALE = 0.0625
THETA = 1000000.0
ROOT_HALF = 0.7071067811865476
BETA_ONE = 0.5
BETA_TWO = 0.5
ADAM_EPS = 1e-08
RATE_TILE = 0.02
RATE_SMALL = 0.04
RATE_GAIN = 0.3
DECAY = 0.01
NEGATIVE = -1e30
VMEM_BYTES = 32 * 1024 * 1024


def rms_norm(value, gain):
    return value * lax.rsqrt(jnp.mean(value * value, axis=-1, keepdims=True) + EPS) * gain


def rotary(value, position):
    half = value.shape[-1] // 2
    freq = THETA ** (-2.0 * jnp.arange(half).astype(jnp.float32) / value.shape[-1])
    angle = position.astype(jnp.float32)[:, None] * freq[None, :]
    cosine = jnp.cos(angle)[:, None, :]
    sine = jnp.sin(angle)[:, None, :]
    first = value[..., :half]
    second = value[..., half:]
    return jnp.concatenate(
        [first * cosine - second * sine, second * cosine + first * sine], axis=-1
    )


def documents(lengths, length):
    places = jnp.arange(length)
    ends = jnp.cumsum(lengths)
    passed = places[:, None] >= ends[None, :]
    segment = jnp.sum(passed.astype(jnp.int32), axis=1)
    before = jnp.sum(jnp.where(passed, lengths[None, :], 0), axis=1)
    return (segment, places - before)


def matmul(left, right):
    return jnp.dot(left, right, preferred_element_type=jnp.float32)


def matmul_flip(left, right):
    return lax.dot_general(
        left, right, (((1,), (1,)), ((), ())), preferred_element_type=jnp.float32
    )


def matmul_outer(left, right):
    return lax.dot_general(
        left, right, (((0,), (0,)), ((), ())), preferred_element_type=jnp.float32
    )


def assemble(tiles, row_blocks):
    size = tiles.shape[1]
    column_blocks = tiles.shape[0] // row_blocks
    return (
        tiles.reshape(row_blocks, column_blocks, size, size)
        .transpose(0, 2, 1, 3)
        .reshape(row_blocks * size, column_blocks * size)
    )


def split_tiles(matrix, size):
    row_blocks = matrix.shape[0] // size
    column_blocks = matrix.shape[1] // size
    return (
        matrix.reshape(row_blocks, size, column_blocks, size)
        .transpose(0, 2, 1, 3)
        .reshape(row_blocks * column_blocks, size, size)
    )


def gelu_product(first, second):
    return jax.nn.gelu(first, approximate=True) * second


def room(count, share):
    mean = count * share
    return math.ceil(mean + 3.6 * math.sqrt(mean * (1.0 - share)) + 3.0)


def count_earlier(group, valid):
    size = group.shape[-1]
    order = jnp.arange(size)
    same = (group[..., :, None] == group[..., None, :]) & valid[..., None, :]
    same = same & (order[None, :] < order[:, None])
    return jnp.sum(same.astype(jnp.int32), axis=-1)


def pick(match, value):
    return jnp.sum(jnp.where(match, value, 0), axis=-1)


def steps_of(count):
    for steps in range(4, 65):
        if count % steps == 0 and 16 <= count // steps <= 160:
            return steps
    return 2 if count % 2 == 0 else 1


def tile_kernel_call(kernel, index, arrays, out_shape, out_specs, steps):
    moved = sum(math.prod(one.shape) * 2 for one in jax.tree.leaves(out_shape))
    return pl.pallas_call(
        kernel,
        grid=(steps,),
        cost_estimate=pl.CostEstimate(flops=0, transcendentals=0, bytes_accessed=2 * moved),
        out_shape=out_shape,
        in_specs=[pl.BlockSpec(memory_space=pltpu.SMEM)]
        + [pl.BlockSpec(memory_space=pl.ANY)] * len(arrays),
        out_specs=out_specs,
        scratch_shapes=[pltpu.SemaphoreType.DMA],
        compiler_params=pltpu.CompilerParams(vmem_limit_bytes=VMEM_BYTES),
    )(index, *arrays)


def start_copy(sources, place, target, sem):
    start = 0
    for ref in sources:
        size = ref.shape[0]

        @pl.when((place >= start) & (place < start + size))
        def _(ref=ref, start=start):
            pltpu.make_async_copy(ref.at[place - start], target, sem).start()

        start = start + size


def gather_tiles(arrays, index):
    tile = arrays[0].shape[-1]
    count = index.shape[0]
    steps = steps_of(count)
    each = count // steps

    def kernel(index_ref, *refs):
        sources, out, sem = refs[:-2], refs[-2], refs[-1]
        base = pl.program_id(0) * each

        def step(i, carry):
            start_copy(sources, index_ref[base + i], out.at[i], sem)
            return carry

        lax.fori_loop(0, each, step, 0)
        pltpu.make_async_copy(out, out, sem).wait()

    total = sum(array.shape[0] for array in arrays)
    return tile_kernel_call(
        kernel,
        jnp.clip(index, 0, total - 1),
        arrays,
        jax.ShapeDtypeStruct((count, tile, tile), arrays[0].dtype),
        pl.BlockSpec((each, tile, tile), lambda i: (i, 0, 0)),
        steps,
    )


def join_tiles(arrays, index, row_blocks, columns):
    tile = arrays[0].shape[-1]
    steps = 4
    each = row_blocks // steps

    def kernel(index_ref, *refs):
        sources, outs, sem = refs[: len(arrays)], refs[len(arrays) : -1], refs[-1]
        base = pl.program_id(0) * each
        start = 0
        for out, width in zip(outs, columns):

            def step(i, carry, out=out, start=start, width=width):
                row = i // width
                column = i - row * width
                target = out.at[
                    pl.ds(pl.multiple_of(row * tile, tile), tile),
                    pl.ds(pl.multiple_of(column * tile, tile), tile),
                ]
                start_copy(sources, index_ref[start + base * width + i], target, sem)
                return carry

            lax.fori_loop(0, each * width, step, 0)
            start = start + row_blocks * width
        for out in outs:
            pltpu.make_async_copy(out, out, sem).wait()

    total = sum(array.shape[0] for array in arrays)
    out_shape = tuple(
        jax.ShapeDtypeStruct((row_blocks * tile, width * tile), arrays[0].dtype)
        for width in columns
    )
    out_specs = tuple(pl.BlockSpec((each * tile, width * tile), lambda i: (i, 0)) for width in columns)
    return tile_kernel_call(
        kernel, jnp.clip(index, 0, total - 1), arrays, out_shape, out_specs, steps
    )


def cut_tiles(matrices, index, tile):
    row_blocks = matrices[0].shape[0] // tile
    widths = [matrix.shape[1] // tile for matrix in matrices]
    count = index.shape[0]
    steps = steps_of(count)
    each = count // steps

    def kernel(index_ref, *refs):
        sources, out, sem = refs[:-2], refs[-2], refs[-1]
        base = pl.program_id(0) * each

        def step(i, carry):
            place = index_ref[base + i]
            start = 0
            for ref, width in zip(sources, widths):
                size = row_blocks * width

                @pl.when((place >= start) & (place < start + size))
                def _(ref=ref, start=start, width=width):
                    row = (place - start) // width
                    column = place - start - row * width
                    source = ref.at[
                        pl.ds(pl.multiple_of(row * tile, tile), tile),
                        pl.ds(pl.multiple_of(column * tile, tile), tile),
                    ]
                    pltpu.make_async_copy(source, out.at[i], sem).start()

                start = start + size
            return carry

        lax.fori_loop(0, each, step, 0)
        pltpu.make_async_copy(out, out, sem).wait()

    return tile_kernel_call(
        kernel,
        jnp.clip(index, 0, row_blocks * sum(widths) - 1),
        matrices,
        jax.ShapeDtypeStruct((count, tile, tile), matrices[0].dtype),
        pl.BlockSpec((each, tile, tile), lambda i: (i, 0, 0)),
        steps,
    )


def split_low(value):
    high = value.astype(jnp.bfloat16)
    return high, (value - high.astype(jnp.float32)).astype(jnp.bfloat16)


def rotate_update(grads, index, master, first, second, left, right, rate):
    count, tile, _ = master.shape
    each = 4 if count % 4 == 0 else 1
    correct_one = 1.0 - BETA_ONE**STEP
    correct_two = 1.0 - BETA_TWO**STEP

    def product(one, two, dims):
        return lax.dot_general(one, two, (dims, ((), ())), preferred_element_type=jnp.float32)

    def kernel(index_ref, *refs):
        sources, refs = refs[: len(grads)], refs[len(grads) :]
        master_ref, first_ref, second_ref, left_ref, right_ref = refs[:5]
        master_out, first_out, second_out, held, sems = refs[5:]
        now = pl.program_id(0)

        @pl.when(now == 0)
        def _():
            def step(i, carry):
                start_copy(sources, index_ref[i], held.at[i], sems.at[i // each])
                return carry

            lax.fori_loop(0, count, step, 0)

        block = held.at[pl.ds(now * each, each)]
        pltpu.make_async_copy(block, block, sems.at[now]).wait()
        lefts, rights, turns = [], [], []
        for i in range(each):
            grad = held[now * each + i]
            lefts.append(split_low(left_ref[i]))
            rights.append(split_low(right_ref[i]))
            half_turned = product(
                jnp.concatenate([grad, grad], axis=1),
                jnp.concatenate(rights[i], axis=0),
                ((1,), (0,)),
            )
            turns.append(split_low(half_turned))
        for i in range(each):
            (left_high, left_low), (high, low) = lefts[i], turns[i]
            turns[i] = product(
                jnp.concatenate([left_high, left_high, left_low], axis=0),
                jnp.concatenate([high, low, high], axis=0),
                ((0,), (0,)),
            )
        for i in range(each):
            right_high, right_low = rights[i]
            first_new = BETA_ONE * first_ref[i] + (1.0 - BETA_ONE) * turns[i]
            second_new = BETA_TWO * second_ref[i] + (1.0 - BETA_TWO) * turns[i] * turns[i]
            first_out[i] = first_new
            second_out[i] = second_new
            high, low = split_low(
                first_new / correct_one / (jnp.sqrt(second_new / correct_two) + ADAM_EPS)
            )
            half_back = product(
                jnp.concatenate([high, low, high], axis=1),
                jnp.concatenate([right_high, right_high, right_low], axis=1),
                ((1,), (1,)),
            )
            turns[i] = split_low(half_back)
        for i in range(each):
            (left_high, left_low), (high, low) = lefts[i], turns[i]
            back = product(
                jnp.concatenate([left_high, left_high, left_low], axis=1),
                jnp.concatenate([high, low, high], axis=0),
                ((1,), (0,)),
            )
            weight = master_ref[i]
            master_out[i] = weight - rate * (back + DECAY * weight)

    spec = pl.BlockSpec((each, tile, tile), lambda i: (i, 0, 0))
    shape = jax.ShapeDtypeStruct(master.shape, jnp.float32)
    total = sum(array.shape[0] for array in grads)
    return pl.pallas_call(
        kernel,
        grid=(count // each,),
        out_shape=(shape, shape, shape),
        in_specs=[pl.BlockSpec(memory_space=pltpu.SMEM)]
        + [pl.BlockSpec(memory_space=pl.ANY)] * len(grads)
        + [spec] * 5,
        out_specs=(spec, spec, spec),
        scratch_shapes=[
            pltpu.VMEM((count, tile, tile), jnp.bfloat16),
            pltpu.SemaphoreType.DMA((count // each,)),
        ],
        compiler_params=pltpu.CompilerParams(vmem_limit_bytes=VMEM_BYTES),
    )(jnp.clip(index, 0, total - 1), *grads, master, first, second, left, right)


def seq_swap(value, flip):
    size = lax.axis_size("seq")
    return lax.ppermute(value, "seq", [(i, i ^ flip) for i in range(size)])


def take_blocks(value, order):
    return jnp.stack(
        [lax.dynamic_index_in_dim(value, order[i], 0, False) for i in range(order.shape[0])]
    )


def core_swap(value):
    size = lax.axis_size("fsdp")
    return lax.ppermute(value, "fsdp", [(i, i ^ 1) for i in range(size)])


def chip_shift(value, offset):
    size = lax.axis_size("fsdp")
    chips = size // 2
    return lax.ppermute(
        value, "fsdp", [(i, (i // 2 + offset) % chips * 2 + i % 2) for i in range(size)]
    )


def seq_gather(value):
    size = lax.axis_size("seq")
    return jnp.concatenate([value] + [seq_swap(value, flip) for flip in range(1, size)], axis=0)


def seq_ordered(value):
    size = lax.axis_size("seq")
    parts = jnp.stack([value] + [seq_swap(value, flip) for flip in range(1, size)], axis=0)
    return take_blocks(parts, lax.axis_index("seq") ^ jnp.arange(size))


def seq_exchange(values):
    return [values[0]] + [seq_swap(values[flip], flip) for flip in range(1, len(values))]


def seq_sum(value, wire, ordered=False):
    size = lax.axis_size("seq")
    parts = value.reshape((size, value.shape[0] // size) + value.shape[1:])
    if ordered:
        parts = take_blocks(parts, lax.axis_index("seq") ^ jnp.arange(size))
    total = parts[0]
    for flip in range(1, size):
        total = total + seq_swap(parts[flip].astype(wire), flip).astype(jnp.float32)
    return total


def chip_exchange(values):
    return [values[0]] + [chip_shift(values[offset], offset) for offset in range(1, len(values))]


def core_pair(value):
    other = core_swap(value)
    even = lax.axis_index("fsdp") % 2 == 0
    return jnp.where(even, jnp.stack([value, other]), jnp.stack([other, value]))


def small_sum(value):
    seq_size = lax.axis_size("seq")
    chips = lax.axis_size("fsdp") // 2
    chip = lax.axis_index("fsdp") // 2
    even = lax.axis_index("fsdp") % 2 == 0
    low = value.astype(jnp.bfloat16)
    parts = low.reshape((seq_size, 2, low.shape[0] // (2 * seq_size)) + low.shape[1:])
    kept = jnp.where(even, parts[:, 0], parts[:, 1]).astype(jnp.float32)
    given = jnp.where(even, parts[:, 1], parts[:, 0])
    kept = kept + core_swap(given).astype(jnp.float32)
    kept = seq_sum(kept.reshape((-1,) + low.shape[1:]), jnp.bfloat16, True)
    kept = kept.reshape((chips, kept.shape[0] // chips) + kept.shape[1:])
    kept = take_blocks(kept, (chip + jnp.arange(chips)) % chips)
    total = kept[0]
    for offset in range(1, chips):
        total = total + chip_shift(kept[offset].astype(jnp.bfloat16), offset).astype(jnp.float32)
    total = total.astype(jnp.bfloat16)
    parts = jnp.stack([total] + [chip_shift(total, offset) for offset in range(1, chips)])
    parts = take_blocks(parts, (chip - jnp.arange(chips)) % chips)
    return core_pair(parts).reshape((value.shape[0] // seq_size,) + value.shape[1:])


def turn(value, cosine, sine):
    half = value.shape[-1] // 2
    first, second = value[..., :half], value[..., half:]
    return jnp.concatenate(
        [first * cosine - second * sine, second * cosine + first * sine], axis=-1
    )


def added(one, two):
    return one.astype(jnp.float32) + two.astype(jnp.float32)


def on_device(
    tokens,
    layer_vectors,
    doc_lengths,
    cotangent,
    tile_owner,
    tile_master,
    tile_first,
    tile_second,
    left_basis,
    right_basis,
    small_master,
    small_first,
    small_second,
    small_left,
    small_right,
    gains,
    gain_first,
    gain_second,
):
    bf16 = jnp.bfloat16
    f32 = jnp.float32
    tile = tile_master.shape[1]
    width = tokens.shape[2]
    row_blocks = width // tile
    rows = tokens.shape[1]
    seq_size = lax.axis_size("seq")
    fsdp_size = lax.axis_size("fsdp")
    chips = fsdp_size // 2
    mine = tile_master.shape[0]
    tiles = tile_owner.shape[0]
    length = rows * seq_size
    per_device = HEADS // seq_size
    per_key = seq_size // KV_HEADS
    query_width = HEADS * HEAD_DIM
    key_width = KV_HEADS * HEAD_DIM
    my_seq = lax.axis_index("seq")
    my_fsdp = lax.axis_index("fsdp")
    my_chip = my_fsdp // 2
    my_core = my_fsdp % 2
    flips = jnp.arange(seq_size)
    shifts = jnp.arange(chips)

    query_blocks = query_width // tile
    key_blocks = key_width // tile
    ffn_blocks = FF // tile
    query_each = query_blocks // seq_size
    head_blocks = HEAD_DIM // tile
    ffn_each = ffn_blocks // fsdp_size
    columns = tiles // row_blocks
    attn_first = query_each + head_blocks
    attn_count = row_blocks * (attn_first + query_each)
    ffn_first = 2 * ffn_each
    ffn_count = row_blocks * 3 * ffn_each
    attn_share = (2 * query_blocks + 2 * key_blocks) / columns
    ffn_share = 3 * ffn_blocks / columns
    attn_room = (room(2 * mine, attn_share / seq_size) + 1) // 2
    attn_hold = (room(attn_count, 1.0 / chips) + 1) // 2 + 1
    ffn_room = (room(2 * mine, ffn_share / chips) + 1) // 2
    both_count = row_blocks * ffn_first
    ffn_hold = (room(ffn_count, 1.0 / seq_size) + 3) // 4 * 4
    ffn_half = ffn_hold // 2

    def tile_places(owner):
        row = owner // columns
        column = owner % columns
        key_at = column - query_blocks
        value_at = key_at - key_blocks
        out_at = value_at - key_blocks
        ffn_at = out_at - query_blocks
        is_attn = ffn_at < 0
        kind = ffn_at // ffn_blocks
        ffn_column = ffn_at % ffn_blocks
        ffn_to = jnp.where(is_attn, -1, ffn_column // ffn_each)
        ffn_local = ffn_column % ffn_each
        ffn_place = jnp.where(
            kind == 2,
            both_count + row * ffn_each + ffn_local,
            row * ffn_first + kind * ffn_each + ffn_local,
        )
        attn_to = jnp.where(
            key_at < 0,
            column // query_each,
            jnp.where(
                value_at < 0,
                key_at // head_blocks * per_key,
                jnp.where(
                    out_at < 0,
                    value_at // head_blocks * per_key + per_key - 1,
                    out_at // query_each,
                ),
            ),
        )
        attn_place = jnp.where(
            key_at < 0,
            row * attn_first + column % query_each,
            jnp.where(
                out_at < 0,
                row * attn_first + query_each + key_at % head_blocks,
                row_blocks * attn_first + row * query_each + out_at % query_each,
            ),
        )
        attn_to = jnp.where(is_attn, attn_to, -1)
        return (ffn_to, ffn_place, attn_to, attn_place)

    owners = tile_owner.reshape(seq_size, fsdp_size, mine)
    slot_seq = jnp.arange(seq_size)[:, None, None]
    slot_fsdp = jnp.arange(fsdp_size)[None, :, None]
    slot_chip = slot_fsdp // 2
    local_slots = jnp.arange(mine)
    both_slots = jnp.arange(2 * mine)
    both_slots = jnp.where(
        both_slots // mine == my_core, both_slots % mine, mine + both_slots % mine
    )

    ffn_to = tile_places(owners)[0]
    ffn_chip = jnp.where(ffn_to < 0, -1, ffn_to // 2)
    chip_view = ffn_chip.reshape(seq_size, chips, 2 * mine)
    chip_rank = count_earlier(chip_view, chip_view >= 0).reshape(owners.shape)
    ffn_slots = lax.dynamic_slice(
        jnp.stack([ffn_chip, chip_rank]), (0, my_seq, 2 * my_chip, 0), (2, 1, 2, mine)
    ).reshape(2, 1, 1, 2 * mine)
    ffn_pack = pick(
        (ffn_slots[0] == ((my_chip + shifts) % chips)[:, None, None])
        & (ffn_slots[1] == (my_core * ffn_room + jnp.arange(ffn_room))[None, :, None]),
        both_slots,
    )
    master_low = tile_master.astype(bf16)
    masters = [master_low, core_swap(master_low)]
    ffn_sent = [gather_tiles(masters, ffn_pack[i]) for i in range(chips)]
    small_rows = small_master.shape[0] // 2
    small_half = lax.dynamic_slice_in_dim(small_master, my_core * small_rows, small_rows)
    masters, ffn_sent, chip_rank, owners, own_tokens, own_gains, small_half = (
        lax.optimization_barrier(
            (
                masters,
                ffn_sent,
                chip_rank,
                owners,
                tokens[0],
                gains.astype(bf16),
                small_half.astype(bf16),
            )
        )
    )
    ffn_got = chip_exchange(ffn_sent)

    ffn_to, ffn_place, attn_to, attn_place = tile_places(owners)
    ffn_chip = jnp.where(ffn_to < 0, -1, ffn_to // 2)
    seq_view = ffn_to.reshape(seq_size, fsdp_size * mine)
    ffn_rank = count_earlier(seq_view, seq_view >= 0).reshape(owners.shape)
    attn_view = attn_to.reshape(seq_size, chips, 2 * mine)
    attn_rank = count_earlier(attn_view, attn_view >= 0).reshape(owners.shape)
    attn_core = (attn_rank + slot_seq) % 2
    attn_rank = attn_rank // 2
    attn_key = jnp.where(attn_to < 0, -1, 2 * attn_to + attn_core)

    def by_chip(value):
        value = value.reshape(seq_size, chips, 2 * mine).transpose(1, 0, 2)
        return value.reshape(chips, seq_size * 2 * mine)

    attn_key_chip = by_chip(attn_key)
    attn_order_chip = count_earlier(attn_key_chip, attn_key_chip >= 0)
    attn_order = (
        attn_order_chip.reshape(chips, seq_size, 2 * mine).transpose(1, 0, 2).reshape(owners.shape)
    )
    fits = jnp.all(
        jnp.where(
            ffn_to < 0,
            (attn_rank < attn_room) & (attn_order < attn_hold),
            (chip_rank < 2 * ffn_room) & (ffn_rank < ffn_hold),
        )
    )
    half = chips * ffn_room
    rank_core = chip_rank // ffn_room
    rank_local = chip_rank % ffn_room
    out_place = (
        jnp.where(rank_core == my_core, 0, half)
        + (my_chip - slot_chip) % chips * ffn_room
        + rank_local
    )
    back_place = (
        jnp.where(rank_core == my_core, 0, half) + (my_chip - ffn_chip) % chips * ffn_room + rank_local
    )
    attn_back_place = (
        jnp.where(attn_core == my_core, 0, seq_size * attn_room)
        + (attn_to ^ my_seq) * attn_room
        + attn_rank
    )
    chip_slots = lax.dynamic_slice(
        jnp.stack([attn_key, attn_rank]), (0, my_seq, 2 * my_chip, 0), (2, 1, 2, mine)
    ).reshape(2, 1, 1, 2 * mine)
    my_slots = lax.dynamic_slice(
        jnp.stack([ffn_to, back_place, attn_back_place]), (0, my_seq, my_fsdp, 0), (3, 1, 1, mine)
    ).reshape(3, mine)
    seq_slots = lax.dynamic_slice(
        jnp.stack(
            [
                ffn_to,
                ffn_rank,
                ffn_chip,
                out_place,
                chip_rank,
                jnp.broadcast_to(slot_chip, owners.shape),
            ]
        ),
        (0, my_seq, 0, 0),
        (6, 1, fsdp_size, mine),
    ).reshape(6, fsdp_size * mine)
    column_slots = lax.dynamic_slice(
        jnp.stack([attn_key, attn_order, attn_rank, jnp.broadcast_to(slot_seq, owners.shape)]),
        (0, 0, 2 * my_chip, 0),
        (4, seq_size, 2, mine),
    ).reshape(4, 2 * seq_size * mine)
    my_key = 2 * my_seq + my_core

    attn_message = attn_room + row_blocks * rows // tile + small_rows + -(-own_gains.shape[0] // tile**2)
    attn_pack = pick(
        (chip_slots[0] == (2 * (my_seq ^ flips) + my_core)[:, None, None])
        & (chip_slots[1] == jnp.arange(attn_room)[None, :, None]),
        both_slots,
    )
    attn_keep = pick(
        (column_slots[0][None, :] == my_key)
        & (column_slots[1][None, :] == jnp.arange(attn_hold)[:, None]),
        jnp.where(
            column_slots[3] == my_seq,
            0,
            attn_room + ((column_slots[3] ^ my_seq) - 1) * attn_message,
        )
        + column_slots[2],
    )
    attn_join = pick(
        (attn_to.reshape(1, -1) == my_seq)
        & (attn_place.reshape(1, -1) == jnp.arange(attn_count)[:, None]),
        (
            jnp.where(attn_core == my_core, 0, chips * attn_hold)
            + (my_chip - slot_chip) % chips * attn_hold
            + attn_order
        ).reshape(1, -1),
    )
    ffn_keep = pick(
        (seq_slots[0][None, :] == my_fsdp) & (seq_slots[1][None, :] == jnp.arange(ffn_hold)[:, None]),
        seq_slots[3][None, :],
    )
    ffn_join = pick(
        (ffn_to.reshape(1, -1) == my_fsdp)
        & (ffn_place.reshape(1, -1) == jnp.arange(ffn_count)[:, None]),
        (
            ffn_rank // ffn_half * (seq_size * ffn_half) + slot_seq * ffn_half + ffn_rank % ffn_half
        ).reshape(1, -1),
    )
    ffn_cut = pick(
        (ffn_to.reshape(seq_size, 1, -1) == my_fsdp)
        & (ffn_rank.reshape(seq_size, 1, -1) == jnp.arange(ffn_hold)[None, :, None]),
        ffn_place.reshape(seq_size, 1, -1),
    )
    ffn_back = pick(
        (seq_slots[5][None, None, :] == ((my_chip + shifts) % chips)[:, None, None])
        & (seq_slots[2][None, None, :] == my_chip)
        & (seq_slots[4][None, None, :] == (my_core * ffn_room + jnp.arange(ffn_room))[None, :, None]),
        jnp.where(seq_slots[0] == my_fsdp, 0, ffn_hold) + seq_slots[1],
    )

    attn_sent = gather_tiles(masters, attn_pack.reshape(-1))
    attn_sent = attn_sent.reshape(seq_size, attn_room, tile, tile)
    token_tiles = own_tokens.reshape(rows, row_blocks, tile).transpose(1, 0, 2)
    token_tiles = token_tiles.reshape(-1, tile, tile)
    gain_rows = own_gains.reshape(-1, tile)
    gain_tiles = jnp.pad(gain_rows, ((0, -gain_rows.shape[0] % tile), (0, 0))).reshape(-1, tile, tile)
    common = jnp.concatenate([token_tiles, small_half, gain_tiles])
    attn_got = [attn_sent[0]] + [
        seq_swap(jnp.concatenate([attn_sent[flip], common]), flip) for flip in range(1, seq_size)
    ]
    segment, position = documents(doc_lengths[0], length)
    places = ((my_seq ^ flips)[:, None] * rows + jnp.arange(rows)[None, :]).reshape(-1)

    def reorder(values):
        blocks = values.reshape(seq_size, rows)
        return jnp.concatenate(
            [lax.dynamic_index_in_dim(blocks, my_seq ^ i, 0, False) for i in range(seq_size)]
        )

    pack_segment = reorder(segment)
    allow = (pack_segment[:, None] == pack_segment[None, :]) & (
        places[None, :] <= places[:, None]
    )
    turns = jnp.arange(HEAD_DIM // 2).astype(f32)
    angle = reorder(position).astype(f32)[:, None] * (THETA ** (-2.0 * turns / HEAD_DIM))[None, :]
    cosine, sine = jnp.cos(angle)[:, None, :], jnp.sin(angle)[:, None, :]
    ready = (allow, cosine, sine, attn_join, ffn_join)
    ffn_got, attn_got, common, ready = lax.optimization_barrier((ffn_got, attn_got, common, ready))
    allow, cosine, sine, attn_join, ffn_join = ready
    parts = [common] + [value[attn_room:] for value in attn_got[1:]]
    token_end = token_tiles.shape[0]
    small_end = token_end + small_rows

    def seq_order(value):
        return take_blocks(value, my_seq ^ flips)

    pack_tokens = jnp.concatenate(
        [
            part[:token_end].reshape(row_blocks, rows, tile).transpose(1, 0, 2).reshape(rows, width)
            for part in parts
        ]
    )
    gain_full = seq_order(
        jnp.stack([part[small_end:].reshape(-1, tile)[: gain_rows.shape[0]] for part in parts])
    )
    gain_full = gain_full.reshape(-1).astype(f32)
    gain_in = gain_full[0:width]
    small_got = core_pair(seq_order(jnp.stack([part[token_end:small_end] for part in parts])))
    small_got = small_got.transpose(1, 0, 2, 3, 4)
    small_table = assemble(small_got.reshape((-1,) + small_master.shape[1:]), row_blocks)
    pack_normed = rms_norm(pack_tokens.astype(f32), gain_in).astype(bf16)
    attn_kept = gather_tiles(attn_got, attn_keep)
    ffn_got = ffn_got + [core_swap(value) for value in ffn_got]
    ffn_kept = [
        gather_tiles(ffn_got, ffn_keep[:ffn_half]),
        gather_tiles(ffn_got, ffn_keep[ffn_half:]),
    ]
    ffn_kept, attn_kept = lax.optimization_barrier((ffn_kept, attn_kept))
    ffn_all = [lax.all_gather(value, "seq", axis=0, tiled=True) for value in ffn_kept]
    attn_all = [attn_kept] + [chip_shift(attn_kept, offset) for offset in range(1, chips)]
    attn_all = attn_all + [core_swap(value) for value in attn_all]

    attn_all, ffn_all[0], pack_normed, gain_full = lax.optimization_barrier(
        (attn_all, ffn_all[0], pack_normed, gain_full)
    )
    gain_in = gain_full[0:width]

    def fetch(arrays, index, to, me, place, columns_of):
        def fast():
            return join_tiles(arrays, index, row_blocks, columns_of)

        def slow():
            whole = lax.all_to_all(
                jnp.broadcast_to(master_low[None], (seq_size * fsdp_size,) + master_low.shape),
                ("seq", "fsdp"),
                split_axis=0,
                concat_axis=0,
                tiled=True,
            ).reshape(-1, tile, tile)
            count = row_blocks * sum(columns_of)
            slots = pick(
                (to.reshape(1, -1) == me) & (place.reshape(1, -1) == jnp.arange(count)[:, None]),
                jnp.arange(tiles)[None, :],
            )
            return join_tiles([whole], slots, row_blocks, columns_of)

        return lax.cond(fits, fast, slow)

    w_first, w_out = fetch(
        attn_all, attn_join, attn_to, my_seq, attn_place, (attn_first, query_each)
    )
    gain_attn = gain_full[width : 2 * width]
    gain_laurel = gain_full[2 * width : 3 * width]
    gain_pre = gain_full[3 * width : 4 * width]
    gain_post = gain_full[4 * width : 5 * width]
    gain_vec = gain_full[5 * width : 6 * width]
    gain_query = gain_full[6 * width : 6 * width + HEAD_DIM]
    gain_key = gain_full[6 * width + HEAD_DIM : 6 * width + 2 * HEAD_DIM]
    stream = own_tokens.astype(f32)
    vectors = layer_vectors[0].astype(f32)
    normed, normed_pull = jax.vjp(rms_norm, stream, gain_in)
    normed_low = normed.astype(bf16)
    first_pre = matmul(pack_normed, w_first)
    is_key = my_seq % per_key == 0

    def shape_query(query_in, query_gain):
        value = rms_norm(query_in.reshape(length, per_device, HEAD_DIM), query_gain)
        return turn(value, cosine, sine)

    def shape_key(key_in, key_gain):
        return turn(rms_norm(key_in.reshape(length, 1, HEAD_DIM), key_gain), cosine, sine)

    query_pre = first_pre[:, : per_device * HEAD_DIM]
    other_pre = first_pre[:, per_device * HEAD_DIM :]
    query_rot, query_pull = jax.vjp(shape_query, query_pre, gain_query)
    key_rot, key_pull = jax.vjp(shape_key, other_pre, gain_key)
    query_heads = query_rot.astype(bf16)
    other_low = jnp.where(is_key, key_rot[:, 0, :], other_pre).astype(bf16)
    partner_low = seq_swap(other_low, 1).reshape(seq_size // 2, 2, rows, HEAD_DIM)
    partner_low = partner_low[:, ::-1].reshape(length, HEAD_DIM)
    key_single = jnp.where(is_key, other_low, partner_low)
    value_single = jnp.where(is_key, partner_low, other_low)

    raw = (
        jnp.einsum("qhd,kd->qhk", query_heads, key_single, preferred_element_type=f32) * SCALE
    )
    scores = jnp.where(allow[:, None, :], raw, NEGATIVE)
    powers = jnp.exp(scores - jnp.max(scores, axis=-1, keepdims=True))
    prob = powers / jnp.sum(powers, axis=-1, keepdims=True)
    prob_low = prob.astype(bf16)
    attended_low = (
        jnp.einsum("qhk,kd->qhd", prob_low, value_single, preferred_element_type=f32)
        .astype(bf16)
        .reshape(length, per_device * HEAD_DIM)
    )
    attn_pre = seq_sum(matmul_flip(attended_low, w_out), bf16)
    attn_pre, small_table = lax.optimization_barrier((attn_pre, small_table))
    laurel_left = small_table[:, :RANK]
    laurel_right = small_table[:, RANK : 2 * RANK]
    vector_gate_w = small_table[:, 2 * RANK : 2 * RANK + PLD]
    vector_proj_w = small_table[:, 2 * RANK + PLD :]

    attn_normed, attn_pull = jax.vjp(rms_norm, attn_pre, gain_attn)
    first_sum = stream + attn_normed
    left_pre = matmul(normed_low, laurel_left)
    left_low = left_pre.astype(bf16)
    right_pre = matmul_flip(left_low, laurel_right)
    laurel_normed, laurel_pull = jax.vjp(rms_norm, right_pre, gain_laurel)
    second_sum = (first_sum + normed + laurel_normed) * ROOT_HALF
    feed_normed, feed_pull = jax.vjp(rms_norm, second_sum, gain_pre)
    feed_own = feed_normed.astype(bf16)
    feed_low = lax.all_gather(feed_own, "fsdp", axis=0, tiled=True)
    ffn_all, _ = lax.optimization_barrier((ffn_all, feed_own))
    w_both, w_down = fetch(
        ffn_all, ffn_join, ffn_to, my_fsdp, ffn_place, (ffn_first, ffn_each)
    )
    both_pre = matmul(feed_low, w_both)
    ffn_width = w_down.shape[1]
    hidden, hidden_pull = jax.vjp(gelu_product, both_pre[:, :ffn_width], both_pre[:, ffn_width:])
    hidden_low = hidden.astype(bf16)
    down_pre = lax.psum_scatter(
        matmul_flip(hidden_low, w_down).astype(bf16), "fsdp", scatter_dimension=0, tiled=True
    ).astype(f32)
    down_normed, down_pull = jax.vjp(rms_norm, down_pre, gain_post)
    third_sum = second_sum + down_normed
    third_low = third_sum.astype(bf16)
    vector_pre = matmul(third_low, vector_gate_w)
    vector_gated, vector_pull = jax.vjp(lambda inner: gelu_product(inner, vectors), vector_pre)
    vector_low = vector_gated.astype(bf16)
    proj_pre = matmul_flip(vector_low, vector_proj_w)
    proj_normed, proj_pull = jax.vjp(rms_norm, proj_pre, gain_vec)
    result = third_sum + proj_normed
    output = result.astype(bf16)[None]

    grad_out = cotangent[0].astype(f32)
    grad_proj, grad_gain_vec = proj_pull(grad_out)
    proj_grad_low = grad_proj.astype(bf16)
    (grad_vector_pre,) = vector_pull(matmul(proj_grad_low, vector_proj_w))
    vector_grad_low = grad_vector_pre.astype(bf16)
    grad_third = grad_out + matmul_flip(vector_grad_low, vector_gate_w)
    grad_down, grad_gain_post = down_pull(grad_third)
    down_grad_low = lax.all_gather(grad_down.astype(bf16), "fsdp", axis=0, tiled=True)
    grad_gate, grad_up = hidden_pull(matmul(down_grad_low, w_down))
    both_grad_low = jnp.concatenate([grad_gate, grad_up], axis=1).astype(bf16)

    early_full = jnp.concatenate(
        [matmul_outer(third_low, vector_grad_low), matmul_outer(proj_grad_low, vector_low)], axis=1
    )
    small_early = small_sum(split_tiles(early_full, tile).reshape(-1, tile))
    both_grad_low, small_early = lax.optimization_barrier((both_grad_low, small_early))
    grad_feed = lax.psum_scatter(
        matmul_flip(both_grad_low, w_both).astype(bf16), "fsdp", scatter_dimension=0, tiled=True
    ).astype(f32)
    both_grad_w = matmul_outer(feed_low, both_grad_low).astype(bf16)
    down_grad_w = matmul_outer(down_grad_low, hidden_low).astype(bf16)
    ffn_parts = [
        cut_tiles([both_grad_w, down_grad_w], index.reshape(-1), tile)
        for index in (ffn_cut[:, :ffn_half], ffn_cut[:, ffn_half:])
    ]
    ffn_parts, grad_feed = lax.optimization_barrier((ffn_parts, grad_feed))
    ffn_sums = [
        lax.psum_scatter(value, "seq", scatter_dimension=0, tiled=True) for value in ffn_parts
    ]

    grad_second_norm, grad_gain_pre = feed_pull(grad_feed)
    half_grad = (grad_third + grad_second_norm) * ROOT_HALF
    grad_right, grad_gain_laurel = laurel_pull(half_grad)
    right_grad_low = grad_right.astype(bf16)
    left_grad_low = matmul(right_grad_low, laurel_right).astype(bf16)
    grad_attn, grad_gain_attn = attn_pull(half_grad)
    attn_grad_low = seq_gather(grad_attn.astype(bf16))
    grad_attended = (
        matmul(attn_grad_low, w_out).astype(bf16).reshape(length, per_device, HEAD_DIM)
    )
    out_grad_w = matmul_outer(attn_grad_low, attended_low).astype(bf16)
    value_grad = jnp.einsum("qhk,qhd->kd", prob_low, grad_attended, preferred_element_type=f32)
    grad_prob = jnp.einsum("qhd,kd->qhk", grad_attended, value_single, preferred_element_type=f32)
    inner = jnp.sum(prob * grad_prob, axis=-1, keepdims=True)
    grad_score = (prob * (grad_prob - inner)).astype(bf16)
    grad_query = (
        jnp.einsum("qhk,kd->qhd", grad_score, key_single, preferred_element_type=f32) * SCALE
    ).astype(bf16)
    key_grad = (
        jnp.einsum("qhk,qhd->kd", grad_score, query_heads, preferred_element_type=f32) * SCALE
    ).astype(bf16)
    value_grad = value_grad.astype(bf16)
    partner_grad = seq_swap(jnp.where(is_key, value_grad, key_grad), 1)
    partner_grad = partner_grad.reshape(seq_size // 2, 2, rows, HEAD_DIM)[:, ::-1]
    other_grad = jnp.where(is_key, key_grad, value_grad).astype(f32) + partner_grad.reshape(
        length, HEAD_DIM
    ).astype(f32)
    grad_query_pre, grad_gain_query = query_pull(grad_query.astype(f32))
    grad_key_pre, grad_gain_key = key_pull(other_grad[:, None, :])
    grad_gain_key = jnp.where(is_key, grad_gain_key, 0.0)
    first_grad_low = jnp.concatenate(
        [grad_query_pre, jnp.where(is_key, grad_key_pre, other_grad)], axis=1
    ).astype(bf16)
    first_grad_w = matmul_outer(pack_normed, first_grad_low).astype(bf16)
    near = (my_chip + shifts) % chips
    near_key = take_blocks(attn_key_chip, near)[:, None, :]
    near_order = take_blocks(attn_order_chip, near)[:, None, :]
    near_place = take_blocks(by_chip(attn_place), near)[:, None, :]

    def attn_cut(core):
        index = pick(
            (near_key == 2 * my_seq + core)
            & (near_order == jnp.arange(attn_hold)[None, :, None]),
            near_place,
        )
        return cut_tiles([first_grad_w, out_grad_w], index.reshape(-1), tile)

    attn_given, attn_own = attn_cut(1 - my_core), attn_cut(my_core)
    attn_given, attn_own, ffn_sums[0] = lax.optimization_barrier(
        (attn_given, attn_own, ffn_sums[0])
    )
    attn_parts = added(attn_own, core_swap(attn_given)).reshape(chips, attn_hold, tile, tile)
    attn_sum = attn_parts[0]
    attn_parts = [attn_parts[offset].astype(bf16) for offset in range(1, chips)]
    normed_pre = matmul_flip(first_grad_low, w_first)
    attn_sum, attn_parts, normed_pre = lax.optimization_barrier((attn_sum, attn_parts, normed_pre))
    normed_sum = seq_sum(normed_pre, bf16)
    for offset in range(1, chips):
        attn_sum = attn_sum + chip_shift(attn_parts[offset - 1], offset).astype(f32)
    attn_sum = attn_sum.astype(bf16)
    attn_back = pick(
        (column_slots[3][None, None, :] == (my_seq ^ flips)[:, None, None])
        & (column_slots[0][None, None, :] == my_key)
        & (column_slots[2][None, None, :] == jnp.arange(attn_room)[None, :, None]),
        column_slots[1],
    )

    grad_normed = half_grad + matmul_flip(left_grad_low, laurel_left) + normed_sum
    grad_stream_norm, grad_gain_in = normed_pull(grad_normed)
    input_grad = (half_grad + grad_stream_norm)[None]
    gain_grad = jnp.concatenate(
        [
            grad_gain_in,
            grad_gain_attn,
            grad_gain_laurel,
            grad_gain_pre,
            grad_gain_post,
            grad_gain_vec,
            grad_gain_query,
            grad_gain_key,
        ]
    )
    late_full = jnp.concatenate(
        [matmul_outer(normed_low, left_grad_low), matmul_outer(right_grad_low, left_low)], axis=1
    )
    late = jnp.concatenate(
        [late_full.reshape(seq_size, -1), gain_grad.reshape(seq_size, -1)], axis=1
    ).reshape(seq_size, -1, tile)
    late = seq_sum(late.reshape(-1, tile), bf16, True)

    late = late + core_swap(late.astype(bf16)).astype(f32)
    late_low = late.astype(bf16)
    for offset in range(1, chips):
        late = late + chip_shift(late_low, offset).astype(f32)
    ffn_sums, attn_sum, late, input_grad = lax.optimization_barrier(
        (ffn_sums, attn_sum, late, input_grad)
    )
    ffn_sums = ffn_sums + [core_swap(value) for value in ffn_sums]
    ffn_return = [gather_tiles(ffn_sums, ffn_back[i]) for i in range(chips)]
    ffn_return, attn_sum = lax.optimization_barrier((ffn_return, attn_sum))
    ffn_returned = chip_exchange(ffn_return)
    ffn_returned = ffn_returned + [core_swap(value) for value in ffn_returned]
    late_rows = late_full.shape[0] // seq_size
    late_tiles = late[:late_rows].reshape(-1, 1, tile, tile)
    gain_grad_mine = late[late_rows:].reshape(-1)
    small_grad = jnp.concatenate(
        [
            late_tiles.astype(bf16),
            small_early.reshape(late_tiles.shape[0], -1, tile, tile),
        ],
        axis=1,
    ).reshape(small_master.shape)
    attn_returned = seq_exchange([gather_tiles([attn_sum], attn_back[i]) for i in range(seq_size)])
    attn_returned = attn_returned + [core_swap(value) for value in attn_returned]
    slot_grad = jnp.where(my_slots[0] >= 0, my_slots[1], 2 * half + my_slots[2])

    def slow_return():
        own_ffn = split_tiles(both_grad_w, tile), split_tiles(down_grad_w, tile)
        own_attn = split_tiles(first_grad_w, tile), split_tiles(out_grad_w, tile)
        parts = jnp.concatenate(own_ffn + own_attn + (jnp.zeros((1, tile, tile), bf16),))
        index = jnp.where(
            ffn_to == my_fsdp,
            ffn_place,
            jnp.where(attn_to == my_seq, ffn_count + attn_place, ffn_count + attn_count),
        )
        spread = gather_tiles([parts], index.reshape(-1))
        spread = lax.all_to_all(
            spread.reshape((seq_size * fsdp_size, mine, tile, tile)),
            ("seq", "fsdp"),
            split_axis=0,
            concat_axis=0,
            tiled=True,
        )
        return jnp.sum(spread.astype(f32), axis=0).astype(bf16)

    tile_grads = ffn_returned + attn_returned
    slow_start = 2 * half + 2 * seq_size * attn_room
    slow_grads = lax.cond(fits, lambda: jnp.zeros((mine, tile, tile), bf16), slow_return)
    tile_grads = tile_grads + [slow_grads]
    slot_grad = jnp.where(fits, slot_grad, slow_start + local_slots)

    tile_new, tile_first_new, tile_second_new = rotate_update(
        tile_grads, slot_grad, tile_master, tile_first, tile_second, left_basis, right_basis, RATE_TILE
    )
    small_new, small_first_new, small_second_new = rotate_update(
        [small_grad],
        jnp.arange(small_master.shape[0]),
        small_master,
        small_first,
        small_second,
        small_left,
        small_right,
        RATE_SMALL,
    )
    gain_first_new = BETA_ONE * gain_first + (1.0 - BETA_ONE) * gain_grad_mine
    gain_second_new = BETA_TWO * gain_second + (1.0 - BETA_TWO) * gain_grad_mine * gain_grad_mine
    correct_one = 1.0 - BETA_ONE**STEP
    correct_two = 1.0 - BETA_TWO**STEP
    gain_new = gains - RATE_GAIN * (gain_first_new / correct_one) / (
        jnp.sqrt(gain_second_new / correct_two) + ADAM_EPS
    )
    return (
        output,
        input_grad,
        tile_new,
        tile_first_new,
        tile_second_new,
        small_new,
        small_first_new,
        small_second_new,
        gain_new,
        gain_first_new,
        gain_second_new,
    )


def solution(mesh):
    return jax.shard_map(
        on_device,
        mesh=mesh,
        in_specs=(
            P("fsdp", "seq", None),
            P("fsdp", "seq", None),
            P("fsdp", None),
            P("fsdp", "seq", None),
            P(),
            P(("seq", "fsdp"), None, None),
            P(("seq", "fsdp"), None, None),
            P(("seq", "fsdp"), None, None),
            P(("seq", "fsdp"), None, None),
            P(("seq", "fsdp"), None, None),
            P("seq", None, None),
            P("seq", None, None),
            P("seq", None, None),
            P("seq", None, None),
            P("seq", None, None),
            P("seq"),
            P("seq"),
            P("seq"),
        ),
        out_specs=(
            P("fsdp", "seq", None),
            P("fsdp", "seq", None),
            P(("seq", "fsdp"), None, None),
            P(("seq", "fsdp"), None, None),
            P(("seq", "fsdp"), None, None),
            P("seq", None, None),
            P("seq", None, None),
            P("seq", None, None),
            P("seq"),
            P("seq"),
            P("seq"),
        ),
        check_vma=False,
    )
```

```python
import math

import jax
import jax.numpy as jnp
from jax import lax
from jax.experimental import pallas as pl
from jax.experimental.pallas import tpu as pltpu
from jax.sharding import PartitionSpec as P

HEADS = 8
KV_HEADS = 2
HEAD_DIM = 256
FF = 8192
RANK = 64
PLD = 256
STEP = 5


EPS = 1e-06
SCALE = 0.0625
THETA = 1000000.0
ROOT_HALF = 0.7071067811865476
BETA_ONE = 0.5
BETA_TWO = 0.5
ADAM_EPS = 1e-08
RATE_TILE = 0.02
RATE_SMALL = 0.04
RATE_GAIN = 0.3
DECAY = 0.01
NEGATIVE = -1e30
VMEM_BYTES = 32 * 1024 * 1024


def rms_norm(value, gain):
    return value * lax.rsqrt(jnp.mean(value * value, axis=-1, keepdims=True) + EPS) * gain


def rotary(value, position):
    half = value.shape[-1] // 2
    freq = THETA ** (-2.0 * jnp.arange(half).astype(jnp.float32) / value.shape[-1])
    angle = position.astype(jnp.float32)[:, None] * freq[None, :]
    cosine = jnp.cos(angle)[:, None, :]
    sine = jnp.sin(angle)[:, None, :]
    first = value[..., :half]
    second = value[..., half:]
    return jnp.concatenate(
        [first * cosine - second * sine, second * cosine + first * sine], axis=-1
    )


def documents(lengths, length):
    places = jnp.arange(length)
    ends = jnp.cumsum(lengths)
    passed = places[:, None] >= ends[None, :]
    segment = jnp.sum(passed.astype(jnp.int32), axis=1)
    before = jnp.sum(jnp.where(passed, lengths[None, :], 0), axis=1)
    return (segment, places - before)


def matmul(left, right):
    return jnp.dot(left, right, preferred_element_type=jnp.float32)


def matmul_flip(left, right):
    return lax.dot_general(
        left, right, (((1,), (1,)), ((), ())), preferred_element_type=jnp.float32
    )


def matmul_outer(left, right):
    return lax.dot_general(
        left, right, (((0,), (0,)), ((), ())), preferred_element_type=jnp.float32
    )


def assemble(tiles, row_blocks):
    size = tiles.shape[1]
    column_blocks = tiles.shape[0] // row_blocks
    return (
        tiles.reshape(row_blocks, column_blocks, size, size)
        .transpose(0, 2, 1, 3)
        .reshape(row_blocks * size, column_blocks * size)
    )


def split_tiles(matrix, size):
    row_blocks = matrix.shape[0] // size
    column_blocks = matrix.shape[1] // size
    return (
        matrix.reshape(row_blocks, size, column_blocks, size)
        .transpose(0, 2, 1, 3)
        .reshape(row_blocks * column_blocks, size, size)
    )


def gelu_product(first, second):
    return jax.nn.gelu(first, approximate=True) * second


def room(count, share):
    mean = count * share
    return math.ceil(mean + 3.6 * math.sqrt(mean * (1.0 - share)) + 3.0)


def count_earlier(group, valid):
    size = group.shape[-1]
    order = jnp.arange(size)
    same = (group[..., :, None] == group[..., None, :]) & valid[..., None, :]
    same = same & (order[None, :] < order[:, None])
    return jnp.sum(same.astype(jnp.int32), axis=-1)


def count_long(keys):
    groups, size = keys.shape

    def kernel(row_ref, column_ref, out_ref):
        row = row_ref[0]
        column = column_ref[0]
        here = lax.broadcasted_iota(jnp.int32, (size, size), 1)
        other = lax.broadcasted_iota(jnp.int32, (size, size), 0)
        earlier = (column == row) & (other < here)
        out_ref[0] = jnp.sum(earlier.astype(jnp.int32), axis=0, keepdims=True)

    return pl.pallas_call(
        kernel,
        grid=(groups,),
        out_shape=jax.ShapeDtypeStruct((groups, 1, size), jnp.int32),
        in_specs=[
            pl.BlockSpec((1, 1, size), lambda i: (i, 0, 0)),
            pl.BlockSpec((1, size, 1), lambda i: (i, 0, 0)),
        ],
        out_specs=pl.BlockSpec((1, 1, size), lambda i: (i, 0, 0)),
        cost_estimate=pl.CostEstimate(flops=0, transcendentals=0, bytes_accessed=0),
        compiler_params=pltpu.CompilerParams(vmem_limit_bytes=VMEM_BYTES),
    )(keys[:, None, :], keys[:, :, None]).reshape(groups, size)


def pick(match, value):
    return jnp.sum(jnp.where(match, value, 0), axis=-1)


def steps_of(count):
    for steps in range(4, 65):
        if count % steps == 0 and 16 <= count // steps <= 160:
            return steps
    return 2 if count % 2 == 0 else 1


def tile_kernel_call(kernel, index, arrays, out_shape, out_specs, steps):
    moved = sum(math.prod(one.shape) * 2 for one in jax.tree.leaves(out_shape))
    return pl.pallas_call(
        kernel,
        grid=(steps,),
        cost_estimate=pl.CostEstimate(flops=0, transcendentals=0, bytes_accessed=2 * moved),
        out_shape=out_shape,
        in_specs=[pl.BlockSpec(memory_space=pltpu.SMEM)]
        + [pl.BlockSpec(memory_space=pl.ANY)] * len(arrays),
        out_specs=out_specs,
        scratch_shapes=[pltpu.SemaphoreType.DMA],
        compiler_params=pltpu.CompilerParams(vmem_limit_bytes=VMEM_BYTES),
    )(index, *arrays)


def start_copy(sources, place, target, sem, start=0):
    if len(sources) == 1:
        pltpu.make_async_copy(sources[0].at[place - start], target, sem).start()
        return
    half = len(sources) // 2
    middle = start + sum(ref.shape[0] for ref in sources[:half])

    @pl.when(place < middle)
    def _():
        start_copy(sources[:half], place, target, sem, start)

    @pl.when(place >= middle)
    def _():
        start_copy(sources[half:], place, target, sem, middle)


def gather_tiles(arrays, index):
    tile = arrays[0].shape[-1]
    count = index.shape[0]
    steps = steps_of(count)
    each = count // steps

    def kernel(index_ref, *refs):
        sources, out, sem = refs[:-2], refs[-2], refs[-1]
        base = pl.program_id(0) * each

        def step(i, carry):
            start_copy(sources, index_ref[base + i], out.at[i], sem)
            return carry

        lax.fori_loop(0, each, step, 0)
        pltpu.make_async_copy(out, out, sem).wait()

    total = sum(array.shape[0] for array in arrays)
    return tile_kernel_call(
        kernel,
        jnp.clip(index, 0, total - 1),
        arrays,
        jax.ShapeDtypeStruct((count, tile, tile), arrays[0].dtype),
        pl.BlockSpec((each, tile, tile), lambda i: (i, 0, 0)),
        steps,
    )


def join_tiles(arrays, index, row_blocks, columns):
    tile = arrays[0].shape[-1]
    steps = 4
    each = row_blocks // steps

    def kernel(index_ref, *refs):
        sources, outs, sem = refs[: len(arrays)], refs[len(arrays) : -1], refs[-1]
        base = pl.program_id(0) * each
        start = 0
        for out, width in zip(outs, columns):

            def step(i, carry, out=out, start=start, width=width):
                row = i // width
                column = i - row * width
                target = out.at[
                    pl.ds(pl.multiple_of(row * tile, tile), tile),
                    pl.ds(pl.multiple_of(column * tile, tile), tile),
                ]
                start_copy(sources, index_ref[start + base * width + i], target, sem)
                return carry

            lax.fori_loop(0, each * width, step, 0)
            start = start + row_blocks * width
        for out in outs:
            pltpu.make_async_copy(out, out, sem).wait()

    total = sum(array.shape[0] for array in arrays)
    out_shape = tuple(
        jax.ShapeDtypeStruct((row_blocks * tile, width * tile), arrays[0].dtype)
        for width in columns
    )
    out_specs = tuple(pl.BlockSpec((each * tile, width * tile), lambda i: (i, 0)) for width in columns)
    return tile_kernel_call(
        kernel, jnp.clip(index, 0, total - 1), arrays, out_shape, out_specs, steps
    )


def cut_tiles(matrices, index, tile):
    row_blocks = matrices[0].shape[0] // tile
    widths = [matrix.shape[1] // tile for matrix in matrices]
    count = index.shape[0]
    steps = steps_of(count)
    each = count // steps

    def kernel(index_ref, *refs):
        sources, out, sem = refs[:-2], refs[-2], refs[-1]
        base = pl.program_id(0) * each

        def step(i, carry):
            place = index_ref[base + i]
            start = 0
            for ref, width in zip(sources, widths):
                size = row_blocks * width

                @pl.when((place >= start) & (place < start + size))
                def _(ref=ref, start=start, width=width):
                    row = (place - start) // width
                    column = place - start - row * width
                    source = ref.at[
                        pl.ds(pl.multiple_of(row * tile, tile), tile),
                        pl.ds(pl.multiple_of(column * tile, tile), tile),
                    ]
                    pltpu.make_async_copy(source, out.at[i], sem).start()

                start = start + size
            return carry

        lax.fori_loop(0, each, step, 0)
        pltpu.make_async_copy(out, out, sem).wait()

    return tile_kernel_call(
        kernel,
        jnp.clip(index, 0, row_blocks * sum(widths) - 1),
        matrices,
        jax.ShapeDtypeStruct((count, tile, tile), matrices[0].dtype),
        pl.BlockSpec((each, tile, tile), lambda i: (i, 0, 0)),
        steps,
    )


def split_low(value):
    high = value.astype(jnp.bfloat16)
    return high, (value - high.astype(jnp.float32)).astype(jnp.bfloat16)


def rotate_update(grads, index, master, first, second, left, right, rate):
    count, tile, _ = master.shape
    each = 4 if count % 4 == 0 else 1
    correct_one = 1.0 - BETA_ONE**STEP
    correct_two = 1.0 - BETA_TWO**STEP

    def product(one, two, dims):
        return lax.dot_general(one, two, (dims, ((), ())), preferred_element_type=jnp.float32)

    def kernel(index_ref, *refs):
        sources, refs = refs[: len(grads)], refs[len(grads) :]
        master_ref, first_ref, second_ref, left_ref, right_ref = refs[:5]
        master_out, first_out, second_out, held, sems = refs[5:]
        now = pl.program_id(0)

        @pl.when(now == 0)
        def _():
            def step(i, carry):
                start_copy(sources, index_ref[i], held.at[i], sems.at[i // each])
                return carry

            lax.fori_loop(0, count, step, 0)

        block = held.at[pl.ds(now * each, each)]
        pltpu.make_async_copy(block, block, sems.at[now]).wait()
        lefts, rights, turns = [], [], []
        for i in range(each):
            grad = held[now * each + i]
            lefts.append(split_low(left_ref[i]))
            rights.append(split_low(right_ref[i]))
            half_turned = product(
                jnp.concatenate([grad, grad], axis=1),
                jnp.concatenate(rights[i], axis=0),
                ((1,), (0,)),
            )
            turns.append(split_low(half_turned))
        for i in range(each):
            (left_high, left_low), (high, low) = lefts[i], turns[i]
            turns[i] = product(
                jnp.concatenate([left_high, left_high, left_low], axis=0),
                jnp.concatenate([high, low, high], axis=0),
                ((0,), (0,)),
            )
        for i in range(each):
            right_high, right_low = rights[i]
            first_new = BETA_ONE * first_ref[i] + (1.0 - BETA_ONE) * turns[i]
            second_new = BETA_TWO * second_ref[i] + (1.0 - BETA_TWO) * turns[i] * turns[i]
            first_out[i] = first_new
            second_out[i] = second_new
            high, low = split_low(
                first_new / correct_one / (jnp.sqrt(second_new / correct_two) + ADAM_EPS)
            )
            half_back = product(
                jnp.concatenate([high, low, high], axis=1),
                jnp.concatenate([right_high, right_high, right_low], axis=1),
                ((1,), (1,)),
            )
            turns[i] = split_low(half_back)
        for i in range(each):
            (left_high, left_low), (high, low) = lefts[i], turns[i]
            back = product(
                jnp.concatenate([left_high, left_high, left_low], axis=1),
                jnp.concatenate([high, low, high], axis=0),
                ((1,), (0,)),
            )
            weight = master_ref[i]
            master_out[i] = weight - rate * (back + DECAY * weight)

    spec = pl.BlockSpec((each, tile, tile), lambda i: (i, 0, 0))
    shape = jax.ShapeDtypeStruct(master.shape, jnp.float32)
    total = sum(array.shape[0] for array in grads)
    return pl.pallas_call(
        kernel,
        grid=(count // each,),
        out_shape=(shape, shape, shape),
        in_specs=[pl.BlockSpec(memory_space=pltpu.SMEM)]
        + [pl.BlockSpec(memory_space=pl.ANY)] * len(grads)
        + [spec] * 5,
        out_specs=(spec, spec, spec),
        scratch_shapes=[
            pltpu.VMEM((count, tile, tile), jnp.bfloat16),
            pltpu.SemaphoreType.DMA((count // each,)),
        ],
        compiler_params=pltpu.CompilerParams(vmem_limit_bytes=VMEM_BYTES),
    )(jnp.clip(index, 0, total - 1), *grads, master, first, second, left, right)


def seq_swap(value, flip):
    size = lax.axis_size("seq")
    return lax.ppermute(value, "seq", [(i, i ^ flip) for i in range(size)])


def take_blocks(value, order):
    return jnp.stack(
        [lax.dynamic_index_in_dim(value, order[i], 0, False) for i in range(order.shape[0])]
    )


def core_swap(value):
    size = lax.axis_size("fsdp")
    return lax.ppermute(value, "fsdp", [(i, i ^ 1) for i in range(size)])


def chip_shift(value, offset):
    size = lax.axis_size("fsdp")
    chips = size // 2
    return lax.ppermute(
        value, "fsdp", [(i, (i // 2 + offset) % chips * 2 + i % 2) for i in range(size)]
    )


def seq_gather(value):
    size = lax.axis_size("seq")
    return jnp.concatenate([value] + [seq_swap(value, flip) for flip in range(1, size)], axis=0)


def seq_ordered(value):
    size = lax.axis_size("seq")
    parts = jnp.stack([value] + [seq_swap(value, flip) for flip in range(1, size)], axis=0)
    return take_blocks(parts, lax.axis_index("seq") ^ jnp.arange(size))


def seq_exchange(values):
    return [values[0]] + [seq_swap(values[flip], flip) for flip in range(1, len(values))]


def seq_sum(value, wire, ordered=False):
    size = lax.axis_size("seq")
    parts = value.reshape((size, value.shape[0] // size) + value.shape[1:])
    if ordered:
        parts = take_blocks(parts, lax.axis_index("seq") ^ jnp.arange(size))
    total = parts[0]
    for flip in range(1, size):
        total = total + seq_swap(parts[flip].astype(wire), flip).astype(jnp.float32)
    return total


def chip_exchange(values):
    return [values[0]] + [chip_shift(values[offset], offset) for offset in range(1, len(values))]


def core_pair(value):
    other = core_swap(value)
    even = lax.axis_index("fsdp") % 2 == 0
    return jnp.where(even, jnp.stack([value, other]), jnp.stack([other, value]))


def small_sum(value):
    seq_size = lax.axis_size("seq")
    chips = lax.axis_size("fsdp") // 2
    chip = lax.axis_index("fsdp") // 2
    even = lax.axis_index("fsdp") % 2 == 0
    low = value.astype(jnp.bfloat16)
    parts = low.reshape((seq_size, 2, low.shape[0] // (2 * seq_size)) + low.shape[1:])
    kept = jnp.where(even, parts[:, 0], parts[:, 1]).astype(jnp.float32)
    given = jnp.where(even, parts[:, 1], parts[:, 0])
    kept = kept + core_swap(given).astype(jnp.float32)
    kept = seq_sum(kept.reshape((-1,) + low.shape[1:]), jnp.bfloat16, True)
    kept = kept.reshape((chips, kept.shape[0] // chips) + kept.shape[1:])
    kept = take_blocks(kept, (chip + jnp.arange(chips)) % chips)
    total = kept[0]
    for offset in range(1, chips):
        total = total + chip_shift(kept[offset].astype(jnp.bfloat16), offset).astype(jnp.float32)
    total = total.astype(jnp.bfloat16)
    parts = jnp.stack([total] + [chip_shift(total, offset) for offset in range(1, chips)])
    parts = take_blocks(parts, (chip - jnp.arange(chips)) % chips)
    return core_pair(parts).reshape((value.shape[0] // seq_size,) + value.shape[1:])


def turn(value, cosine, sine):
    half = value.shape[-1] // 2
    first, second = value[..., :half], value[..., half:]
    return jnp.concatenate(
        [first * cosine - second * sine, second * cosine + first * sine], axis=-1
    )


def added(one, two):
    return one.astype(jnp.float32) + two.astype(jnp.float32)


def on_device(
    tokens,
    layer_vectors,
    doc_lengths,
    cotangent,
    tile_owner,
    tile_master,
    tile_first,
    tile_second,
    left_basis,
    right_basis,
    small_master,
    small_first,
    small_second,
    small_left,
    small_right,
    gains,
    gain_first,
    gain_second,
):
    bf16 = jnp.bfloat16
    f32 = jnp.float32
    tile = tile_master.shape[1]
    width = tokens.shape[2]
    row_blocks = width // tile
    rows = tokens.shape[1]
    seq_size = lax.axis_size("seq")
    fsdp_size = lax.axis_size("fsdp")
    chips = fsdp_size // 2
    mine = tile_master.shape[0]
    tiles = tile_owner.shape[0]
    length = rows * seq_size
    per_device = HEADS // seq_size
    per_key = seq_size // KV_HEADS
    query_width = HEADS * HEAD_DIM
    key_width = KV_HEADS * HEAD_DIM
    my_seq = lax.axis_index("seq")
    my_fsdp = lax.axis_index("fsdp")
    my_chip = my_fsdp // 2
    my_core = my_fsdp % 2
    flips = jnp.arange(seq_size)
    shifts = jnp.arange(chips)

    query_blocks = query_width // tile
    key_blocks = key_width // tile
    ffn_blocks = FF // tile
    query_each = query_blocks // seq_size
    head_blocks = HEAD_DIM // tile
    ffn_each = ffn_blocks // fsdp_size
    columns = tiles // row_blocks
    attn_first = query_each + head_blocks
    attn_count = row_blocks * (attn_first + query_each)
    ffn_first = 2 * ffn_each
    ffn_count = row_blocks * 3 * ffn_each
    attn_share = (2 * query_blocks + 2 * key_blocks) / columns
    ffn_share = 3 * ffn_blocks / columns
    attn_room = (room(2 * mine, attn_share / seq_size) + 1) // 2
    attn_hold = (room(attn_count, 1.0 / chips) + 1) // 2 + 1
    ffn_room = (room(2 * mine, ffn_share / chips) + 1) // 2
    both_count = row_blocks * ffn_first
    ffn_hold = (room(ffn_count, 1.0 / seq_size) + 3) // 4 * 4
    ffn_half = ffn_hold * 3 // 7 // 4 * 4
    ffn_rest = ffn_hold - ffn_half

    def tile_places(owner):
        row = owner // columns
        column = owner % columns
        key_at = column - query_blocks
        value_at = key_at - key_blocks
        out_at = value_at - key_blocks
        ffn_at = out_at - query_blocks
        is_attn = ffn_at < 0
        kind = ffn_at // ffn_blocks
        ffn_column = ffn_at % ffn_blocks
        ffn_to = jnp.where(is_attn, -1, ffn_column // ffn_each)
        ffn_local = ffn_column % ffn_each
        ffn_place = jnp.where(
            kind == 2,
            both_count + row * ffn_each + ffn_local,
            row * ffn_first + kind * ffn_each + ffn_local,
        )
        attn_to = jnp.where(
            key_at < 0,
            column // query_each,
            jnp.where(
                value_at < 0,
                key_at // head_blocks * per_key,
                jnp.where(
                    out_at < 0,
                    value_at // head_blocks * per_key + per_key - 1,
                    out_at // query_each,
                ),
            ),
        )
        attn_place = jnp.where(
            key_at < 0,
            row * attn_first + column % query_each,
            jnp.where(
                out_at < 0,
                row * attn_first + query_each + key_at % head_blocks,
                row_blocks * attn_first + row * query_each + out_at % query_each,
            ),
        )
        attn_to = jnp.where(is_attn, attn_to, -1)
        return (ffn_to, ffn_place, attn_to, attn_place)

    owners = tile_owner.reshape(seq_size, fsdp_size, mine)
    slot_seq = jnp.arange(seq_size)[:, None, None]
    slot_fsdp = jnp.arange(fsdp_size)[None, :, None]
    slot_chip = slot_fsdp // 2
    local_slots = jnp.arange(mine)
    both_slots = jnp.arange(2 * mine)
    both_slots = jnp.where(
        both_slots // mine == my_core, both_slots % mine, mine + both_slots % mine
    )

    ffn_to = tile_places(owners)[0]
    ffn_chip = jnp.where(ffn_to < 0, -1, ffn_to // 2)
    chip_view = ffn_chip.reshape(seq_size, chips, 2 * mine)
    chip_rank = count_earlier(chip_view, chip_view >= 0).reshape(owners.shape)
    ffn_slots = lax.dynamic_slice(
        jnp.stack([ffn_chip, chip_rank]), (0, my_seq, 2 * my_chip, 0), (2, 1, 2, mine)
    ).reshape(2, 1, 1, 2 * mine)
    ffn_pack = pick(
        (ffn_slots[0] == ((my_chip + shifts) % chips)[:, None, None])
        & (ffn_slots[1] == (my_core * ffn_room + jnp.arange(ffn_room))[None, :, None]),
        both_slots,
    )
    master_low = tile_master.astype(bf16)
    masters = [master_low, core_swap(master_low)]
    ffn_sent = [gather_tiles(masters, ffn_pack[i]) for i in range(chips)]
    small_rows = small_master.shape[0] // 2
    small_half = lax.dynamic_slice_in_dim(small_master, my_core * small_rows, small_rows)
    masters, ffn_sent, chip_rank, owners, own_tokens, own_gains, small_half = (
        lax.optimization_barrier(
            (
                masters,
                ffn_sent,
                chip_rank,
                owners,
                tokens[0],
                gains.astype(bf16),
                small_half.astype(bf16),
            )
        )
    )
    ffn_got = chip_exchange(ffn_sent)

    ffn_to, ffn_place, attn_to, attn_place = tile_places(owners)
    ffn_chip = jnp.where(ffn_to < 0, -1, ffn_to // 2)
    attn_view = attn_to.reshape(seq_size, chips, 2 * mine)
    attn_rank = count_earlier(attn_view, attn_view >= 0).reshape(owners.shape)
    attn_core = (attn_rank + slot_seq) % 2
    attn_rank = attn_rank // 2
    attn_key = jnp.where(attn_to < 0, -1, 2 * attn_to + attn_core)

    chip_slots = lax.dynamic_slice(
        jnp.stack([attn_key, attn_rank]), (0, my_seq, 2 * my_chip, 0), (2, 1, 2, mine)
    ).reshape(2, 1, 1, 2 * mine)
    attn_message = attn_room + row_blocks * rows // tile + small_rows + -(-own_gains.shape[0] // tile**2)
    attn_pack = pick(
        (chip_slots[0] == (2 * (my_seq ^ flips) + my_core)[:, None, None])
        & (chip_slots[1] == jnp.arange(attn_room)[None, :, None]),
        both_slots,
    )
    attn_sent = gather_tiles(masters, attn_pack.reshape(-1))
    attn_sent = attn_sent.reshape(seq_size, attn_room, tile, tile)
    seq_view = ffn_to.reshape(seq_size, fsdp_size * mine)
    ffn_rank = count_long(seq_view).reshape(owners.shape)
    def by_chip(value):
        value = value.reshape(seq_size, chips, 2 * mine).transpose(1, 0, 2)
        return value.reshape(chips, seq_size * 2 * mine)

    attn_key_chip = by_chip(attn_key)
    attn_order_chip = count_long(attn_key_chip)
    attn_order = (
        attn_order_chip.reshape(chips, seq_size, 2 * mine).transpose(1, 0, 2).reshape(owners.shape)
    )
    fits = jnp.all(
        jnp.where(
            ffn_to < 0,
            (attn_rank < attn_room) & (attn_order < attn_hold),
            (chip_rank < 2 * ffn_room) & (ffn_rank < ffn_hold),
        )
    )
    half = chips * ffn_room
    rank_core = chip_rank // ffn_room
    rank_local = chip_rank % ffn_room
    out_place = (
        jnp.where(rank_core == my_core, 0, half)
        + (my_chip - slot_chip) % chips * ffn_room
        + rank_local
    )
    back_place = (
        jnp.where(rank_core == my_core, 0, half) + (my_chip - ffn_chip) % chips * ffn_room + rank_local
    )
    attn_back_place = (
        jnp.where(attn_core == my_core, 0, seq_size * attn_room)
        + (attn_to ^ my_seq) * attn_room
        + attn_rank
    )
    my_slots = lax.dynamic_slice(
        jnp.stack([ffn_to, back_place, attn_back_place]), (0, my_seq, my_fsdp, 0), (3, 1, 1, mine)
    ).reshape(3, mine)
    seq_slots = lax.dynamic_slice(
        jnp.stack(
            [
                ffn_to,
                ffn_rank,
                ffn_chip,
                out_place,
                chip_rank,
                jnp.broadcast_to(slot_chip, owners.shape),
            ]
        ),
        (0, my_seq, 0, 0),
        (6, 1, fsdp_size, mine),
    ).reshape(6, fsdp_size * mine)
    column_slots = lax.dynamic_slice(
        jnp.stack([attn_key, attn_order, attn_rank, jnp.broadcast_to(slot_seq, owners.shape)]),
        (0, 0, 2 * my_chip, 0),
        (4, seq_size, 2, mine),
    ).reshape(4, 2 * seq_size * mine)
    my_key = 2 * my_seq + my_core

    attn_keep = pick(
        (column_slots[0][None, :] == my_key)
        & (column_slots[1][None, :] == jnp.arange(attn_hold)[:, None]),
        jnp.where(
            column_slots[3] == my_seq,
            0,
            attn_room + ((column_slots[3] ^ my_seq) - 1) * attn_message,
        )
        + column_slots[2],
    )
    attn_join = pick(
        (attn_to.reshape(1, -1) == my_seq)
        & (attn_place.reshape(1, -1) == jnp.arange(attn_count)[:, None]),
        (
            jnp.where(attn_core == my_core, 0, chips * attn_hold)
            + (my_chip - slot_chip) % chips * attn_hold
            + attn_order
        ).reshape(1, -1),
    )
    ffn_keep = pick(
        (seq_slots[0][None, :] == my_fsdp) & (seq_slots[1][None, :] == jnp.arange(ffn_hold)[:, None]),
        seq_slots[3][None, :],
    )
    ffn_join = pick(
        (ffn_to.reshape(1, -1) == my_fsdp)
        & (ffn_place.reshape(1, -1) == jnp.arange(ffn_count)[:, None]),
        (
            jnp.where(
                ffn_rank < ffn_half,
                slot_seq * ffn_half + ffn_rank,
                seq_size * ffn_half + slot_seq * ffn_rest + ffn_rank - ffn_half,
            )
        ).reshape(1, -1),
    )
    ffn_cut = pick(
        (ffn_to.reshape(seq_size, 1, -1) == my_fsdp)
        & (ffn_rank.reshape(seq_size, 1, -1) == jnp.arange(ffn_hold)[None, :, None]),
        ffn_place.reshape(seq_size, 1, -1),
    )
    ffn_back = pick(
        (seq_slots[5][None, None, :] == ((my_chip + shifts) % chips)[:, None, None])
        & (seq_slots[2][None, None, :] == my_chip)
        & (seq_slots[4][None, None, :] == (my_core * ffn_room + jnp.arange(ffn_room))[None, :, None]),
        jnp.where(seq_slots[0] == my_fsdp, 0, ffn_hold) + seq_slots[1],
    )

    token_tiles = own_tokens.reshape(rows, row_blocks, tile).transpose(1, 0, 2)
    token_tiles = token_tiles.reshape(-1, tile, tile)
    gain_rows = own_gains.reshape(-1, tile)
    gain_tiles = jnp.pad(gain_rows, ((0, -gain_rows.shape[0] % tile), (0, 0))).reshape(-1, tile, tile)
    common = jnp.concatenate([token_tiles, small_half, gain_tiles])
    attn_got = [attn_sent[0]] + [
        seq_swap(jnp.concatenate([attn_sent[flip], common]), flip) for flip in range(1, seq_size)
    ]
    segment, position = documents(doc_lengths[0], length)
    places = ((my_seq ^ flips)[:, None] * rows + jnp.arange(rows)[None, :]).reshape(-1)

    def reorder(values):
        blocks = values.reshape(seq_size, rows)
        return jnp.concatenate(
            [lax.dynamic_index_in_dim(blocks, my_seq ^ i, 0, False) for i in range(seq_size)]
        )

    pack_segment = reorder(segment)
    allow = (pack_segment[:, None] == pack_segment[None, :]) & (
        places[None, :] <= places[:, None]
    )
    turns = jnp.arange(HEAD_DIM // 2).astype(f32)
    angle = reorder(position).astype(f32)[:, None] * (THETA ** (-2.0 * turns / HEAD_DIM))[None, :]
    cosine, sine = jnp.cos(angle)[:, None, :], jnp.sin(angle)[:, None, :]
    parts = [common] + [value[attn_room:] for value in attn_got[1:]]
    token_end = token_tiles.shape[0]
    small_end = token_end + small_rows

    def seq_order(value):
        return take_blocks(value, my_seq ^ flips)

    pack_tokens = jnp.concatenate(
        [
            part[:token_end].reshape(row_blocks, rows, tile).transpose(1, 0, 2).reshape(rows, width)
            for part in parts
        ]
    )
    gain_full = seq_order(
        jnp.stack([part[small_end:].reshape(-1, tile)[: gain_rows.shape[0]] for part in parts])
    )
    gain_full = gain_full.reshape(-1).astype(f32)
    gain_in = gain_full[0:width]
    pack_normed = rms_norm(pack_tokens.astype(f32), gain_in).astype(bf16)
    ready = (allow, cosine, sine, ffn_keep, attn_keep, pack_normed, gain_full)
    ffn_got, attn_got, parts, ready = lax.optimization_barrier((ffn_got, attn_got, parts, ready))
    allow, cosine, sine, ffn_keep, attn_keep, pack_normed, gain_full = ready
    gain_in = gain_full[0:width]
    small_got = core_pair(seq_order(jnp.stack([part[token_end:small_end] for part in parts])))
    small_got = small_got.transpose(1, 0, 2, 3, 4)
    small_table = assemble(small_got.reshape((-1,) + small_master.shape[1:]), row_blocks)
    attn_kept = gather_tiles(attn_got, attn_keep)
    ffn_got = ffn_got + [core_swap(value) for value in ffn_got]
    ffn_kept = [
        gather_tiles(ffn_got, ffn_keep[:ffn_half]),
        gather_tiles(ffn_got, ffn_keep[ffn_half:]),
    ]
    ffn_kept, attn_kept = lax.optimization_barrier((ffn_kept, attn_kept))
    ffn_all = [lax.all_gather(value, "seq", axis=0, tiled=True) for value in ffn_kept]
    attn_all = [attn_kept] + [chip_shift(attn_kept, offset) for offset in range(1, chips)]
    attn_all = attn_all + [core_swap(value) for value in attn_all]

    attn_all, ffn_all[0] = lax.optimization_barrier((attn_all, ffn_all[0]))

    def fetch(arrays, index, to, me, place, columns_of):
        def fast():
            return join_tiles(arrays, index, row_blocks, columns_of)

        def slow():
            whole = lax.all_to_all(
                jnp.broadcast_to(master_low[None], (seq_size * fsdp_size,) + master_low.shape),
                ("seq", "fsdp"),
                split_axis=0,
                concat_axis=0,
                tiled=True,
            ).reshape(-1, tile, tile)
            count = row_blocks * sum(columns_of)
            slots = pick(
                (to.reshape(1, -1) == me) & (place.reshape(1, -1) == jnp.arange(count)[:, None]),
                jnp.arange(tiles)[None, :],
            )
            return join_tiles([whole], slots, row_blocks, columns_of)

        return lax.cond(fits, fast, slow)

    w_first, w_out = fetch(
        attn_all, attn_join, attn_to, my_seq, attn_place, (attn_first, query_each)
    )
    gain_attn = gain_full[width : 2 * width]
    gain_laurel = gain_full[2 * width : 3 * width]
    gain_pre = gain_full[3 * width : 4 * width]
    gain_post = gain_full[4 * width : 5 * width]
    gain_vec = gain_full[5 * width : 6 * width]
    gain_query = gain_full[6 * width : 6 * width + HEAD_DIM]
    gain_key = gain_full[6 * width + HEAD_DIM : 6 * width + 2 * HEAD_DIM]
    stream = own_tokens.astype(f32)
    vectors = layer_vectors[0].astype(f32)
    normed, normed_pull = jax.vjp(rms_norm, stream, gain_in)
    normed_low = normed.astype(bf16)
    first_pre = matmul(pack_normed, w_first)
    is_key = my_seq % per_key == 0

    def shape_query(query_in, query_gain):
        value = rms_norm(query_in.reshape(length, per_device, HEAD_DIM), query_gain)
        return turn(value, cosine, sine)

    def shape_key(key_in, key_gain):
        return turn(rms_norm(key_in.reshape(length, 1, HEAD_DIM), key_gain), cosine, sine)

    query_pre = first_pre[:, : per_device * HEAD_DIM]
    other_pre = first_pre[:, per_device * HEAD_DIM :]
    query_rot, query_pull = jax.vjp(shape_query, query_pre, gain_query)
    key_rot, key_pull = jax.vjp(shape_key, other_pre, gain_key)
    query_heads = query_rot.astype(bf16)
    other_low = jnp.where(is_key, key_rot[:, 0, :], other_pre).astype(bf16)
    partner_low = seq_swap(other_low, 1).reshape(seq_size // 2, 2, rows, HEAD_DIM)
    partner_low = partner_low[:, ::-1].reshape(length, HEAD_DIM)
    key_single = jnp.where(is_key, other_low, partner_low)
    value_single = jnp.where(is_key, partner_low, other_low)

    raw = (
        jnp.einsum("qhd,kd->qhk", query_heads, key_single, preferred_element_type=f32) * SCALE
    )
    scores = jnp.where(allow[:, None, :], raw, NEGATIVE)
    powers = jnp.exp(scores - jnp.max(scores, axis=-1, keepdims=True))
    prob = powers / jnp.sum(powers, axis=-1, keepdims=True)
    prob_low = prob.astype(bf16)
    attended_low = (
        jnp.einsum("qhk,kd->qhd", prob_low, value_single, preferred_element_type=f32)
        .astype(bf16)
        .reshape(length, per_device * HEAD_DIM)
    )
    attn_pre = seq_sum(matmul_flip(attended_low, w_out), bf16)
    attn_pre, small_table = lax.optimization_barrier((attn_pre, small_table))
    laurel_left = small_table[:, :RANK]
    laurel_right = small_table[:, RANK : 2 * RANK]
    vector_gate_w = small_table[:, 2 * RANK : 2 * RANK + PLD]
    vector_proj_w = small_table[:, 2 * RANK + PLD :]

    attn_normed, attn_pull = jax.vjp(rms_norm, attn_pre, gain_attn)
    first_sum = stream + attn_normed
    left_pre = matmul(normed_low, laurel_left)
    left_low = left_pre.astype(bf16)
    right_pre = matmul_flip(left_low, laurel_right)
    laurel_normed, laurel_pull = jax.vjp(rms_norm, right_pre, gain_laurel)
    second_sum = (first_sum + normed + laurel_normed) * ROOT_HALF
    feed_normed, feed_pull = jax.vjp(rms_norm, second_sum, gain_pre)
    feed_own = feed_normed.astype(bf16)
    feed_low = lax.all_gather(feed_own, "fsdp", axis=0, tiled=True)
    ffn_all, _ = lax.optimization_barrier((ffn_all, feed_own))
    w_both, w_down = fetch(
        ffn_all, ffn_join, ffn_to, my_fsdp, ffn_place, (ffn_first, ffn_each)
    )
    both_pre = matmul(feed_low, w_both)
    ffn_width = w_down.shape[1]
    hidden, hidden_pull = jax.vjp(gelu_product, both_pre[:, :ffn_width], both_pre[:, ffn_width:])
    hidden_low = hidden.astype(bf16)
    down_pre = lax.psum_scatter(
        matmul_flip(hidden_low, w_down).astype(bf16), "fsdp", scatter_dimension=0, tiled=True
    ).astype(f32)
    down_normed, down_pull = jax.vjp(rms_norm, down_pre, gain_post)
    third_sum = second_sum + down_normed
    third_low = third_sum.astype(bf16)
    vector_pre = matmul(third_low, vector_gate_w)
    vector_gated, vector_pull = jax.vjp(lambda inner: gelu_product(inner, vectors), vector_pre)
    vector_low = vector_gated.astype(bf16)
    proj_pre = matmul_flip(vector_low, vector_proj_w)
    proj_normed, proj_pull = jax.vjp(rms_norm, proj_pre, gain_vec)
    result = third_sum + proj_normed
    output = result.astype(bf16)[None]

    grad_out = cotangent[0].astype(f32)
    grad_proj, grad_gain_vec = proj_pull(grad_out)
    proj_grad_low = grad_proj.astype(bf16)
    (grad_vector_pre,) = vector_pull(matmul(proj_grad_low, vector_proj_w))
    vector_grad_low = grad_vector_pre.astype(bf16)
    grad_third = grad_out + matmul_flip(vector_grad_low, vector_gate_w)
    grad_down, grad_gain_post = down_pull(grad_third)
    down_grad_low = lax.all_gather(grad_down.astype(bf16), "fsdp", axis=0, tiled=True)
    grad_gate, grad_up = hidden_pull(matmul(down_grad_low, w_down))
    both_grad_low = jnp.concatenate([grad_gate, grad_up], axis=1).astype(bf16)

    early_full = jnp.concatenate(
        [matmul_outer(third_low, vector_grad_low), matmul_outer(proj_grad_low, vector_low)], axis=1
    )
    small_early = small_sum(split_tiles(early_full, tile).reshape(-1, tile))
    feed_part = matmul_flip(both_grad_low, w_both).astype(bf16)
    feed_part, small_early = lax.optimization_barrier((feed_part, small_early))
    grad_feed = lax.psum_scatter(feed_part, "fsdp", scatter_dimension=0, tiled=True).astype(f32)
    both_grad_w = matmul_outer(feed_low, both_grad_low).astype(bf16)
    down_grad_w = matmul_outer(down_grad_low, hidden_low).astype(bf16)
    ffn_parts = [
        cut_tiles([both_grad_w, down_grad_w], index.reshape(-1), tile)
        for index in (ffn_cut[:, :ffn_half], ffn_cut[:, ffn_half:])
    ]
    ffn_parts, grad_feed = lax.optimization_barrier((ffn_parts, grad_feed))
    ffn_sums = [
        lax.psum_scatter(value, "seq", scatter_dimension=0, tiled=True) for value in ffn_parts
    ]

    grad_second_norm, grad_gain_pre = feed_pull(grad_feed)
    half_grad = (grad_third + grad_second_norm) * ROOT_HALF
    grad_right, grad_gain_laurel = laurel_pull(half_grad)
    right_grad_low = grad_right.astype(bf16)
    left_grad_low = matmul(right_grad_low, laurel_right).astype(bf16)
    grad_attn, grad_gain_attn = attn_pull(half_grad)
    attn_grad_low = seq_gather(grad_attn.astype(bf16))
    grad_attended = (
        matmul(attn_grad_low, w_out).astype(bf16).reshape(length, per_device, HEAD_DIM)
    )
    out_grad_w = matmul_outer(attn_grad_low, attended_low).astype(bf16)
    value_grad = jnp.einsum("qhk,qhd->kd", prob_low, grad_attended, preferred_element_type=f32)
    grad_prob = jnp.einsum("qhd,kd->qhk", grad_attended, value_single, preferred_element_type=f32)
    inner = jnp.sum(prob * grad_prob, axis=-1, keepdims=True)
    grad_score = (prob * (grad_prob - inner)).astype(bf16)
    grad_query = (
        jnp.einsum("qhk,kd->qhd", grad_score, key_single, preferred_element_type=f32) * SCALE
    ).astype(bf16)
    key_grad = (
        jnp.einsum("qhk,qhd->kd", grad_score, query_heads, preferred_element_type=f32) * SCALE
    ).astype(bf16)
    value_grad = value_grad.astype(bf16)
    partner_grad = seq_swap(jnp.where(is_key, value_grad, key_grad), 1)
    partner_grad = partner_grad.reshape(seq_size // 2, 2, rows, HEAD_DIM)[:, ::-1]
    other_grad = jnp.where(is_key, key_grad, value_grad).astype(f32) + partner_grad.reshape(
        length, HEAD_DIM
    ).astype(f32)
    grad_query_pre, grad_gain_query = query_pull(grad_query.astype(f32))
    grad_key_pre, grad_gain_key = key_pull(other_grad[:, None, :])
    grad_gain_key = jnp.where(is_key, grad_gain_key, 0.0)
    first_grad_low = jnp.concatenate(
        [grad_query_pre, jnp.where(is_key, grad_key_pre, other_grad)], axis=1
    ).astype(bf16)
    first_grad_w = matmul_outer(pack_normed, first_grad_low).astype(bf16)
    near = (my_chip + shifts) % chips
    near_key = take_blocks(attn_key_chip, near)[:, None, :]
    near_order = take_blocks(attn_order_chip, near)[:, None, :]
    near_place = take_blocks(by_chip(attn_place), near)[:, None, :]

    def attn_cut(core):
        index = pick(
            (near_key == 2 * my_seq + core)
            & (near_order == jnp.arange(attn_hold)[None, :, None]),
            near_place,
        )
        return cut_tiles([first_grad_w, out_grad_w], index.reshape(-1), tile)

    attn_given, attn_own = attn_cut(1 - my_core), attn_cut(my_core)
    attn_given, attn_own, ffn_sums[0] = lax.optimization_barrier(
        (attn_given, attn_own, ffn_sums[0])
    )
    attn_parts = added(attn_own, core_swap(attn_given)).reshape(chips, attn_hold, tile, tile)
    attn_sum = attn_parts[0]
    attn_parts = [attn_parts[offset].astype(bf16) for offset in range(1, chips)]
    normed_sum = seq_sum(matmul_flip(first_grad_low, w_first), bf16)
    attn_sum, attn_parts, normed_sum = lax.optimization_barrier((attn_sum, attn_parts, normed_sum))
    for offset in range(1, chips):
        attn_sum = attn_sum + chip_shift(attn_parts[offset - 1], offset).astype(f32)
    attn_sum = attn_sum.astype(bf16)
    attn_back = pick(
        (column_slots[3][None, None, :] == (my_seq ^ flips)[:, None, None])
        & (column_slots[0][None, None, :] == my_key)
        & (column_slots[2][None, None, :] == jnp.arange(attn_room)[None, :, None]),
        column_slots[1],
    )

    grad_normed = half_grad + matmul_flip(left_grad_low, laurel_left) + normed_sum
    grad_stream_norm, grad_gain_in = normed_pull(grad_normed)
    input_grad = (half_grad + grad_stream_norm)[None]
    gain_grad = jnp.concatenate(
        [
            grad_gain_in,
            grad_gain_attn,
            grad_gain_laurel,
            grad_gain_pre,
            grad_gain_post,
            grad_gain_vec,
            grad_gain_query,
            grad_gain_key,
        ]
    )
    late_full = jnp.concatenate(
        [matmul_outer(normed_low, left_grad_low), matmul_outer(right_grad_low, left_low)], axis=1
    )
    late = jnp.concatenate(
        [late_full.reshape(seq_size, -1), gain_grad.reshape(seq_size, -1)], axis=1
    ).reshape(seq_size, -1, tile)
    late = seq_sum(late.reshape(-1, tile), bf16, True)

    late = late.astype(bf16)
    ffn_sums, attn_sum, late, input_grad = lax.optimization_barrier(
        (ffn_sums, attn_sum, late, input_grad)
    )
    ffn_sums = ffn_sums + [core_swap(value) for value in ffn_sums]
    ffn_return = [gather_tiles(ffn_sums, ffn_back[i]) for i in range(chips)]
    ffn_return, attn_sum, late = lax.optimization_barrier((ffn_return, attn_sum, late))
    late = lax.psum(late, "fsdp").astype(f32)
    ffn_returned = chip_exchange(ffn_return)
    late_rows = late_full.shape[0] // seq_size
    late_tiles = late[:late_rows].reshape(-1, 1, tile, tile)
    gain_grad_mine = late[late_rows:].reshape(-1)
    small_grad = jnp.concatenate(
        [
            late_tiles.astype(bf16),
            small_early.reshape(late_tiles.shape[0], -1, tile, tile),
        ],
        axis=1,
    ).reshape(small_master.shape)
    attn_returned = seq_exchange([gather_tiles([attn_sum], attn_back[i]) for i in range(seq_size)])
    attn_returned = attn_returned + [core_swap(value) for value in attn_returned]
    slot_grad = jnp.where(my_slots[0] >= 0, my_slots[1], 2 * half + my_slots[2])

    def slow_return():
        own_ffn = split_tiles(both_grad_w, tile), split_tiles(down_grad_w, tile)
        own_attn = split_tiles(first_grad_w, tile), split_tiles(out_grad_w, tile)
        parts = jnp.concatenate(own_ffn + own_attn + (jnp.zeros((1, tile, tile), bf16),))
        index = jnp.where(
            ffn_to == my_fsdp,
            ffn_place,
            jnp.where(attn_to == my_seq, ffn_count + attn_place, ffn_count + attn_count),
        )
        spread = gather_tiles([parts], index.reshape(-1))
        spread = lax.all_to_all(
            spread.reshape((seq_size * fsdp_size, mine, tile, tile)),
            ("seq", "fsdp"),
            split_axis=0,
            concat_axis=0,
            tiled=True,
        )
        return jnp.sum(spread.astype(f32), axis=0).astype(bf16)

    slow_start = 2 * half + 2 * seq_size * attn_room
    slow_grads = lax.cond(fits, lambda: jnp.zeros((mine, tile, tile), bf16), slow_return)
    small_new, small_first_new, small_second_new = rotate_update(
        [small_grad],
        jnp.arange(small_master.shape[0]),
        small_master,
        small_first,
        small_second,
        small_left,
        small_right,
        RATE_SMALL,
    )
    ffn_returned, slow_grads, small_new = lax.optimization_barrier(
        (ffn_returned, slow_grads, small_new)
    )
    ffn_returned = ffn_returned + [core_swap(value) for value in ffn_returned]
    tile_grads = ffn_returned + attn_returned + [slow_grads]
    slot_grad = jnp.where(fits, slot_grad, slow_start + local_slots)

    tile_new, tile_first_new, tile_second_new = rotate_update(
        tile_grads, slot_grad, tile_master, tile_first, tile_second, left_basis, right_basis, RATE_TILE
    )
    gain_first_new = BETA_ONE * gain_first + (1.0 - BETA_ONE) * gain_grad_mine
    gain_second_new = BETA_TWO * gain_second + (1.0 - BETA_TWO) * gain_grad_mine * gain_grad_mine
    correct_one = 1.0 - BETA_ONE**STEP
    correct_two = 1.0 - BETA_TWO**STEP
    gain_new = gains - RATE_GAIN * (gain_first_new / correct_one) / (
        jnp.sqrt(gain_second_new / correct_two) + ADAM_EPS
    )
    return (
        output,
        input_grad,
        tile_new,
        tile_first_new,
        tile_second_new,
        small_new,
        small_first_new,
        small_second_new,
        gain_new,
        gain_first_new,
        gain_second_new,
    )


def solution(mesh):
    return jax.shard_map(
        on_device,
        mesh=mesh,
        in_specs=(
            P("fsdp", "seq", None),
            P("fsdp", "seq", None),
            P("fsdp", None),
            P("fsdp", "seq", None),
            P(),
            P(("seq", "fsdp"), None, None),
            P(("seq", "fsdp"), None, None),
            P(("seq", "fsdp"), None, None),
            P(("seq", "fsdp"), None, None),
            P(("seq", "fsdp"), None, None),
            P("seq", None, None),
            P("seq", None, None),
            P("seq", None, None),
            P("seq", None, None),
            P("seq", None, None),
            P("seq"),
            P("seq"),
            P("seq"),
        ),
        out_specs=(
            P("fsdp", "seq", None),
            P("fsdp", "seq", None),
            P(("seq", "fsdp"), None, None),
            P(("seq", "fsdp"), None, None),
            P(("seq", "fsdp"), None, None),
            P("seq", None, None),
            P("seq", None, None),
            P("seq", None, None),
            P("seq"),
            P("seq"),
            P("seq"),
        ),
        check_vma=False,
    )
```

```python
import math

import jax
import jax.numpy as jnp
from jax import lax
from jax.experimental import pallas as pl
from jax.experimental.pallas import tpu as pltpu
from jax.sharding import PartitionSpec as P

HEADS = 8
KV_HEADS = 2
HEAD_DIM = 256
FF = 8192
RANK = 64
PLD = 256
STEP = 5


EPS = 1e-06
SCALE = 0.0625
THETA = 1000000.0
ROOT_HALF = 0.7071067811865476
BETA_ONE = 0.5
BETA_TWO = 0.5
ADAM_EPS = 1e-08
RATE_TILE = 0.02
RATE_SMALL = 0.04
RATE_GAIN = 0.3
DECAY = 0.01
NEGATIVE = -1e30
VMEM_BYTES = 32 * 1024 * 1024


def rms_norm(value, gain):
    return value * lax.rsqrt(jnp.mean(value * value, axis=-1, keepdims=True) + EPS) * gain


def rotary(value, position):
    half = value.shape[-1] // 2
    freq = THETA ** (-2.0 * jnp.arange(half).astype(jnp.float32) / value.shape[-1])
    angle = position.astype(jnp.float32)[:, None] * freq[None, :]
    cosine = jnp.cos(angle)[:, None, :]
    sine = jnp.sin(angle)[:, None, :]
    first = value[..., :half]
    second = value[..., half:]
    return jnp.concatenate(
        [first * cosine - second * sine, second * cosine + first * sine], axis=-1
    )


def documents(lengths, length):
    places = jnp.arange(length)
    ends = jnp.cumsum(lengths)
    passed = places[:, None] >= ends[None, :]
    segment = jnp.sum(passed.astype(jnp.int32), axis=1)
    before = jnp.sum(jnp.where(passed, lengths[None, :], 0), axis=1)
    return (segment, places - before)


def matmul(left, right):
    return jnp.dot(left, right, preferred_element_type=jnp.float32)


def matmul_flip(left, right):
    return lax.dot_general(
        left, right, (((1,), (1,)), ((), ())), preferred_element_type=jnp.float32
    )


def matmul_outer(left, right):
    return lax.dot_general(
        left, right, (((0,), (0,)), ((), ())), preferred_element_type=jnp.float32
    )


def assemble(tiles, row_blocks):
    size = tiles.shape[1]
    column_blocks = tiles.shape[0] // row_blocks
    return (
        tiles.reshape(row_blocks, column_blocks, size, size)
        .transpose(0, 2, 1, 3)
        .reshape(row_blocks * size, column_blocks * size)
    )


def split_tiles(matrix, size):
    row_blocks = matrix.shape[0] // size
    column_blocks = matrix.shape[1] // size
    return (
        matrix.reshape(row_blocks, size, column_blocks, size)
        .transpose(0, 2, 1, 3)
        .reshape(row_blocks * column_blocks, size, size)
    )


def gelu_product(first, second):
    return jax.nn.gelu(first, approximate=True) * second


def room(count, share):
    mean = count * share
    return math.ceil(mean + 3.6 * math.sqrt(mean * (1.0 - share)) + 3.0)


def count_earlier(group, valid):
    size = group.shape[-1]
    order = jnp.arange(size)
    same = (group[..., :, None] == group[..., None, :]) & valid[..., None, :]
    same = same & (order[None, :] < order[:, None])
    return jnp.sum(same.astype(jnp.int32), axis=-1)


def count_long(keys):
    groups, size = keys.shape

    def kernel(row_ref, column_ref, out_ref):
        row = row_ref[0]
        column = column_ref[0]
        here = lax.broadcasted_iota(jnp.int32, (size, size), 1)
        other = lax.broadcasted_iota(jnp.int32, (size, size), 0)
        earlier = (column == row) & (other < here)
        out_ref[0] = jnp.sum(earlier.astype(jnp.int32), axis=0, keepdims=True)

    return pl.pallas_call(
        kernel,
        grid=(groups,),
        out_shape=jax.ShapeDtypeStruct((groups, 1, size), jnp.int32),
        in_specs=[
            pl.BlockSpec((1, 1, size), lambda i: (i, 0, 0)),
            pl.BlockSpec((1, size, 1), lambda i: (i, 0, 0)),
        ],
        out_specs=pl.BlockSpec((1, 1, size), lambda i: (i, 0, 0)),
        cost_estimate=pl.CostEstimate(flops=0, transcendentals=0, bytes_accessed=0),
        compiler_params=pltpu.CompilerParams(vmem_limit_bytes=VMEM_BYTES),
    )(keys[:, None, :], keys[:, :, None]).reshape(groups, size)


def pick(match, value):
    return jnp.sum(jnp.where(match, value, 0), axis=-1)


def steps_of(count):
    for steps in range(4, 129):
        if count % steps == 0 and 16 <= count // steps <= 66:
            return steps
    return 2 if count % 2 == 0 else 1


def tile_kernel_call(kernel, index, arrays, out_shape, out_specs, steps):
    moved = sum(math.prod(one.shape) * 2 for one in jax.tree.leaves(out_shape))
    return pl.pallas_call(
        kernel,
        grid=(steps,),
        cost_estimate=pl.CostEstimate(flops=0, transcendentals=0, bytes_accessed=2 * moved),
        out_shape=out_shape,
        in_specs=[pl.BlockSpec(memory_space=pltpu.SMEM)]
        + [pl.BlockSpec(memory_space=pl.ANY)] * len(arrays),
        out_specs=out_specs,
        scratch_shapes=[pltpu.SemaphoreType.DMA],
        compiler_params=pltpu.CompilerParams(vmem_limit_bytes=VMEM_BYTES),
    )(index, *arrays)


def start_copy(sources, place, target, sem, start=0):
    if len(sources) == 1:
        pltpu.make_async_copy(sources[0].at[place - start], target, sem).start()
        return
    half = len(sources) // 2
    middle = start + sum(ref.shape[0] for ref in sources[:half])

    @pl.when(place < middle)
    def _():
        start_copy(sources[:half], place, target, sem, start)

    @pl.when(place >= middle)
    def _():
        start_copy(sources[half:], place, target, sem, middle)


def gather_tiles(arrays, index):
    tile = arrays[0].shape[-1]
    count = index.shape[0]
    steps = steps_of(count)
    each = count // steps

    def kernel(index_ref, *refs):
        sources, out, sem = refs[:-2], refs[-2], refs[-1]
        base = pl.program_id(0) * each

        def step(i, carry):
            start_copy(sources, index_ref[base + i], out.at[i], sem)
            return carry

        lax.fori_loop(0, each, step, 0)
        pltpu.make_async_copy(out, out, sem).wait()

    total = sum(array.shape[0] for array in arrays)
    return tile_kernel_call(
        kernel,
        jnp.clip(index, 0, total - 1),
        arrays,
        jax.ShapeDtypeStruct((count, tile, tile), arrays[0].dtype),
        pl.BlockSpec((each, tile, tile), lambda i: (i, 0, 0)),
        steps,
    )


def join_tiles(arrays, index, row_blocks, columns):
    tile = arrays[0].shape[-1]
    steps = 4
    each = row_blocks // steps

    def kernel(index_ref, *refs):
        sources, outs, sem = refs[: len(arrays)], refs[len(arrays) : -1], refs[-1]
        base = pl.program_id(0) * each
        start = 0
        for out, width in zip(outs, columns):

            def step(i, carry, out=out, start=start, width=width):
                row = i // width
                column = i - row * width
                target = out.at[
                    pl.ds(pl.multiple_of(row * tile, tile), tile),
                    pl.ds(pl.multiple_of(column * tile, tile), tile),
                ]
                start_copy(sources, index_ref[start + base * width + i], target, sem)
                return carry

            lax.fori_loop(0, each * width, step, 0)
            start = start + row_blocks * width
        for out in outs:
            pltpu.make_async_copy(out, out, sem).wait()

    total = sum(array.shape[0] for array in arrays)
    out_shape = tuple(
        jax.ShapeDtypeStruct((row_blocks * tile, width * tile), arrays[0].dtype)
        for width in columns
    )
    out_specs = tuple(pl.BlockSpec((each * tile, width * tile), lambda i: (i, 0)) for width in columns)
    return tile_kernel_call(
        kernel, jnp.clip(index, 0, total - 1), arrays, out_shape, out_specs, steps
    )


def cut_tiles(matrices, index, tile):
    row_blocks = matrices[0].shape[0] // tile
    widths = [matrix.shape[1] // tile for matrix in matrices]
    count = index.shape[0]
    steps = steps_of(count)
    each = count // steps

    def kernel(index_ref, *refs):
        sources, out, sem = refs[:-2], refs[-2], refs[-1]
        base = pl.program_id(0) * each

        def step(i, carry):
            place = index_ref[base + i]
            start = 0
            for ref, width in zip(sources, widths):
                size = row_blocks * width

                @pl.when((place >= start) & (place < start + size))
                def _(ref=ref, start=start, width=width):
                    row = (place - start) // width
                    column = place - start - row * width
                    source = ref.at[
                        pl.ds(pl.multiple_of(row * tile, tile), tile),
                        pl.ds(pl.multiple_of(column * tile, tile), tile),
                    ]
                    pltpu.make_async_copy(source, out.at[i], sem).start()

                start = start + size
            return carry

        lax.fori_loop(0, each, step, 0)
        pltpu.make_async_copy(out, out, sem).wait()

    return tile_kernel_call(
        kernel,
        jnp.clip(index, 0, row_blocks * sum(widths) - 1),
        matrices,
        jax.ShapeDtypeStruct((count, tile, tile), matrices[0].dtype),
        pl.BlockSpec((each, tile, tile), lambda i: (i, 0, 0)),
        steps,
    )


def split_low(value):
    high = value.astype(jnp.bfloat16)
    return high, (value - high.astype(jnp.float32)).astype(jnp.bfloat16)


def rotate_update(grads, index, master, first, second, left, right, rate):
    count, tile, _ = master.shape
    each = 4 if count % 4 == 0 else 1
    correct_one = 1.0 - BETA_ONE**STEP
    correct_two = 1.0 - BETA_TWO**STEP

    def product(one, two, dims):
        return lax.dot_general(one, two, (dims, ((), ())), preferred_element_type=jnp.float32)

    def kernel(index_ref, *refs):
        sources, refs = refs[: len(grads)], refs[len(grads) :]
        master_ref, first_ref, second_ref, left_ref, right_ref = refs[:5]
        master_out, first_out, second_out, held, sems = refs[5:]
        now = pl.program_id(0)

        @pl.when(now == 0)
        def _():
            def step(i, carry):
                start_copy(sources, index_ref[i], held.at[i], sems.at[i // each])
                return carry

            lax.fori_loop(0, count, step, 0)

        block = held.at[pl.ds(now * each, each)]
        pltpu.make_async_copy(block, block, sems.at[now]).wait()
        lefts, rights, turns = [], [], []
        for i in range(each):
            grad = held[now * each + i]
            lefts.append(split_low(left_ref[i]))
            rights.append(split_low(right_ref[i]))
            half_turned = product(
                jnp.concatenate([grad, grad], axis=1),
                jnp.concatenate(rights[i], axis=0),
                ((1,), (0,)),
            )
            turns.append(split_low(half_turned))
        for i in range(each):
            (left_high, left_low), (high, low) = lefts[i], turns[i]
            turns[i] = product(
                jnp.concatenate([left_high, left_high, left_low], axis=0),
                jnp.concatenate([high, low, high], axis=0),
                ((0,), (0,)),
            )
        for i in range(each):
            right_high, right_low = rights[i]
            first_new = BETA_ONE * first_ref[i] + (1.0 - BETA_ONE) * turns[i]
            second_new = BETA_TWO * second_ref[i] + (1.0 - BETA_TWO) * turns[i] * turns[i]
            first_out[i] = first_new
            second_out[i] = second_new
            high, low = split_low(
                first_new / correct_one / (jnp.sqrt(second_new / correct_two) + ADAM_EPS)
            )
            half_back = product(
                jnp.concatenate([high, low, high], axis=1),
                jnp.concatenate([right_high, right_high, right_low], axis=1),
                ((1,), (1,)),
            )
            turns[i] = split_low(half_back)
        for i in range(each):
            (left_high, left_low), (high, low) = lefts[i], turns[i]
            back = product(
                jnp.concatenate([left_high, left_high, left_low], axis=1),
                jnp.concatenate([high, low, high], axis=0),
                ((1,), (0,)),
            )
            weight = master_ref[i]
            master_out[i] = weight - rate * (back + DECAY * weight)

    spec = pl.BlockSpec((each, tile, tile), lambda i: (i, 0, 0))
    shape = jax.ShapeDtypeStruct(master.shape, jnp.float32)
    total = sum(array.shape[0] for array in grads)
    return pl.pallas_call(
        kernel,
        grid=(count // each,),
        out_shape=(shape, shape, shape),
        in_specs=[pl.BlockSpec(memory_space=pltpu.SMEM)]
        + [pl.BlockSpec(memory_space=pl.ANY)] * len(grads)
        + [spec] * 5,
        out_specs=(spec, spec, spec),
        scratch_shapes=[
            pltpu.VMEM((count, tile, tile), jnp.bfloat16),
            pltpu.SemaphoreType.DMA((count // each,)),
        ],
        compiler_params=pltpu.CompilerParams(vmem_limit_bytes=VMEM_BYTES),
    )(jnp.clip(index, 0, total - 1), *grads, master, first, second, left, right)


def seq_swap(value, flip):
    size = lax.axis_size("seq")
    return lax.ppermute(value, "seq", [(i, i ^ flip) for i in range(size)])


def take_blocks(value, order):
    return jnp.stack(
        [lax.dynamic_index_in_dim(value, order[i], 0, False) for i in range(order.shape[0])]
    )


def core_swap(value):
    size = lax.axis_size("fsdp")
    return lax.ppermute(value, "fsdp", [(i, i ^ 1) for i in range(size)])


def chip_shift(value, offset):
    size = lax.axis_size("fsdp")
    chips = size // 2
    return lax.ppermute(
        value, "fsdp", [(i, (i // 2 + offset) % chips * 2 + i % 2) for i in range(size)]
    )


def seq_gather(value):
    size = lax.axis_size("seq")
    return jnp.concatenate([value] + [seq_swap(value, flip) for flip in range(1, size)], axis=0)


def seq_ordered(value):
    size = lax.axis_size("seq")
    parts = jnp.stack([value] + [seq_swap(value, flip) for flip in range(1, size)], axis=0)
    return take_blocks(parts, lax.axis_index("seq") ^ jnp.arange(size))


def seq_exchange(values):
    return [values[0]] + [seq_swap(values[flip], flip) for flip in range(1, len(values))]


def seq_sum(value, wire, ordered=False):
    size = lax.axis_size("seq")
    parts = value.reshape((size, value.shape[0] // size) + value.shape[1:])
    if ordered:
        parts = take_blocks(parts, lax.axis_index("seq") ^ jnp.arange(size))
    total = parts[0]
    for flip in range(1, size):
        total = total + seq_swap(parts[flip].astype(wire), flip).astype(jnp.float32)
    return total


def chip_exchange(values):
    return [values[0]] + [chip_shift(values[offset], offset) for offset in range(1, len(values))]


def core_pair(value):
    other = core_swap(value)
    even = lax.axis_index("fsdp") % 2 == 0
    return jnp.where(even, jnp.stack([value, other]), jnp.stack([other, value]))


def small_sum(value):
    seq_size = lax.axis_size("seq")
    chips = lax.axis_size("fsdp") // 2
    chip = lax.axis_index("fsdp") // 2
    even = lax.axis_index("fsdp") % 2 == 0
    low = value.astype(jnp.bfloat16)
    parts = low.reshape((seq_size, 2, low.shape[0] // (2 * seq_size)) + low.shape[1:])
    kept = jnp.where(even, parts[:, 0], parts[:, 1]).astype(jnp.float32)
    given = jnp.where(even, parts[:, 1], parts[:, 0])
    kept = kept + core_swap(given).astype(jnp.float32)
    kept = seq_sum(kept.reshape((-1,) + low.shape[1:]), jnp.bfloat16, True)
    kept = kept.reshape((chips, kept.shape[0] // chips) + kept.shape[1:])
    kept = take_blocks(kept, (chip + jnp.arange(chips)) % chips)
    total = kept[0]
    for offset in range(1, chips):
        total = total + chip_shift(kept[offset].astype(jnp.bfloat16), offset).astype(jnp.float32)
    total = total.astype(jnp.bfloat16)
    parts = jnp.stack([total] + [chip_shift(total, offset) for offset in range(1, chips)])
    parts = take_blocks(parts, (chip - jnp.arange(chips)) % chips)
    return core_pair(parts).reshape((value.shape[0] // seq_size,) + value.shape[1:])


def turn(value, cosine, sine):
    half = value.shape[-1] // 2
    first, second = value[..., :half], value[..., half:]
    return jnp.concatenate(
        [first * cosine - second * sine, second * cosine + first * sine], axis=-1
    )


def added(one, two):
    return one.astype(jnp.float32) + two.astype(jnp.float32)


def on_device(
    tokens,
    layer_vectors,
    doc_lengths,
    cotangent,
    tile_owner,
    tile_master,
    tile_first,
    tile_second,
    left_basis,
    right_basis,
    small_master,
    small_first,
    small_second,
    small_left,
    small_right,
    gains,
    gain_first,
    gain_second,
):
    bf16 = jnp.bfloat16
    f32 = jnp.float32
    tile = tile_master.shape[1]
    width = tokens.shape[2]
    row_blocks = width // tile
    rows = tokens.shape[1]
    seq_size = lax.axis_size("seq")
    fsdp_size = lax.axis_size("fsdp")
    chips = fsdp_size // 2
    mine = tile_master.shape[0]
    tiles = tile_owner.shape[0]
    length = rows * seq_size
    per_device = HEADS // seq_size
    per_key = seq_size // KV_HEADS
    query_width = HEADS * HEAD_DIM
    key_width = KV_HEADS * HEAD_DIM
    my_seq = lax.axis_index("seq")
    my_fsdp = lax.axis_index("fsdp")
    my_chip = my_fsdp // 2
    my_core = my_fsdp % 2
    flips = jnp.arange(seq_size)
    shifts = jnp.arange(chips)

    query_blocks = query_width // tile
    key_blocks = key_width // tile
    ffn_blocks = FF // tile
    query_each = query_blocks // seq_size
    head_blocks = HEAD_DIM // tile
    ffn_each = ffn_blocks // fsdp_size
    columns = tiles // row_blocks
    attn_first = query_each + head_blocks
    attn_count = row_blocks * (attn_first + query_each)
    ffn_first = 2 * ffn_each
    ffn_count = row_blocks * 3 * ffn_each
    attn_share = (2 * query_blocks + 2 * key_blocks) / columns
    ffn_share = 3 * ffn_blocks / columns
    attn_room = (room(2 * mine, attn_share / seq_size) + 1) // 2
    attn_hold = (room(attn_count, 1.0 / chips) + 1) // 2 + 1
    ffn_room = (room(2 * mine, ffn_share / chips) + 1) // 2
    both_count = row_blocks * ffn_first
    ffn_hold = (room(ffn_count, 1.0 / seq_size) + 3) // 4 * 4
    ffn_half = ffn_hold * 3 // 7 // 4 * 4
    ffn_rest = ffn_hold - ffn_half

    def tile_places(owner):
        row = owner // columns
        column = owner % columns
        key_at = column - query_blocks
        value_at = key_at - key_blocks
        out_at = value_at - key_blocks
        ffn_at = out_at - query_blocks
        is_attn = ffn_at < 0
        kind = ffn_at // ffn_blocks
        ffn_column = ffn_at % ffn_blocks
        ffn_to = jnp.where(is_attn, -1, ffn_column // ffn_each)
        ffn_local = ffn_column % ffn_each
        ffn_place = jnp.where(
            kind == 2,
            both_count + row * ffn_each + ffn_local,
            row * ffn_first + kind * ffn_each + ffn_local,
        )
        attn_to = jnp.where(
            key_at < 0,
            column // query_each,
            jnp.where(
                value_at < 0,
                key_at // head_blocks * per_key,
                jnp.where(
                    out_at < 0,
                    value_at // head_blocks * per_key + per_key - 1,
                    out_at // query_each,
                ),
            ),
        )
        attn_place = jnp.where(
            key_at < 0,
            row * attn_first + column % query_each,
            jnp.where(
                out_at < 0,
                row * attn_first + query_each + key_at % head_blocks,
                row_blocks * attn_first + row * query_each + out_at % query_each,
            ),
        )
        attn_to = jnp.where(is_attn, attn_to, -1)
        return (ffn_to, ffn_place, attn_to, attn_place)

    owners = tile_owner.reshape(seq_size, fsdp_size, mine)
    slot_seq = jnp.arange(seq_size)[:, None, None]
    slot_fsdp = jnp.arange(fsdp_size)[None, :, None]
    slot_chip = slot_fsdp // 2
    local_slots = jnp.arange(mine)
    both_slots = jnp.arange(2 * mine)
    both_slots = jnp.where(
        both_slots // mine == my_core, both_slots % mine, mine + both_slots % mine
    )

    ffn_to = tile_places(owners)[0]
    ffn_chip = jnp.where(ffn_to < 0, -1, ffn_to // 2)
    chip_view = ffn_chip.reshape(seq_size, chips, 2 * mine)
    chip_rank = count_earlier(chip_view, chip_view >= 0).reshape(owners.shape)
    ffn_slots = lax.dynamic_slice(
        jnp.stack([ffn_chip, chip_rank]), (0, my_seq, 2 * my_chip, 0), (2, 1, 2, mine)
    ).reshape(2, 1, 1, 2 * mine)
    ffn_pack = pick(
        (ffn_slots[0] == ((my_chip + shifts) % chips)[:, None, None])
        & (ffn_slots[1] == (my_core * ffn_room + jnp.arange(ffn_room))[None, :, None]),
        both_slots,
    )
    master_low = tile_master.astype(bf16)
    masters = [master_low, core_swap(master_low)]
    ffn_sent = [gather_tiles(masters, ffn_pack[i]) for i in range(chips)]
    small_rows = small_master.shape[0] // 2
    small_half = lax.dynamic_slice_in_dim(small_master, my_core * small_rows, small_rows)
    masters, ffn_sent, chip_rank, owners, own_tokens, own_gains, small_half = (
        lax.optimization_barrier(
            (
                masters,
                ffn_sent,
                chip_rank,
                owners,
                tokens[0],
                gains.astype(bf16),
                small_half.astype(bf16),
            )
        )
    )
    ffn_got = chip_exchange(ffn_sent)

    ffn_to, ffn_place, attn_to, attn_place = tile_places(owners)
    ffn_chip = jnp.where(ffn_to < 0, -1, ffn_to // 2)
    attn_view = attn_to.reshape(seq_size, chips, 2 * mine)
    attn_rank = count_earlier(attn_view, attn_view >= 0).reshape(owners.shape)
    attn_core = (attn_rank + slot_seq) % 2
    attn_rank = attn_rank // 2
    attn_key = jnp.where(attn_to < 0, -1, 2 * attn_to + attn_core)

    chip_slots = lax.dynamic_slice(
        jnp.stack([attn_key, attn_rank]), (0, my_seq, 2 * my_chip, 0), (2, 1, 2, mine)
    ).reshape(2, 1, 1, 2 * mine)
    attn_message = attn_room + row_blocks * rows // tile + small_rows + -(-own_gains.shape[0] // tile**2)
    attn_pack = pick(
        (chip_slots[0] == (2 * (my_seq ^ flips) + my_core)[:, None, None])
        & (chip_slots[1] == jnp.arange(attn_room)[None, :, None]),
        both_slots,
    )
    attn_sent = gather_tiles(masters, attn_pack.reshape(-1))
    attn_sent = attn_sent.reshape(seq_size, attn_room, tile, tile)
    seq_view = ffn_to.reshape(seq_size, fsdp_size * mine)
    ffn_rank = count_long(seq_view).reshape(owners.shape)
    def by_chip(value):
        value = value.reshape(seq_size, chips, 2 * mine).transpose(1, 0, 2)
        return value.reshape(chips, seq_size * 2 * mine)

    attn_key_chip = by_chip(attn_key)
    attn_order_chip = count_long(attn_key_chip)
    attn_order = (
        attn_order_chip.reshape(chips, seq_size, 2 * mine).transpose(1, 0, 2).reshape(owners.shape)
    )
    fits = jnp.all(
        jnp.where(
            ffn_to < 0,
            (attn_rank < attn_room) & (attn_order < attn_hold),
            (chip_rank < 2 * ffn_room) & (ffn_rank < ffn_hold),
        )
    )
    half = chips * ffn_room
    rows_late = 2 * RANK * row_blocks // seq_size
    rank_core = chip_rank // ffn_room
    rank_local = chip_rank % ffn_room
    out_place = (
        jnp.where(rank_core == my_core, 0, half)
        + (my_chip - slot_chip) % chips * ffn_room
        + rank_local
    )
    late_count = -(-(rows_late + own_gains.shape[0] // tile) // (2 * tile))
    return_size = ffn_room + late_count
    back_place = (
        jnp.where(rank_core == my_core, 0, chips * return_size)
        + (my_chip - ffn_chip) % chips * return_size
        + rank_local
    )
    attn_back_place = (
        jnp.where(attn_core == my_core, 0, seq_size * attn_room)
        + (attn_to ^ my_seq) * attn_room
        + attn_rank
    )
    my_slots = lax.dynamic_slice(
        jnp.stack([ffn_to, back_place, attn_back_place]), (0, my_seq, my_fsdp, 0), (3, 1, 1, mine)
    ).reshape(3, mine)
    seq_slots = lax.dynamic_slice(
        jnp.stack(
            [
                ffn_to,
                ffn_rank,
                ffn_chip,
                out_place,
                chip_rank,
                jnp.broadcast_to(slot_chip, owners.shape),
            ]
        ),
        (0, my_seq, 0, 0),
        (6, 1, fsdp_size, mine),
    ).reshape(6, fsdp_size * mine)
    column_slots = lax.dynamic_slice(
        jnp.stack([attn_key, attn_order, attn_rank, jnp.broadcast_to(slot_seq, owners.shape)]),
        (0, 0, 2 * my_chip, 0),
        (4, seq_size, 2, mine),
    ).reshape(4, 2 * seq_size * mine)
    my_key = 2 * my_seq + my_core

    attn_keep = pick(
        (column_slots[0][None, :] == my_key)
        & (column_slots[1][None, :] == jnp.arange(attn_hold)[:, None]),
        jnp.where(
            column_slots[3] == my_seq,
            0,
            attn_room + ((column_slots[3] ^ my_seq) - 1) * attn_message,
        )
        + column_slots[2],
    )
    attn_join = pick(
        (attn_to.reshape(1, -1) == my_seq)
        & (attn_place.reshape(1, -1) == jnp.arange(attn_count)[:, None]),
        (
            jnp.where(attn_core == my_core, 0, chips * attn_hold)
            + (my_chip - slot_chip) % chips * attn_hold
            + attn_order
        ).reshape(1, -1),
    )
    ffn_keep = pick(
        (seq_slots[0][None, :] == my_fsdp) & (seq_slots[1][None, :] == jnp.arange(ffn_hold)[:, None]),
        seq_slots[3][None, :],
    )
    ffn_join = pick(
        (ffn_to.reshape(1, -1) == my_fsdp)
        & (ffn_place.reshape(1, -1) == jnp.arange(ffn_count)[:, None]),
        (
            jnp.where(
                ffn_rank < ffn_half,
                slot_seq * ffn_half + ffn_rank,
                seq_size * ffn_half + slot_seq * ffn_rest + ffn_rank - ffn_half,
            )
        ).reshape(1, -1),
    )
    ffn_cut = pick(
        (ffn_to.reshape(seq_size, 1, -1) == my_fsdp)
        & (ffn_rank.reshape(seq_size, 1, -1) == jnp.arange(ffn_hold)[None, :, None]),
        ffn_place.reshape(seq_size, 1, -1),
    )
    ffn_back = pick(
        (seq_slots[5][None, None, :] == ((my_chip + shifts) % chips)[:, None, None])
        & (seq_slots[2][None, None, :] == my_chip)
        & (seq_slots[4][None, None, :] == (my_core * ffn_room + jnp.arange(ffn_room))[None, :, None]),
        jnp.where(seq_slots[0] == my_fsdp, 0, ffn_hold) + seq_slots[1],
    )

    token_tiles = own_tokens.reshape(rows, row_blocks, tile).transpose(1, 0, 2)
    token_tiles = token_tiles.reshape(-1, tile, tile)
    gain_rows = own_gains.reshape(-1, tile)
    gain_tiles = jnp.pad(gain_rows, ((0, -gain_rows.shape[0] % tile), (0, 0))).reshape(-1, tile, tile)
    common = jnp.concatenate([token_tiles, small_half, gain_tiles])
    attn_got = [attn_sent[0]] + [
        seq_swap(jnp.concatenate([attn_sent[flip], common]), flip) for flip in range(1, seq_size)
    ]
    segment, position = documents(doc_lengths[0], length)
    places = ((my_seq ^ flips)[:, None] * rows + jnp.arange(rows)[None, :]).reshape(-1)

    def reorder(values):
        blocks = values.reshape(seq_size, rows)
        return jnp.concatenate(
            [lax.dynamic_index_in_dim(blocks, my_seq ^ i, 0, False) for i in range(seq_size)]
        )

    pack_segment = reorder(segment)
    allow = (pack_segment[:, None] == pack_segment[None, :]) & (
        places[None, :] <= places[:, None]
    )
    turns = jnp.arange(HEAD_DIM // 2).astype(f32)
    angle = reorder(position).astype(f32)[:, None] * (THETA ** (-2.0 * turns / HEAD_DIM))[None, :]
    cosine, sine = jnp.cos(angle)[:, None, :], jnp.sin(angle)[:, None, :]
    parts = [common] + [value[attn_room:] for value in attn_got[1:]]
    token_end = token_tiles.shape[0]
    small_end = token_end + small_rows

    def seq_order(value):
        return take_blocks(value, my_seq ^ flips)

    pack_tokens = jnp.concatenate(
        [
            part[:token_end].reshape(row_blocks, rows, tile).transpose(1, 0, 2).reshape(rows, width)
            for part in parts
        ]
    )
    gain_full = seq_order(
        jnp.stack([part[small_end:].reshape(-1, tile)[: gain_rows.shape[0]] for part in parts])
    )
    gain_full = gain_full.reshape(-1).astype(f32)
    gain_in = gain_full[0:width]
    pack_normed = rms_norm(pack_tokens.astype(f32), gain_in).astype(bf16)
    ready = (allow, cosine, sine, ffn_keep, attn_keep, pack_normed, gain_full)
    ffn_got, attn_got, parts, ready = lax.optimization_barrier((ffn_got, attn_got, parts, ready))
    allow, cosine, sine, ffn_keep, attn_keep, pack_normed, gain_full = ready
    gain_in = gain_full[0:width]
    small_got = core_pair(seq_order(jnp.stack([part[token_end:small_end] for part in parts])))
    small_got = small_got.transpose(1, 0, 2, 3, 4)
    small_table = assemble(small_got.reshape((-1,) + small_master.shape[1:]), row_blocks)
    attn_kept = gather_tiles(attn_got, attn_keep)
    ffn_got = ffn_got + [core_swap(value) for value in ffn_got]
    ffn_kept = [
        gather_tiles(ffn_got, ffn_keep[:ffn_half]),
        gather_tiles(ffn_got, ffn_keep[ffn_half:]),
    ]
    ffn_kept, attn_kept = lax.optimization_barrier((ffn_kept, attn_kept))
    ffn_all = [lax.all_gather(value, "seq", axis=0, tiled=True) for value in ffn_kept]
    attn_all = [attn_kept] + [chip_shift(attn_kept, offset) for offset in range(1, chips)]
    attn_all = attn_all + [core_swap(value) for value in attn_all]

    attn_all, ffn_all[0], attn_join = lax.optimization_barrier((attn_all, ffn_all[0], attn_join))

    def fetch(arrays, index, to, me, place, columns_of):
        def fast():
            return join_tiles(arrays, index, row_blocks, columns_of)

        def slow():
            whole = lax.all_to_all(
                jnp.broadcast_to(master_low[None], (seq_size * fsdp_size,) + master_low.shape),
                ("seq", "fsdp"),
                split_axis=0,
                concat_axis=0,
                tiled=True,
            ).reshape(-1, tile, tile)
            count = row_blocks * sum(columns_of)
            slots = pick(
                (to.reshape(1, -1) == me) & (place.reshape(1, -1) == jnp.arange(count)[:, None]),
                jnp.arange(tiles)[None, :],
            )
            return join_tiles([whole], slots, row_blocks, columns_of)

        return lax.cond(fits, fast, slow)

    w_first, w_out = fetch(
        attn_all, attn_join, attn_to, my_seq, attn_place, (attn_first, query_each)
    )
    gain_attn = gain_full[width : 2 * width]
    gain_laurel = gain_full[2 * width : 3 * width]
    gain_pre = gain_full[3 * width : 4 * width]
    gain_post = gain_full[4 * width : 5 * width]
    gain_vec = gain_full[5 * width : 6 * width]
    gain_query = gain_full[6 * width : 6 * width + HEAD_DIM]
    gain_key = gain_full[6 * width + HEAD_DIM : 6 * width + 2 * HEAD_DIM]
    stream = own_tokens.astype(f32)
    vectors = layer_vectors[0].astype(f32)
    normed, normed_pull = jax.vjp(rms_norm, stream, gain_in)
    normed_low = normed.astype(bf16)
    first_pre = matmul(pack_normed, w_first)
    is_key = my_seq % per_key == 0

    def shape_query(query_in, query_gain):
        value = rms_norm(query_in.reshape(length, per_device, HEAD_DIM), query_gain)
        return turn(value, cosine, sine)

    def shape_key(key_in, key_gain):
        return turn(rms_norm(key_in.reshape(length, 1, HEAD_DIM), key_gain), cosine, sine)

    query_pre = first_pre[:, : per_device * HEAD_DIM]
    other_pre = first_pre[:, per_device * HEAD_DIM :]
    query_rot, query_pull = jax.vjp(shape_query, query_pre, gain_query)
    key_rot, key_pull = jax.vjp(shape_key, other_pre, gain_key)
    query_heads = query_rot.astype(bf16)
    other_low = jnp.where(is_key, key_rot[:, 0, :], other_pre).astype(bf16)
    partner_low = seq_swap(other_low, 1).reshape(seq_size // 2, 2, rows, HEAD_DIM)
    partner_low = partner_low[:, ::-1].reshape(length, HEAD_DIM)
    key_single = jnp.where(is_key, other_low, partner_low)
    value_single = jnp.where(is_key, partner_low, other_low)

    raw = (
        jnp.einsum("qhd,kd->qhk", query_heads, key_single, preferred_element_type=f32) * SCALE
    )
    scores = jnp.where(allow[:, None, :], raw, NEGATIVE)
    powers = jnp.exp(scores - jnp.max(scores, axis=-1, keepdims=True))
    prob = powers / jnp.sum(powers, axis=-1, keepdims=True)
    prob_low = prob.astype(bf16)
    attended_low = (
        jnp.einsum("qhk,kd->qhd", prob_low, value_single, preferred_element_type=f32)
        .astype(bf16)
        .reshape(length, per_device * HEAD_DIM)
    )
    attn_pre = seq_sum(matmul_flip(attended_low, w_out), bf16)
    attn_pre, small_table, ffn_join = lax.optimization_barrier((attn_pre, small_table, ffn_join))
    laurel_left = small_table[:, :RANK]
    laurel_right = small_table[:, RANK : 2 * RANK]
    vector_gate_w = small_table[:, 2 * RANK : 2 * RANK + PLD]
    vector_proj_w = small_table[:, 2 * RANK + PLD :]

    attn_normed, attn_pull = jax.vjp(rms_norm, attn_pre, gain_attn)
    first_sum = stream + attn_normed
    left_pre = matmul(normed_low, laurel_left)
    left_low = left_pre.astype(bf16)
    right_pre = matmul_flip(left_low, laurel_right)
    laurel_normed, laurel_pull = jax.vjp(rms_norm, right_pre, gain_laurel)
    second_sum = (first_sum + normed + laurel_normed) * ROOT_HALF
    feed_normed, feed_pull = jax.vjp(rms_norm, second_sum, gain_pre)
    feed_own = feed_normed.astype(bf16)
    feed_low = lax.all_gather(feed_own, "fsdp", axis=0, tiled=True)
    ffn_all, _ = lax.optimization_barrier((ffn_all, feed_own))
    w_both, w_down = fetch(
        ffn_all, ffn_join, ffn_to, my_fsdp, ffn_place, (ffn_first, ffn_each)
    )
    both_pre = matmul(feed_low, w_both)
    ffn_width = w_down.shape[1]
    hidden, hidden_pull = jax.vjp(gelu_product, both_pre[:, :ffn_width], both_pre[:, ffn_width:])
    hidden_low = hidden.astype(bf16)
    down_pre = lax.psum_scatter(
        matmul_flip(hidden_low, w_down).astype(bf16), "fsdp", scatter_dimension=0, tiled=True
    ).astype(f32)
    down_normed, down_pull = jax.vjp(rms_norm, down_pre, gain_post)
    third_sum = second_sum + down_normed
    third_low = third_sum.astype(bf16)
    vector_pre = matmul(third_low, vector_gate_w)
    vector_gated, vector_pull = jax.vjp(lambda inner: gelu_product(inner, vectors), vector_pre)
    vector_low = vector_gated.astype(bf16)
    proj_pre = matmul_flip(vector_low, vector_proj_w)
    proj_normed, proj_pull = jax.vjp(rms_norm, proj_pre, gain_vec)
    result = third_sum + proj_normed
    output = result.astype(bf16)[None]

    grad_out = cotangent[0].astype(f32)
    grad_proj, grad_gain_vec = proj_pull(grad_out)
    proj_grad_low = grad_proj.astype(bf16)
    (grad_vector_pre,) = vector_pull(matmul(proj_grad_low, vector_proj_w))
    vector_grad_low = grad_vector_pre.astype(bf16)
    grad_third = grad_out + matmul_flip(vector_grad_low, vector_gate_w)
    grad_down, grad_gain_post = down_pull(grad_third)
    down_grad_low = lax.all_gather(grad_down.astype(bf16), "fsdp", axis=0, tiled=True)
    grad_gate, grad_up = hidden_pull(matmul(down_grad_low, w_down))
    both_grad_low = jnp.concatenate([grad_gate, grad_up], axis=1).astype(bf16)

    early_full = jnp.concatenate(
        [matmul_outer(third_low, vector_grad_low), matmul_outer(proj_grad_low, vector_low)], axis=1
    )
    small_early = small_sum(split_tiles(early_full, tile).reshape(-1, tile))
    feed_part = matmul_flip(both_grad_low, w_both).astype(bf16)
    feed_part, small_early = lax.optimization_barrier((feed_part, small_early))
    grad_feed = lax.psum_scatter(feed_part, "fsdp", scatter_dimension=0, tiled=True).astype(f32)
    both_grad_w = matmul_outer(feed_low, both_grad_low).astype(bf16)
    down_grad_w = matmul_outer(down_grad_low, hidden_low).astype(bf16)
    ffn_parts = [
        cut_tiles([both_grad_w, down_grad_w], index.reshape(-1), tile)
        for index in (ffn_cut[:, :ffn_half], ffn_cut[:, ffn_half:])
    ]
    ffn_parts, grad_feed = lax.optimization_barrier((ffn_parts, grad_feed))
    ffn_sums = [
        lax.psum_scatter(value, "seq", scatter_dimension=0, tiled=True) for value in ffn_parts
    ]

    grad_second_norm, grad_gain_pre = feed_pull(grad_feed)
    half_grad = (grad_third + grad_second_norm) * ROOT_HALF
    grad_right, grad_gain_laurel = laurel_pull(half_grad)
    right_grad_low = grad_right.astype(bf16)
    left_grad_low = matmul(right_grad_low, laurel_right).astype(bf16)
    grad_attn, grad_gain_attn = attn_pull(half_grad)
    attn_grad_low = seq_gather(grad_attn.astype(bf16))
    grad_attended = (
        matmul(attn_grad_low, w_out).astype(bf16).reshape(length, per_device, HEAD_DIM)
    )
    out_grad_w = matmul_outer(attn_grad_low, attended_low).astype(bf16)
    value_grad = jnp.einsum("qhk,qhd->kd", prob_low, grad_attended, preferred_element_type=f32)
    grad_prob = jnp.einsum("qhd,kd->qhk", grad_attended, value_single, preferred_element_type=f32)
    inner = jnp.sum(prob * grad_prob, axis=-1, keepdims=True)
    grad_score = (prob * (grad_prob - inner)).astype(bf16)
    grad_query = (
        jnp.einsum("qhk,kd->qhd", grad_score, key_single, preferred_element_type=f32) * SCALE
    ).astype(bf16)
    key_grad = (
        jnp.einsum("qhk,qhd->kd", grad_score, query_heads, preferred_element_type=f32) * SCALE
    ).astype(bf16)
    value_grad = value_grad.astype(bf16)
    partner_grad = seq_swap(jnp.where(is_key, value_grad, key_grad), 1)
    partner_grad = partner_grad.reshape(seq_size // 2, 2, rows, HEAD_DIM)[:, ::-1]
    other_grad = jnp.where(is_key, key_grad, value_grad).astype(f32) + partner_grad.reshape(
        length, HEAD_DIM
    ).astype(f32)
    grad_query_pre, grad_gain_query = query_pull(grad_query.astype(f32))
    grad_key_pre, grad_gain_key = key_pull(other_grad[:, None, :])
    grad_gain_key = jnp.where(is_key, grad_gain_key, 0.0)
    first_grad_low = jnp.concatenate(
        [grad_query_pre, jnp.where(is_key, grad_key_pre, other_grad)], axis=1
    ).astype(bf16)
    first_grad_w = matmul_outer(pack_normed, first_grad_low).astype(bf16)
    near = (my_chip + shifts) % chips
    near_key = take_blocks(attn_key_chip, near)[:, None, :]
    near_order = take_blocks(attn_order_chip, near)[:, None, :]
    near_place = take_blocks(by_chip(attn_place), near)[:, None, :]

    def attn_cut(core):
        index = pick(
            (near_key == 2 * my_seq + core)
            & (near_order == jnp.arange(attn_hold)[None, :, None]),
            near_place,
        )
        return cut_tiles([first_grad_w, out_grad_w], index.reshape(-1), tile)

    attn_given, attn_own = attn_cut(1 - my_core), attn_cut(my_core)
    attn_given, attn_own, ffn_sums[0] = lax.optimization_barrier(
        (attn_given, attn_own, ffn_sums[0])
    )
    attn_parts = added(attn_own, core_swap(attn_given)).reshape(chips, attn_hold, tile, tile)
    attn_sum = attn_parts[0]
    attn_parts = [attn_parts[offset].astype(bf16) for offset in range(1, chips)]
    normed_sum = seq_sum(matmul_flip(first_grad_low, w_first), bf16)
    attn_sum, attn_parts, normed_sum = lax.optimization_barrier((attn_sum, attn_parts, normed_sum))
    for offset in range(1, chips):
        attn_sum = attn_sum + chip_shift(attn_parts[offset - 1], offset).astype(f32)
    attn_sum = attn_sum.astype(bf16)
    attn_back = pick(
        (column_slots[3][None, None, :] == (my_seq ^ flips)[:, None, None])
        & (column_slots[0][None, None, :] == my_key)
        & (column_slots[2][None, None, :] == jnp.arange(attn_room)[None, :, None]),
        column_slots[1],
    )

    grad_normed = half_grad + matmul_flip(left_grad_low, laurel_left) + normed_sum
    grad_stream_norm, grad_gain_in = normed_pull(grad_normed)
    input_grad = (half_grad + grad_stream_norm)[None]
    gain_grad = jnp.concatenate(
        [
            grad_gain_in,
            grad_gain_attn,
            grad_gain_laurel,
            grad_gain_pre,
            grad_gain_post,
            grad_gain_vec,
            grad_gain_query,
            grad_gain_key,
        ]
    )
    late_full = jnp.concatenate(
        [matmul_outer(normed_low, left_grad_low), matmul_outer(right_grad_low, left_low)], axis=1
    )
    late = jnp.concatenate(
        [late_full.reshape(seq_size, -1), gain_grad.reshape(seq_size, -1)], axis=1
    ).reshape(seq_size, -1, tile)
    late = seq_sum(late.reshape(-1, tile), bf16, True)

    late = late.astype(bf16)
    late = added(late, core_swap(late)).astype(bf16)
    ffn_sums, attn_sum, late, input_grad = lax.optimization_barrier(
        (ffn_sums, attn_sum, late, input_grad)
    )
    ffn_sums = ffn_sums + [core_swap(value) for value in ffn_sums]
    late = jnp.pad(late, ((0, 2 * late_count * tile - late.shape[0]), (0, 0)))
    late = late.reshape(2, late_count, tile, tile)
    late = lax.dynamic_index_in_dim(late, my_core, 0, False)
    late_index = 2 * ffn_hold + jnp.arange(late_count)
    ffn_return = [
        gather_tiles(ffn_sums + [late], jnp.concatenate([ffn_back[i], late_index]))
        for i in range(chips)
    ]
    ffn_return, attn_sum = lax.optimization_barrier((ffn_return, attn_sum))
    ffn_returned = chip_exchange(ffn_return)
    attn_returned = seq_exchange([gather_tiles([attn_sum], attn_back[i]) for i in range(seq_size)])
    attn_returned = attn_returned + [core_swap(value) for value in attn_returned]
    back_size = 2 * chips * return_size
    slot_grad = jnp.where(my_slots[0] >= 0, my_slots[1], back_size + my_slots[2])

    def slow_return():
        own_ffn = split_tiles(both_grad_w, tile), split_tiles(down_grad_w, tile)
        own_attn = split_tiles(first_grad_w, tile), split_tiles(out_grad_w, tile)
        parts = jnp.concatenate(own_ffn + own_attn + (jnp.zeros((1, tile, tile), bf16),))
        index = jnp.where(
            ffn_to == my_fsdp,
            ffn_place,
            jnp.where(attn_to == my_seq, ffn_count + attn_place, ffn_count + attn_count),
        )
        spread = gather_tiles([parts], index.reshape(-1))
        spread = lax.all_to_all(
            spread.reshape((seq_size * fsdp_size, mine, tile, tile)),
            ("seq", "fsdp"),
            split_axis=0,
            concat_axis=0,
            tiled=True,
        )
        return jnp.sum(spread.astype(f32), axis=0).astype(bf16)

    slow_start = back_size + 2 * seq_size * attn_room
    slow_grads = lax.cond(fits, lambda: jnp.zeros((mine, tile, tile), bf16), slow_return)
    ffn_returned, slow_grads = lax.optimization_barrier((ffn_returned, slow_grads))
    late = sum(value[ffn_room:].astype(f32) for value in ffn_returned).astype(bf16)
    late = core_pair(late).reshape(-1, tile).astype(f32)
    ffn_returned = ffn_returned + [core_swap(value) for value in ffn_returned]
    tile_grads = ffn_returned + attn_returned + [slow_grads]
    slot_grad = jnp.where(fits, slot_grad, slow_start + local_slots)

    tile_new, tile_first_new, tile_second_new = rotate_update(
        tile_grads, slot_grad, tile_master, tile_first, tile_second, left_basis, right_basis, RATE_TILE
    )
    late_rows = late_full.shape[0] // seq_size
    late_tiles = late[:late_rows].reshape(-1, 1, tile, tile)
    gain_grad_mine = late[late_rows : late_rows + own_gains.shape[0] // tile].reshape(-1)
    small_grad = jnp.concatenate(
        [
            late_tiles.astype(bf16),
            small_early.reshape(late_tiles.shape[0], -1, tile, tile),
        ],
        axis=1,
    ).reshape(small_master.shape)
    small_new, small_first_new, small_second_new = rotate_update(
        [small_grad],
        jnp.arange(small_master.shape[0]),
        small_master,
        small_first,
        small_second,
        small_left,
        small_right,
        RATE_SMALL,
    )
    gain_first_new = BETA_ONE * gain_first + (1.0 - BETA_ONE) * gain_grad_mine
    gain_second_new = BETA_TWO * gain_second + (1.0 - BETA_TWO) * gain_grad_mine * gain_grad_mine
    correct_one = 1.0 - BETA_ONE**STEP
    correct_two = 1.0 - BETA_TWO**STEP
    gain_new = gains - RATE_GAIN * (gain_first_new / correct_one) / (
        jnp.sqrt(gain_second_new / correct_two) + ADAM_EPS
    )
    return (
        output,
        input_grad,
        tile_new,
        tile_first_new,
        tile_second_new,
        small_new,
        small_first_new,
        small_second_new,
        gain_new,
        gain_first_new,
        gain_second_new,
    )


def solution(mesh):
    return jax.shard_map(
        on_device,
        mesh=mesh,
        in_specs=(
            P("fsdp", "seq", None),
            P("fsdp", "seq", None),
            P("fsdp", None),
            P("fsdp", "seq", None),
            P(),
            P(("seq", "fsdp"), None, None),
            P(("seq", "fsdp"), None, None),
            P(("seq", "fsdp"), None, None),
            P(("seq", "fsdp"), None, None),
            P(("seq", "fsdp"), None, None),
            P("seq", None, None),
            P("seq", None, None),
            P("seq", None, None),
            P("seq", None, None),
            P("seq", None, None),
            P("seq"),
            P("seq"),
            P("seq"),
        ),
        out_specs=(
            P("fsdp", "seq", None),
            P("fsdp", "seq", None),
            P(("seq", "fsdp"), None, None),
            P(("seq", "fsdp"), None, None),
            P(("seq", "fsdp"), None, None),
            P("seq", None, None),
            P("seq", None, None),
            P("seq", None, None),
            P("seq"),
            P("seq"),
            P("seq"),
        ),
        check_vma=False,
    )
```

```python
import math

import jax
import jax.numpy as jnp
from jax import lax
from jax.experimental import pallas as pl
from jax.experimental.pallas import tpu as pltpu
from jax.sharding import PartitionSpec as P

HEADS = 8
KV_HEADS = 2
HEAD_DIM = 256
FF = 8192
RANK = 64
PLD = 256
STEP = 5


EPS = 1e-06
SCALE = 0.0625
THETA = 1000000.0
ROOT_HALF = 0.7071067811865476
BETA_ONE = 0.5
BETA_TWO = 0.5
ADAM_EPS = 1e-08
RATE_TILE = 0.02
RATE_SMALL = 0.04
RATE_GAIN = 0.3
DECAY = 0.01
NEGATIVE = -1e30
VMEM_BYTES = 32 * 1024 * 1024


def rms_norm(value, gain):
    return value * lax.rsqrt(jnp.mean(value * value, axis=-1, keepdims=True) + EPS) * gain


def rotary(value, position):
    half = value.shape[-1] // 2
    freq = THETA ** (-2.0 * jnp.arange(half).astype(jnp.float32) / value.shape[-1])
    angle = position.astype(jnp.float32)[:, None] * freq[None, :]
    cosine = jnp.cos(angle)[:, None, :]
    sine = jnp.sin(angle)[:, None, :]
    first = value[..., :half]
    second = value[..., half:]
    return jnp.concatenate(
        [first * cosine - second * sine, second * cosine + first * sine], axis=-1
    )


def documents(lengths, length):
    places = jnp.arange(length)
    ends = jnp.cumsum(lengths)
    passed = places[:, None] >= ends[None, :]
    segment = jnp.sum(passed.astype(jnp.int32), axis=1)
    before = jnp.sum(jnp.where(passed, lengths[None, :], 0), axis=1)
    return (segment, places - before)


def matmul(left, right):
    return jnp.dot(left, right, preferred_element_type=jnp.float32)


def matmul_flip(left, right):
    return lax.dot_general(
        left, right, (((1,), (1,)), ((), ())), preferred_element_type=jnp.float32
    )


def matmul_outer(left, right):
    return lax.dot_general(
        left, right, (((0,), (0,)), ((), ())), preferred_element_type=jnp.float32
    )


def assemble(tiles, row_blocks):
    size = tiles.shape[1]
    column_blocks = tiles.shape[0] // row_blocks
    return (
        tiles.reshape(row_blocks, column_blocks, size, size)
        .transpose(0, 2, 1, 3)
        .reshape(row_blocks * size, column_blocks * size)
    )


def split_tiles(matrix, size):
    row_blocks = matrix.shape[0] // size
    column_blocks = matrix.shape[1] // size
    return (
        matrix.reshape(row_blocks, size, column_blocks, size)
        .transpose(0, 2, 1, 3)
        .reshape(row_blocks * column_blocks, size, size)
    )


def gelu_product(first, second):
    return jax.nn.gelu(first, approximate=True) * second


def room(count, share):
    mean = count * share
    return math.ceil(mean + 3.6 * math.sqrt(mean * (1.0 - share)) + 3.0)


def count_earlier(group, valid):
    size = group.shape[-1]
    order = jnp.arange(size)
    same = (group[..., :, None] == group[..., None, :]) & valid[..., None, :]
    same = same & (order[None, :] < order[:, None])
    return jnp.sum(same.astype(jnp.int32), axis=-1)


def count_long(keys):
    groups, size = keys.shape

    def kernel(row_ref, column_ref, out_ref):
        row = row_ref[0]
        column = column_ref[0]
        here = lax.broadcasted_iota(jnp.int32, (size, size), 1)
        other = lax.broadcasted_iota(jnp.int32, (size, size), 0)
        earlier = (column == row) & (other < here)
        out_ref[0] = jnp.sum(earlier.astype(jnp.int32), axis=0, keepdims=True)

    return pl.pallas_call(
        kernel,
        grid=(groups,),
        out_shape=jax.ShapeDtypeStruct((groups, 1, size), jnp.int32),
        in_specs=[
            pl.BlockSpec((1, 1, size), lambda i: (i, 0, 0)),
            pl.BlockSpec((1, size, 1), lambda i: (i, 0, 0)),
        ],
        out_specs=pl.BlockSpec((1, 1, size), lambda i: (i, 0, 0)),
        cost_estimate=pl.CostEstimate(flops=0, transcendentals=0, bytes_accessed=0),
        compiler_params=pltpu.CompilerParams(vmem_limit_bytes=VMEM_BYTES),
    )(keys[:, None, :], keys[:, :, None]).reshape(groups, size)


def pick(match, value):
    return jnp.sum(jnp.where(match, value, 0), axis=-1)


def steps_of(count):
    for steps in range(4, 129):
        if count % steps == 0 and 16 <= count // steps <= 66:
            return steps
    return 2 if count % 2 == 0 else 1


def tile_kernel_call(kernel, index, arrays, out_shape, out_specs, steps):
    moved = sum(math.prod(one.shape) * 2 for one in jax.tree.leaves(out_shape))
    return pl.pallas_call(
        kernel,
        grid=(steps,),
        cost_estimate=pl.CostEstimate(flops=0, transcendentals=0, bytes_accessed=2 * moved),
        out_shape=out_shape,
        in_specs=[pl.BlockSpec(memory_space=pltpu.SMEM)]
        + [pl.BlockSpec(memory_space=pl.ANY)] * len(arrays),
        out_specs=out_specs,
        scratch_shapes=[pltpu.SemaphoreType.DMA],
        compiler_params=pltpu.CompilerParams(vmem_limit_bytes=VMEM_BYTES),
    )(index, *arrays)


def start_copy(sources, place, target, sem, start=0):
    if len(sources) == 1:
        pltpu.make_async_copy(sources[0].at[place - start], target, sem).start()
        return
    half = len(sources) // 2
    middle = start + sum(ref.shape[0] for ref in sources[:half])

    @pl.when(place < middle)
    def _():
        start_copy(sources[:half], place, target, sem, start)

    @pl.when(place >= middle)
    def _():
        start_copy(sources[half:], place, target, sem, middle)


def gather_tiles(arrays, index):
    tile = arrays[0].shape[-1]
    count = index.shape[0]
    steps = steps_of(count)
    each = count // steps

    def kernel(index_ref, *refs):
        sources, out, sem = refs[:-2], refs[-2], refs[-1]
        base = pl.program_id(0) * each

        def step(i, carry):
            start_copy(sources, index_ref[base + i], out.at[i], sem)
            return carry

        lax.fori_loop(0, each, step, 0)
        pltpu.make_async_copy(out, out, sem).wait()

    total = sum(array.shape[0] for array in arrays)
    return tile_kernel_call(
        kernel,
        jnp.clip(index, 0, total - 1),
        arrays,
        jax.ShapeDtypeStruct((count, tile, tile), arrays[0].dtype),
        pl.BlockSpec((each, tile, tile), lambda i: (i, 0, 0)),
        steps,
    )


def join_tiles(arrays, index, row_blocks, columns):
    tile = arrays[0].shape[-1]
    steps = 4
    each = row_blocks // steps

    def kernel(index_ref, *refs):
        sources, outs, sem = refs[: len(arrays)], refs[len(arrays) : -1], refs[-1]
        base = pl.program_id(0) * each
        start = 0
        for out, width in zip(outs, columns):

            def step(i, carry, out=out, start=start, width=width):
                row = i // width
                column = i - row * width
                target = out.at[
                    pl.ds(pl.multiple_of(row * tile, tile), tile),
                    pl.ds(pl.multiple_of(column * tile, tile), tile),
                ]
                start_copy(sources, index_ref[start + base * width + i], target, sem)
                return carry

            lax.fori_loop(0, each * width, step, 0)
            start = start + row_blocks * width
        for out in outs:
            pltpu.make_async_copy(out, out, sem).wait()

    total = sum(array.shape[0] for array in arrays)
    out_shape = tuple(
        jax.ShapeDtypeStruct((row_blocks * tile, width * tile), arrays[0].dtype)
        for width in columns
    )
    out_specs = tuple(pl.BlockSpec((each * tile, width * tile), lambda i: (i, 0)) for width in columns)
    return tile_kernel_call(
        kernel, jnp.clip(index, 0, total - 1), arrays, out_shape, out_specs, steps
    )


def cut_tiles(matrices, index, tile):
    row_blocks = matrices[0].shape[0] // tile
    widths = [matrix.shape[1] // tile for matrix in matrices]
    count = index.shape[0]
    steps = steps_of(count)
    each = count // steps

    def kernel(index_ref, *refs):
        sources, out, sem = refs[:-2], refs[-2], refs[-1]
        base = pl.program_id(0) * each

        def step(i, carry):
            place = index_ref[base + i]
            start = 0
            for ref, width in zip(sources, widths):
                size = row_blocks * width

                @pl.when((place >= start) & (place < start + size))
                def _(ref=ref, start=start, width=width):
                    row = (place - start) // width
                    column = place - start - row * width
                    source = ref.at[
                        pl.ds(pl.multiple_of(row * tile, tile), tile),
                        pl.ds(pl.multiple_of(column * tile, tile), tile),
                    ]
                    pltpu.make_async_copy(source, out.at[i], sem).start()

                start = start + size
            return carry

        lax.fori_loop(0, each, step, 0)
        pltpu.make_async_copy(out, out, sem).wait()

    return tile_kernel_call(
        kernel,
        jnp.clip(index, 0, row_blocks * sum(widths) - 1),
        matrices,
        jax.ShapeDtypeStruct((count, tile, tile), matrices[0].dtype),
        pl.BlockSpec((each, tile, tile), lambda i: (i, 0, 0)),
        steps,
    )


def split_low(value):
    high = value.astype(jnp.bfloat16)
    return high, (value - high.astype(jnp.float32)).astype(jnp.bfloat16)


def rotate_update(grads, index, master, first, second, left, right, rate):
    count, tile, _ = master.shape
    each = 4 if count % 4 == 0 else 1
    correct_one = 1.0 - BETA_ONE**STEP
    correct_two = 1.0 - BETA_TWO**STEP

    def product(one, two, dims):
        return lax.dot_general(one, two, (dims, ((), ())), preferred_element_type=jnp.float32)

    def kernel(index_ref, *refs):
        sources, refs = refs[: len(grads)], refs[len(grads) :]
        master_ref, first_ref, second_ref, left_ref, right_ref = refs[:5]
        master_out, first_out, second_out, held, sems = refs[5:]
        now = pl.program_id(0)

        @pl.when(now == 0)
        def _():
            def step(i, carry):
                start_copy(sources, index_ref[i], held.at[i], sems.at[i // each])
                return carry

            lax.fori_loop(0, count, step, 0)

        block = held.at[pl.ds(now * each, each)]
        pltpu.make_async_copy(block, block, sems.at[now]).wait()
        lefts, rights, turns = [], [], []
        for i in range(each):
            grad = held[now * each + i]
            lefts.append(split_low(left_ref[i]))
            rights.append(split_low(right_ref[i]))
            half_turned = product(
                jnp.concatenate([grad, grad], axis=1),
                jnp.concatenate(rights[i], axis=0),
                ((1,), (0,)),
            )
            turns.append(split_low(half_turned))
        for i in range(each):
            (left_high, left_low), (high, low) = lefts[i], turns[i]
            turns[i] = product(
                jnp.concatenate([left_high, left_high, left_low], axis=0),
                jnp.concatenate([high, low, high], axis=0),
                ((0,), (0,)),
            )
        for i in range(each):
            right_high, right_low = rights[i]
            first_new = BETA_ONE * first_ref[i] + (1.0 - BETA_ONE) * turns[i]
            second_new = BETA_TWO * second_ref[i] + (1.0 - BETA_TWO) * turns[i] * turns[i]
            first_out[i] = first_new
            second_out[i] = second_new
            high, low = split_low(
                first_new / correct_one / (jnp.sqrt(second_new / correct_two) + ADAM_EPS)
            )
            half_back = product(
                jnp.concatenate([high, low, high], axis=1),
                jnp.concatenate([right_high, right_high, right_low], axis=1),
                ((1,), (1,)),
            )
            turns[i] = split_low(half_back)
        for i in range(each):
            (left_high, left_low), (high, low) = lefts[i], turns[i]
            back = product(
                jnp.concatenate([left_high, left_high, left_low], axis=1),
                jnp.concatenate([high, low, high], axis=0),
                ((1,), (0,)),
            )
            weight = master_ref[i]
            master_out[i] = weight - rate * (back + DECAY * weight)

    spec = pl.BlockSpec((each, tile, tile), lambda i: (i, 0, 0))
    shape = jax.ShapeDtypeStruct(master.shape, jnp.float32)
    total = sum(array.shape[0] for array in grads)
    return pl.pallas_call(
        kernel,
        grid=(count // each,),
        out_shape=(shape, shape, shape),
        in_specs=[pl.BlockSpec(memory_space=pltpu.SMEM)]
        + [pl.BlockSpec(memory_space=pl.ANY)] * len(grads)
        + [spec] * 5,
        out_specs=(spec, spec, spec),
        scratch_shapes=[
            pltpu.VMEM((count, tile, tile), jnp.bfloat16),
            pltpu.SemaphoreType.DMA((count // each,)),
        ],
        compiler_params=pltpu.CompilerParams(vmem_limit_bytes=VMEM_BYTES),
    )(jnp.clip(index, 0, total - 1), *grads, master, first, second, left, right)


def seq_swap(value, flip):
    size = lax.axis_size("seq")
    return lax.ppermute(value, "seq", [(i, i ^ flip) for i in range(size)])


def take_blocks(value, order):
    return jnp.stack(
        [lax.dynamic_index_in_dim(value, order[i], 0, False) for i in range(order.shape[0])]
    )


def core_swap(value):
    size = lax.axis_size("fsdp")
    return lax.ppermute(value, "fsdp", [(i, i ^ 1) for i in range(size)])


def chip_shift(value, offset):
    size = lax.axis_size("fsdp")
    chips = size // 2
    return lax.ppermute(
        value, "fsdp", [(i, (i // 2 + offset) % chips * 2 + i % 2) for i in range(size)]
    )


def seq_gather(value):
    size = lax.axis_size("seq")
    return jnp.concatenate([value] + [seq_swap(value, flip) for flip in range(1, size)], axis=0)


def seq_ordered(value):
    size = lax.axis_size("seq")
    parts = jnp.stack([value] + [seq_swap(value, flip) for flip in range(1, size)], axis=0)
    return take_blocks(parts, lax.axis_index("seq") ^ jnp.arange(size))


def seq_exchange(values):
    return [values[0]] + [seq_swap(values[flip], flip) for flip in range(1, len(values))]


def seq_sum(value, wire, ordered=False):
    size = lax.axis_size("seq")
    parts = value.reshape((size, value.shape[0] // size) + value.shape[1:])
    if ordered:
        parts = take_blocks(parts, lax.axis_index("seq") ^ jnp.arange(size))
    total = parts[0]
    for flip in range(1, size):
        total = total + seq_swap(parts[flip].astype(wire), flip).astype(jnp.float32)
    return total


def chip_exchange(values):
    return [values[0]] + [chip_shift(values[offset], offset) for offset in range(1, len(values))]


def core_pair(value):
    other = core_swap(value)
    even = lax.axis_index("fsdp") % 2 == 0
    return jnp.where(even, jnp.stack([value, other]), jnp.stack([other, value]))


def small_sum(value):
    seq_size = lax.axis_size("seq")
    even = lax.axis_index("fsdp") % 2 == 0
    low = value.astype(jnp.bfloat16)
    parts = low.reshape((seq_size, 2, low.shape[0] // (2 * seq_size)) + low.shape[1:])
    kept = jnp.where(even, parts[:, 0], parts[:, 1]).astype(jnp.float32)
    given = jnp.where(even, parts[:, 1], parts[:, 0])
    kept = kept + core_swap(given).astype(jnp.float32)
    return seq_sum(kept.reshape((-1,) + low.shape[1:]), jnp.bfloat16, True)


def small_all(kept):
    chips = lax.axis_size("fsdp") // 2
    chip = lax.axis_index("fsdp") // 2
    rows = kept.shape[0]
    kept = kept.reshape((chips, rows // chips) + kept.shape[1:])
    kept = take_blocks(kept, (chip + jnp.arange(chips)) % chips)
    total = kept[0]
    for offset in range(1, chips):
        total = total + chip_shift(kept[offset].astype(jnp.bfloat16), offset).astype(jnp.float32)
    total = total.astype(jnp.bfloat16)
    parts = jnp.stack([total] + [chip_shift(total, offset) for offset in range(1, chips)])
    parts = take_blocks(parts, (chip - jnp.arange(chips)) % chips)
    return core_pair(parts).reshape((2 * rows,) + parts.shape[2:])


def turn(value, cosine, sine):
    half = value.shape[-1] // 2
    first, second = value[..., :half], value[..., half:]
    return jnp.concatenate(
        [first * cosine - second * sine, second * cosine + first * sine], axis=-1
    )


def added(one, two):
    return one.astype(jnp.float32) + two.astype(jnp.float32)


def on_device(
    tokens,
    layer_vectors,
    doc_lengths,
    cotangent,
    tile_owner,
    tile_master,
    tile_first,
    tile_second,
    left_basis,
    right_basis,
    small_master,
    small_first,
    small_second,
    small_left,
    small_right,
    gains,
    gain_first,
    gain_second,
):
    bf16 = jnp.bfloat16
    f32 = jnp.float32
    tile = tile_master.shape[1]
    width = tokens.shape[2]
    row_blocks = width // tile
    rows = tokens.shape[1]
    seq_size = lax.axis_size("seq")
    fsdp_size = lax.axis_size("fsdp")
    chips = fsdp_size // 2
    mine = tile_master.shape[0]
    tiles = tile_owner.shape[0]
    length = rows * seq_size
    per_device = HEADS // seq_size
    per_key = seq_size // KV_HEADS
    query_width = HEADS * HEAD_DIM
    key_width = KV_HEADS * HEAD_DIM
    my_seq = lax.axis_index("seq")
    my_fsdp = lax.axis_index("fsdp")
    my_chip = my_fsdp // 2
    my_core = my_fsdp % 2
    flips = jnp.arange(seq_size)
    shifts = jnp.arange(chips)

    query_blocks = query_width // tile
    key_blocks = key_width // tile
    ffn_blocks = FF // tile
    query_each = query_blocks // seq_size
    head_blocks = HEAD_DIM // tile
    ffn_each = ffn_blocks // fsdp_size
    columns = tiles // row_blocks
    attn_first = query_each + head_blocks
    attn_count = row_blocks * (attn_first + query_each)
    ffn_first = 2 * ffn_each
    ffn_count = row_blocks * 3 * ffn_each
    attn_share = (2 * query_blocks + 2 * key_blocks) / columns
    ffn_share = 3 * ffn_blocks / columns
    attn_room = (room(2 * mine, attn_share / seq_size) + 1) // 2
    attn_hold = (room(attn_count, 1.0 / chips) + 1) // 2 + 1
    ffn_room = (room(2 * mine, ffn_share / chips) + 1) // 2
    both_count = row_blocks * ffn_first
    both_hold, down_hold = (
        (room(count, 1.0 / seq_size) + 3) // 4 * 4 for count in (both_count, ffn_count - both_count)
    )

    def tile_places(owner):
        row = owner // columns
        column = owner % columns
        key_at = column - query_blocks
        value_at = key_at - key_blocks
        out_at = value_at - key_blocks
        ffn_at = out_at - query_blocks
        is_attn = ffn_at < 0
        kind = ffn_at // ffn_blocks
        ffn_column = ffn_at % ffn_blocks
        ffn_to = jnp.where(is_attn, -1, ffn_column // ffn_each)
        ffn_local = ffn_column % ffn_each
        ffn_place = jnp.where(
            kind == 2, row * ffn_each + ffn_local, row * ffn_first + kind * ffn_each + ffn_local
        )
        is_down = (kind == 2).astype(jnp.int32)
        attn_to = jnp.where(
            key_at < 0,
            column // query_each,
            jnp.where(
                value_at < 0,
                key_at // head_blocks * per_key,
                jnp.where(
                    out_at < 0,
                    value_at // head_blocks * per_key + per_key - 1,
                    out_at // query_each,
                ),
            ),
        )
        attn_place = jnp.where(
            key_at < 0,
            row * attn_first + column % query_each,
            jnp.where(
                out_at < 0,
                row * attn_first + query_each + key_at % head_blocks,
                row_blocks * attn_first + row * query_each + out_at % query_each,
            ),
        )
        attn_to = jnp.where(is_attn, attn_to, -1)
        return (ffn_to, is_down, ffn_place, attn_to, attn_place)

    owners = tile_owner.reshape(seq_size, fsdp_size, mine)
    slot_seq = jnp.arange(seq_size)[:, None, None]
    slot_fsdp = jnp.arange(fsdp_size)[None, :, None]
    slot_chip = slot_fsdp // 2
    local_slots = jnp.arange(mine)
    both_slots = jnp.arange(2 * mine)
    both_slots = jnp.where(
        both_slots // mine == my_core, both_slots % mine, mine + both_slots % mine
    )

    ffn_to = tile_places(owners)[0]
    ffn_chip = jnp.where(ffn_to < 0, -1, ffn_to // 2)
    chip_view = ffn_chip.reshape(seq_size, chips, 2 * mine)
    chip_rank = count_earlier(chip_view, chip_view >= 0).reshape(owners.shape)
    ffn_slots = lax.dynamic_slice(
        jnp.stack([ffn_chip, chip_rank]), (0, my_seq, 2 * my_chip, 0), (2, 1, 2, mine)
    ).reshape(2, 1, 1, 2 * mine)
    ffn_pack = pick(
        (ffn_slots[0] == ((my_chip + shifts) % chips)[:, None, None])
        & (ffn_slots[1] == (my_core * ffn_room + jnp.arange(ffn_room))[None, :, None]),
        both_slots,
    )
    master_low = tile_master.astype(bf16)
    masters = [master_low, core_swap(master_low)]
    ffn_sent = [gather_tiles(masters, ffn_pack[i]) for i in range(chips)]
    small_rows = small_master.shape[0] // 2
    small_half = lax.dynamic_slice_in_dim(small_master, my_core * small_rows, small_rows)
    masters, ffn_sent, chip_rank, owners, own_tokens, own_gains, small_half = (
        lax.optimization_barrier(
            (
                masters,
                ffn_sent,
                chip_rank,
                owners,
                tokens[0],
                gains.astype(bf16),
                small_half.astype(bf16),
            )
        )
    )
    ffn_got = chip_exchange(ffn_sent)

    ffn_to, is_down, ffn_place, attn_to, attn_place = tile_places(owners)
    ffn_chip = jnp.where(ffn_to < 0, -1, ffn_to // 2)
    ffn_key = jnp.where(ffn_to < 0, -1, 2 * ffn_to + is_down)
    ffn_hold = jnp.where(is_down == 1, down_hold, both_hold)
    attn_view = attn_to.reshape(seq_size, chips, 2 * mine)
    attn_rank = count_earlier(attn_view, attn_view >= 0).reshape(owners.shape)
    attn_core = (attn_rank + slot_seq) % 2
    attn_rank = attn_rank // 2
    attn_key = jnp.where(attn_to < 0, -1, 2 * attn_to + attn_core)

    chip_slots = lax.dynamic_slice(
        jnp.stack([attn_key, attn_rank]), (0, my_seq, 2 * my_chip, 0), (2, 1, 2, mine)
    ).reshape(2, 1, 1, 2 * mine)
    attn_message = attn_room + row_blocks * rows // tile + small_rows + -(-own_gains.shape[0] // tile**2)
    attn_pack = pick(
        (chip_slots[0] == (2 * (my_seq ^ flips) + my_core)[:, None, None])
        & (chip_slots[1] == jnp.arange(attn_room)[None, :, None]),
        both_slots,
    )
    attn_sent = gather_tiles(masters, attn_pack.reshape(-1))
    attn_sent = attn_sent.reshape(seq_size, attn_room, tile, tile)
    seq_view = ffn_key.reshape(seq_size, fsdp_size * mine)
    ffn_rank = count_long(seq_view).reshape(owners.shape)
    def by_chip(value):
        value = value.reshape(seq_size, chips, 2 * mine).transpose(1, 0, 2)
        return value.reshape(chips, seq_size * 2 * mine)

    attn_key_chip = by_chip(attn_key)
    attn_order_chip = count_long(attn_key_chip)
    attn_order = (
        attn_order_chip.reshape(chips, seq_size, 2 * mine).transpose(1, 0, 2).reshape(owners.shape)
    )
    fits = jnp.all(
        jnp.where(
            ffn_to < 0,
            (attn_rank < attn_room) & (attn_order < attn_hold),
            (chip_rank < 2 * ffn_room) & (ffn_rank < ffn_hold),
        )
    )
    half = chips * ffn_room
    rows_late = 2 * RANK * row_blocks // seq_size
    rank_core = chip_rank // ffn_room
    rank_local = chip_rank % ffn_room
    out_place = (
        jnp.where(rank_core == my_core, 0, half)
        + (my_chip - slot_chip) % chips * ffn_room
        + rank_local
    )
    late_count = -(-(rows_late + own_gains.shape[0] // tile) // (2 * tile))
    return_size = ffn_room + late_count
    back_place = (
        jnp.where(rank_core == my_core, 0, chips * return_size)
        + (my_chip - ffn_chip) % chips * return_size
        + rank_local
    )
    attn_back_place = (
        jnp.where(attn_core == my_core, 0, seq_size * attn_room)
        + (attn_to ^ my_seq) * attn_room
        + attn_rank
    )
    my_slots = lax.dynamic_slice(
        jnp.stack([ffn_to, back_place, attn_back_place]), (0, my_seq, my_fsdp, 0), (3, 1, 1, mine)
    ).reshape(3, mine)
    seq_slots = lax.dynamic_slice(
        jnp.stack(
            [
                ffn_key,
                ffn_rank,
                ffn_chip,
                out_place,
                chip_rank,
                jnp.broadcast_to(slot_chip, owners.shape),
            ]
        ),
        (0, my_seq, 0, 0),
        (6, 1, fsdp_size, mine),
    ).reshape(6, fsdp_size * mine)
    column_slots = lax.dynamic_slice(
        jnp.stack([attn_key, attn_order, attn_rank, jnp.broadcast_to(slot_seq, owners.shape)]),
        (0, 0, 2 * my_chip, 0),
        (4, seq_size, 2, mine),
    ).reshape(4, 2 * seq_size * mine)
    my_key = 2 * my_seq + my_core

    attn_keep = pick(
        (column_slots[0][None, :] == my_key)
        & (column_slots[1][None, :] == jnp.arange(attn_hold)[:, None]),
        jnp.where(
            column_slots[3] == my_seq,
            0,
            attn_room + ((column_slots[3] ^ my_seq) - 1) * attn_message,
        )
        + column_slots[2],
    )
    attn_join = pick(
        (attn_to.reshape(1, -1) == my_seq)
        & (attn_place.reshape(1, -1) == jnp.arange(attn_count)[:, None]),
        (
            jnp.where(attn_core == my_core, 0, chips * attn_hold)
            + (my_chip - slot_chip) % chips * attn_hold
            + attn_order
        ).reshape(1, -1),
    )
    def ffn_tables(kind, hold, count):
        key = 2 * my_fsdp + kind
        keep = pick(
            (seq_slots[0][None, :] == key) & (seq_slots[1][None, :] == jnp.arange(hold)[:, None]),
            seq_slots[3][None, :],
        )
        join = pick(
            (ffn_key.reshape(1, -1) == key)
            & (ffn_place.reshape(1, -1) == jnp.arange(count)[:, None]),
            (slot_seq * hold + ffn_rank).reshape(1, -1),
        )
        cut = pick(
            (ffn_key.reshape(seq_size, 1, -1) == key)
            & (ffn_rank.reshape(seq_size, 1, -1) == jnp.arange(hold)[None, :, None]),
            ffn_place.reshape(seq_size, 1, -1),
        )
        return (keep, join, cut)

    both_keep, both_join, both_cut = ffn_tables(0, both_hold, both_count)
    down_keep, down_join, down_cut = ffn_tables(1, down_hold, ffn_count - both_count)
    ffn_back = pick(
        (seq_slots[5][None, None, :] == ((my_chip + shifts) % chips)[:, None, None])
        & (seq_slots[2][None, None, :] == my_chip)
        & (seq_slots[4][None, None, :] == (my_core * ffn_room + jnp.arange(ffn_room))[None, :, None]),
        jnp.where(seq_slots[0] % 2 == 1, 2 * both_hold, 0)
        + jnp.where(
            seq_slots[0] // 2 == my_fsdp, 0, jnp.where(seq_slots[0] % 2 == 1, down_hold, both_hold)
        )
        + seq_slots[1],
    )

    token_tiles = own_tokens.reshape(rows, row_blocks, tile).transpose(1, 0, 2)
    token_tiles = token_tiles.reshape(-1, tile, tile)
    gain_rows = own_gains.reshape(-1, tile)
    gain_tiles = jnp.pad(gain_rows, ((0, -gain_rows.shape[0] % tile), (0, 0))).reshape(-1, tile, tile)
    common = jnp.concatenate([token_tiles, small_half, gain_tiles])
    attn_got = [attn_sent[0]] + [
        seq_swap(jnp.concatenate([attn_sent[flip], common]), flip) for flip in range(1, seq_size)
    ]
    segment, position = documents(doc_lengths[0], length)
    places = ((my_seq ^ flips)[:, None] * rows + jnp.arange(rows)[None, :]).reshape(-1)

    def reorder(values):
        blocks = values.reshape(seq_size, rows)
        return jnp.concatenate(
            [lax.dynamic_index_in_dim(blocks, my_seq ^ i, 0, False) for i in range(seq_size)]
        )

    pack_segment = reorder(segment)
    allow = (pack_segment[:, None] == pack_segment[None, :]) & (
        places[None, :] <= places[:, None]
    )
    turns = jnp.arange(HEAD_DIM // 2).astype(f32)
    angle = reorder(position).astype(f32)[:, None] * (THETA ** (-2.0 * turns / HEAD_DIM))[None, :]
    cosine, sine = jnp.cos(angle)[:, None, :], jnp.sin(angle)[:, None, :]
    parts = [common] + [value[attn_room:] for value in attn_got[1:]]
    token_end = token_tiles.shape[0]
    small_end = token_end + small_rows

    def seq_order(value):
        return take_blocks(value, my_seq ^ flips)

    pack_tokens = jnp.concatenate(
        [
            part[:token_end].reshape(row_blocks, rows, tile).transpose(1, 0, 2).reshape(rows, width)
            for part in parts
        ]
    )
    gain_full = seq_order(
        jnp.stack([part[small_end:].reshape(-1, tile)[: gain_rows.shape[0]] for part in parts])
    )
    gain_full = gain_full.reshape(-1).astype(f32)
    gain_in = gain_full[0:width]
    pack_normed = rms_norm(pack_tokens.astype(f32), gain_in).astype(bf16)
    keeps = (both_keep, down_keep, attn_keep)
    ready = (allow, cosine, sine, keeps, pack_normed, gain_full)
    ffn_got, attn_got, parts, ready = lax.optimization_barrier((ffn_got, attn_got, parts, ready))
    allow, cosine, sine, (both_keep, down_keep, attn_keep), pack_normed, gain_full = ready
    gain_in = gain_full[0:width]
    small_got = core_pair(seq_order(jnp.stack([part[token_end:small_end] for part in parts])))
    small_got = small_got.transpose(1, 0, 2, 3, 4)
    small_table = assemble(small_got.reshape((-1,) + small_master.shape[1:]), row_blocks)
    attn_kept = gather_tiles(attn_got, attn_keep)
    ffn_got = ffn_got + [core_swap(value) for value in ffn_got]
    both_kept, down_kept = gather_tiles(ffn_got, both_keep), gather_tiles(ffn_got, down_keep)
    both_kept, down_kept, attn_kept = lax.optimization_barrier((both_kept, down_kept, attn_kept))
    down_all = lax.all_gather(down_kept, "seq", axis=0, tiled=True)
    both_all = lax.all_gather(both_kept, "seq", axis=0, tiled=True)
    attn_all = [attn_kept] + [chip_shift(attn_kept, offset) for offset in range(1, chips)]
    attn_all = attn_all + [core_swap(value) for value in attn_all]

    attn_all, down_all, attn_join = lax.optimization_barrier((attn_all, down_all, attn_join))

    def fetch(arrays, index, to, me, place, columns_of):
        def fast():
            return join_tiles(arrays, index, row_blocks, columns_of)

        def slow():
            whole = lax.all_to_all(
                jnp.broadcast_to(master_low[None], (seq_size * fsdp_size,) + master_low.shape),
                ("seq", "fsdp"),
                split_axis=0,
                concat_axis=0,
                tiled=True,
            ).reshape(-1, tile, tile)
            count = row_blocks * sum(columns_of)
            slots = pick(
                (to.reshape(1, -1) == me) & (place.reshape(1, -1) == jnp.arange(count)[:, None]),
                jnp.arange(tiles)[None, :],
            )
            return join_tiles([whole], slots, row_blocks, columns_of)

        return lax.cond(fits, fast, slow)

    w_first, w_out = fetch(
        attn_all, attn_join, attn_to, my_seq, attn_place, (attn_first, query_each)
    )
    gain_attn = gain_full[width : 2 * width]
    gain_laurel = gain_full[2 * width : 3 * width]
    gain_pre = gain_full[3 * width : 4 * width]
    gain_post = gain_full[4 * width : 5 * width]
    gain_vec = gain_full[5 * width : 6 * width]
    gain_query = gain_full[6 * width : 6 * width + HEAD_DIM]
    gain_key = gain_full[6 * width + HEAD_DIM : 6 * width + 2 * HEAD_DIM]
    stream = own_tokens.astype(f32)
    vectors = layer_vectors[0].astype(f32)
    normed, normed_pull = jax.vjp(rms_norm, stream, gain_in)
    normed_low = normed.astype(bf16)
    first_pre = matmul(pack_normed, w_first)
    is_key = my_seq % per_key == 0

    def shape_query(query_in, query_gain):
        value = rms_norm(query_in.reshape(length, per_device, HEAD_DIM), query_gain)
        return turn(value, cosine, sine)

    def shape_key(key_in, key_gain):
        return turn(rms_norm(key_in.reshape(length, 1, HEAD_DIM), key_gain), cosine, sine)

    query_pre = first_pre[:, : per_device * HEAD_DIM]
    other_pre = first_pre[:, per_device * HEAD_DIM :]
    query_rot, query_pull = jax.vjp(shape_query, query_pre, gain_query)
    key_rot, key_pull = jax.vjp(shape_key, other_pre, gain_key)
    query_heads = query_rot.astype(bf16)
    other_low = jnp.where(is_key, key_rot[:, 0, :], other_pre).astype(bf16)
    partner_low = seq_swap(other_low, 1).reshape(seq_size // 2, 2, rows, HEAD_DIM)
    partner_low = partner_low[:, ::-1].reshape(length, HEAD_DIM)
    key_single = jnp.where(is_key, other_low, partner_low)
    value_single = jnp.where(is_key, partner_low, other_low)

    raw = (
        jnp.einsum("qhd,kd->qhk", query_heads, key_single, preferred_element_type=f32) * SCALE
    )
    scores = jnp.where(allow[:, None, :], raw, NEGATIVE)
    powers = jnp.exp(scores - jnp.max(scores, axis=-1, keepdims=True))
    prob = powers / jnp.sum(powers, axis=-1, keepdims=True)
    prob_low = prob.astype(bf16)
    attended_low = (
        jnp.einsum("qhk,kd->qhd", prob_low, value_single, preferred_element_type=f32)
        .astype(bf16)
        .reshape(length, per_device * HEAD_DIM)
    )
    attn_pre = seq_sum(matmul_flip(attended_low, w_out), bf16)
    (w_down,) = fetch([down_all], down_join, ffn_key, 2 * my_fsdp + 1, ffn_place, (ffn_each,))
    attn_pre, small_table, both_join, w_down = lax.optimization_barrier(
        (attn_pre, small_table, both_join, w_down)
    )
    laurel_left = small_table[:, :RANK]
    laurel_right = small_table[:, RANK : 2 * RANK]
    vector_gate_w = small_table[:, 2 * RANK : 2 * RANK + PLD]
    vector_proj_w = small_table[:, 2 * RANK + PLD :]

    attn_normed, attn_pull = jax.vjp(rms_norm, attn_pre, gain_attn)
    first_sum = stream + attn_normed
    left_pre = matmul(normed_low, laurel_left)
    left_low = left_pre.astype(bf16)
    right_pre = matmul_flip(left_low, laurel_right)
    laurel_normed, laurel_pull = jax.vjp(rms_norm, right_pre, gain_laurel)
    second_sum = (first_sum + normed + laurel_normed) * ROOT_HALF
    feed_normed, feed_pull = jax.vjp(rms_norm, second_sum, gain_pre)
    feed_own = feed_normed.astype(bf16)
    feed_low = lax.all_gather(feed_own, "fsdp", axis=0, tiled=True)
    both_all, _ = lax.optimization_barrier((both_all, feed_own))
    (w_both,) = fetch([both_all], both_join, ffn_key, 2 * my_fsdp, ffn_place, (ffn_first,))
    both_pre = matmul(feed_low, w_both)
    ffn_width = w_down.shape[1]
    hidden, hidden_pull = jax.vjp(gelu_product, both_pre[:, :ffn_width], both_pre[:, ffn_width:])
    hidden_low = hidden.astype(bf16)
    down_pre = lax.psum_scatter(
        matmul_flip(hidden_low, w_down).astype(bf16), "fsdp", scatter_dimension=0, tiled=True
    ).astype(f32)
    down_normed, down_pull = jax.vjp(rms_norm, down_pre, gain_post)
    third_sum = second_sum + down_normed
    third_low = third_sum.astype(bf16)
    vector_pre = matmul(third_low, vector_gate_w)
    vector_gated, vector_pull = jax.vjp(lambda inner: gelu_product(inner, vectors), vector_pre)
    vector_low = vector_gated.astype(bf16)
    proj_pre = matmul_flip(vector_low, vector_proj_w)
    proj_normed, proj_pull = jax.vjp(rms_norm, proj_pre, gain_vec)
    result = third_sum + proj_normed
    output = result.astype(bf16)[None]

    grad_out = cotangent[0].astype(f32)
    grad_proj, grad_gain_vec = proj_pull(grad_out)
    proj_grad_low = grad_proj.astype(bf16)
    (grad_vector_pre,) = vector_pull(matmul(proj_grad_low, vector_proj_w))
    vector_grad_low = grad_vector_pre.astype(bf16)
    grad_third = grad_out + matmul_flip(vector_grad_low, vector_gate_w)
    grad_down, grad_gain_post = down_pull(grad_third)
    down_grad_low = lax.all_gather(grad_down.astype(bf16), "fsdp", axis=0, tiled=True)
    grad_gate, grad_up = hidden_pull(matmul(down_grad_low, w_down))
    both_grad_low = jnp.concatenate([grad_gate, grad_up], axis=1).astype(bf16)

    early_full = jnp.concatenate(
        [matmul_outer(third_low, vector_grad_low), matmul_outer(proj_grad_low, vector_low)], axis=1
    )
    small_early = small_sum(split_tiles(early_full, tile).reshape(-1, tile))
    feed_part = matmul_flip(both_grad_low, w_both).astype(bf16)
    feed_part, small_early = lax.optimization_barrier((feed_part, small_early))
    grad_feed = lax.psum_scatter(feed_part, "fsdp", scatter_dimension=0, tiled=True).astype(f32)

    def cut_parts(flips_of, half):
        half_now = down_hold // 2
        rows_of = [lax.dynamic_index_in_dim(down_cut, my_seq ^ flip, 0, False) for flip in flips_of]
        index = jnp.stack(rows_of)[:, half * half_now : (half + 1) * half_now]
        return cut_tiles([down_grad_w], index.reshape(-1), tile)

    down_grad_w = matmul_outer(down_grad_low, hidden_low).astype(bf16)
    down_cuts = cut_parts([1, 3], 0), cut_parts([2, 3], 1)
    feed_low, down_cuts = lax.optimization_barrier((feed_low, down_cuts))
    down_one = added(cut_parts([0, 2], 0), seq_swap(down_cuts[0], 1))
    down_two = added(cut_parts([0, 1], 1), seq_swap(down_cuts[1], 2))
    both_grad_w = matmul_outer(feed_low, both_grad_low).astype(bf16)
    both_half = both_hold * 3 // 7 // 4 * 4
    both_parts = [
        cut_tiles([both_grad_w], index.reshape(-1), tile)
        for index in (both_cut[:, :both_half], both_cut[:, both_half:])
    ]
    both_parts, down_one, down_two, grad_feed, small_early = lax.optimization_barrier(
        (both_parts, down_one, down_two, grad_feed, small_early)
    )
    both_sums = [
        lax.psum_scatter(value, "seq", scatter_dimension=0, tiled=True) for value in both_parts
    ]
    down_half = down_one.shape[0] // 2
    down_one = added(down_one[:down_half], seq_swap(down_one[down_half:].astype(bf16), 2))
    down_two = added(down_two[:down_half], seq_swap(down_two[down_half:].astype(bf16), 1))
    down_sum = jnp.concatenate([down_one, down_two]).astype(bf16)
    small_early = small_all(small_early)

    grad_second_norm, grad_gain_pre = feed_pull(grad_feed)
    half_grad = (grad_third + grad_second_norm) * ROOT_HALF
    grad_right, grad_gain_laurel = laurel_pull(half_grad)
    right_grad_low = grad_right.astype(bf16)
    left_grad_low = matmul(right_grad_low, laurel_right).astype(bf16)
    grad_attn, grad_gain_attn = attn_pull(half_grad)
    attn_grad_low = seq_gather(grad_attn.astype(bf16))
    grad_attended = (
        matmul(attn_grad_low, w_out).astype(bf16).reshape(length, per_device, HEAD_DIM)
    )
    out_grad_w = matmul_outer(attn_grad_low, attended_low).astype(bf16)
    value_grad = jnp.einsum("qhk,qhd->kd", prob_low, grad_attended, preferred_element_type=f32)
    grad_prob = jnp.einsum("qhd,kd->qhk", grad_attended, value_single, preferred_element_type=f32)
    inner = jnp.sum(prob * grad_prob, axis=-1, keepdims=True)
    grad_score = (prob * (grad_prob - inner)).astype(bf16)
    grad_query = (
        jnp.einsum("qhk,kd->qhd", grad_score, key_single, preferred_element_type=f32) * SCALE
    ).astype(bf16)
    key_grad = (
        jnp.einsum("qhk,qhd->kd", grad_score, query_heads, preferred_element_type=f32) * SCALE
    ).astype(bf16)
    value_grad = value_grad.astype(bf16)
    partner_grad = seq_swap(jnp.where(is_key, value_grad, key_grad), 1)
    partner_grad = partner_grad.reshape(seq_size // 2, 2, rows, HEAD_DIM)[:, ::-1]
    other_grad = jnp.where(is_key, key_grad, value_grad).astype(f32) + partner_grad.reshape(
        length, HEAD_DIM
    ).astype(f32)
    grad_query_pre, grad_gain_query = query_pull(grad_query.astype(f32))
    grad_key_pre, grad_gain_key = key_pull(other_grad[:, None, :])
    grad_gain_key = jnp.where(is_key, grad_gain_key, 0.0)
    first_grad_low = jnp.concatenate(
        [grad_query_pre, jnp.where(is_key, grad_key_pre, other_grad)], axis=1
    ).astype(bf16)
    first_grad_w = matmul_outer(pack_normed, first_grad_low).astype(bf16)
    near = (my_chip + shifts) % chips
    near_key = take_blocks(attn_key_chip, near)[:, None, :]
    near_order = take_blocks(attn_order_chip, near)[:, None, :]
    near_place = take_blocks(by_chip(attn_place), near)[:, None, :]

    def attn_cut(core):
        index = pick(
            (near_key == 2 * my_seq + core)
            & (near_order == jnp.arange(attn_hold)[None, :, None]),
            near_place,
        )
        return cut_tiles([first_grad_w, out_grad_w], index.reshape(-1), tile)

    attn_given, attn_own = attn_cut(1 - my_core), attn_cut(my_core)
    attn_given, attn_own, small_early, down_sum, both_sums[0] = lax.optimization_barrier(
        (attn_given, attn_own, small_early, down_sum, both_sums[0])
    )
    attn_parts = added(attn_own, core_swap(attn_given)).reshape(chips, attn_hold, tile, tile)
    attn_sum = attn_parts[0]
    attn_parts = [attn_parts[offset].astype(bf16) for offset in range(1, chips)]
    normed_pre = matmul_flip(first_grad_low, w_first)
    attn_sum, attn_parts, normed_pre = lax.optimization_barrier((attn_sum, attn_parts, normed_pre))
    normed_sum = seq_sum(normed_pre, bf16)
    for offset in range(1, chips):
        attn_sum = attn_sum + chip_shift(attn_parts[offset - 1], offset).astype(f32)
    attn_sum = attn_sum.astype(bf16)
    attn_sum, normed_sum = lax.optimization_barrier((attn_sum, normed_sum))
    attn_back = pick(
        (column_slots[3][None, None, :] == (my_seq ^ flips)[:, None, None])
        & (column_slots[0][None, None, :] == my_key)
        & (column_slots[2][None, None, :] == jnp.arange(attn_room)[None, :, None]),
        column_slots[1],
    )

    grad_normed = half_grad + matmul_flip(left_grad_low, laurel_left) + normed_sum
    grad_stream_norm, grad_gain_in = normed_pull(grad_normed)
    input_grad = (half_grad + grad_stream_norm)[None]
    gain_grad = jnp.concatenate(
        [
            grad_gain_in,
            grad_gain_attn,
            grad_gain_laurel,
            grad_gain_pre,
            grad_gain_post,
            grad_gain_vec,
            grad_gain_query,
            grad_gain_key,
        ]
    )
    late_full = jnp.concatenate(
        [matmul_outer(normed_low, left_grad_low), matmul_outer(right_grad_low, left_low)], axis=1
    )
    late = jnp.concatenate(
        [late_full.reshape(seq_size, -1), gain_grad.reshape(seq_size, -1)], axis=1
    ).reshape(seq_size, -1, tile)
    late = seq_sum(late.reshape(-1, tile), bf16, True)

    late = late.astype(bf16)
    late = added(late, core_swap(late)).astype(bf16)
    both_sums, late, input_grad = lax.optimization_barrier((both_sums, late, input_grad))
    ffn_sums = both_sums + [core_swap(value) for value in both_sums]
    ffn_sums = ffn_sums + [down_sum, core_swap(down_sum)]
    late = jnp.pad(late, ((0, 2 * late_count * tile - late.shape[0]), (0, 0)))
    late = late.reshape(2, late_count, tile, tile)
    late = lax.dynamic_index_in_dim(late, my_core, 0, False)
    late_index = 2 * (both_hold + down_hold) + jnp.arange(late_count)
    ffn_return = [
        gather_tiles(ffn_sums + [late], jnp.concatenate([ffn_back[i], late_index]))
        for i in range(chips)
    ]
    ffn_return, attn_sum = lax.optimization_barrier((ffn_return, attn_sum))
    ffn_returned = chip_exchange(ffn_return)
    attn_returned = seq_exchange([gather_tiles([attn_sum], attn_back[i]) for i in range(seq_size)])
    attn_returned = attn_returned + [core_swap(value) for value in attn_returned]
    back_size = 2 * chips * return_size
    slot_grad = jnp.where(my_slots[0] >= 0, my_slots[1], back_size + my_slots[2])

    def slow_return():
        own_ffn = split_tiles(both_grad_w, tile), split_tiles(down_grad_w, tile)
        own_attn = split_tiles(first_grad_w, tile), split_tiles(out_grad_w, tile)
        parts = jnp.concatenate(own_ffn + own_attn + (jnp.zeros((1, tile, tile), bf16),))
        index = jnp.where(
            ffn_to == my_fsdp,
            is_down * both_count + ffn_place,
            jnp.where(attn_to == my_seq, ffn_count + attn_place, ffn_count + attn_count),
        )
        spread = gather_tiles([parts], index.reshape(-1))
        spread = lax.all_to_all(
            spread.reshape((seq_size * fsdp_size, mine, tile, tile)),
            ("seq", "fsdp"),
            split_axis=0,
            concat_axis=0,
            tiled=True,
        )
        return jnp.sum(spread.astype(f32), axis=0).astype(bf16)

    slow_start = back_size + 2 * seq_size * attn_room
    slow_grads = lax.cond(fits, lambda: jnp.zeros((mine, tile, tile), bf16), slow_return)
    ffn_returned, slow_grads = lax.optimization_barrier((ffn_returned, slow_grads))
    late = sum(value[ffn_room:].astype(f32) for value in ffn_returned).astype(bf16)
    late = core_pair(late).reshape(-1, tile).astype(f32)
    ffn_returned = ffn_returned + [core_swap(value) for value in ffn_returned]
    tile_grads = ffn_returned + attn_returned + [slow_grads]
    slot_grad = jnp.where(fits, slot_grad, slow_start + local_slots)

    tile_new, tile_first_new, tile_second_new = rotate_update(
        tile_grads, slot_grad, tile_master, tile_first, tile_second, left_basis, right_basis, RATE_TILE
    )
    late_rows = late_full.shape[0] // seq_size
    late_tiles = late[:late_rows].reshape(-1, 1, tile, tile)
    gain_grad_mine = late[late_rows : late_rows + own_gains.shape[0] // tile].reshape(-1)
    small_grad = jnp.concatenate(
        [
            late_tiles.astype(bf16),
            small_early.reshape(late_tiles.shape[0], -1, tile, tile),
        ],
        axis=1,
    ).reshape(small_master.shape)
    small_new, small_first_new, small_second_new = rotate_update(
        [small_grad],
        jnp.arange(small_master.shape[0]),
        small_master,
        small_first,
        small_second,
        small_left,
        small_right,
        RATE_SMALL,
    )
    gain_first_new = BETA_ONE * gain_first + (1.0 - BETA_ONE) * gain_grad_mine
    gain_second_new = BETA_TWO * gain_second + (1.0 - BETA_TWO) * gain_grad_mine * gain_grad_mine
    correct_one = 1.0 - BETA_ONE**STEP
    correct_two = 1.0 - BETA_TWO**STEP
    gain_new = gains - RATE_GAIN * (gain_first_new / correct_one) / (
        jnp.sqrt(gain_second_new / correct_two) + ADAM_EPS
    )
    return (
        output,
        input_grad,
        tile_new,
        tile_first_new,
        tile_second_new,
        small_new,
        small_first_new,
        small_second_new,
        gain_new,
        gain_first_new,
        gain_second_new,
    )


def solution(mesh):
    return jax.shard_map(
        on_device,
        mesh=mesh,
        in_specs=(
            P("fsdp", "seq", None),
            P("fsdp", "seq", None),
            P("fsdp", None),
            P("fsdp", "seq", None),
            P(),
            P(("seq", "fsdp"), None, None),
            P(("seq", "fsdp"), None, None),
            P(("seq", "fsdp"), None, None),
            P(("seq", "fsdp"), None, None),
            P(("seq", "fsdp"), None, None),
            P("seq", None, None),
            P("seq", None, None),
            P("seq", None, None),
            P("seq", None, None),
            P("seq", None, None),
            P("seq"),
            P("seq"),
            P("seq"),
        ),
        out_specs=(
            P("fsdp", "seq", None),
            P("fsdp", "seq", None),
            P(("seq", "fsdp"), None, None),
            P(("seq", "fsdp"), None, None),
            P(("seq", "fsdp"), None, None),
            P("seq", None, None),
            P("seq", None, None),
            P("seq", None, None),
            P("seq"),
            P("seq"),
            P("seq"),
        ),
        check_vma=False,
    )
```

```python
import math

import jax
import jax.numpy as jnp
from jax import lax
from jax.experimental import pallas as pl
from jax.experimental.pallas import tpu as pltpu
from jax.sharding import PartitionSpec as P

HEADS = 8
KV_HEADS = 2
HEAD_DIM = 256
FF = 8192
RANK = 64
PLD = 256
STEP = 5


EPS = 1e-06
SCALE = 0.0625
THETA = 1000000.0
ROOT_HALF = 0.7071067811865476
BETA_ONE = 0.5
BETA_TWO = 0.5
ADAM_EPS = 1e-08
RATE_TILE = 0.02
RATE_SMALL = 0.04
RATE_GAIN = 0.3
DECAY = 0.01
NEGATIVE = -1e30
TILE = 128
VMEM_BYTES = 4 * 1024 * 1024


def rms_norm(value, gain):
    return value * lax.rsqrt(jnp.mean(value * value, axis=-1, keepdims=True) + EPS) * gain


def rotary(value, position):
    half = value.shape[-1] // 2
    freq = THETA ** (-2.0 * jnp.arange(half).astype(jnp.float32) / value.shape[-1])
    angle = position.astype(jnp.float32)[:, None] * freq[None, :]
    cosine = jnp.cos(angle)[:, None, :]
    sine = jnp.sin(angle)[:, None, :]
    first = value[..., :half]
    second = value[..., half:]
    return jnp.concatenate(
        [first * cosine - second * sine, second * cosine + first * sine], axis=-1
    )


def documents(lengths, length):
    places = jnp.arange(length)
    ends = jnp.cumsum(lengths)
    passed = places[:, None] >= ends[None, :]
    segment = jnp.sum(passed.astype(jnp.int32), axis=1)
    before = jnp.sum(jnp.where(passed, lengths[None, :], 0), axis=1)
    return (segment, places - before)


def matmul(left, right):
    return jnp.dot(left, right, preferred_element_type=jnp.float32)


def matmul_flip(left, right):
    return lax.dot_general(
        left, right, (((1,), (1,)), ((), ())), preferred_element_type=jnp.float32
    )


def matmul_outer(left, right):
    return lax.dot_general(
        left, right, (((0,), (0,)), ((), ())), preferred_element_type=jnp.float32
    )


def assemble(tiles, row_blocks):
    size = tiles.shape[1]
    column_blocks = tiles.shape[0] // row_blocks
    return (
        tiles.reshape(row_blocks, column_blocks, size, size)
        .transpose(0, 2, 1, 3)
        .reshape(row_blocks * size, column_blocks * size)
    )


def split_tiles(matrix, size):
    row_blocks = matrix.shape[0] // size
    column_blocks = matrix.shape[1] // size
    return (
        matrix.reshape(row_blocks, size, column_blocks, size)
        .transpose(0, 2, 1, 3)
        .reshape(row_blocks * column_blocks, size, size)
    )


def gelu_product(first, second):
    return jax.nn.gelu(first, approximate=True) * second


def room(count, share):
    mean = count * share
    return math.ceil(mean + 3.6 * math.sqrt(mean * (1.0 - share)) + 3.0)


def count_earlier(group, valid):
    size = group.shape[-1]
    order = jnp.arange(size)
    same = (group[..., :, None] == group[..., None, :]) & valid[..., None, :]
    same = same & (order[None, :] < order[:, None])
    return jnp.sum(same.astype(jnp.int32), axis=-1)


def count_long(keys):
    groups, size = keys.shape

    def kernel(row_ref, column_ref, out_ref):
        row = row_ref[0]
        column = column_ref[0]
        here = lax.broadcasted_iota(jnp.int32, (size, size), 1)
        other = lax.broadcasted_iota(jnp.int32, (size, size), 0)
        earlier = (column == row) & (other < here)
        out_ref[0] = jnp.sum(earlier.astype(jnp.int32), axis=0, keepdims=True)

    return pl.pallas_call(
        kernel,
        grid=(groups,),
        out_shape=jax.ShapeDtypeStruct((groups, 1, size), jnp.int32),
        in_specs=[
            pl.BlockSpec((1, 1, size), lambda i: (i, 0, 0)),
            pl.BlockSpec((1, size, 1), lambda i: (i, 0, 0)),
        ],
        out_specs=pl.BlockSpec((1, 1, size), lambda i: (i, 0, 0)),
        cost_estimate=pl.CostEstimate(flops=0, transcendentals=0, bytes_accessed=0),
        compiler_params=pltpu.CompilerParams(vmem_limit_bytes=4 * VMEM_BYTES),
    )(keys[:, None, :], keys[:, :, None]).reshape(groups, size)


def pick(match, value):
    return jnp.sum(jnp.where(match, value, 0), axis=-1)


def steps_of(counts):
    for steps in (8, 4, 2):
        if all(count % steps == 0 for count in counts) and sum(counts) // steps >= 24:
            return steps
    return 1


def tile_kernel_call(kernel, index, arrays, out_shape, out_specs, steps):
    moved = sum(math.prod(one.shape) * 2 for one in jax.tree.leaves(out_shape))
    return pl.pallas_call(
        kernel,
        grid=(steps,),
        cost_estimate=pl.CostEstimate(flops=0, transcendentals=0, bytes_accessed=2 * moved),
        out_shape=out_shape,
        in_specs=[pl.BlockSpec(memory_space=pltpu.SMEM)]
        + [pl.BlockSpec(memory_space=pl.ANY)] * len(arrays),
        out_specs=out_specs,
        scratch_shapes=[pltpu.SemaphoreType.DMA],
        compiler_params=pltpu.CompilerParams(vmem_limit_bytes=2 * moved // steps + VMEM_BYTES),
    )(index, *arrays)


def start_copy(sources, place, target, sem, start=0):
    if len(sources) == 1:
        pltpu.make_async_copy(sources[0].at[place - start], target, sem).start()
        return
    half = len(sources) // 2
    middle = start + sum(ref.shape[0] for ref in sources[:half])

    @pl.when(place < middle)
    def _():
        start_copy(sources[:half], place, target, sem, start)

    @pl.when(place >= middle)
    def _():
        start_copy(sources[half:], place, target, sem, middle)


def fill_tiles(arrays, indices, total, start):
    tile = arrays[0].shape[-1] if arrays[0].ndim == 3 else TILE
    counts = [index.shape[0] for index in indices]
    steps = steps_of(counts)

    def kernel(index_ref, *refs):
        sources, outs, sem = refs[: len(arrays)], refs[len(arrays) : -1], refs[-1]
        first = 0
        for out, count in zip(outs, counts):
            each = count // steps
            base = first + pl.program_id(0) * each

            def step(i, carry, out=out, base=base):
                start(sources, index_ref[base + i], out.at[i], sem)
                return carry

            lax.fori_loop(0, each, step, 0)
            first = first + count
        for out in outs:
            pltpu.make_async_copy(out, out, sem).wait()

    return tile_kernel_call(
        kernel,
        jnp.clip(jnp.concatenate(indices), 0, total - 1),
        arrays,
        [jax.ShapeDtypeStruct((count, tile, tile), arrays[0].dtype) for count in counts],
        [pl.BlockSpec((count // steps, tile, tile), lambda i: (i, 0, 0)) for count in counts],
        steps,
    )


def gather_tiles(arrays, indices):
    return fill_tiles(arrays, indices, sum(array.shape[0] for array in arrays), start_copy)


def cut_tiles(matrices, indices):
    row_blocks = matrices[0].shape[0] // TILE
    widths = [matrix.shape[1] // TILE for matrix in matrices]

    def start(sources, place, target, sem):
        first = 0
        for ref, width in zip(sources, widths):
            size = row_blocks * width

            @pl.when((place >= first) & (place < first + size))
            def _(ref=ref, first=first, width=width):
                row = (place - first) // width
                column = place - first - row * width
                source = ref.at[
                    pl.ds(pl.multiple_of(row * TILE, TILE), TILE),
                    pl.ds(pl.multiple_of(column * TILE, TILE), TILE),
                ]
                pltpu.make_async_copy(source, target, sem).start()

            first = first + size

    return fill_tiles(matrices, indices, row_blocks * sum(widths), start)


def join_tiles(arrays, index, row_blocks, columns):
    tile = arrays[0].shape[-1]
    steps = 4
    each = row_blocks // steps

    def kernel(index_ref, *refs):
        sources, outs, sem = refs[: len(arrays)], refs[len(arrays) : -1], refs[-1]
        base = pl.program_id(0) * each
        start = 0
        for out, width in zip(outs, columns):

            def step(i, carry, out=out, start=start, width=width):
                row = i // width
                column = i - row * width
                target = out.at[
                    pl.ds(pl.multiple_of(row * tile, tile), tile),
                    pl.ds(pl.multiple_of(column * tile, tile), tile),
                ]
                start_copy(sources, index_ref[start + base * width + i], target, sem)
                return carry

            lax.fori_loop(0, each * width, step, 0)
            start = start + row_blocks * width
        for out in outs:
            pltpu.make_async_copy(out, out, sem).wait()

    total = sum(array.shape[0] for array in arrays)
    out_shape = tuple(
        jax.ShapeDtypeStruct((row_blocks * tile, width * tile), arrays[0].dtype)
        for width in columns
    )
    out_specs = tuple(pl.BlockSpec((each * tile, width * tile), lambda i: (i, 0)) for width in columns)
    return tile_kernel_call(
        kernel, jnp.clip(index, 0, total - 1), arrays, out_shape, out_specs, steps
    )


def split_low(value):
    high = value.astype(jnp.bfloat16)
    return high, (value - high.astype(jnp.float32)).astype(jnp.bfloat16)


def rotate_update(grads, index, master, first, second, left, right, rate):
    count, tile, _ = master.shape
    each = 4 if count % 4 == 0 else 1
    correct_one = 1.0 - BETA_ONE**STEP
    correct_two = 1.0 - BETA_TWO**STEP

    def product(one, two, dims):
        return lax.dot_general(one, two, (dims, ((), ())), preferred_element_type=jnp.float32)

    def kernel(index_ref, *refs):
        sources, refs = refs[: len(grads)], refs[len(grads) :]
        master_ref, first_ref, second_ref, left_ref, right_ref = refs[:5]
        master_out, first_out, second_out, held, sems = refs[5:]
        now = pl.program_id(0)

        @pl.when(now == 0)
        def _():
            def step(i, carry):
                start_copy(sources, index_ref[i], held.at[i], sems.at[i // each])
                return carry

            lax.fori_loop(0, count, step, 0)

        block = held.at[pl.ds(now * each, each)]
        pltpu.make_async_copy(block, block, sems.at[now]).wait()
        lefts, rights, turns = [], [], []
        for i in range(each):
            grad = held[now * each + i]
            lefts.append(split_low(left_ref[i]))
            rights.append(split_low(right_ref[i]))
            half_turned = product(
                jnp.concatenate([grad, grad], axis=1),
                jnp.concatenate(rights[i], axis=0),
                ((1,), (0,)),
            )
            turns.append(split_low(half_turned))
        for i in range(each):
            (left_high, left_low), (high, low) = lefts[i], turns[i]
            turns[i] = product(
                jnp.concatenate([left_high, left_high, left_low], axis=0),
                jnp.concatenate([high, low, high], axis=0),
                ((0,), (0,)),
            )
        for i in range(each):
            right_high, right_low = rights[i]
            first_new = BETA_ONE * first_ref[i] + (1.0 - BETA_ONE) * turns[i]
            second_new = BETA_TWO * second_ref[i] + (1.0 - BETA_TWO) * turns[i] * turns[i]
            first_out[i] = first_new
            second_out[i] = second_new
            high, low = split_low(
                first_new / correct_one / (jnp.sqrt(second_new / correct_two) + ADAM_EPS)
            )
            half_back = product(
                jnp.concatenate([high, low, high], axis=1),
                jnp.concatenate([right_high, right_high, right_low], axis=1),
                ((1,), (1,)),
            )
            turns[i] = split_low(half_back)
        for i in range(each):
            (left_high, left_low), (high, low) = lefts[i], turns[i]
            back = product(
                jnp.concatenate([left_high, left_high, left_low], axis=1),
                jnp.concatenate([high, low, high], axis=0),
                ((1,), (0,)),
            )
            weight = master_ref[i]
            master_out[i] = weight - rate * (back + DECAY * weight)

    spec = pl.BlockSpec((each, tile, tile), lambda i: (i, 0, 0))
    shape = jax.ShapeDtypeStruct(master.shape, jnp.float32)
    total = sum(array.shape[0] for array in grads)
    return pl.pallas_call(
        kernel,
        grid=(count // each,),
        out_shape=(shape, shape, shape),
        in_specs=[pl.BlockSpec(memory_space=pltpu.SMEM)]
        + [pl.BlockSpec(memory_space=pl.ANY)] * len(grads)
        + [spec] * 5,
        out_specs=(spec, spec, spec),
        scratch_shapes=[
            pltpu.VMEM((count, tile, tile), jnp.bfloat16),
            pltpu.SemaphoreType.DMA((count // each,)),
        ],
        compiler_params=pltpu.CompilerParams(vmem_limit_bytes=4 * VMEM_BYTES),
    )(jnp.clip(index, 0, total - 1), *grads, master, first, second, left, right)


def seq_swap(value, flip):
    size = lax.axis_size("seq")
    return lax.ppermute(value, "seq", [(i, i ^ flip) for i in range(size)])


def take_blocks(value, order):
    return jnp.stack(
        [lax.dynamic_index_in_dim(value, order[i], 0, False) for i in range(order.shape[0])]
    )


def core_swap(value):
    size = lax.axis_size("fsdp")
    return lax.ppermute(value, "fsdp", [(i, i ^ 1) for i in range(size)])


def chip_shift(value, offset):
    size = lax.axis_size("fsdp")
    chips = size // 2
    return lax.ppermute(
        value, "fsdp", [(i, (i // 2 + offset) % chips * 2 + i % 2) for i in range(size)]
    )


def seq_gather(value):
    size = lax.axis_size("seq")
    return jnp.concatenate([value] + [seq_swap(value, flip) for flip in range(1, size)], axis=0)


def seq_ordered(value):
    size = lax.axis_size("seq")
    parts = jnp.stack([value] + [seq_swap(value, flip) for flip in range(1, size)], axis=0)
    return take_blocks(parts, lax.axis_index("seq") ^ jnp.arange(size))


def seq_exchange(values):
    return [values[0]] + [seq_swap(values[flip], flip) for flip in range(1, len(values))]


def seq_sum(value, wire, ordered=False):
    size = lax.axis_size("seq")
    parts = value.reshape((size, value.shape[0] // size) + value.shape[1:])
    if ordered:
        parts = take_blocks(parts, lax.axis_index("seq") ^ jnp.arange(size))
    total = parts[0]
    for flip in range(1, size):
        total = total + seq_swap(parts[flip].astype(wire), flip).astype(jnp.float32)
    return total


def chip_exchange(values):
    return [values[0]] + [chip_shift(values[offset], offset) for offset in range(1, len(values))]


def core_pair(value):
    other = core_swap(value)
    even = lax.axis_index("fsdp") % 2 == 0
    return jnp.where(even, jnp.stack([value, other]), jnp.stack([other, value]))


def small_sum(value):
    seq_size = lax.axis_size("seq")
    chips = lax.axis_size("fsdp") // 2
    chip = lax.axis_index("fsdp") // 2
    even = lax.axis_index("fsdp") % 2 == 0
    low = value.astype(jnp.bfloat16)
    parts = low.reshape((seq_size, 2, low.shape[0] // (2 * seq_size)) + low.shape[1:])
    kept = jnp.where(even, parts[:, 0], parts[:, 1]).astype(jnp.float32)
    given = jnp.where(even, parts[:, 1], parts[:, 0])
    kept = kept + core_swap(given).astype(jnp.float32)
    kept = seq_sum(kept.reshape((-1,) + low.shape[1:]), jnp.bfloat16, True)
    kept = kept.reshape((chips, kept.shape[0] // chips) + kept.shape[1:])
    kept = take_blocks(kept, (chip + jnp.arange(chips)) % chips)
    total = kept[0]
    for offset in range(1, chips):
        total = total + chip_shift(kept[offset].astype(jnp.bfloat16), offset).astype(jnp.float32)
    total = total.astype(jnp.bfloat16)
    parts = jnp.stack([total] + [chip_shift(total, offset) for offset in range(1, chips)])
    parts = take_blocks(parts, (chip - jnp.arange(chips)) % chips)
    return core_pair(parts).reshape((value.shape[0] // seq_size,) + value.shape[1:])


def turn(value, cosine, sine):
    half = value.shape[-1] // 2
    first, second = value[..., :half], value[..., half:]
    return jnp.concatenate(
        [first * cosine - second * sine, second * cosine + first * sine], axis=-1
    )


def added(one, two):
    return one.astype(jnp.float32) + two.astype(jnp.float32)


def on_device(
    tokens,
    layer_vectors,
    doc_lengths,
    cotangent,
    tile_owner,
    tile_master,
    tile_first,
    tile_second,
    left_basis,
    right_basis,
    small_master,
    small_first,
    small_second,
    small_left,
    small_right,
    gains,
    gain_first,
    gain_second,
):
    bf16 = jnp.bfloat16
    f32 = jnp.float32
    tile = tile_master.shape[1]
    width = tokens.shape[2]
    row_blocks = width // tile
    rows = tokens.shape[1]
    seq_size = lax.axis_size("seq")
    fsdp_size = lax.axis_size("fsdp")
    chips = fsdp_size // 2
    mine = tile_master.shape[0]
    tiles = tile_owner.shape[0]
    length = rows * seq_size
    per_device = HEADS // seq_size
    per_key = seq_size // KV_HEADS
    query_width = HEADS * HEAD_DIM
    key_width = KV_HEADS * HEAD_DIM
    my_seq = lax.axis_index("seq")
    my_fsdp = lax.axis_index("fsdp")
    my_chip = my_fsdp // 2
    my_core = my_fsdp % 2
    flips = jnp.arange(seq_size)
    shifts = jnp.arange(chips)

    query_blocks = query_width // tile
    key_blocks = key_width // tile
    ffn_blocks = FF // tile
    query_each = query_blocks // seq_size
    head_blocks = HEAD_DIM // tile
    ffn_each = ffn_blocks // fsdp_size
    columns = tiles // row_blocks
    attn_first = query_each + head_blocks
    attn_count = row_blocks * (attn_first + query_each)
    ffn_first = 2 * ffn_each
    ffn_count = row_blocks * 3 * ffn_each
    attn_share = (2 * query_blocks + 2 * key_blocks) / columns
    ffn_share = 3 * ffn_blocks / columns
    attn_room = (room(2 * mine, attn_share / seq_size) + 1) // 2
    attn_hold = (room(attn_count, 1.0 / chips) + 1) // 2 + 1
    ffn_room = (room(2 * mine, ffn_share / chips) + 1) // 2
    both_count = row_blocks * ffn_first
    ffn_hold = (room(ffn_count, 1.0 / seq_size) + 3) // 4 * 4
    ffn_half = ffn_hold * 3 // 7 // 4 * 4
    ffn_rest = ffn_hold - ffn_half

    def tile_places(owner):
        row = owner // columns
        column = owner % columns
        key_at = column - query_blocks
        value_at = key_at - key_blocks
        out_at = value_at - key_blocks
        ffn_at = out_at - query_blocks
        is_attn = ffn_at < 0
        kind = ffn_at // ffn_blocks
        ffn_column = ffn_at % ffn_blocks
        ffn_to = jnp.where(is_attn, -1, ffn_column // ffn_each)
        ffn_local = ffn_column % ffn_each
        ffn_place = jnp.where(
            kind == 2,
            both_count + row * ffn_each + ffn_local,
            row * ffn_first + kind * ffn_each + ffn_local,
        )
        attn_to = jnp.where(
            key_at < 0,
            column // query_each,
            jnp.where(
                value_at < 0,
                key_at // head_blocks * per_key,
                jnp.where(
                    out_at < 0,
                    value_at // head_blocks * per_key + per_key - 1,
                    out_at // query_each,
                ),
            ),
        )
        attn_place = jnp.where(
            key_at < 0,
            row * attn_first + column % query_each,
            jnp.where(
                out_at < 0,
                row * attn_first + query_each + key_at % head_blocks,
                row_blocks * attn_first + row * query_each + out_at % query_each,
            ),
        )
        attn_to = jnp.where(is_attn, attn_to, -1)
        return (ffn_to, ffn_place, attn_to, attn_place)

    owners = tile_owner.reshape(seq_size, fsdp_size, mine)
    slot_seq = jnp.arange(seq_size)[:, None, None]
    slot_fsdp = jnp.arange(fsdp_size)[None, :, None]
    slot_chip = slot_fsdp // 2
    local_slots = jnp.arange(mine)
    both_slots = jnp.arange(2 * mine)
    both_slots = jnp.where(
        both_slots // mine == my_core, both_slots % mine, mine + both_slots % mine
    )

    ffn_to = tile_places(owners)[0]
    ffn_chip = jnp.where(ffn_to < 0, -1, ffn_to // 2)
    chip_view = ffn_chip.reshape(seq_size, chips, 2 * mine)
    chip_rank = count_earlier(chip_view, chip_view >= 0).reshape(owners.shape)
    ffn_slots = lax.dynamic_slice(
        jnp.stack([ffn_chip, chip_rank]), (0, my_seq, 2 * my_chip, 0), (2, 1, 2, mine)
    ).reshape(2, 1, 1, 2 * mine)
    ffn_pack = pick(
        (ffn_slots[0] == ((my_chip + shifts) % chips)[:, None, None])
        & (ffn_slots[1] == (my_core * ffn_room + jnp.arange(ffn_room))[None, :, None]),
        both_slots,
    )
    master_low = tile_master.astype(bf16)
    masters = [master_low, core_swap(master_low)]
    ffn_sent = gather_tiles(masters, [ffn_pack[i] for i in range(chips)])
    small_rows = small_master.shape[0] // 2
    small_half = lax.dynamic_slice_in_dim(small_master, my_core * small_rows, small_rows)
    masters, ffn_sent, chip_rank, owners, own_tokens, own_gains, small_half = (
        lax.optimization_barrier(
            (
                masters,
                ffn_sent,
                chip_rank,
                owners,
                tokens[0],
                gains.astype(bf16),
                small_half.astype(bf16),
            )
        )
    )
    ffn_got = chip_exchange(ffn_sent)

    ffn_to, ffn_place, attn_to, attn_place = tile_places(owners)
    ffn_chip = jnp.where(ffn_to < 0, -1, ffn_to // 2)
    attn_view = attn_to.reshape(seq_size, chips, 2 * mine)
    attn_rank = count_earlier(attn_view, attn_view >= 0).reshape(owners.shape)
    attn_core = (attn_rank + slot_seq) % 2
    attn_rank = attn_rank // 2
    attn_key = jnp.where(attn_to < 0, -1, 2 * attn_to + attn_core)

    chip_slots = lax.dynamic_slice(
        jnp.stack([attn_key, attn_rank]), (0, my_seq, 2 * my_chip, 0), (2, 1, 2, mine)
    ).reshape(2, 1, 1, 2 * mine)
    attn_message = attn_room + row_blocks * rows // tile + small_rows + -(-own_gains.shape[0] // tile**2)
    attn_pack = pick(
        (chip_slots[0] == (2 * (my_seq ^ flips) + my_core)[:, None, None])
        & (chip_slots[1] == jnp.arange(attn_room)[None, :, None]),
        both_slots,
    )
    attn_sent = gather_tiles(masters, [attn_pack[i] for i in range(seq_size)])
    seq_view = ffn_to.reshape(seq_size, fsdp_size * mine)
    ffn_rank = count_long(seq_view).reshape(owners.shape)
    def by_chip(value):
        value = value.reshape(seq_size, chips, 2 * mine).transpose(1, 0, 2)
        return value.reshape(chips, seq_size * 2 * mine)

    attn_key_chip = by_chip(attn_key)
    attn_order_chip = count_long(attn_key_chip)
    attn_order = (
        attn_order_chip.reshape(chips, seq_size, 2 * mine).transpose(1, 0, 2).reshape(owners.shape)
    )
    fits = jnp.all(
        jnp.where(
            ffn_to < 0,
            (attn_rank < attn_room) & (attn_order < attn_hold),
            (chip_rank < 2 * ffn_room) & (ffn_rank < ffn_hold),
        )
    )
    half = chips * ffn_room
    rows_late = 2 * RANK * row_blocks // seq_size
    rank_core = chip_rank // ffn_room
    rank_local = chip_rank % ffn_room
    out_place = (
        jnp.where(rank_core == my_core, 0, half)
        + (my_chip - slot_chip) % chips * ffn_room
        + rank_local
    )
    late_count = -(-(rows_late + own_gains.shape[0] // tile) // (2 * tile))
    return_size = ffn_room + late_count
    back_place = (
        jnp.where(rank_core == my_core, 0, chips * return_size)
        + (my_chip - ffn_chip) % chips * return_size
        + rank_local
    )
    attn_back_place = (
        jnp.where(attn_core == my_core, 0, seq_size * attn_room)
        + (attn_to ^ my_seq) * attn_room
        + attn_rank
    )
    my_slots = lax.dynamic_slice(
        jnp.stack([ffn_to, back_place, attn_back_place]), (0, my_seq, my_fsdp, 0), (3, 1, 1, mine)
    ).reshape(3, mine)
    seq_slots = lax.dynamic_slice(
        jnp.stack(
            [
                ffn_to,
                ffn_rank,
                ffn_chip,
                out_place,
                chip_rank,
                jnp.broadcast_to(slot_chip, owners.shape),
            ]
        ),
        (0, my_seq, 0, 0),
        (6, 1, fsdp_size, mine),
    ).reshape(6, fsdp_size * mine)
    column_slots = lax.dynamic_slice(
        jnp.stack([attn_key, attn_order, attn_rank, jnp.broadcast_to(slot_seq, owners.shape)]),
        (0, 0, 2 * my_chip, 0),
        (4, seq_size, 2, mine),
    ).reshape(4, 2 * seq_size * mine)
    my_key = 2 * my_seq + my_core

    attn_keep = pick(
        (column_slots[0][None, :] == my_key)
        & (column_slots[1][None, :] == jnp.arange(attn_hold)[:, None]),
        jnp.where(
            column_slots[3] == my_seq,
            0,
            attn_room + ((column_slots[3] ^ my_seq) - 1) * attn_message,
        )
        + column_slots[2],
    )
    attn_join = pick(
        (attn_to.reshape(1, -1) == my_seq)
        & (attn_place.reshape(1, -1) == jnp.arange(attn_count)[:, None]),
        (
            jnp.where(attn_core == my_core, 0, chips * attn_hold)
            + (my_chip - slot_chip) % chips * attn_hold
            + attn_order
        ).reshape(1, -1),
    )
    ffn_keep = pick(
        (seq_slots[0][None, :] == my_fsdp) & (seq_slots[1][None, :] == jnp.arange(ffn_hold)[:, None]),
        seq_slots[3][None, :],
    )
    ffn_join = pick(
        (ffn_to.reshape(1, -1) == my_fsdp)
        & (ffn_place.reshape(1, -1) == jnp.arange(ffn_count)[:, None]),
        (
            jnp.where(
                ffn_rank < ffn_half,
                slot_seq * ffn_half + ffn_rank,
                seq_size * ffn_half + slot_seq * ffn_rest + ffn_rank - ffn_half,
            )
        ).reshape(1, -1),
    )
    ffn_cut = pick(
        (ffn_to.reshape(seq_size, 1, -1) == my_fsdp)
        & (ffn_rank.reshape(seq_size, 1, -1) == jnp.arange(ffn_hold)[None, :, None]),
        ffn_place.reshape(seq_size, 1, -1),
    )
    ffn_back = pick(
        (seq_slots[5][None, None, :] == ((my_chip + shifts) % chips)[:, None, None])
        & (seq_slots[2][None, None, :] == my_chip)
        & (seq_slots[4][None, None, :] == (my_core * ffn_room + jnp.arange(ffn_room))[None, :, None]),
        jnp.where(seq_slots[0] == my_fsdp, 0, ffn_hold) + seq_slots[1],
    )

    token_tiles = own_tokens.reshape(rows, row_blocks, tile).transpose(1, 0, 2)
    token_tiles = token_tiles.reshape(-1, tile, tile)
    gain_rows = own_gains.reshape(-1, tile)
    gain_tiles = jnp.pad(gain_rows, ((0, -gain_rows.shape[0] % tile), (0, 0))).reshape(-1, tile, tile)
    common = jnp.concatenate([token_tiles, small_half, gain_tiles])
    attn_got = [attn_sent[0]] + [
        seq_swap(jnp.concatenate([attn_sent[flip], common]), flip) for flip in range(1, seq_size)
    ]
    segment, position = documents(doc_lengths[0], length)
    places = ((my_seq ^ flips)[:, None] * rows + jnp.arange(rows)[None, :]).reshape(-1)

    def reorder(values):
        blocks = values.reshape(seq_size, rows)
        return jnp.concatenate(
            [lax.dynamic_index_in_dim(blocks, my_seq ^ i, 0, False) for i in range(seq_size)]
        )

    pack_segment = reorder(segment)
    allow = (pack_segment[:, None] == pack_segment[None, :]) & (
        places[None, :] <= places[:, None]
    )
    turns = jnp.arange(HEAD_DIM // 2).astype(f32)
    angle = reorder(position).astype(f32)[:, None] * (THETA ** (-2.0 * turns / HEAD_DIM))[None, :]
    cosine, sine = jnp.cos(angle)[:, None, :], jnp.sin(angle)[:, None, :]
    parts = [common] + [value[attn_room:] for value in attn_got[1:]]
    token_end = token_tiles.shape[0]
    small_end = token_end + small_rows

    def seq_order(value):
        return take_blocks(value, my_seq ^ flips)

    pack_tokens = jnp.concatenate(
        [
            part[:token_end].reshape(row_blocks, rows, tile).transpose(1, 0, 2).reshape(rows, width)
            for part in parts
        ]
    )
    gain_full = seq_order(
        jnp.stack([part[small_end:].reshape(-1, tile)[: gain_rows.shape[0]] for part in parts])
    )
    gain_full = gain_full.reshape(-1).astype(f32)
    gain_in = gain_full[0:width]
    pack_normed = rms_norm(pack_tokens.astype(f32), gain_in).astype(bf16)
    ready = (allow, cosine, sine, ffn_keep, attn_keep, pack_normed, gain_full)
    ffn_got, attn_got, parts, ready = lax.optimization_barrier((ffn_got, attn_got, parts, ready))
    allow, cosine, sine, ffn_keep, attn_keep, pack_normed, gain_full = ready
    gain_in = gain_full[0:width]
    small_got = core_pair(seq_order(jnp.stack([part[token_end:small_end] for part in parts])))
    small_got = small_got.transpose(1, 0, 2, 3, 4)
    small_table = assemble(small_got.reshape((-1,) + small_master.shape[1:]), row_blocks)
    (attn_kept,) = gather_tiles(attn_got, [attn_keep])
    ffn_got = ffn_got + [core_swap(value) for value in ffn_got]
    ffn_kept = gather_tiles(ffn_got, [ffn_keep[:ffn_half], ffn_keep[ffn_half:]])
    ffn_kept, attn_kept = lax.optimization_barrier((ffn_kept, attn_kept))
    ffn_all = [lax.all_gather(value, "seq", axis=0, tiled=True) for value in ffn_kept]
    attn_all = [attn_kept] + [chip_shift(attn_kept, offset) for offset in range(1, chips)]
    attn_all = attn_all + [core_swap(value) for value in attn_all]

    attn_all, ffn_all[0], attn_join = lax.optimization_barrier((attn_all, ffn_all[0], attn_join))

    def fetch(arrays, index, to, me, place, columns_of):
        def fast():
            return join_tiles(arrays, index, row_blocks, columns_of)

        def slow():
            whole = lax.all_to_all(
                jnp.broadcast_to(master_low[None], (seq_size * fsdp_size,) + master_low.shape),
                ("seq", "fsdp"),
                split_axis=0,
                concat_axis=0,
                tiled=True,
            ).reshape(-1, tile, tile)
            count = row_blocks * sum(columns_of)
            slots = pick(
                (to.reshape(1, -1) == me) & (place.reshape(1, -1) == jnp.arange(count)[:, None]),
                jnp.arange(tiles)[None, :],
            )
            return join_tiles([whole], slots, row_blocks, columns_of)

        return lax.cond(fits, fast, slow)

    w_first, w_out = fetch(
        attn_all, attn_join, attn_to, my_seq, attn_place, (attn_first, query_each)
    )
    gain_attn = gain_full[width : 2 * width]
    gain_laurel = gain_full[2 * width : 3 * width]
    gain_pre = gain_full[3 * width : 4 * width]
    gain_post = gain_full[4 * width : 5 * width]
    gain_vec = gain_full[5 * width : 6 * width]
    gain_query = gain_full[6 * width : 6 * width + HEAD_DIM]
    gain_key = gain_full[6 * width + HEAD_DIM : 6 * width + 2 * HEAD_DIM]
    stream = own_tokens.astype(f32)
    vectors = layer_vectors[0].astype(f32)
    normed, normed_pull = jax.vjp(rms_norm, stream, gain_in)
    normed_low = normed.astype(bf16)
    first_pre = matmul(pack_normed, w_first)
    is_key = my_seq % per_key == 0

    def shape_query(query_in, query_gain):
        value = rms_norm(query_in.reshape(length, per_device, HEAD_DIM), query_gain)
        return turn(value, cosine, sine)

    def shape_key(key_in, key_gain):
        return turn(rms_norm(key_in.reshape(length, 1, HEAD_DIM), key_gain), cosine, sine)

    query_pre = first_pre[:, : per_device * HEAD_DIM]
    other_pre = first_pre[:, per_device * HEAD_DIM :]
    query_rot, query_pull = jax.vjp(shape_query, query_pre, gain_query)
    key_rot, key_pull = jax.vjp(shape_key, other_pre, gain_key)
    query_heads = query_rot.astype(bf16)
    other_low = jnp.where(is_key, key_rot[:, 0, :], other_pre).astype(bf16)
    partner_low = seq_swap(other_low, 1).reshape(seq_size // 2, 2, rows, HEAD_DIM)
    partner_low = partner_low[:, ::-1].reshape(length, HEAD_DIM)
    key_single = jnp.where(is_key, other_low, partner_low)
    value_single = jnp.where(is_key, partner_low, other_low)

    raw = (
        jnp.einsum("qhd,kd->qhk", query_heads, key_single, preferred_element_type=f32) * SCALE
    )
    scores = jnp.where(allow[:, None, :], raw, NEGATIVE)
    powers = jnp.exp(scores - jnp.max(scores, axis=-1, keepdims=True))
    prob = powers / jnp.sum(powers, axis=-1, keepdims=True)
    prob_low = prob.astype(bf16)
    attended_low = (
        jnp.einsum("qhk,kd->qhd", prob_low, value_single, preferred_element_type=f32)
        .astype(bf16)
        .reshape(length, per_device * HEAD_DIM)
    )
    attn_pre = seq_sum(matmul_flip(attended_low, w_out), bf16)
    attn_pre, small_table, ffn_join = lax.optimization_barrier((attn_pre, small_table, ffn_join))
    laurel_left = small_table[:, :RANK]
    laurel_right = small_table[:, RANK : 2 * RANK]
    vector_gate_w = small_table[:, 2 * RANK : 2 * RANK + PLD]
    vector_proj_w = small_table[:, 2 * RANK + PLD :]

    attn_normed, attn_pull = jax.vjp(rms_norm, attn_pre, gain_attn)
    first_sum = stream + attn_normed
    left_pre = matmul(normed_low, laurel_left)
    left_low = left_pre.astype(bf16)
    right_pre = matmul_flip(left_low, laurel_right)
    laurel_normed, laurel_pull = jax.vjp(rms_norm, right_pre, gain_laurel)
    second_sum = (first_sum + normed + laurel_normed) * ROOT_HALF
    feed_normed, feed_pull = jax.vjp(rms_norm, second_sum, gain_pre)
    feed_own = feed_normed.astype(bf16)
    feed_low = lax.all_gather(feed_own, "fsdp", axis=0, tiled=True)
    ffn_all, _ = lax.optimization_barrier((ffn_all, feed_own))
    w_both, w_down = fetch(
        ffn_all, ffn_join, ffn_to, my_fsdp, ffn_place, (ffn_first, ffn_each)
    )
    both_pre = matmul(feed_low, w_both)
    ffn_width = w_down.shape[1]
    hidden, hidden_pull = jax.vjp(gelu_product, both_pre[:, :ffn_width], both_pre[:, ffn_width:])
    hidden_low = hidden.astype(bf16)
    down_pre = lax.psum_scatter(
        matmul_flip(hidden_low, w_down).astype(bf16), "fsdp", scatter_dimension=0, tiled=True
    ).astype(f32)
    down_normed, down_pull = jax.vjp(rms_norm, down_pre, gain_post)
    third_sum = second_sum + down_normed
    third_low = third_sum.astype(bf16)
    vector_pre = matmul(third_low, vector_gate_w)
    vector_gated, vector_pull = jax.vjp(lambda inner: gelu_product(inner, vectors), vector_pre)
    vector_low = vector_gated.astype(bf16)
    proj_pre = matmul_flip(vector_low, vector_proj_w)
    proj_normed, proj_pull = jax.vjp(rms_norm, proj_pre, gain_vec)
    result = third_sum + proj_normed
    output = result.astype(bf16)[None]

    grad_out = cotangent[0].astype(f32)
    grad_proj, grad_gain_vec = proj_pull(grad_out)
    proj_grad_low = grad_proj.astype(bf16)
    (grad_vector_pre,) = vector_pull(matmul(proj_grad_low, vector_proj_w))
    vector_grad_low = grad_vector_pre.astype(bf16)
    grad_third = grad_out + matmul_flip(vector_grad_low, vector_gate_w)
    grad_down, grad_gain_post = down_pull(grad_third)
    down_grad_low = lax.all_gather(grad_down.astype(bf16), "fsdp", axis=0, tiled=True)
    grad_gate, grad_up = hidden_pull(matmul(down_grad_low, w_down))
    both_grad_low = jnp.concatenate([grad_gate, grad_up], axis=1).astype(bf16)

    early_full = jnp.concatenate(
        [matmul_outer(third_low, vector_grad_low), matmul_outer(proj_grad_low, vector_low)], axis=1
    )
    small_early = small_sum(split_tiles(early_full, tile).reshape(-1, tile))
    feed_part = matmul_flip(both_grad_low, w_both).astype(bf16)
    feed_part, small_early = lax.optimization_barrier((feed_part, small_early))
    grad_feed = lax.psum_scatter(feed_part, "fsdp", scatter_dimension=0, tiled=True).astype(f32)
    both_grad_w = matmul_outer(feed_low, both_grad_low).astype(bf16)
    down_grad_w = matmul_outer(down_grad_low, hidden_low).astype(bf16)
    ffn_parts = cut_tiles(
        [both_grad_w, down_grad_w],
        [ffn_cut[:, :ffn_half].reshape(-1), ffn_cut[:, ffn_half:].reshape(-1)],
    )
    ffn_parts, grad_feed = lax.optimization_barrier((ffn_parts, grad_feed))
    ffn_sums = [
        lax.psum_scatter(value, "seq", scatter_dimension=0, tiled=True) for value in ffn_parts
    ]

    grad_second_norm, grad_gain_pre = feed_pull(grad_feed)
    half_grad = (grad_third + grad_second_norm) * ROOT_HALF
    grad_right, grad_gain_laurel = laurel_pull(half_grad)
    right_grad_low = grad_right.astype(bf16)
    left_grad_low = matmul(right_grad_low, laurel_right).astype(bf16)
    grad_attn, grad_gain_attn = attn_pull(half_grad)
    attn_grad_low = seq_gather(grad_attn.astype(bf16))
    grad_attended = (
        matmul(attn_grad_low, w_out).astype(bf16).reshape(length, per_device, HEAD_DIM)
    )
    out_grad_w = matmul_outer(attn_grad_low, attended_low).astype(bf16)
    value_grad = jnp.einsum("qhk,qhd->kd", prob_low, grad_attended, preferred_element_type=f32)
    grad_prob = jnp.einsum("qhd,kd->qhk", grad_attended, value_single, preferred_element_type=f32)
    inner = jnp.sum(prob * grad_prob, axis=-1, keepdims=True)
    grad_score = (prob * (grad_prob - inner)).astype(bf16)
    grad_query = (
        jnp.einsum("qhk,kd->qhd", grad_score, key_single, preferred_element_type=f32) * SCALE
    ).astype(bf16)
    key_grad = (
        jnp.einsum("qhk,qhd->kd", grad_score, query_heads, preferred_element_type=f32) * SCALE
    ).astype(bf16)
    value_grad = value_grad.astype(bf16)
    partner_grad = seq_swap(jnp.where(is_key, value_grad, key_grad), 1)
    partner_grad = partner_grad.reshape(seq_size // 2, 2, rows, HEAD_DIM)[:, ::-1]
    other_grad = jnp.where(is_key, key_grad, value_grad).astype(f32) + partner_grad.reshape(
        length, HEAD_DIM
    ).astype(f32)
    grad_query_pre, grad_gain_query = query_pull(grad_query.astype(f32))
    grad_key_pre, grad_gain_key = key_pull(other_grad[:, None, :])
    grad_gain_key = jnp.where(is_key, grad_gain_key, 0.0)
    first_grad_low = jnp.concatenate(
        [grad_query_pre, jnp.where(is_key, grad_key_pre, other_grad)], axis=1
    ).astype(bf16)
    first_grad_w = matmul_outer(pack_normed, first_grad_low).astype(bf16)
    near = (my_chip + shifts) % chips
    near_key = take_blocks(attn_key_chip, near)[:, None, :]
    near_order = take_blocks(attn_order_chip, near)[:, None, :]
    near_place = take_blocks(by_chip(attn_place), near)[:, None, :]

    def attn_cut(core):
        return pick(
            (near_key == 2 * my_seq + core)
            & (near_order == jnp.arange(attn_hold)[None, :, None]),
            near_place,
        ).reshape(-1)

    attn_given, attn_own = cut_tiles(
        [first_grad_w, out_grad_w], [attn_cut(1 - my_core), attn_cut(my_core)]
    )
    attn_given, attn_own, ffn_sums[0] = lax.optimization_barrier(
        (attn_given, attn_own, ffn_sums[0])
    )
    attn_parts = added(attn_own, core_swap(attn_given)).reshape(chips, attn_hold, tile, tile)
    attn_sum = attn_parts[0]
    attn_parts = [attn_parts[offset].astype(bf16) for offset in range(1, chips)]
    normed_pre = matmul_flip(first_grad_low, w_first)
    attn_sum, attn_parts, normed_pre = lax.optimization_barrier((attn_sum, attn_parts, normed_pre))
    normed_sum = seq_sum(normed_pre, bf16)
    for offset in range(1, chips):
        attn_sum = attn_sum + chip_shift(attn_parts[offset - 1], offset).astype(f32)
    attn_sum = attn_sum.astype(bf16)
    attn_sum, normed_sum = lax.optimization_barrier((attn_sum, normed_sum))
    attn_back = pick(
        (column_slots[3][None, None, :] == (my_seq ^ flips)[:, None, None])
        & (column_slots[0][None, None, :] == my_key)
        & (column_slots[2][None, None, :] == jnp.arange(attn_room)[None, :, None]),
        column_slots[1],
    )

    grad_normed = half_grad + matmul_flip(left_grad_low, laurel_left) + normed_sum
    grad_stream_norm, grad_gain_in = normed_pull(grad_normed)
    input_grad = (half_grad + grad_stream_norm)[None]
    gain_grad = jnp.concatenate(
        [
            grad_gain_in,
            grad_gain_attn,
            grad_gain_laurel,
            grad_gain_pre,
            grad_gain_post,
            grad_gain_vec,
            grad_gain_query,
            grad_gain_key,
        ]
    )
    late_full = jnp.concatenate(
        [matmul_outer(normed_low, left_grad_low), matmul_outer(right_grad_low, left_low)], axis=1
    )
    late = jnp.concatenate(
        [late_full.reshape(seq_size, -1), gain_grad.reshape(seq_size, -1)], axis=1
    ).reshape(seq_size, -1, tile)
    late = seq_sum(late.reshape(-1, tile), bf16, True)

    late = late.astype(bf16)
    late = added(late, core_swap(late)).astype(bf16)
    ffn_sums, attn_sum, late, input_grad = lax.optimization_barrier(
        (ffn_sums, attn_sum, late, input_grad)
    )
    ffn_sums = ffn_sums + [core_swap(value) for value in ffn_sums]
    late = jnp.pad(late, ((0, 2 * late_count * tile - late.shape[0]), (0, 0)))
    late = late.reshape(2, late_count, tile, tile)
    late = lax.dynamic_index_in_dim(late, my_core, 0, False)
    late_index = 2 * ffn_hold + jnp.arange(late_count)
    ffn_return = gather_tiles(
        ffn_sums + [late], [jnp.concatenate([ffn_back[i], late_index]) for i in range(chips)]
    )
    ffn_return, attn_sum = lax.optimization_barrier((ffn_return, attn_sum))
    ffn_returned = chip_exchange(ffn_return)
    attn_returned = seq_exchange(gather_tiles([attn_sum], [attn_back[i] for i in range(seq_size)]))
    attn_returned = attn_returned + [core_swap(value) for value in attn_returned]
    back_size = 2 * chips * return_size
    slot_grad = jnp.where(my_slots[0] >= 0, my_slots[1], back_size + my_slots[2])

    def slow_return():
        own_ffn = split_tiles(both_grad_w, tile), split_tiles(down_grad_w, tile)
        own_attn = split_tiles(first_grad_w, tile), split_tiles(out_grad_w, tile)
        parts = jnp.concatenate(own_ffn + own_attn + (jnp.zeros((1, tile, tile), bf16),))
        index = jnp.where(
            ffn_to == my_fsdp,
            ffn_place,
            jnp.where(attn_to == my_seq, ffn_count + attn_place, ffn_count + attn_count),
        )
        spread = jnp.concatenate(
            [gather_tiles([parts], [rows_of])[0] for rows_of in index.reshape(8, -1)]
        )
        spread = lax.all_to_all(
            spread.reshape((seq_size * fsdp_size, mine, tile, tile)),
            ("seq", "fsdp"),
            split_axis=0,
            concat_axis=0,
            tiled=True,
        )
        return jnp.sum(spread.astype(f32), axis=0).astype(bf16)

    slow_start = back_size + 2 * seq_size * attn_room
    slow_grads = lax.cond(fits, lambda: jnp.zeros((mine, tile, tile), bf16), slow_return)
    ffn_returned, slow_grads = lax.optimization_barrier((ffn_returned, slow_grads))
    late = sum(value[ffn_room:].astype(f32) for value in ffn_returned).astype(bf16)
    late = core_pair(late).reshape(-1, tile).astype(f32)
    ffn_returned = ffn_returned + [core_swap(value) for value in ffn_returned]
    tile_grads = ffn_returned + attn_returned + [slow_grads]
    slot_grad = jnp.where(fits, slot_grad, slow_start + local_slots)

    tile_new, tile_first_new, tile_second_new = rotate_update(
        tile_grads, slot_grad, tile_master, tile_first, tile_second, left_basis, right_basis, RATE_TILE
    )
    late_rows = late_full.shape[0] // seq_size
    late_tiles = late[:late_rows].reshape(-1, 1, tile, tile)
    gain_grad_mine = late[late_rows : late_rows + own_gains.shape[0] // tile].reshape(-1)
    small_grad = jnp.concatenate(
        [
            late_tiles.astype(bf16),
            small_early.reshape(late_tiles.shape[0], -1, tile, tile),
        ],
        axis=1,
    ).reshape(small_master.shape)
    small_new, small_first_new, small_second_new = rotate_update(
        [small_grad],
        jnp.arange(small_master.shape[0]),
        small_master,
        small_first,
        small_second,
        small_left,
        small_right,
        RATE_SMALL,
    )
    gain_first_new = BETA_ONE * gain_first + (1.0 - BETA_ONE) * gain_grad_mine
    gain_second_new = BETA_TWO * gain_second + (1.0 - BETA_TWO) * gain_grad_mine * gain_grad_mine
    correct_one = 1.0 - BETA_ONE**STEP
    correct_two = 1.0 - BETA_TWO**STEP
    gain_new = gains - RATE_GAIN * (gain_first_new / correct_one) / (
        jnp.sqrt(gain_second_new / correct_two) + ADAM_EPS
    )
    return (
        output,
        input_grad,
        tile_new,
        tile_first_new,
        tile_second_new,
        small_new,
        small_first_new,
        small_second_new,
        gain_new,
        gain_first_new,
        gain_second_new,
    )


def solution(mesh):
    return jax.shard_map(
        on_device,
        mesh=mesh,
        in_specs=(
            P("fsdp", "seq", None),
            P("fsdp", "seq", None),
            P("fsdp", None),
            P("fsdp", "seq", None),
            P(),
            P(("seq", "fsdp"), None, None),
            P(("seq", "fsdp"), None, None),
            P(("seq", "fsdp"), None, None),
            P(("seq", "fsdp"), None, None),
            P(("seq", "fsdp"), None, None),
            P("seq", None, None),
            P("seq", None, None),
            P("seq", None, None),
            P("seq", None, None),
            P("seq", None, None),
            P("seq"),
            P("seq"),
            P("seq"),
        ),
        out_specs=(
            P("fsdp", "seq", None),
            P("fsdp", "seq", None),
            P(("seq", "fsdp"), None, None),
            P(("seq", "fsdp"), None, None),
            P(("seq", "fsdp"), None, None),
            P("seq", None, None),
            P("seq", None, None),
            P("seq", None, None),
            P("seq"),
            P("seq"),
            P("seq"),
        ),
        check_vma=False,
    )
```

```python
import math

import jax
import jax.numpy as jnp
from jax import lax
from jax.experimental import pallas as pl
from jax.experimental.pallas import tpu as pltpu
from jax.sharding import PartitionSpec as P

HEADS = 8
KV_HEADS = 2
HEAD_DIM = 256
FF = 8192
RANK = 64
PLD = 256
STEP = 5


EPS = 1e-06
SCALE = 0.0625
THETA = 1000000.0
ROOT_HALF = 0.7071067811865476
BETA_ONE = 0.5
BETA_TWO = 0.5
ADAM_EPS = 1e-08
RATE_TILE = 0.02
RATE_SMALL = 0.04
RATE_GAIN = 0.3
DECAY = 0.01
NEGATIVE = -1e30
TILE = 128
VMEM_BYTES = 4 * 1024 * 1024


def rms_norm(value, gain):
    return value * lax.rsqrt(jnp.mean(value * value, axis=-1, keepdims=True) + EPS) * gain


def rotary(value, position):
    half = value.shape[-1] // 2
    freq = THETA ** (-2.0 * jnp.arange(half).astype(jnp.float32) / value.shape[-1])
    angle = position.astype(jnp.float32)[:, None] * freq[None, :]
    cosine = jnp.cos(angle)[:, None, :]
    sine = jnp.sin(angle)[:, None, :]
    first = value[..., :half]
    second = value[..., half:]
    return jnp.concatenate(
        [first * cosine - second * sine, second * cosine + first * sine], axis=-1
    )


def documents(lengths, length):
    places = jnp.arange(length)
    ends = jnp.cumsum(lengths)
    passed = places[:, None] >= ends[None, :]
    segment = jnp.sum(passed.astype(jnp.int32), axis=1)
    before = jnp.sum(jnp.where(passed, lengths[None, :], 0), axis=1)
    return (segment, places - before)


def matmul(left, right):
    return jnp.dot(left, right, preferred_element_type=jnp.float32)


def matmul_flip(left, right):
    return lax.dot_general(
        left, right, (((1,), (1,)), ((), ())), preferred_element_type=jnp.float32
    )


def matmul_outer(left, right):
    return lax.dot_general(
        left, right, (((0,), (0,)), ((), ())), preferred_element_type=jnp.float32
    )


def assemble(tiles, row_blocks):
    size = tiles.shape[1]
    column_blocks = tiles.shape[0] // row_blocks
    return (
        tiles.reshape(row_blocks, column_blocks, size, size)
        .transpose(0, 2, 1, 3)
        .reshape(row_blocks * size, column_blocks * size)
    )


def split_tiles(matrix, size):
    row_blocks = matrix.shape[0] // size
    column_blocks = matrix.shape[1] // size
    return (
        matrix.reshape(row_blocks, size, column_blocks, size)
        .transpose(0, 2, 1, 3)
        .reshape(row_blocks * column_blocks, size, size)
    )


def gelu_product(first, second):
    return jax.nn.gelu(first, approximate=True) * second


def room(count, share):
    mean = count * share
    return math.ceil(mean + 3.6 * math.sqrt(mean * (1.0 - share)) + 3.0)


def count_earlier(group, valid):
    size = group.shape[-1]
    order = jnp.arange(size)
    same = (group[..., :, None] == group[..., None, :]) & valid[..., None, :]
    same = same & (order[None, :] < order[:, None])
    return jnp.sum(same.astype(jnp.int32), axis=-1)


def count_long(keys):
    groups, size = keys.shape

    def kernel(row_ref, column_ref, out_ref):
        row = row_ref[0]
        column = column_ref[0]
        here = lax.broadcasted_iota(jnp.int32, (size, size), 1)
        other = lax.broadcasted_iota(jnp.int32, (size, size), 0)
        earlier = (column == row) & (other < here)
        out_ref[0] = jnp.sum(earlier.astype(jnp.int32), axis=0, keepdims=True)

    return pl.pallas_call(
        kernel,
        grid=(groups,),
        out_shape=jax.ShapeDtypeStruct((groups, 1, size), jnp.int32),
        in_specs=[
            pl.BlockSpec((1, 1, size), lambda i: (i, 0, 0)),
            pl.BlockSpec((1, size, 1), lambda i: (i, 0, 0)),
        ],
        out_specs=pl.BlockSpec((1, 1, size), lambda i: (i, 0, 0)),
        cost_estimate=pl.CostEstimate(flops=0, transcendentals=0, bytes_accessed=0),
        compiler_params=pltpu.CompilerParams(vmem_limit_bytes=4 * VMEM_BYTES),
    )(keys[:, None, :], keys[:, :, None]).reshape(groups, size)


def pick(match, value):
    return jnp.sum(jnp.where(match, value, 0), axis=-1)


def steps_of(counts):
    for steps in (8, 4, 2):
        if all(count % steps == 0 for count in counts) and sum(counts) // steps >= 24:
            return steps
    return 1


def tile_kernel_call(kernel, index, arrays, out_shape, out_specs, steps):
    moved = sum(math.prod(one.shape) * 2 for one in jax.tree.leaves(out_shape))
    return pl.pallas_call(
        kernel,
        grid=(steps,),
        cost_estimate=pl.CostEstimate(flops=0, transcendentals=0, bytes_accessed=2 * moved),
        out_shape=out_shape,
        in_specs=[pl.BlockSpec(memory_space=pltpu.SMEM)]
        + [pl.BlockSpec(memory_space=pl.ANY)] * len(arrays),
        out_specs=out_specs,
        scratch_shapes=[pltpu.SemaphoreType.DMA],
        compiler_params=pltpu.CompilerParams(vmem_limit_bytes=2 * moved // steps + VMEM_BYTES),
    )(index, *arrays)


def start_copy(sources, place, target, sem, start=0):
    if len(sources) == 1:
        pltpu.make_async_copy(sources[0].at[place - start], target, sem).start()
        return
    half = len(sources) // 2
    middle = start + sum(ref.shape[0] for ref in sources[:half])

    @pl.when(place < middle)
    def _():
        start_copy(sources[:half], place, target, sem, start)

    @pl.when(place >= middle)
    def _():
        start_copy(sources[half:], place, target, sem, middle)


def fill_tiles(arrays, indices, total, start):
    tile = arrays[0].shape[-1] if arrays[0].ndim == 3 else TILE
    counts = [index.shape[0] for index in indices]
    steps = steps_of(counts)

    def kernel(index_ref, *refs):
        sources, outs, sem = refs[: len(arrays)], refs[len(arrays) : -1], refs[-1]
        first = 0
        for out, count in zip(outs, counts):
            each = count // steps
            base = first + pl.program_id(0) * each

            def step(i, carry, out=out, base=base):
                start(sources, index_ref[base + i], out.at[i], sem)
                return carry

            lax.fori_loop(0, each, step, 0)
            first = first + count
        for out in outs:
            pltpu.make_async_copy(out, out, sem).wait()

    return tile_kernel_call(
        kernel,
        jnp.clip(jnp.concatenate(indices), 0, total - 1),
        arrays,
        [jax.ShapeDtypeStruct((count, tile, tile), arrays[0].dtype) for count in counts],
        [pl.BlockSpec((count // steps, tile, tile), lambda i: (i, 0, 0)) for count in counts],
        steps,
    )


def gather_tiles(arrays, indices):
    return fill_tiles(arrays, indices, sum(array.shape[0] for array in arrays), start_copy)


def cut_tiles(matrices, indices):
    row_blocks = matrices[0].shape[0] // TILE
    widths = [matrix.shape[1] // TILE for matrix in matrices]

    def start(sources, place, target, sem):
        first = 0
        for ref, width in zip(sources, widths):
            size = row_blocks * width

            @pl.when((place >= first) & (place < first + size))
            def _(ref=ref, first=first, width=width):
                row = (place - first) // width
                column = place - first - row * width
                source = ref.at[
                    pl.ds(pl.multiple_of(row * TILE, TILE), TILE),
                    pl.ds(pl.multiple_of(column * TILE, TILE), TILE),
                ]
                pltpu.make_async_copy(source, target, sem).start()

            first = first + size

    return fill_tiles(matrices, indices, row_blocks * sum(widths), start)


def join_tiles(arrays, index, row_blocks, columns):
    tile = arrays[0].shape[-1]
    steps = 4
    each = row_blocks // steps

    def kernel(index_ref, *refs):
        sources, outs, sem = refs[: len(arrays)], refs[len(arrays) : -1], refs[-1]
        base = pl.program_id(0) * each
        start = 0
        for out, width in zip(outs, columns):

            def step(i, carry, out=out, start=start, width=width):
                row = i // width
                column = i - row * width
                target = out.at[
                    pl.ds(pl.multiple_of(row * tile, tile), tile),
                    pl.ds(pl.multiple_of(column * tile, tile), tile),
                ]
                start_copy(sources, index_ref[start + base * width + i], target, sem)
                return carry

            lax.fori_loop(0, each * width, step, 0)
            start = start + row_blocks * width
        for out in outs:
            pltpu.make_async_copy(out, out, sem).wait()

    total = sum(array.shape[0] for array in arrays)
    out_shape = tuple(
        jax.ShapeDtypeStruct((row_blocks * tile, width * tile), arrays[0].dtype)
        for width in columns
    )
    out_specs = tuple(pl.BlockSpec((each * tile, width * tile), lambda i: (i, 0)) for width in columns)
    return tile_kernel_call(
        kernel, jnp.clip(index, 0, total - 1), arrays, out_shape, out_specs, steps
    )


def split_low(value):
    high = value.astype(jnp.bfloat16)
    return high, (value - high.astype(jnp.float32)).astype(jnp.bfloat16)


def rotate_update(grads, index, master, first, second, left, right, rate):
    count, tile, _ = master.shape
    each = 4 if count % 4 == 0 else 1
    correct_one = 1.0 - BETA_ONE**STEP
    correct_two = 1.0 - BETA_TWO**STEP

    def product(one, two, dims):
        return lax.dot_general(one, two, (dims, ((), ())), preferred_element_type=jnp.float32)

    def kernel(index_ref, *refs):
        sources, refs = refs[: len(grads)], refs[len(grads) :]
        master_ref, first_ref, second_ref, left_ref, right_ref = refs[:5]
        master_out, first_out, second_out, held, sems = refs[5:]
        now = pl.program_id(0)

        @pl.when(now == 0)
        def _():
            def step(i, carry):
                start_copy(sources, index_ref[i], held.at[i], sems.at[i // each])
                return carry

            lax.fori_loop(0, count, step, 0)

        block = held.at[pl.ds(now * each, each)]
        pltpu.make_async_copy(block, block, sems.at[now]).wait()
        lefts, rights, turns = [], [], []
        for i in range(each):
            grad = held[now * each + i]
            lefts.append(split_low(left_ref[i]))
            rights.append(split_low(right_ref[i]))
            half_turned = product(
                jnp.concatenate([grad, grad], axis=1),
                jnp.concatenate(rights[i], axis=0),
                ((1,), (0,)),
            )
            turns.append(split_low(half_turned))
        for i in range(each):
            (left_high, left_low), (high, low) = lefts[i], turns[i]
            turns[i] = product(
                jnp.concatenate([left_high, left_high, left_low], axis=0),
                jnp.concatenate([high, low, high], axis=0),
                ((0,), (0,)),
            )
        for i in range(each):
            right_high, right_low = rights[i]
            first_new = BETA_ONE * first_ref[i] + (1.0 - BETA_ONE) * turns[i]
            second_new = BETA_TWO * second_ref[i] + (1.0 - BETA_TWO) * turns[i] * turns[i]
            first_out[i] = first_new
            second_out[i] = second_new
            high, low = split_low(
                first_new / correct_one / (jnp.sqrt(second_new / correct_two) + ADAM_EPS)
            )
            half_back = product(
                jnp.concatenate([high, low, high], axis=1),
                jnp.concatenate([right_high, right_high, right_low], axis=1),
                ((1,), (1,)),
            )
            turns[i] = split_low(half_back)
        for i in range(each):
            (left_high, left_low), (high, low) = lefts[i], turns[i]
            back = product(
                jnp.concatenate([left_high, left_high, left_low], axis=1),
                jnp.concatenate([high, low, high], axis=0),
                ((1,), (0,)),
            )
            weight = master_ref[i]
            master_out[i] = weight - rate * (back + DECAY * weight)

    spec = pl.BlockSpec((each, tile, tile), lambda i: (i, 0, 0))
    shape = jax.ShapeDtypeStruct(master.shape, jnp.float32)
    total = sum(array.shape[0] for array in grads)
    return pl.pallas_call(
        kernel,
        grid=(count // each,),
        out_shape=(shape, shape, shape),
        cost_estimate=pl.CostEstimate(
            flops=count * 22 * tile**3, transcendentals=0, bytes_accessed=count * tile**2 * 34
        ),
        in_specs=[pl.BlockSpec(memory_space=pltpu.SMEM)]
        + [pl.BlockSpec(memory_space=pl.ANY)] * len(grads)
        + [spec] * 5,
        out_specs=(spec, spec, spec),
        scratch_shapes=[
            pltpu.VMEM((count, tile, tile), jnp.bfloat16),
            pltpu.SemaphoreType.DMA((count // each,)),
        ],
        compiler_params=pltpu.CompilerParams(vmem_limit_bytes=4 * VMEM_BYTES),
    )(jnp.clip(index, 0, total - 1), *grads, master, first, second, left, right)


def seq_swap(value, flip):
    size = lax.axis_size("seq")
    return lax.ppermute(value, "seq", [(i, i ^ flip) for i in range(size)])


def take_blocks(value, order):
    return jnp.stack(
        [lax.dynamic_index_in_dim(value, order[i], 0, False) for i in range(order.shape[0])]
    )


def core_swap(value):
    size = lax.axis_size("fsdp")
    return lax.ppermute(value, "fsdp", [(i, i ^ 1) for i in range(size)])


def chip_shift(value, offset):
    size = lax.axis_size("fsdp")
    chips = size // 2
    return lax.ppermute(
        value, "fsdp", [(i, (i // 2 + offset) % chips * 2 + i % 2) for i in range(size)]
    )


def seq_gather(value):
    size = lax.axis_size("seq")
    return jnp.concatenate([value] + [seq_swap(value, flip) for flip in range(1, size)], axis=0)


def seq_ordered(value):
    size = lax.axis_size("seq")
    parts = jnp.stack([value] + [seq_swap(value, flip) for flip in range(1, size)], axis=0)
    return take_blocks(parts, lax.axis_index("seq") ^ jnp.arange(size))


def seq_exchange(values):
    return [values[0]] + [seq_swap(values[flip], flip) for flip in range(1, len(values))]


def seq_sum(value, wire, ordered=False):
    size = lax.axis_size("seq")
    parts = value.reshape((size, value.shape[0] // size) + value.shape[1:])
    if ordered:
        parts = take_blocks(parts, lax.axis_index("seq") ^ jnp.arange(size))
    total = parts[0]
    for flip in range(1, size):
        total = total + seq_swap(parts[flip].astype(wire), flip).astype(jnp.float32)
    return total


def chip_exchange(values):
    return [values[0]] + [chip_shift(values[offset], offset) for offset in range(1, len(values))]


def core_pair(value):
    other = core_swap(value)
    even = lax.axis_index("fsdp") % 2 == 0
    return jnp.where(even, jnp.stack([value, other]), jnp.stack([other, value]))


def small_sum(value):
    seq_size = lax.axis_size("seq")
    chips = lax.axis_size("fsdp") // 2
    chip = lax.axis_index("fsdp") // 2
    even = lax.axis_index("fsdp") % 2 == 0
    low = value.astype(jnp.bfloat16)
    parts = low.reshape((seq_size, 2, low.shape[0] // (2 * seq_size)) + low.shape[1:])
    kept = jnp.where(even, parts[:, 0], parts[:, 1]).astype(jnp.float32)
    given = jnp.where(even, parts[:, 1], parts[:, 0])
    kept = kept + core_swap(given).astype(jnp.float32)
    kept = seq_sum(kept.reshape((-1,) + low.shape[1:]), jnp.bfloat16, True)
    kept = kept.reshape((chips, kept.shape[0] // chips) + kept.shape[1:])
    kept = take_blocks(kept, (chip + jnp.arange(chips)) % chips)
    total = kept[0]
    for offset in range(1, chips):
        total = total + chip_shift(kept[offset].astype(jnp.bfloat16), offset).astype(jnp.float32)
    total = total.astype(jnp.bfloat16)
    parts = jnp.stack([total] + [chip_shift(total, offset) for offset in range(1, chips)])
    parts = take_blocks(parts, (chip - jnp.arange(chips)) % chips)
    return core_pair(parts).reshape((value.shape[0] // seq_size,) + value.shape[1:])


def turn(value, cosine, sine):
    half = value.shape[-1] // 2
    first, second = value[..., :half], value[..., half:]
    return jnp.concatenate(
        [first * cosine - second * sine, second * cosine + first * sine], axis=-1
    )


def added(one, two):
    return one.astype(jnp.float32) + two.astype(jnp.float32)


def on_device(
    tokens,
    layer_vectors,
    doc_lengths,
    cotangent,
    tile_owner,
    tile_master,
    tile_first,
    tile_second,
    left_basis,
    right_basis,
    small_master,
    small_first,
    small_second,
    small_left,
    small_right,
    gains,
    gain_first,
    gain_second,
):
    bf16 = jnp.bfloat16
    f32 = jnp.float32
    tile = tile_master.shape[1]
    width = tokens.shape[2]
    row_blocks = width // tile
    rows = tokens.shape[1]
    seq_size = lax.axis_size("seq")
    fsdp_size = lax.axis_size("fsdp")
    chips = fsdp_size // 2
    mine = tile_master.shape[0]
    tiles = tile_owner.shape[0]
    length = rows * seq_size
    per_device = HEADS // seq_size
    per_key = seq_size // KV_HEADS
    query_width = HEADS * HEAD_DIM
    key_width = KV_HEADS * HEAD_DIM
    my_seq = lax.axis_index("seq")
    my_fsdp = lax.axis_index("fsdp")
    my_chip = my_fsdp // 2
    my_core = my_fsdp % 2
    flips = jnp.arange(seq_size)
    shifts = jnp.arange(chips)

    query_blocks = query_width // tile
    key_blocks = key_width // tile
    ffn_blocks = FF // tile
    query_each = query_blocks // seq_size
    head_blocks = HEAD_DIM // tile
    ffn_each = ffn_blocks // fsdp_size
    columns = tiles // row_blocks
    attn_first = query_each + head_blocks
    attn_count = row_blocks * (attn_first + query_each)
    ffn_first = 2 * ffn_each
    ffn_count = row_blocks * 3 * ffn_each
    attn_share = (2 * query_blocks + 2 * key_blocks) / columns
    ffn_share = 3 * ffn_blocks / columns
    attn_room = (room(2 * mine, attn_share / seq_size) + 1) // 2
    attn_hold = (room(attn_count, 1.0 / chips) + 1) // 2 + 1
    ffn_room = (room(2 * mine, ffn_share / chips) + 1) // 2
    both_count = row_blocks * ffn_first
    near_hold = (room(2 * mine, ffn_share / fsdp_size) + 3) // 4 * 4
    far_hold = (room(ffn_count * (1.0 - 1.0 / chips), 1.0 / seq_size) + 3) // 4 * 4
    far_half = far_hold * 3 // 7 // 4 * 4
    far_rest = far_hold - far_half

    def tile_places(owner):
        row = owner // columns
        column = owner % columns
        key_at = column - query_blocks
        value_at = key_at - key_blocks
        out_at = value_at - key_blocks
        ffn_at = out_at - query_blocks
        is_attn = ffn_at < 0
        kind = ffn_at // ffn_blocks
        ffn_column = ffn_at % ffn_blocks
        ffn_to = jnp.where(is_attn, -1, ffn_column // ffn_each)
        ffn_local = ffn_column % ffn_each
        ffn_place = jnp.where(
            kind == 2,
            both_count + row * ffn_each + ffn_local,
            row * ffn_first + kind * ffn_each + ffn_local,
        )
        attn_to = jnp.where(
            key_at < 0,
            column // query_each,
            jnp.where(
                value_at < 0,
                key_at // head_blocks * per_key,
                jnp.where(
                    out_at < 0,
                    value_at // head_blocks * per_key + per_key - 1,
                    out_at // query_each,
                ),
            ),
        )
        attn_place = jnp.where(
            key_at < 0,
            row * attn_first + column % query_each,
            jnp.where(
                out_at < 0,
                row * attn_first + query_each + key_at % head_blocks,
                row_blocks * attn_first + row * query_each + out_at % query_each,
            ),
        )
        attn_to = jnp.where(is_attn, attn_to, -1)
        return (ffn_to, ffn_place, attn_to, attn_place)

    owners = tile_owner.reshape(seq_size, fsdp_size, mine)
    slot_seq = jnp.arange(seq_size)[:, None, None]
    slot_fsdp = jnp.arange(fsdp_size)[None, :, None]
    slot_chip = slot_fsdp // 2
    local_slots = jnp.arange(mine)
    both_slots = jnp.arange(2 * mine)
    both_slots = jnp.where(
        both_slots // mine == my_core, both_slots % mine, mine + both_slots % mine
    )

    ffn_to = tile_places(owners)[0]
    ffn_chip = jnp.where(ffn_to < 0, -1, ffn_to // 2)
    chip_view = ffn_chip.reshape(seq_size, chips, 2 * mine)
    chip_rank = count_earlier(chip_view, chip_view >= 0).reshape(owners.shape)
    near_view = jnp.where(slot_chip == ffn_chip, ffn_to, -1).reshape(chip_view.shape)
    near_rank = count_earlier(near_view, near_view >= 0).reshape(owners.shape)
    ffn_slots = lax.dynamic_slice(
        jnp.stack([ffn_chip, chip_rank, near_view.reshape(owners.shape), near_rank]),
        (0, my_seq, 2 * my_chip, 0),
        (4, 1, 2, mine),
    ).reshape(4, 1, 1, 2 * mine)
    near_keep = pick(
        (ffn_slots[2][0] == my_fsdp) & (ffn_slots[3][0] == jnp.arange(near_hold)[:, None]),
        both_slots,
    )
    ffn_pack = pick(
        (ffn_slots[0] == ((my_chip + shifts) % chips)[:, None, None])
        & (ffn_slots[1] == (my_core * ffn_room + jnp.arange(ffn_room))[None, :, None]),
        both_slots,
    )
    master_low = tile_master.astype(bf16)
    masters = [master_low, core_swap(master_low)]
    *ffn_sent, near_kept = gather_tiles(
        masters, [ffn_pack[i] for i in range(1, chips)] + [near_keep]
    )
    small_rows = small_master.shape[0] // 2
    small_half = lax.dynamic_slice_in_dim(small_master, my_core * small_rows, small_rows)
    masters, ffn_sent, near_kept, chip_rank, near_rank, owners, own_tokens, own_gains, small_half = (
        lax.optimization_barrier(
            (
                masters,
                ffn_sent,
                near_kept,
                chip_rank,
                near_rank,
                owners,
                tokens[0],
                gains.astype(bf16),
                small_half.astype(bf16),
            )
        )
    )
    ffn_got = [chip_shift(value, i + 1) for i, value in enumerate(ffn_sent)]
    near_all = lax.all_gather(near_kept, "seq", axis=0, tiled=True)

    ffn_to, ffn_place, attn_to, attn_place = tile_places(owners)
    ffn_chip = jnp.where(ffn_to < 0, -1, ffn_to // 2)
    attn_view = attn_to.reshape(seq_size, chips, 2 * mine)
    attn_rank = count_earlier(attn_view, attn_view >= 0).reshape(owners.shape)
    attn_core = (attn_rank + slot_seq) % 2
    attn_rank = attn_rank // 2
    attn_key = jnp.where(attn_to < 0, -1, 2 * attn_to + attn_core)

    chip_slots = lax.dynamic_slice(
        jnp.stack([attn_key, attn_rank]), (0, my_seq, 2 * my_chip, 0), (2, 1, 2, mine)
    ).reshape(2, 1, 1, 2 * mine)
    attn_message = attn_room + row_blocks * rows // tile + small_rows + -(-own_gains.shape[0] // tile**2)
    attn_pack = pick(
        (chip_slots[0] == (2 * (my_seq ^ flips) + my_core)[:, None, None])
        & (chip_slots[1] == jnp.arange(attn_room)[None, :, None]),
        both_slots,
    )
    attn_sent = gather_tiles(masters, [attn_pack[i] for i in range(seq_size)])
    is_near = slot_chip == ffn_chip
    near_key = jnp.where(is_near, ffn_to, -1)
    far_key = jnp.where(is_near, -1, ffn_to)
    far_rank = count_long(far_key.reshape(seq_size, fsdp_size * mine)).reshape(owners.shape)
    def by_chip(value):
        value = value.reshape(seq_size, chips, 2 * mine).transpose(1, 0, 2)
        return value.reshape(chips, seq_size * 2 * mine)

    attn_key_chip = by_chip(attn_key)
    attn_order_chip = count_long(attn_key_chip)
    attn_order = (
        attn_order_chip.reshape(chips, seq_size, 2 * mine).transpose(1, 0, 2).reshape(owners.shape)
    )
    fits = jnp.all(
        jnp.where(
            ffn_to < 0,
            (attn_rank < attn_room) & (attn_order < attn_hold),
            jnp.where(
                is_near, near_rank < near_hold, (chip_rank < 2 * ffn_room) & (far_rank < far_hold)
            ),
        )
    )
    rank_core = chip_rank // ffn_room
    rank_local = chip_rank % ffn_room
    out_place = (
        jnp.where(rank_core == my_core, 0, (chips - 1) * ffn_room)
        + ((my_chip - slot_chip) % chips - 1) * ffn_room
        + rank_local
    )
    near_start = 2 * (chips - 1) * ffn_room
    back_size = near_start + 2 * near_hold
    back_place = jnp.where(
        is_near,
        near_start + jnp.where(ffn_to == my_fsdp, 0, near_hold) + near_rank,
        jnp.where(rank_core == my_core, 0, (chips - 1) * ffn_room)
        + ((my_chip - ffn_chip) % chips - 1) * ffn_room
        + rank_local,
    )
    attn_back_place = (
        jnp.where(attn_core == my_core, 0, seq_size * attn_room)
        + (attn_to ^ my_seq) * attn_room
        + attn_rank
    )
    my_slots = lax.dynamic_slice(
        jnp.stack([ffn_to, back_place, attn_back_place]), (0, my_seq, my_fsdp, 0), (3, 1, 1, mine)
    ).reshape(3, mine)
    seq_slots = lax.dynamic_slice(
        jnp.stack(
            [
                far_key,
                far_rank,
                ffn_chip,
                out_place,
                chip_rank,
                jnp.broadcast_to(slot_chip, owners.shape),
            ]
        ),
        (0, my_seq, 0, 0),
        (6, 1, fsdp_size, mine),
    ).reshape(6, fsdp_size * mine)
    column_slots = lax.dynamic_slice(
        jnp.stack([attn_key, attn_order, attn_rank, jnp.broadcast_to(slot_seq, owners.shape)]),
        (0, 0, 2 * my_chip, 0),
        (4, seq_size, 2, mine),
    ).reshape(4, 2 * seq_size * mine)
    my_key = 2 * my_seq + my_core

    attn_keep = pick(
        (column_slots[0][None, :] == my_key)
        & (column_slots[1][None, :] == jnp.arange(attn_hold)[:, None]),
        jnp.where(
            column_slots[3] == my_seq,
            0,
            attn_room + ((column_slots[3] ^ my_seq) - 1) * attn_message,
        )
        + column_slots[2],
    )
    attn_join = pick(
        (attn_to.reshape(1, -1) == my_seq)
        & (attn_place.reshape(1, -1) == jnp.arange(attn_count)[:, None]),
        (
            jnp.where(attn_core == my_core, 0, chips * attn_hold)
            + (my_chip - slot_chip) % chips * attn_hold
            + attn_order
        ).reshape(1, -1),
    )
    ffn_keep = pick(
        (seq_slots[0][None, :] == my_fsdp) & (seq_slots[1][None, :] == jnp.arange(far_hold)[:, None]),
        seq_slots[3][None, :],
    )
    ffn_join = pick(
        (ffn_to.reshape(1, -1) == my_fsdp)
        & (ffn_place.reshape(1, -1) == jnp.arange(ffn_count)[:, None]),
        jnp.where(
            is_near,
            slot_seq * near_hold + near_rank,
            seq_size * near_hold
            + jnp.where(
                far_rank < far_half,
                slot_seq * far_half + far_rank,
                seq_size * far_half + slot_seq * far_rest + far_rank - far_half,
            ),
        ).reshape(1, -1),
    )

    def cut_index(key, rank, hold):
        return pick(
            (key.reshape(seq_size, 1, -1) == my_fsdp)
            & (rank.reshape(seq_size, 1, -1) == jnp.arange(hold)[None, :, None]),
            ffn_place.reshape(seq_size, 1, -1),
        )

    far_cut = cut_index(far_key, far_rank, far_hold)
    near_cut = cut_index(near_key, near_rank, near_hold)
    ffn_back = pick(
        (seq_slots[5][None, None, :] == ((my_chip + shifts) % chips)[:, None, None])
        & (seq_slots[2][None, None, :] == my_chip)
        & (seq_slots[4][None, None, :] == (my_core * ffn_room + jnp.arange(ffn_room))[None, :, None]),
        jnp.where(seq_slots[0] == my_fsdp, 0, far_hold) + seq_slots[1],
    )

    token_tiles = own_tokens.reshape(rows, row_blocks, tile).transpose(1, 0, 2)
    token_tiles = token_tiles.reshape(-1, tile, tile)
    gain_rows = own_gains.reshape(-1, tile)
    gain_tiles = jnp.pad(gain_rows, ((0, -gain_rows.shape[0] % tile), (0, 0))).reshape(-1, tile, tile)
    common = jnp.concatenate([token_tiles, small_half, gain_tiles])
    attn_got = [attn_sent[0]] + [
        seq_swap(jnp.concatenate([attn_sent[flip], common]), flip) for flip in range(1, seq_size)
    ]
    segment, position = documents(doc_lengths[0], length)
    places = ((my_seq ^ flips)[:, None] * rows + jnp.arange(rows)[None, :]).reshape(-1)

    def reorder(values):
        blocks = values.reshape(seq_size, rows)
        return jnp.concatenate(
            [lax.dynamic_index_in_dim(blocks, my_seq ^ i, 0, False) for i in range(seq_size)]
        )

    pack_segment = reorder(segment)
    allow = (pack_segment[:, None] == pack_segment[None, :]) & (
        places[None, :] <= places[:, None]
    )
    turns = jnp.arange(HEAD_DIM // 2).astype(f32)
    angle = reorder(position).astype(f32)[:, None] * (THETA ** (-2.0 * turns / HEAD_DIM))[None, :]
    cosine, sine = jnp.cos(angle)[:, None, :], jnp.sin(angle)[:, None, :]
    parts = [common] + [value[attn_room:] for value in attn_got[1:]]
    token_end = token_tiles.shape[0]
    small_end = token_end + small_rows

    def seq_order(value):
        return take_blocks(value, my_seq ^ flips)

    pack_tokens = jnp.concatenate(
        [
            part[:token_end].reshape(row_blocks, rows, tile).transpose(1, 0, 2).reshape(rows, width)
            for part in parts
        ]
    )
    gain_full = seq_order(
        jnp.stack([part[small_end:].reshape(-1, tile)[: gain_rows.shape[0]] for part in parts])
    )
    gain_full = gain_full.reshape(-1).astype(f32)
    gain_in = gain_full[0:width]
    pack_normed = rms_norm(pack_tokens.astype(f32), gain_in).astype(bf16)
    ready = (allow, cosine, sine, ffn_keep, attn_keep, pack_normed, gain_full)
    ffn_got, attn_got, parts, ready, near_all = lax.optimization_barrier(
        (ffn_got, attn_got, parts, ready, near_all)
    )
    allow, cosine, sine, ffn_keep, attn_keep, pack_normed, gain_full = ready
    gain_in = gain_full[0:width]
    small_got = core_pair(seq_order(jnp.stack([part[token_end:small_end] for part in parts])))
    small_got = small_got.transpose(1, 0, 2, 3, 4)
    small_table = assemble(small_got.reshape((-1,) + small_master.shape[1:]), row_blocks)
    (attn_kept,) = gather_tiles(attn_got, [attn_keep])
    ffn_got = ffn_got + [core_swap(value) for value in ffn_got]
    ffn_kept = gather_tiles(ffn_got, [ffn_keep[:far_half], ffn_keep[far_half:]])
    ffn_kept, attn_kept = lax.optimization_barrier((ffn_kept, attn_kept))
    ffn_all = [lax.all_gather(value, "seq", axis=0, tiled=True) for value in ffn_kept]
    attn_all = [attn_kept] + [chip_shift(attn_kept, offset) for offset in range(1, chips)]
    attn_all = attn_all + [core_swap(value) for value in attn_all]

    attn_all, ffn_all[0], attn_join = lax.optimization_barrier((attn_all, ffn_all[0], attn_join))

    def fetch(arrays, index, to, me, place, columns_of):
        def fast():
            return join_tiles(arrays, index, row_blocks, columns_of)

        def slow():
            whole = lax.all_to_all(
                jnp.broadcast_to(master_low[None], (seq_size * fsdp_size,) + master_low.shape),
                ("seq", "fsdp"),
                split_axis=0,
                concat_axis=0,
                tiled=True,
            ).reshape(-1, tile, tile)
            count = row_blocks * sum(columns_of)
            slots = pick(
                (to.reshape(1, -1) == me) & (place.reshape(1, -1) == jnp.arange(count)[:, None]),
                jnp.arange(tiles)[None, :],
            )
            return join_tiles([whole], slots, row_blocks, columns_of)

        return lax.cond(fits, fast, slow)

    w_first, w_out = fetch(
        attn_all, attn_join, attn_to, my_seq, attn_place, (attn_first, query_each)
    )
    gain_attn = gain_full[width : 2 * width]
    gain_laurel = gain_full[2 * width : 3 * width]
    gain_pre = gain_full[3 * width : 4 * width]
    gain_post = gain_full[4 * width : 5 * width]
    gain_vec = gain_full[5 * width : 6 * width]
    gain_query = gain_full[6 * width : 6 * width + HEAD_DIM]
    gain_key = gain_full[6 * width + HEAD_DIM : 6 * width + 2 * HEAD_DIM]
    stream = own_tokens.astype(f32)
    vectors = layer_vectors[0].astype(f32)
    normed, normed_pull = jax.vjp(rms_norm, stream, gain_in)
    normed_low = normed.astype(bf16)
    first_pre = matmul(pack_normed, w_first)
    is_key = my_seq % per_key == 0

    def shape_query(query_in, query_gain):
        value = rms_norm(query_in.reshape(length, per_device, HEAD_DIM), query_gain)
        return turn(value, cosine, sine)

    def shape_key(key_in, key_gain):
        return turn(rms_norm(key_in.reshape(length, 1, HEAD_DIM), key_gain), cosine, sine)

    query_pre = first_pre[:, : per_device * HEAD_DIM]
    other_pre = first_pre[:, per_device * HEAD_DIM :]
    query_rot, query_pull = jax.vjp(shape_query, query_pre, gain_query)
    key_rot, key_pull = jax.vjp(shape_key, other_pre, gain_key)
    query_heads = query_rot.astype(bf16)
    other_low = jnp.where(is_key, key_rot[:, 0, :], other_pre).astype(bf16)
    partner_low = seq_swap(other_low, 1).reshape(seq_size // 2, 2, rows, HEAD_DIM)
    partner_low = partner_low[:, ::-1].reshape(length, HEAD_DIM)
    key_single = jnp.where(is_key, other_low, partner_low)
    value_single = jnp.where(is_key, partner_low, other_low)

    raw = (
        jnp.einsum("qhd,kd->qhk", query_heads, key_single, preferred_element_type=f32) * SCALE
    )
    scores = jnp.where(allow[:, None, :], raw, NEGATIVE)
    powers = jnp.exp(scores - jnp.max(scores, axis=-1, keepdims=True))
    prob = powers / jnp.sum(powers, axis=-1, keepdims=True)
    prob_low = prob.astype(bf16)
    attended_low = (
        jnp.einsum("qhk,kd->qhd", prob_low, value_single, preferred_element_type=f32)
        .astype(bf16)
        .reshape(length, per_device * HEAD_DIM)
    )
    attn_pre = seq_sum(matmul_flip(attended_low, w_out), bf16)
    attn_pre, small_table, ffn_join = lax.optimization_barrier((attn_pre, small_table, ffn_join))
    laurel_left = small_table[:, :RANK]
    laurel_right = small_table[:, RANK : 2 * RANK]
    vector_gate_w = small_table[:, 2 * RANK : 2 * RANK + PLD]
    vector_proj_w = small_table[:, 2 * RANK + PLD :]

    attn_normed, attn_pull = jax.vjp(rms_norm, attn_pre, gain_attn)
    first_sum = stream + attn_normed
    left_pre = matmul(normed_low, laurel_left)
    left_low = left_pre.astype(bf16)
    right_pre = matmul_flip(left_low, laurel_right)
    laurel_normed, laurel_pull = jax.vjp(rms_norm, right_pre, gain_laurel)
    second_sum = (first_sum + normed + laurel_normed) * ROOT_HALF
    feed_normed, feed_pull = jax.vjp(rms_norm, second_sum, gain_pre)
    feed_own = feed_normed.astype(bf16)
    feed_low = lax.all_gather(feed_own, "fsdp", axis=0, tiled=True)
    ffn_all, _ = lax.optimization_barrier((ffn_all, feed_own))
    w_both, w_down = fetch(
        [near_all] + ffn_all, ffn_join, ffn_to, my_fsdp, ffn_place, (ffn_first, ffn_each)
    )
    both_pre = matmul(feed_low, w_both)
    ffn_width = w_down.shape[1]
    hidden, hidden_pull = jax.vjp(gelu_product, both_pre[:, :ffn_width], both_pre[:, ffn_width:])
    hidden_low = hidden.astype(bf16)
    down_pre = lax.psum_scatter(
        matmul_flip(hidden_low, w_down).astype(bf16), "fsdp", scatter_dimension=0, tiled=True
    ).astype(f32)
    down_normed, down_pull = jax.vjp(rms_norm, down_pre, gain_post)
    third_sum = second_sum + down_normed
    third_low = third_sum.astype(bf16)
    vector_pre = matmul(third_low, vector_gate_w)
    vector_gated, vector_pull = jax.vjp(lambda inner: gelu_product(inner, vectors), vector_pre)
    vector_low = vector_gated.astype(bf16)
    proj_pre = matmul_flip(vector_low, vector_proj_w)
    proj_normed, proj_pull = jax.vjp(rms_norm, proj_pre, gain_vec)
    result = third_sum + proj_normed
    output = result.astype(bf16)[None]

    grad_out = cotangent[0].astype(f32)
    grad_proj, grad_gain_vec = proj_pull(grad_out)
    proj_grad_low = grad_proj.astype(bf16)
    (grad_vector_pre,) = vector_pull(matmul(proj_grad_low, vector_proj_w))
    vector_grad_low = grad_vector_pre.astype(bf16)
    grad_third = grad_out + matmul_flip(vector_grad_low, vector_gate_w)
    grad_down, grad_gain_post = down_pull(grad_third)
    down_grad_low = lax.all_gather(grad_down.astype(bf16), "fsdp", axis=0, tiled=True)
    grad_gate, grad_up = hidden_pull(matmul(down_grad_low, w_down))
    both_grad_low = jnp.concatenate([grad_gate, grad_up], axis=1).astype(bf16)

    early_full = jnp.concatenate(
        [matmul_outer(third_low, vector_grad_low), matmul_outer(proj_grad_low, vector_low)], axis=1
    )
    small_early = small_sum(split_tiles(early_full, tile).reshape(-1, tile))
    feed_part = matmul_flip(both_grad_low, w_both).astype(bf16)
    feed_part, small_early = lax.optimization_barrier((feed_part, small_early))
    grad_feed = lax.psum_scatter(feed_part, "fsdp", scatter_dimension=0, tiled=True).astype(f32)
    both_grad_w = matmul_outer(feed_low, both_grad_low).astype(bf16)
    down_grad_w = matmul_outer(down_grad_low, hidden_low).astype(bf16)
    ffn_parts = cut_tiles(
        [both_grad_w, down_grad_w],
        [index.reshape(-1) for index in (far_cut[:, :far_half], far_cut[:, far_half:], near_cut)],
    )
    ffn_parts, grad_feed = lax.optimization_barrier((ffn_parts, grad_feed))
    *ffn_sums, near_sum = [
        lax.psum_scatter(value, "seq", scatter_dimension=0, tiled=True) for value in ffn_parts
    ]

    grad_second_norm, grad_gain_pre = feed_pull(grad_feed)
    half_grad = (grad_third + grad_second_norm) * ROOT_HALF
    grad_right, grad_gain_laurel = laurel_pull(half_grad)
    right_grad_low = grad_right.astype(bf16)
    left_grad_low = matmul(right_grad_low, laurel_right).astype(bf16)
    grad_attn, grad_gain_attn = attn_pull(half_grad)
    attn_grad_low = seq_gather(grad_attn.astype(bf16))
    grad_attended = (
        matmul(attn_grad_low, w_out).astype(bf16).reshape(length, per_device, HEAD_DIM)
    )
    out_grad_w = matmul_outer(attn_grad_low, attended_low).astype(bf16)
    value_grad = jnp.einsum("qhk,qhd->kd", prob_low, grad_attended, preferred_element_type=f32)
    grad_prob = jnp.einsum("qhd,kd->qhk", grad_attended, value_single, preferred_element_type=f32)
    inner = jnp.sum(prob * grad_prob, axis=-1, keepdims=True)
    grad_score = (prob * (grad_prob - inner)).astype(bf16)
    grad_query = (
        jnp.einsum("qhk,kd->qhd", grad_score, key_single, preferred_element_type=f32) * SCALE
    ).astype(bf16)
    key_grad = (
        jnp.einsum("qhk,qhd->kd", grad_score, query_heads, preferred_element_type=f32) * SCALE
    ).astype(bf16)
    value_grad = value_grad.astype(bf16)
    partner_grad = seq_swap(jnp.where(is_key, value_grad, key_grad), 1)
    partner_grad = partner_grad.reshape(seq_size // 2, 2, rows, HEAD_DIM)[:, ::-1]
    other_grad = jnp.where(is_key, key_grad, value_grad).astype(f32) + partner_grad.reshape(
        length, HEAD_DIM
    ).astype(f32)
    grad_query_pre, grad_gain_query = query_pull(grad_query.astype(f32))
    grad_key_pre, grad_gain_key = key_pull(other_grad[:, None, :])
    grad_gain_key = jnp.where(is_key, grad_gain_key, 0.0)
    first_grad_low = jnp.concatenate(
        [grad_query_pre, jnp.where(is_key, grad_key_pre, other_grad)], axis=1
    ).astype(bf16)
    first_grad_w = matmul_outer(pack_normed, first_grad_low).astype(bf16)
    near = (my_chip + shifts) % chips
    near_key = take_blocks(attn_key_chip, near)[:, None, :]
    near_order = take_blocks(attn_order_chip, near)[:, None, :]
    near_place = take_blocks(by_chip(attn_place), near)[:, None, :]

    def attn_cut(core):
        return pick(
            (near_key == 2 * my_seq + core)
            & (near_order == jnp.arange(attn_hold)[None, :, None]),
            near_place,
        ).reshape(-1)

    attn_given, attn_own = cut_tiles(
        [first_grad_w, out_grad_w], [attn_cut(1 - my_core), attn_cut(my_core)]
    )
    attn_given, attn_own, ffn_sums[0] = lax.optimization_barrier(
        (attn_given, attn_own, ffn_sums[0])
    )
    attn_parts = added(attn_own, core_swap(attn_given)).reshape(chips, attn_hold, tile, tile)
    attn_sum = attn_parts[0]
    attn_parts = [attn_parts[offset].astype(bf16) for offset in range(1, chips)]
    normed_pre = matmul_flip(first_grad_low, w_first)
    attn_sum, attn_parts, normed_pre = lax.optimization_barrier((attn_sum, attn_parts, normed_pre))
    normed_sum = seq_sum(normed_pre, bf16)
    for offset in range(1, chips):
        attn_sum = attn_sum + chip_shift(attn_parts[offset - 1], offset).astype(f32)
    attn_sum = attn_sum.astype(bf16)
    attn_back = pick(
        (column_slots[3][None, None, :] == (my_seq ^ flips)[:, None, None])
        & (column_slots[0][None, None, :] == my_key)
        & (column_slots[2][None, None, :] == jnp.arange(attn_room)[None, :, None]),
        column_slots[1],
    )

    grad_normed = half_grad + matmul_flip(left_grad_low, laurel_left) + normed_sum
    grad_stream_norm, grad_gain_in = normed_pull(grad_normed)
    input_grad = (half_grad + grad_stream_norm)[None]
    ffn_sums, attn_sum, grad_gain_in, input_grad = lax.optimization_barrier(
        (ffn_sums, attn_sum, grad_gain_in, input_grad)
    )
    ffn_sums = ffn_sums + [core_swap(value) for value in ffn_sums]
    ffn_return = gather_tiles(ffn_sums, [ffn_back[i] for i in range(1, chips)])
    ffn_return, attn_sum, grad_gain_in = lax.optimization_barrier(
        (ffn_return, attn_sum, grad_gain_in)
    )
    ffn_returned = [chip_shift(value, i + 1) for i, value in enumerate(ffn_return)]
    gain_grad = jnp.concatenate(
        [
            grad_gain_in,
            grad_gain_attn,
            grad_gain_laurel,
            grad_gain_pre,
            grad_gain_post,
            grad_gain_vec,
            grad_gain_query,
            grad_gain_key,
        ]
    )
    late_full = jnp.concatenate(
        [matmul_outer(normed_low, left_grad_low), matmul_outer(right_grad_low, left_low)], axis=1
    )
    late = jnp.concatenate(
        [late_full.reshape(seq_size, -1), gain_grad.reshape(seq_size, -1)], axis=1
    ).reshape(seq_size, -1, tile)
    late = seq_sum(late.reshape(-1, tile), bf16, True)

    late = late.astype(bf16)
    late = added(late, core_swap(late)).astype(bf16)
    attn_returned = seq_exchange(gather_tiles([attn_sum], [attn_back[i] for i in range(seq_size)]))
    attn_returned = attn_returned + [core_swap(value) for value in attn_returned]
    slot_grad = jnp.where(my_slots[0] >= 0, my_slots[1], back_size + my_slots[2])

    def slow_return():
        own_ffn = split_tiles(both_grad_w, tile), split_tiles(down_grad_w, tile)
        own_attn = split_tiles(first_grad_w, tile), split_tiles(out_grad_w, tile)
        parts = jnp.concatenate(own_ffn + own_attn + (jnp.zeros((1, tile, tile), bf16),))
        index = jnp.where(
            ffn_to == my_fsdp,
            ffn_place,
            jnp.where(attn_to == my_seq, ffn_count + attn_place, ffn_count + attn_count),
        )
        spread = jnp.concatenate(
            [gather_tiles([parts], [rows_of])[0] for rows_of in index.reshape(8, -1)]
        )
        spread = lax.all_to_all(
            spread.reshape((seq_size * fsdp_size, mine, tile, tile)),
            ("seq", "fsdp"),
            split_axis=0,
            concat_axis=0,
            tiled=True,
        )
        return jnp.sum(spread.astype(f32), axis=0).astype(bf16)

    slow_start = back_size + 2 * seq_size * attn_room
    slow_grads = lax.cond(fits, lambda: jnp.zeros((mine, tile, tile), bf16), slow_return)
    ffn_returned, slow_grads, near_sum, late = lax.optimization_barrier(
        (ffn_returned, slow_grads, near_sum, late)
    )
    late_sum = late.astype(f32)
    for offset in range(1, chips):
        late_sum = late_sum + chip_shift(late, offset).astype(f32)
    late = late_sum
    ffn_returned = ffn_returned + [core_swap(value) for value in ffn_returned]
    near_sums = [near_sum, core_swap(near_sum)]
    tile_grads = ffn_returned + near_sums + attn_returned + [slow_grads]
    slot_grad = jnp.where(fits, slot_grad, slow_start + local_slots)

    tile_new, tile_first_new, tile_second_new = rotate_update(
        tile_grads, slot_grad, tile_master, tile_first, tile_second, left_basis, right_basis, RATE_TILE
    )
    late_rows = late_full.shape[0] // seq_size
    late_tiles = late[:late_rows].reshape(-1, 1, tile, tile)
    gain_grad_mine = late[late_rows : late_rows + own_gains.shape[0] // tile].reshape(-1)
    small_grad = jnp.concatenate(
        [
            late_tiles.astype(bf16),
            small_early.reshape(late_tiles.shape[0], -1, tile, tile),
        ],
        axis=1,
    ).reshape(small_master.shape)
    small_new, small_first_new, small_second_new = rotate_update(
        [small_grad],
        jnp.arange(small_master.shape[0]),
        small_master,
        small_first,
        small_second,
        small_left,
        small_right,
        RATE_SMALL,
    )
    gain_first_new = BETA_ONE * gain_first + (1.0 - BETA_ONE) * gain_grad_mine
    gain_second_new = BETA_TWO * gain_second + (1.0 - BETA_TWO) * gain_grad_mine * gain_grad_mine
    correct_one = 1.0 - BETA_ONE**STEP
    correct_two = 1.0 - BETA_TWO**STEP
    gain_new = gains - RATE_GAIN * (gain_first_new / correct_one) / (
        jnp.sqrt(gain_second_new / correct_two) + ADAM_EPS
    )
    return (
        output,
        input_grad,
        tile_new,
        tile_first_new,
        tile_second_new,
        small_new,
        small_first_new,
        small_second_new,
        gain_new,
        gain_first_new,
        gain_second_new,
    )


def solution(mesh):
    return jax.shard_map(
        on_device,
        mesh=mesh,
        in_specs=(
            P("fsdp", "seq", None),
            P("fsdp", "seq", None),
            P("fsdp", None),
            P("fsdp", "seq", None),
            P(),
            P(("seq", "fsdp"), None, None),
            P(("seq", "fsdp"), None, None),
            P(("seq", "fsdp"), None, None),
            P(("seq", "fsdp"), None, None),
            P(("seq", "fsdp"), None, None),
            P("seq", None, None),
            P("seq", None, None),
            P("seq", None, None),
            P("seq", None, None),
            P("seq", None, None),
            P("seq"),
            P("seq"),
            P("seq"),
        ),
        out_specs=(
            P("fsdp", "seq", None),
            P("fsdp", "seq", None),
            P(("seq", "fsdp"), None, None),
            P(("seq", "fsdp"), None, None),
            P(("seq", "fsdp"), None, None),
            P("seq", None, None),
            P("seq", None, None),
            P("seq", None, None),
            P("seq"),
            P("seq"),
            P("seq"),
        ),
        check_vma=False,
    )
```

```python
import math

import jax
import jax.numpy as jnp
from jax import lax
from jax.experimental import pallas as pl
from jax.experimental.pallas import tpu as pltpu
from jax.sharding import PartitionSpec as P

HEADS = 8
KV_HEADS = 2
HEAD_DIM = 256
FF = 8192
RANK = 64
PLD = 256
STEP = 5


EPS = 1e-06
SCALE = 0.0625
THETA = 1000000.0
ROOT_HALF = 0.7071067811865476
BETA_ONE = 0.5
BETA_TWO = 0.5
ADAM_EPS = 1e-08
RATE_TILE = 0.02
RATE_SMALL = 0.04
RATE_GAIN = 0.3
DECAY = 0.01
NEGATIVE = -1e30
TILE = 128
VMEM_BYTES = 4 * 1024 * 1024


def rms_norm(value, gain):
    return value * lax.rsqrt(jnp.mean(value * value, axis=-1, keepdims=True) + EPS) * gain


def rotary(value, position):
    half = value.shape[-1] // 2
    freq = THETA ** (-2.0 * jnp.arange(half).astype(jnp.float32) / value.shape[-1])
    angle = position.astype(jnp.float32)[:, None] * freq[None, :]
    cosine = jnp.cos(angle)[:, None, :]
    sine = jnp.sin(angle)[:, None, :]
    first = value[..., :half]
    second = value[..., half:]
    return jnp.concatenate(
        [first * cosine - second * sine, second * cosine + first * sine], axis=-1
    )


def documents(lengths, length):
    places = jnp.arange(length)
    ends = jnp.cumsum(lengths)
    passed = places[:, None] >= ends[None, :]
    segment = jnp.sum(passed.astype(jnp.int32), axis=1)
    before = jnp.sum(jnp.where(passed, lengths[None, :], 0), axis=1)
    return (segment, places - before)


def matmul(left, right):
    return jnp.dot(left, right, preferred_element_type=jnp.float32)


def matmul_flip(left, right):
    return lax.dot_general(
        left, right, (((1,), (1,)), ((), ())), preferred_element_type=jnp.float32
    )


def matmul_outer(left, right):
    return lax.dot_general(
        left, right, (((0,), (0,)), ((), ())), preferred_element_type=jnp.float32
    )


def assemble(tiles, row_blocks):
    size = tiles.shape[1]
    column_blocks = tiles.shape[0] // row_blocks
    return (
        tiles.reshape(row_blocks, column_blocks, size, size)
        .transpose(0, 2, 1, 3)
        .reshape(row_blocks * size, column_blocks * size)
    )


def split_tiles(matrix, size):
    row_blocks = matrix.shape[0] // size
    column_blocks = matrix.shape[1] // size
    return (
        matrix.reshape(row_blocks, size, column_blocks, size)
        .transpose(0, 2, 1, 3)
        .reshape(row_blocks * column_blocks, size, size)
    )


def gelu_product(first, second):
    return jax.nn.gelu(first, approximate=True) * second


def room(count, share):
    mean = count * share
    return math.ceil(mean + 3.6 * math.sqrt(mean * (1.0 - share)) + 3.0)


def count_earlier(group, valid):
    size = group.shape[-1]
    order = jnp.arange(size)
    same = (group[..., :, None] == group[..., None, :]) & valid[..., None, :]
    same = same & (order[None, :] < order[:, None])
    return jnp.sum(same.astype(jnp.int32), axis=-1)


def count_long(keys):
    groups, size = keys.shape

    def kernel(row_ref, column_ref, out_ref):
        row = row_ref[0]
        column = column_ref[0]
        here = lax.broadcasted_iota(jnp.int32, (size, size), 1)
        other = lax.broadcasted_iota(jnp.int32, (size, size), 0)
        earlier = (column == row) & (other < here)
        out_ref[0] = jnp.sum(earlier.astype(jnp.int32), axis=0, keepdims=True)

    return pl.pallas_call(
        kernel,
        grid=(groups,),
        out_shape=jax.ShapeDtypeStruct((groups, 1, size), jnp.int32),
        in_specs=[
            pl.BlockSpec((1, 1, size), lambda i: (i, 0, 0)),
            pl.BlockSpec((1, size, 1), lambda i: (i, 0, 0)),
        ],
        out_specs=pl.BlockSpec((1, 1, size), lambda i: (i, 0, 0)),
        cost_estimate=pl.CostEstimate(flops=0, transcendentals=0, bytes_accessed=0),
        compiler_params=pltpu.CompilerParams(vmem_limit_bytes=4 * VMEM_BYTES),
    )(keys[:, None, :], keys[:, :, None]).reshape(groups, size)


def pick(match, value):
    return jnp.sum(jnp.where(match, value, 0), axis=-1)


def steps_of(counts):
    for steps in (8, 4, 2):
        if all(count % steps == 0 for count in counts) and sum(counts) // steps >= 24:
            return steps
    return 1


def tile_kernel_call(kernel, index, arrays, out_shape, out_specs, steps):
    moved = sum(math.prod(one.shape) * 2 for one in jax.tree.leaves(out_shape))
    return pl.pallas_call(
        kernel,
        grid=(steps,),
        cost_estimate=pl.CostEstimate(flops=0, transcendentals=0, bytes_accessed=2 * moved),
        out_shape=out_shape,
        in_specs=[pl.BlockSpec(memory_space=pltpu.SMEM)]
        + [pl.BlockSpec(memory_space=pl.ANY)] * len(arrays),
        out_specs=out_specs,
        scratch_shapes=[pltpu.SemaphoreType.DMA],
        compiler_params=pltpu.CompilerParams(vmem_limit_bytes=2 * moved // steps + VMEM_BYTES),
    )(index, *arrays)


def start_copy(sources, place, target, sem, start=0):
    if len(sources) == 1:
        pltpu.make_async_copy(sources[0].at[place - start], target, sem).start()
        return
    half = len(sources) // 2
    middle = start + sum(ref.shape[0] for ref in sources[:half])

    @pl.when(place < middle)
    def _():
        start_copy(sources[:half], place, target, sem, start)

    @pl.when(place >= middle)
    def _():
        start_copy(sources[half:], place, target, sem, middle)


def fill_tiles(arrays, indices, total, start):
    tile = arrays[0].shape[-1] if arrays[0].ndim == 3 else TILE
    counts = [index.shape[0] for index in indices]
    steps = steps_of(counts)

    def kernel(index_ref, *refs):
        sources, outs, sem = refs[: len(arrays)], refs[len(arrays) : -1], refs[-1]
        first = 0
        for out, count in zip(outs, counts):
            each = count // steps
            base = first + pl.program_id(0) * each

            def step(i, carry, out=out, base=base):
                start(sources, index_ref[base + i], out.at[i], sem)
                return carry

            lax.fori_loop(0, each, step, 0)
            first = first + count
        for out in outs:
            pltpu.make_async_copy(out, out, sem).wait()

    return tile_kernel_call(
        kernel,
        jnp.clip(jnp.concatenate(indices), 0, total - 1),
        arrays,
        [jax.ShapeDtypeStruct((count, tile, tile), arrays[0].dtype) for count in counts],
        [pl.BlockSpec((count // steps, tile, tile), lambda i: (i, 0, 0)) for count in counts],
        steps,
    )


def gather_tiles(arrays, indices):
    return fill_tiles(arrays, indices, sum(array.shape[0] for array in arrays), start_copy)


def cut_tiles(matrices, indices):
    row_blocks = matrices[0].shape[0] // TILE
    widths = [matrix.shape[1] // TILE for matrix in matrices]

    def start(sources, place, target, sem):
        first = 0
        for ref, width in zip(sources, widths):
            size = row_blocks * width

            @pl.when((place >= first) & (place < first + size))
            def _(ref=ref, first=first, width=width):
                row = (place - first) // width
                column = place - first - row * width
                source = ref.at[
                    pl.ds(pl.multiple_of(row * TILE, TILE), TILE),
                    pl.ds(pl.multiple_of(column * TILE, TILE), TILE),
                ]
                pltpu.make_async_copy(source, target, sem).start()

            first = first + size

    return fill_tiles(matrices, indices, row_blocks * sum(widths), start)


def join_tiles(arrays, index, row_blocks, columns):
    tile = arrays[0].shape[-1]
    steps = 4
    each = row_blocks // steps

    def kernel(index_ref, *refs):
        sources, outs, sem = refs[: len(arrays)], refs[len(arrays) : -1], refs[-1]
        base = pl.program_id(0) * each
        start = 0
        for out, width in zip(outs, columns):

            def step(i, carry, out=out, start=start, width=width):
                row = i // width
                column = i - row * width
                target = out.at[
                    pl.ds(pl.multiple_of(row * tile, tile), tile),
                    pl.ds(pl.multiple_of(column * tile, tile), tile),
                ]
                start_copy(sources, index_ref[start + base * width + i], target, sem)
                return carry

            lax.fori_loop(0, each * width, step, 0)
            start = start + row_blocks * width
        for out in outs:
            pltpu.make_async_copy(out, out, sem).wait()

    total = sum(array.shape[0] for array in arrays)
    out_shape = tuple(
        jax.ShapeDtypeStruct((row_blocks * tile, width * tile), arrays[0].dtype)
        for width in columns
    )
    out_specs = tuple(pl.BlockSpec((each * tile, width * tile), lambda i: (i, 0)) for width in columns)
    return tile_kernel_call(
        kernel, jnp.clip(index, 0, total - 1), arrays, out_shape, out_specs, steps
    )


def split_low(value):
    high = value.astype(jnp.bfloat16)
    return high, (value - high.astype(jnp.float32)).astype(jnp.bfloat16)


def rotate_update(grads, index, master, first, second, left, right, rate):
    count, tile, _ = master.shape
    each = 4 if count % 4 == 0 else 1
    correct_one = 1.0 - BETA_ONE**STEP
    correct_two = 1.0 - BETA_TWO**STEP

    def product(one, two, dims):
        return lax.dot_general(one, two, (dims, ((), ())), preferred_element_type=jnp.float32)

    def kernel(index_ref, *refs):
        sources, refs = refs[: len(grads)], refs[len(grads) :]
        master_ref, first_ref, second_ref, left_ref, right_ref = refs[:5]
        master_out, first_out, second_out, held, sems = refs[5:]
        now = pl.program_id(0)

        @pl.when(now == 0)
        def _():
            def step(i, carry):
                start_copy(sources, index_ref[i], held.at[i], sems.at[i // each])
                return carry

            lax.fori_loop(0, count, step, 0)

        block = held.at[pl.ds(now * each, each)]
        pltpu.make_async_copy(block, block, sems.at[now]).wait()
        lefts, rights, turns = [], [], []
        for i in range(each):
            grad = held[now * each + i]
            lefts.append(split_low(left_ref[i]))
            rights.append(split_low(right_ref[i]))
            half_turned = product(
                jnp.concatenate([grad, grad], axis=1),
                jnp.concatenate(rights[i], axis=0),
                ((1,), (0,)),
            )
            turns.append(split_low(half_turned))
        for i in range(each):
            (left_high, left_low), (high, low) = lefts[i], turns[i]
            turns[i] = product(
                jnp.concatenate([left_high, left_high, left_low], axis=0),
                jnp.concatenate([high, low, high], axis=0),
                ((0,), (0,)),
            )
        for i in range(each):
            right_high, right_low = rights[i]
            first_new = BETA_ONE * first_ref[i] + (1.0 - BETA_ONE) * turns[i]
            second_new = BETA_TWO * second_ref[i] + (1.0 - BETA_TWO) * turns[i] * turns[i]
            first_out[i] = first_new
            second_out[i] = second_new
            high, low = split_low(
                first_new / correct_one / (jnp.sqrt(second_new / correct_two) + ADAM_EPS)
            )
            half_back = product(
                jnp.concatenate([high, low, high], axis=1),
                jnp.concatenate([right_high, right_high, right_low], axis=1),
                ((1,), (1,)),
            )
            turns[i] = split_low(half_back)
        for i in range(each):
            (left_high, left_low), (high, low) = lefts[i], turns[i]
            back = product(
                jnp.concatenate([left_high, left_high, left_low], axis=1),
                jnp.concatenate([high, low, high], axis=0),
                ((1,), (0,)),
            )
            weight = master_ref[i]
            master_out[i] = weight - rate * (back + DECAY * weight)

    spec = pl.BlockSpec((each, tile, tile), lambda i: (i, 0, 0))
    shape = jax.ShapeDtypeStruct(master.shape, jnp.float32)
    total = sum(array.shape[0] for array in grads)
    return pl.pallas_call(
        kernel,
        grid=(count // each,),
        out_shape=(shape, shape, shape),
        cost_estimate=pl.CostEstimate(
            flops=count * 22 * tile**3, transcendentals=0, bytes_accessed=count * tile**2 * 34
        ),
        in_specs=[pl.BlockSpec(memory_space=pltpu.SMEM)]
        + [pl.BlockSpec(memory_space=pl.ANY)] * len(grads)
        + [spec] * 5,
        out_specs=(spec, spec, spec),
        scratch_shapes=[
            pltpu.VMEM((count, tile, tile), jnp.bfloat16),
            pltpu.SemaphoreType.DMA((count // each,)),
        ],
        compiler_params=pltpu.CompilerParams(vmem_limit_bytes=4 * VMEM_BYTES),
    )(jnp.clip(index, 0, total - 1), *grads, master, first, second, left, right)


def seq_swap(value, flip):
    size = lax.axis_size("seq")
    return lax.ppermute(value, "seq", [(i, i ^ flip) for i in range(size)])


def take_blocks(value, order):
    return jnp.stack(
        [lax.dynamic_index_in_dim(value, order[i], 0, False) for i in range(order.shape[0])]
    )


def core_swap(value):
    size = lax.axis_size("fsdp")
    return lax.ppermute(value, "fsdp", [(i, i ^ 1) for i in range(size)])


def chip_shift(value, offset):
    size = lax.axis_size("fsdp")
    chips = size // 2
    return lax.ppermute(
        value, "fsdp", [(i, (i // 2 + offset) % chips * 2 + i % 2) for i in range(size)]
    )


def seq_gather(value):
    size = lax.axis_size("seq")
    return jnp.concatenate([value] + [seq_swap(value, flip) for flip in range(1, size)], axis=0)


def seq_ordered(value):
    size = lax.axis_size("seq")
    parts = jnp.stack([value] + [seq_swap(value, flip) for flip in range(1, size)], axis=0)
    return take_blocks(parts, lax.axis_index("seq") ^ jnp.arange(size))


def seq_exchange(values):
    return [values[0]] + [seq_swap(values[flip], flip) for flip in range(1, len(values))]


def seq_sum(value, wire, ordered=False):
    size = lax.axis_size("seq")
    parts = value.reshape((size, value.shape[0] // size) + value.shape[1:])
    if ordered:
        parts = take_blocks(parts, lax.axis_index("seq") ^ jnp.arange(size))
    total = parts[0]
    for flip in range(1, size):
        total = total + seq_swap(parts[flip].astype(wire), flip).astype(jnp.float32)
    return total


def chip_exchange(values):
    return [values[0]] + [chip_shift(values[offset], offset) for offset in range(1, len(values))]


def core_pair(value):
    other = core_swap(value)
    even = lax.axis_index("fsdp") % 2 == 0
    return jnp.where(even, jnp.stack([value, other]), jnp.stack([other, value]))


def small_sum(value):
    seq_size = lax.axis_size("seq")
    chips = lax.axis_size("fsdp") // 2
    chip = lax.axis_index("fsdp") // 2
    even = lax.axis_index("fsdp") % 2 == 0
    low = value.astype(jnp.bfloat16)
    parts = low.reshape((seq_size, 2, low.shape[0] // (2 * seq_size)) + low.shape[1:])
    kept = jnp.where(even, parts[:, 0], parts[:, 1]).astype(jnp.float32)
    given = jnp.where(even, parts[:, 1], parts[:, 0])
    kept = kept + core_swap(given).astype(jnp.float32)
    kept = seq_sum(kept.reshape((-1,) + low.shape[1:]), jnp.bfloat16, True)
    kept = kept.reshape((chips, kept.shape[0] // chips) + kept.shape[1:])
    kept = take_blocks(kept, (chip + jnp.arange(chips)) % chips)
    total = kept[0]
    for offset in range(1, chips):
        total = total + chip_shift(kept[offset].astype(jnp.bfloat16), offset).astype(jnp.float32)
    total = total.astype(jnp.bfloat16)
    parts = jnp.stack([total] + [chip_shift(total, offset) for offset in range(1, chips)])
    parts = take_blocks(parts, (chip - jnp.arange(chips)) % chips)
    return core_pair(parts).reshape((value.shape[0] // seq_size,) + value.shape[1:])


def turn(value, cosine, sine):
    half = value.shape[-1] // 2
    first, second = value[..., :half], value[..., half:]
    return jnp.concatenate(
        [first * cosine - second * sine, second * cosine + first * sine], axis=-1
    )


def added(one, two):
    return one.astype(jnp.float32) + two.astype(jnp.float32)


def on_device(
    tokens,
    layer_vectors,
    doc_lengths,
    cotangent,
    tile_owner,
    tile_master,
    tile_first,
    tile_second,
    left_basis,
    right_basis,
    small_master,
    small_first,
    small_second,
    small_left,
    small_right,
    gains,
    gain_first,
    gain_second,
):
    bf16 = jnp.bfloat16
    f32 = jnp.float32
    tile = tile_master.shape[1]
    width = tokens.shape[2]
    row_blocks = width // tile
    rows = tokens.shape[1]
    seq_size = lax.axis_size("seq")
    fsdp_size = lax.axis_size("fsdp")
    chips = fsdp_size // 2
    mine = tile_master.shape[0]
    tiles = tile_owner.shape[0]
    length = rows * seq_size
    per_device = HEADS // seq_size
    per_key = seq_size // KV_HEADS
    query_width = HEADS * HEAD_DIM
    key_width = KV_HEADS * HEAD_DIM
    my_seq = lax.axis_index("seq")
    my_fsdp = lax.axis_index("fsdp")
    my_chip = my_fsdp // 2
    my_core = my_fsdp % 2
    flips = jnp.arange(seq_size)
    shifts = jnp.arange(chips)

    query_blocks = query_width // tile
    key_blocks = key_width // tile
    ffn_blocks = FF // tile
    query_each = query_blocks // seq_size
    head_blocks = HEAD_DIM // tile
    ffn_each = ffn_blocks // fsdp_size
    columns = tiles // row_blocks
    attn_first = query_each + head_blocks
    attn_count = row_blocks * (attn_first + query_each)
    ffn_first = 2 * ffn_each
    ffn_count = row_blocks * 3 * ffn_each
    attn_share = (2 * query_blocks + 2 * key_blocks) / columns
    ffn_share = 3 * ffn_blocks / columns
    attn_room = (room(2 * mine, attn_share / seq_size) + 1) // 2
    attn_hold = (room(attn_count, 1.0 / chips) + 1) // 2 + 1
    ffn_room = (room(2 * mine, ffn_share / chips) + 1) // 2
    both_count = row_blocks * ffn_first
    near_hold = (room(2 * mine, ffn_share / fsdp_size) + 3) // 4 * 4
    far_hold = (room(ffn_count * (1.0 - 1.0 / chips), 1.0 / seq_size) + 3) // 4 * 4
    far_half = far_hold * 3 // 7 // 4 * 4
    far_rest = far_hold - far_half

    def tile_places(owner):
        row = owner // columns
        column = owner % columns
        key_at = column - query_blocks
        value_at = key_at - key_blocks
        out_at = value_at - key_blocks
        ffn_at = out_at - query_blocks
        is_attn = ffn_at < 0
        kind = ffn_at // ffn_blocks
        ffn_column = ffn_at % ffn_blocks
        ffn_to = jnp.where(is_attn, -1, ffn_column // ffn_each)
        ffn_local = ffn_column % ffn_each
        ffn_place = jnp.where(
            kind == 2,
            both_count + row * ffn_each + ffn_local,
            row * ffn_first + kind * ffn_each + ffn_local,
        )
        attn_to = jnp.where(
            key_at < 0,
            column // query_each,
            jnp.where(
                value_at < 0,
                key_at // head_blocks * per_key,
                jnp.where(
                    out_at < 0,
                    value_at // head_blocks * per_key + per_key - 1,
                    out_at // query_each,
                ),
            ),
        )
        attn_place = jnp.where(
            key_at < 0,
            row * attn_first + column % query_each,
            jnp.where(
                out_at < 0,
                row * attn_first + query_each + key_at % head_blocks,
                row_blocks * attn_first + row * query_each + out_at % query_each,
            ),
        )
        attn_to = jnp.where(is_attn, attn_to, -1)
        return (ffn_to, ffn_place, attn_to, attn_place)

    owners = tile_owner.reshape(seq_size, fsdp_size, mine)
    slot_seq = jnp.arange(seq_size)[:, None, None]
    slot_fsdp = jnp.arange(fsdp_size)[None, :, None]
    slot_chip = slot_fsdp // 2
    local_slots = jnp.arange(mine)
    both_slots = jnp.arange(2 * mine)
    both_slots = jnp.where(
        both_slots // mine == my_core, both_slots % mine, mine + both_slots % mine
    )

    ffn_to = tile_places(owners)[0]
    ffn_chip = jnp.where(ffn_to < 0, -1, ffn_to // 2)
    chip_view = ffn_chip.reshape(seq_size, chips, 2 * mine)
    chip_rank = count_earlier(chip_view, chip_view >= 0).reshape(owners.shape)
    near_view = jnp.where(slot_chip == ffn_chip, ffn_to, -1).reshape(chip_view.shape)
    near_rank = count_earlier(near_view, near_view >= 0).reshape(owners.shape)
    ffn_slots = lax.dynamic_slice(
        jnp.stack([ffn_chip, chip_rank, near_view.reshape(owners.shape), near_rank]),
        (0, my_seq, 2 * my_chip, 0),
        (4, 1, 2, mine),
    ).reshape(4, 1, 1, 2 * mine)
    near_keep = pick(
        (ffn_slots[2][0] == my_fsdp) & (ffn_slots[3][0] == jnp.arange(near_hold)[:, None]),
        both_slots,
    )
    ffn_pack = pick(
        (ffn_slots[0] == ((my_chip + shifts) % chips)[:, None, None])
        & (ffn_slots[1] == (my_core * ffn_room + jnp.arange(ffn_room))[None, :, None]),
        both_slots,
    )
    master_low = tile_master.astype(bf16)
    masters = [master_low, core_swap(master_low)]
    *ffn_sent, near_kept = gather_tiles(
        masters, [ffn_pack[i] for i in range(1, chips)] + [near_keep]
    )
    small_rows = small_master.shape[0] // 2
    small_half = lax.dynamic_slice_in_dim(small_master, my_core * small_rows, small_rows)
    masters, ffn_sent, near_kept, chip_rank, near_rank, owners, own_tokens, own_gains, small_half = (
        lax.optimization_barrier(
            (
                masters,
                ffn_sent,
                near_kept,
                chip_rank,
                near_rank,
                owners,
                tokens[0],
                gains.astype(bf16),
                small_half.astype(bf16),
            )
        )
    )
    ffn_got = [chip_shift(value, i + 1) for i, value in enumerate(ffn_sent)]
    near_all = lax.all_gather(near_kept, "seq", axis=0, tiled=True)

    ffn_to, ffn_place, attn_to, attn_place = tile_places(owners)
    ffn_chip = jnp.where(ffn_to < 0, -1, ffn_to // 2)
    attn_view = attn_to.reshape(seq_size, chips, 2 * mine)
    attn_rank = count_earlier(attn_view, attn_view >= 0).reshape(owners.shape)
    attn_core = (attn_rank + slot_seq) % 2
    attn_rank = attn_rank // 2
    attn_key = jnp.where(attn_to < 0, -1, 2 * attn_to + attn_core)

    chip_slots = lax.dynamic_slice(
        jnp.stack([attn_key, attn_rank]), (0, my_seq, 2 * my_chip, 0), (2, 1, 2, mine)
    ).reshape(2, 1, 1, 2 * mine)
    attn_message = attn_room + row_blocks * rows // tile + small_rows + -(-own_gains.shape[0] // tile**2)
    attn_pack = pick(
        (chip_slots[0] == (2 * (my_seq ^ flips) + my_core)[:, None, None])
        & (chip_slots[1] == jnp.arange(attn_room)[None, :, None]),
        both_slots,
    )
    attn_sent = gather_tiles(masters, [attn_pack[i] for i in range(seq_size)])
    is_near = slot_chip == ffn_chip
    near_key = jnp.where(is_near, ffn_to, -1)
    far_key = jnp.where(is_near, -1, ffn_to)
    far_rank = count_long(far_key.reshape(seq_size, fsdp_size * mine)).reshape(owners.shape)
    def by_chip(value):
        value = value.reshape(seq_size, chips, 2 * mine).transpose(1, 0, 2)
        return value.reshape(chips, seq_size * 2 * mine)

    attn_key_chip = by_chip(attn_key)
    attn_order_chip = count_long(attn_key_chip)
    attn_order = (
        attn_order_chip.reshape(chips, seq_size, 2 * mine).transpose(1, 0, 2).reshape(owners.shape)
    )
    fits = jnp.all(
        jnp.where(
            ffn_to < 0,
            (attn_rank < attn_room) & (attn_order < attn_hold),
            jnp.where(
                is_near, near_rank < near_hold, (chip_rank < 2 * ffn_room) & (far_rank < far_hold)
            ),
        )
    )
    rank_core = chip_rank // ffn_room
    rank_local = chip_rank % ffn_room
    out_place = (
        jnp.where(rank_core == my_core, 0, (chips - 1) * ffn_room)
        + ((my_chip - slot_chip) % chips - 1) * ffn_room
        + rank_local
    )
    near_start = 2 * (chips - 1) * ffn_room
    back_size = near_start + 2 * near_hold
    back_place = jnp.where(
        is_near,
        near_start + jnp.where(ffn_to == my_fsdp, 0, near_hold) + near_rank,
        jnp.where(rank_core == my_core, 0, (chips - 1) * ffn_room)
        + ((my_chip - ffn_chip) % chips - 1) * ffn_room
        + rank_local,
    )
    attn_back_place = (
        jnp.where(attn_core == my_core, 0, seq_size * attn_room)
        + (attn_to ^ my_seq) * attn_room
        + attn_rank
    )
    my_slots = lax.dynamic_slice(
        jnp.stack([ffn_to, back_place, attn_back_place]), (0, my_seq, my_fsdp, 0), (3, 1, 1, mine)
    ).reshape(3, mine)
    seq_slots = lax.dynamic_slice(
        jnp.stack(
            [
                far_key,
                far_rank,
                ffn_chip,
                out_place,
                chip_rank,
                jnp.broadcast_to(slot_chip, owners.shape),
            ]
        ),
        (0, my_seq, 0, 0),
        (6, 1, fsdp_size, mine),
    ).reshape(6, fsdp_size * mine)
    column_slots = lax.dynamic_slice(
        jnp.stack([attn_key, attn_order, attn_rank, jnp.broadcast_to(slot_seq, owners.shape)]),
        (0, 0, 2 * my_chip, 0),
        (4, seq_size, 2, mine),
    ).reshape(4, 2 * seq_size * mine)
    my_key = 2 * my_seq + my_core

    attn_keep = pick(
        (column_slots[0][None, :] == my_key)
        & (column_slots[1][None, :] == jnp.arange(attn_hold)[:, None]),
        jnp.where(
            column_slots[3] == my_seq,
            0,
            attn_room + ((column_slots[3] ^ my_seq) - 1) * attn_message,
        )
        + column_slots[2],
    )
    attn_join = pick(
        (attn_to.reshape(1, -1) == my_seq)
        & (attn_place.reshape(1, -1) == jnp.arange(attn_count)[:, None]),
        (
            jnp.where(attn_core == my_core, 0, chips * attn_hold)
            + (my_chip - slot_chip) % chips * attn_hold
            + attn_order
        ).reshape(1, -1),
    )
    ffn_keep = pick(
        (seq_slots[0][None, :] == my_fsdp) & (seq_slots[1][None, :] == jnp.arange(far_hold)[:, None]),
        seq_slots[3][None, :],
    )
    ffn_join = pick(
        (ffn_to.reshape(1, -1) == my_fsdp)
        & (ffn_place.reshape(1, -1) == jnp.arange(ffn_count)[:, None]),
        jnp.where(
            is_near,
            slot_seq * near_hold + near_rank,
            seq_size * near_hold
            + jnp.where(
                far_rank < far_half,
                slot_seq * far_half + far_rank,
                seq_size * far_half + slot_seq * far_rest + far_rank - far_half,
            ),
        ).reshape(1, -1),
    )

    def cut_index(key, rank, hold):
        return pick(
            (key.reshape(seq_size, 1, -1) == my_fsdp)
            & (rank.reshape(seq_size, 1, -1) == jnp.arange(hold)[None, :, None]),
            ffn_place.reshape(seq_size, 1, -1),
        )

    far_cut = cut_index(far_key, far_rank, far_hold)
    near_cut = cut_index(near_key, near_rank, near_hold)
    ffn_back = pick(
        (seq_slots[5][None, None, :] == ((my_chip + shifts) % chips)[:, None, None])
        & (seq_slots[2][None, None, :] == my_chip)
        & (seq_slots[4][None, None, :] == (my_core * ffn_room + jnp.arange(ffn_room))[None, :, None]),
        jnp.where(seq_slots[0] == my_fsdp, 0, far_hold) + seq_slots[1],
    )

    token_tiles = own_tokens.reshape(rows, row_blocks, tile).transpose(1, 0, 2)
    token_tiles = token_tiles.reshape(-1, tile, tile)
    gain_rows = own_gains.reshape(-1, tile)
    gain_tiles = jnp.pad(gain_rows, ((0, -gain_rows.shape[0] % tile), (0, 0))).reshape(-1, tile, tile)
    common = jnp.concatenate([token_tiles, small_half, gain_tiles])
    attn_got = [attn_sent[0]] + [
        seq_swap(jnp.concatenate([attn_sent[flip], common]), flip) for flip in range(1, seq_size)
    ]
    segment, position = documents(doc_lengths[0], length)
    places = ((my_seq ^ flips)[:, None] * rows + jnp.arange(rows)[None, :]).reshape(-1)

    def reorder(values):
        blocks = values.reshape(seq_size, rows)
        return jnp.concatenate(
            [lax.dynamic_index_in_dim(blocks, my_seq ^ i, 0, False) for i in range(seq_size)]
        )

    pack_segment = reorder(segment)
    allow = (pack_segment[:, None] == pack_segment[None, :]) & (
        places[None, :] <= places[:, None]
    )
    turns = jnp.arange(HEAD_DIM // 2).astype(f32)
    angle = reorder(position).astype(f32)[:, None] * (THETA ** (-2.0 * turns / HEAD_DIM))[None, :]
    cosine, sine = jnp.cos(angle)[:, None, :], jnp.sin(angle)[:, None, :]
    parts = [common] + [value[attn_room:] for value in attn_got[1:]]
    token_end = token_tiles.shape[0]
    small_end = token_end + small_rows

    def seq_order(value):
        return take_blocks(value, my_seq ^ flips)

    pack_tokens = jnp.concatenate(
        [
            part[:token_end].reshape(row_blocks, rows, tile).transpose(1, 0, 2).reshape(rows, width)
            for part in parts
        ]
    )
    gain_full = seq_order(
        jnp.stack([part[small_end:].reshape(-1, tile)[: gain_rows.shape[0]] for part in parts])
    )
    gain_full = gain_full.reshape(-1).astype(f32)
    gain_in = gain_full[0:width]
    pack_normed = rms_norm(pack_tokens.astype(f32), gain_in).astype(bf16)
    ready = (allow, cosine, sine, ffn_keep, attn_keep, pack_normed, gain_full)
    ffn_got, attn_got, parts, ready, near_all = lax.optimization_barrier(
        (ffn_got, attn_got, parts, ready, near_all)
    )
    allow, cosine, sine, ffn_keep, attn_keep, pack_normed, gain_full = ready
    gain_in = gain_full[0:width]
    small_got = core_pair(seq_order(jnp.stack([part[token_end:small_end] for part in parts])))
    small_got = small_got.transpose(1, 0, 2, 3, 4)
    small_table = assemble(small_got.reshape((-1,) + small_master.shape[1:]), row_blocks)
    (attn_kept,) = gather_tiles(attn_got, [attn_keep])
    ffn_got = ffn_got + [core_swap(value) for value in ffn_got]
    ffn_kept = gather_tiles(ffn_got, [ffn_keep[:far_half], ffn_keep[far_half:]])
    ffn_kept, attn_kept = lax.optimization_barrier((ffn_kept, attn_kept))
    ffn_all = [lax.all_gather(value, "seq", axis=0, tiled=True) for value in ffn_kept]
    attn_all = [attn_kept] + [chip_shift(attn_kept, offset) for offset in range(1, chips)]
    attn_all = attn_all + [core_swap(value) for value in attn_all]

    attn_all, ffn_all[0], attn_join = lax.optimization_barrier((attn_all, ffn_all[0], attn_join))

    def fetch(arrays, index, to, me, place, columns_of):
        def fast():
            return join_tiles(arrays, index, row_blocks, columns_of)

        def slow():
            whole = lax.all_to_all(
                jnp.broadcast_to(master_low[None], (seq_size * fsdp_size,) + master_low.shape),
                ("seq", "fsdp"),
                split_axis=0,
                concat_axis=0,
                tiled=True,
            ).reshape(-1, tile, tile)
            count = row_blocks * sum(columns_of)
            slots = pick(
                (to.reshape(1, -1) == me) & (place.reshape(1, -1) == jnp.arange(count)[:, None]),
                jnp.arange(tiles)[None, :],
            )
            return join_tiles([whole], slots, row_blocks, columns_of)

        return lax.cond(fits, fast, slow)

    w_first, w_out = fetch(
        attn_all, attn_join, attn_to, my_seq, attn_place, (attn_first, query_each)
    )
    gain_attn = gain_full[width : 2 * width]
    gain_laurel = gain_full[2 * width : 3 * width]
    gain_pre = gain_full[3 * width : 4 * width]
    gain_post = gain_full[4 * width : 5 * width]
    gain_vec = gain_full[5 * width : 6 * width]
    gain_query = gain_full[6 * width : 6 * width + HEAD_DIM]
    gain_key = gain_full[6 * width + HEAD_DIM : 6 * width + 2 * HEAD_DIM]
    stream = own_tokens.astype(f32)
    vectors = layer_vectors[0].astype(f32)
    normed, normed_pull = jax.vjp(rms_norm, stream, gain_in)
    normed_low = normed.astype(bf16)
    first_pre = matmul(pack_normed, w_first)
    is_key = my_seq % per_key == 0

    def shape_query(query_in, query_gain):
        value = rms_norm(query_in.reshape(length, per_device, HEAD_DIM), query_gain)
        return turn(value, cosine, sine)

    def shape_key(key_in, key_gain):
        return turn(rms_norm(key_in.reshape(length, 1, HEAD_DIM), key_gain), cosine, sine)

    query_pre = first_pre[:, : per_device * HEAD_DIM]
    other_pre = first_pre[:, per_device * HEAD_DIM :]
    query_rot, query_pull = jax.vjp(shape_query, query_pre, gain_query)
    key_rot, key_pull = jax.vjp(shape_key, other_pre, gain_key)
    query_heads = query_rot.astype(bf16)
    other_low = jnp.where(is_key, key_rot[:, 0, :], other_pre).astype(bf16)
    partner_low = seq_swap(other_low, 1).reshape(seq_size // 2, 2, rows, HEAD_DIM)
    partner_low = partner_low[:, ::-1].reshape(length, HEAD_DIM)
    key_single = jnp.where(is_key, other_low, partner_low)
    value_single = jnp.where(is_key, partner_low, other_low)

    raw = (
        jnp.einsum("qhd,kd->qhk", query_heads, key_single, preferred_element_type=f32) * SCALE
    )
    scores = jnp.where(allow[:, None, :], raw, NEGATIVE)
    powers = jnp.exp(scores - jnp.max(scores, axis=-1, keepdims=True))
    prob = powers / jnp.sum(powers, axis=-1, keepdims=True)
    prob_low = prob.astype(bf16)
    attended_low = (
        jnp.einsum("qhk,kd->qhd", prob_low, value_single, preferred_element_type=f32)
        .astype(bf16)
        .reshape(length, per_device * HEAD_DIM)
    )
    attn_pre = seq_sum(matmul_flip(attended_low, w_out), bf16)
    attn_pre, small_table, ffn_join = lax.optimization_barrier((attn_pre, small_table, ffn_join))
    laurel_left = small_table[:, :RANK]
    laurel_right = small_table[:, RANK : 2 * RANK]
    vector_gate_w = small_table[:, 2 * RANK : 2 * RANK + PLD]
    vector_proj_w = small_table[:, 2 * RANK + PLD :]

    attn_normed, attn_pull = jax.vjp(rms_norm, attn_pre, gain_attn)
    first_sum = stream + attn_normed
    left_pre = matmul(normed_low, laurel_left)
    left_low = left_pre.astype(bf16)
    right_pre = matmul_flip(left_low, laurel_right)
    laurel_normed, laurel_pull = jax.vjp(rms_norm, right_pre, gain_laurel)
    second_sum = (first_sum + normed + laurel_normed) * ROOT_HALF
    feed_normed, feed_pull = jax.vjp(rms_norm, second_sum, gain_pre)
    feed_own = feed_normed.astype(bf16)
    feed_low = lax.all_gather(feed_own, "fsdp", axis=0, tiled=True)
    ffn_all, _ = lax.optimization_barrier((ffn_all, feed_own))
    w_both, w_down = fetch(
        [near_all] + ffn_all, ffn_join, ffn_to, my_fsdp, ffn_place, (ffn_first, ffn_each)
    )
    both_pre = matmul(feed_low, w_both)
    ffn_width = w_down.shape[1]
    hidden, hidden_pull = jax.vjp(gelu_product, both_pre[:, :ffn_width], both_pre[:, ffn_width:])
    hidden_low = hidden.astype(bf16)
    down_pre = lax.psum_scatter(
        matmul_flip(hidden_low, w_down).astype(bf16), "fsdp", scatter_dimension=0, tiled=True
    ).astype(f32)
    down_normed, down_pull = jax.vjp(rms_norm, down_pre, gain_post)
    third_sum = second_sum + down_normed
    third_low = third_sum.astype(bf16)
    vector_pre = matmul(third_low, vector_gate_w)
    vector_gated, vector_pull = jax.vjp(lambda inner: gelu_product(inner, vectors), vector_pre)
    vector_low = vector_gated.astype(bf16)
    proj_pre = matmul_flip(vector_low, vector_proj_w)
    proj_normed, proj_pull = jax.vjp(rms_norm, proj_pre, gain_vec)
    result = third_sum + proj_normed
    output = result.astype(bf16)[None]

    grad_out = cotangent[0].astype(f32)
    grad_proj, grad_gain_vec = proj_pull(grad_out)
    proj_grad_low = grad_proj.astype(bf16)
    (grad_vector_pre,) = vector_pull(matmul(proj_grad_low, vector_proj_w))
    vector_grad_low = grad_vector_pre.astype(bf16)
    grad_third = grad_out + matmul_flip(vector_grad_low, vector_gate_w)
    grad_down, grad_gain_post = down_pull(grad_third)
    down_grad_low = lax.all_gather(grad_down.astype(bf16), "fsdp", axis=0, tiled=True)
    grad_gate, grad_up = hidden_pull(matmul(down_grad_low, w_down))
    both_grad_low = jnp.concatenate([grad_gate, grad_up], axis=1).astype(bf16)

    early_full = jnp.concatenate(
        [matmul_outer(third_low, vector_grad_low), matmul_outer(proj_grad_low, vector_low)], axis=1
    )
    small_early = small_sum(split_tiles(early_full, tile).reshape(-1, tile))
    feed_part = matmul_flip(both_grad_low, w_both).astype(bf16)
    feed_part, small_early = lax.optimization_barrier((feed_part, small_early))
    grad_feed = lax.psum_scatter(feed_part, "fsdp", scatter_dimension=0, tiled=True).astype(f32)
    both_grad_w = matmul_outer(feed_low, both_grad_low).astype(bf16)
    down_grad_w = matmul_outer(down_grad_low, hidden_low).astype(bf16)
    ffn_parts = cut_tiles(
        [both_grad_w, down_grad_w],
        [index.reshape(-1) for index in (far_cut[:, :far_half], far_cut[:, far_half:], near_cut)],
    )
    ffn_parts, grad_feed = lax.optimization_barrier((ffn_parts, grad_feed))
    *ffn_sums, near_sum = [
        lax.psum_scatter(value, "seq", scatter_dimension=0, tiled=True) for value in ffn_parts
    ]

    grad_second_norm, grad_gain_pre = feed_pull(grad_feed)
    half_grad = (grad_third + grad_second_norm) * ROOT_HALF
    grad_right, grad_gain_laurel = laurel_pull(half_grad)
    right_grad_low = grad_right.astype(bf16)
    left_grad_low = matmul(right_grad_low, laurel_right).astype(bf16)
    grad_attn, grad_gain_attn = attn_pull(half_grad)
    attn_grad_low = seq_gather(grad_attn.astype(bf16))
    grad_attended = (
        matmul(attn_grad_low, w_out).astype(bf16).reshape(length, per_device, HEAD_DIM)
    )
    out_grad_w = matmul_outer(attn_grad_low, attended_low).astype(bf16)
    value_grad = jnp.einsum("qhk,qhd->kd", prob_low, grad_attended, preferred_element_type=f32)
    grad_prob = jnp.einsum("qhd,kd->qhk", grad_attended, value_single, preferred_element_type=f32)
    inner = jnp.sum(prob * grad_prob, axis=-1, keepdims=True)
    grad_score = (prob * (grad_prob - inner)).astype(bf16)
    grad_query = (
        jnp.einsum("qhk,kd->qhd", grad_score, key_single, preferred_element_type=f32) * SCALE
    ).astype(bf16)
    key_grad = (
        jnp.einsum("qhk,qhd->kd", grad_score, query_heads, preferred_element_type=f32) * SCALE
    ).astype(bf16)
    value_grad = value_grad.astype(bf16)
    partner_grad = seq_swap(jnp.where(is_key, value_grad, key_grad), 1)
    partner_grad = partner_grad.reshape(seq_size // 2, 2, rows, HEAD_DIM)[:, ::-1]
    other_grad = jnp.where(is_key, key_grad, value_grad).astype(f32) + partner_grad.reshape(
        length, HEAD_DIM
    ).astype(f32)
    grad_query_pre, grad_gain_query = query_pull(grad_query.astype(f32))
    grad_key_pre, grad_gain_key = key_pull(other_grad[:, None, :])
    grad_gain_key = jnp.where(is_key, grad_gain_key, 0.0)
    first_grad_low = jnp.concatenate(
        [grad_query_pre, jnp.where(is_key, grad_key_pre, other_grad)], axis=1
    ).astype(bf16)
    first_grad_w = matmul_outer(pack_normed, first_grad_low).astype(bf16)
    near = (my_chip + shifts) % chips
    near_key = take_blocks(attn_key_chip, near)[:, None, :]
    near_order = take_blocks(attn_order_chip, near)[:, None, :]
    near_place = take_blocks(by_chip(attn_place), near)[:, None, :]

    def attn_cut(core):
        return pick(
            (near_key == 2 * my_seq + core)
            & (near_order == jnp.arange(attn_hold)[None, :, None]),
            near_place,
        ).reshape(-1)

    attn_given, attn_own = cut_tiles(
        [first_grad_w, out_grad_w], [attn_cut(1 - my_core), attn_cut(my_core)]
    )
    attn_given, attn_own, ffn_sums[0] = lax.optimization_barrier(
        (attn_given, attn_own, ffn_sums[0])
    )
    attn_parts = added(attn_own, core_swap(attn_given)).reshape(chips, attn_hold, tile, tile)
    attn_sum = attn_parts[0]
    attn_parts = [attn_parts[offset].astype(bf16) for offset in range(1, chips)]
    normed_pre = matmul_flip(first_grad_low, w_first)
    attn_sum, attn_parts, normed_pre = lax.optimization_barrier((attn_sum, attn_parts, normed_pre))
    normed_sum = seq_sum(normed_pre, bf16)
    for offset in range(1, chips):
        attn_sum = attn_sum + chip_shift(attn_parts[offset - 1], offset).astype(f32)
    attn_sum = attn_sum.astype(bf16)
    attn_back = pick(
        (column_slots[3][None, None, :] == (my_seq ^ flips)[:, None, None])
        & (column_slots[0][None, None, :] == my_key)
        & (column_slots[2][None, None, :] == jnp.arange(attn_room)[None, :, None]),
        column_slots[1],
    )

    grad_normed = half_grad + matmul_flip(left_grad_low, laurel_left) + normed_sum
    grad_stream_norm, grad_gain_in = normed_pull(grad_normed)
    input_grad = (half_grad + grad_stream_norm)[None]
    ffn_sums, attn_sum, grad_gain_in, input_grad = lax.optimization_barrier(
        (ffn_sums, attn_sum, grad_gain_in, input_grad)
    )
    ffn_sums = ffn_sums + [core_swap(value) for value in ffn_sums]
    ffn_return = gather_tiles(ffn_sums, [ffn_back[i] for i in range(1, chips)])
    ffn_return, attn_sum, grad_gain_in = lax.optimization_barrier(
        (ffn_return, attn_sum, grad_gain_in)
    )
    ffn_returned = [chip_shift(value, i + 1) for i, value in enumerate(ffn_return)]
    gain_grad = jnp.concatenate(
        [
            grad_gain_in,
            grad_gain_attn,
            grad_gain_laurel,
            grad_gain_pre,
            grad_gain_post,
            grad_gain_vec,
            grad_gain_query,
            grad_gain_key,
        ]
    )
    late_full = jnp.concatenate(
        [matmul_outer(normed_low, left_grad_low), matmul_outer(right_grad_low, left_low)], axis=1
    )
    late = jnp.concatenate(
        [late_full.reshape(seq_size, -1), gain_grad.reshape(seq_size, -1)], axis=1
    ).reshape(seq_size, -1, tile)
    late = seq_sum(late.reshape(-1, tile), bf16, True)

    late = late.astype(bf16)
    late = added(late, core_swap(late)).astype(bf16)
    attn_returned = seq_exchange(gather_tiles([attn_sum], [attn_back[i] for i in range(seq_size)]))
    attn_returned = attn_returned + [core_swap(value) for value in attn_returned]
    slot_grad = jnp.where(my_slots[0] >= 0, my_slots[1], back_size + my_slots[2])

    def slow_return():
        own_ffn = split_tiles(both_grad_w, tile), split_tiles(down_grad_w, tile)
        own_attn = split_tiles(first_grad_w, tile), split_tiles(out_grad_w, tile)
        parts = jnp.concatenate(own_ffn + own_attn + (jnp.zeros((1, tile, tile), bf16),))
        index = jnp.where(
            ffn_to == my_fsdp,
            ffn_place,
            jnp.where(attn_to == my_seq, ffn_count + attn_place, ffn_count + attn_count),
        )
        spread = jnp.concatenate(
            [gather_tiles([parts], [rows_of])[0] for rows_of in index.reshape(8, -1)]
        )
        spread = lax.all_to_all(
            spread.reshape((seq_size * fsdp_size, mine, tile, tile)),
            ("seq", "fsdp"),
            split_axis=0,
            concat_axis=0,
            tiled=True,
        )
        return jnp.sum(spread.astype(f32), axis=0).astype(bf16)

    slow_start = back_size + 2 * seq_size * attn_room
    slow_grads = lax.cond(fits, lambda: jnp.zeros((mine, tile, tile), bf16), slow_return)
    late_parts = [late] + [chip_shift(late, offset) for offset in range(1, chips)]
    ffn_returned, slow_grads, near_sum, late_parts = lax.optimization_barrier(
        (ffn_returned, slow_grads, near_sum, late_parts)
    )
    late = sum(value.astype(f32) for value in late_parts)
    ffn_returned = ffn_returned + [core_swap(value) for value in ffn_returned]
    near_sums = [near_sum, core_swap(near_sum)]
    tile_grads = ffn_returned + near_sums + attn_returned + [slow_grads]
    slot_grad = jnp.where(fits, slot_grad, slow_start + local_slots)

    tile_new, tile_first_new, tile_second_new = rotate_update(
        tile_grads, slot_grad, tile_master, tile_first, tile_second, left_basis, right_basis, RATE_TILE
    )
    late_rows = late_full.shape[0] // seq_size
    late_tiles = late[:late_rows].reshape(-1, 1, tile, tile)
    gain_grad_mine = late[late_rows : late_rows + own_gains.shape[0] // tile].reshape(-1)
    small_grad = jnp.concatenate(
        [
            late_tiles.astype(bf16),
            small_early.reshape(late_tiles.shape[0], -1, tile, tile),
        ],
        axis=1,
    ).reshape(small_master.shape)
    small_new, small_first_new, small_second_new = rotate_update(
        [small_grad],
        jnp.arange(small_master.shape[0]),
        small_master,
        small_first,
        small_second,
        small_left,
        small_right,
        RATE_SMALL,
    )
    gain_first_new = BETA_ONE * gain_first + (1.0 - BETA_ONE) * gain_grad_mine
    gain_second_new = BETA_TWO * gain_second + (1.0 - BETA_TWO) * gain_grad_mine * gain_grad_mine
    correct_one = 1.0 - BETA_ONE**STEP
    correct_two = 1.0 - BETA_TWO**STEP
    gain_new = gains - RATE_GAIN * (gain_first_new / correct_one) / (
        jnp.sqrt(gain_second_new / correct_two) + ADAM_EPS
    )
    return (
        output,
        input_grad,
        tile_new,
        tile_first_new,
        tile_second_new,
        small_new,
        small_first_new,
        small_second_new,
        gain_new,
        gain_first_new,
        gain_second_new,
    )


def solution(mesh):
    return jax.shard_map(
        on_device,
        mesh=mesh,
        in_specs=(
            P("fsdp", "seq", None),
            P("fsdp", "seq", None),
            P("fsdp", None),
            P("fsdp", "seq", None),
            P(),
            P(("seq", "fsdp"), None, None),
            P(("seq", "fsdp"), None, None),
            P(("seq", "fsdp"), None, None),
            P(("seq", "fsdp"), None, None),
            P(("seq", "fsdp"), None, None),
            P("seq", None, None),
            P("seq", None, None),
            P("seq", None, None),
            P("seq", None, None),
            P("seq", None, None),
            P("seq"),
            P("seq"),
            P("seq"),
        ),
        out_specs=(
            P("fsdp", "seq", None),
            P("fsdp", "seq", None),
            P(("seq", "fsdp"), None, None),
            P(("seq", "fsdp"), None, None),
            P(("seq", "fsdp"), None, None),
            P("seq", None, None),
            P("seq", None, None),
            P("seq", None, None),
            P("seq"),
            P("seq"),
            P("seq"),
        ),
        check_vma=False,
    )
```

```python
import math

import jax
import jax.numpy as jnp
from jax import lax
from jax.experimental import pallas as pl
from jax.experimental.pallas import tpu as pltpu
from jax.sharding import PartitionSpec as P

HEADS = 8
KV_HEADS = 2
HEAD_DIM = 256
FF = 8192
RANK = 64
PLD = 256
STEP = 5


EPS = 1e-06
SCALE = 0.0625
THETA = 1000000.0
ROOT_HALF = 0.7071067811865476
BETA_ONE = 0.5
BETA_TWO = 0.5
ADAM_EPS = 1e-08
RATE_TILE = 0.02
RATE_SMALL = 0.04
RATE_GAIN = 0.3
DECAY = 0.01
NEGATIVE = -1e30
TILE = 128
VMEM_BYTES = 4 * 1024 * 1024


def rms_norm(value, gain):
    return value * lax.rsqrt(jnp.mean(value * value, axis=-1, keepdims=True) + EPS) * gain


def rotary(value, position):
    half = value.shape[-1] // 2
    freq = THETA ** (-2.0 * jnp.arange(half).astype(jnp.float32) / value.shape[-1])
    angle = position.astype(jnp.float32)[:, None] * freq[None, :]
    cosine = jnp.cos(angle)[:, None, :]
    sine = jnp.sin(angle)[:, None, :]
    first = value[..., :half]
    second = value[..., half:]
    return jnp.concatenate(
        [first * cosine - second * sine, second * cosine + first * sine], axis=-1
    )


def documents(lengths, length):
    places = jnp.arange(length)
    ends = jnp.cumsum(lengths)
    passed = places[:, None] >= ends[None, :]
    segment = jnp.sum(passed.astype(jnp.int32), axis=1)
    before = jnp.sum(jnp.where(passed, lengths[None, :], 0), axis=1)
    return (segment, places - before)


def matmul(left, right):
    return jnp.dot(left, right, preferred_element_type=jnp.float32)


def matmul_flip(left, right):
    return lax.dot_general(
        left, right, (((1,), (1,)), ((), ())), preferred_element_type=jnp.float32
    )


def matmul_outer(left, right):
    return lax.dot_general(
        left, right, (((0,), (0,)), ((), ())), preferred_element_type=jnp.float32
    )


def assemble(tiles, row_blocks):
    size = tiles.shape[1]
    column_blocks = tiles.shape[0] // row_blocks
    return (
        tiles.reshape(row_blocks, column_blocks, size, size)
        .transpose(0, 2, 1, 3)
        .reshape(row_blocks * size, column_blocks * size)
    )


def split_tiles(matrix, size):
    row_blocks = matrix.shape[0] // size
    column_blocks = matrix.shape[1] // size
    return (
        matrix.reshape(row_blocks, size, column_blocks, size)
        .transpose(0, 2, 1, 3)
        .reshape(row_blocks * column_blocks, size, size)
    )


def gelu_product(first, second):
    return jax.nn.gelu(first, approximate=True) * second


def room(count, share):
    mean = count * share
    return math.ceil(mean + 3.6 * math.sqrt(mean * (1.0 - share)) + 3.0)


def count_earlier(group, valid):
    size = group.shape[-1]
    order = jnp.arange(size)
    same = (group[..., :, None] == group[..., None, :]) & valid[..., None, :]
    same = same & (order[None, :] < order[:, None])
    return jnp.sum(same.astype(jnp.int32), axis=-1)


def count_long(keys):
    groups, size = keys.shape

    def kernel(row_ref, column_ref, out_ref):
        row = row_ref[0]
        column = column_ref[0]
        here = lax.broadcasted_iota(jnp.int32, (size, size), 1)
        other = lax.broadcasted_iota(jnp.int32, (size, size), 0)
        earlier = (column == row) & (other < here)
        out_ref[0] = jnp.sum(earlier.astype(jnp.int32), axis=0, keepdims=True)

    return pl.pallas_call(
        kernel,
        grid=(groups,),
        out_shape=jax.ShapeDtypeStruct((groups, 1, size), jnp.int32),
        in_specs=[
            pl.BlockSpec((1, 1, size), lambda i: (i, 0, 0)),
            pl.BlockSpec((1, size, 1), lambda i: (i, 0, 0)),
        ],
        out_specs=pl.BlockSpec((1, 1, size), lambda i: (i, 0, 0)),
        cost_estimate=pl.CostEstimate(flops=0, transcendentals=0, bytes_accessed=0),
        compiler_params=pltpu.CompilerParams(vmem_limit_bytes=4 * VMEM_BYTES),
    )(keys[:, None, :], keys[:, :, None]).reshape(groups, size)


def pick(match, value):
    return jnp.sum(jnp.where(match, value, 0), axis=-1)


def steps_of(counts):
    for steps in (8, 4, 2):
        if all(count % steps == 0 for count in counts) and sum(counts) // steps >= 24:
            return steps
    return 1


def tile_kernel_call(kernel, index, arrays, out_shape, out_specs, steps):
    moved = sum(math.prod(one.shape) * 2 for one in jax.tree.leaves(out_shape))
    return pl.pallas_call(
        kernel,
        grid=(steps,),
        cost_estimate=pl.CostEstimate(flops=0, transcendentals=0, bytes_accessed=2 * moved),
        out_shape=out_shape,
        in_specs=[pl.BlockSpec(memory_space=pltpu.SMEM)]
        + [pl.BlockSpec(memory_space=pl.ANY)] * len(arrays),
        out_specs=out_specs,
        scratch_shapes=[pltpu.SemaphoreType.DMA],
        compiler_params=pltpu.CompilerParams(vmem_limit_bytes=2 * moved // steps + VMEM_BYTES),
    )(index, *arrays)


def start_copy(sources, place, target, sem, start=0):
    if len(sources) == 1:
        pltpu.make_async_copy(sources[0].at[place - start], target, sem).start()
        return
    half = len(sources) // 2
    middle = start + sum(ref.shape[0] for ref in sources[:half])

    @pl.when(place < middle)
    def _():
        start_copy(sources[:half], place, target, sem, start)

    @pl.when(place >= middle)
    def _():
        start_copy(sources[half:], place, target, sem, middle)


def fill_tiles(arrays, indices, total, start):
    tile = arrays[0].shape[-1] if arrays[0].ndim == 3 else TILE
    counts = [index.shape[0] for index in indices]
    steps = steps_of(counts)

    def kernel(index_ref, *refs):
        sources, outs, sem = refs[: len(arrays)], refs[len(arrays) : -1], refs[-1]
        first = 0
        for out, count in zip(outs, counts):
            each = count // steps
            base = first + pl.program_id(0) * each

            def step(i, carry, out=out, base=base):
                start(sources, index_ref[base + i], out.at[i], sem)
                return carry

            lax.fori_loop(0, each, step, 0)
            first = first + count
        for out in outs:
            pltpu.make_async_copy(out, out, sem).wait()

    return tile_kernel_call(
        kernel,
        jnp.clip(jnp.concatenate(indices), 0, total - 1),
        arrays,
        [jax.ShapeDtypeStruct((count, tile, tile), arrays[0].dtype) for count in counts],
        [pl.BlockSpec((count // steps, tile, tile), lambda i: (i, 0, 0)) for count in counts],
        steps,
    )


def gather_tiles(arrays, indices):
    return fill_tiles(arrays, indices, sum(array.shape[0] for array in arrays), start_copy)


def cut_tiles(matrices, indices):
    row_blocks = matrices[0].shape[0] // TILE
    widths = [matrix.shape[1] // TILE for matrix in matrices]

    def start(sources, place, target, sem):
        first = 0
        for ref, width in zip(sources, widths):
            size = row_blocks * width

            @pl.when((place >= first) & (place < first + size))
            def _(ref=ref, first=first, width=width):
                row = (place - first) // width
                column = place - first - row * width
                source = ref.at[
                    pl.ds(pl.multiple_of(row * TILE, TILE), TILE),
                    pl.ds(pl.multiple_of(column * TILE, TILE), TILE),
                ]
                pltpu.make_async_copy(source, target, sem).start()

            first = first + size

    return fill_tiles(matrices, indices, row_blocks * sum(widths), start)


def join_tiles(arrays, index, row_blocks, columns):
    tile = arrays[0].shape[-1]
    steps = 4
    each = row_blocks // steps

    def kernel(index_ref, *refs):
        sources, outs, sem = refs[: len(arrays)], refs[len(arrays) : -1], refs[-1]
        base = pl.program_id(0) * each
        start = 0
        for out, width in zip(outs, columns):

            def step(i, carry, out=out, start=start, width=width):
                row = i // width
                column = i - row * width
                target = out.at[
                    pl.ds(pl.multiple_of(row * tile, tile), tile),
                    pl.ds(pl.multiple_of(column * tile, tile), tile),
                ]
                start_copy(sources, index_ref[start + base * width + i], target, sem)
                return carry

            lax.fori_loop(0, each * width, step, 0)
            start = start + row_blocks * width
        for out in outs:
            pltpu.make_async_copy(out, out, sem).wait()

    total = sum(array.shape[0] for array in arrays)
    out_shape = tuple(
        jax.ShapeDtypeStruct((row_blocks * tile, width * tile), arrays[0].dtype)
        for width in columns
    )
    out_specs = tuple(pl.BlockSpec((each * tile, width * tile), lambda i: (i, 0)) for width in columns)
    return tile_kernel_call(
        kernel, jnp.clip(index, 0, total - 1), arrays, out_shape, out_specs, steps
    )


def split_low(value):
    high = value.astype(jnp.bfloat16)
    return high, (value - high.astype(jnp.float32)).astype(jnp.bfloat16)


def rotate_update(grads, index, master, first, second, left, right, rate):
    count, tile, _ = master.shape
    each = 4 if count % 4 == 0 else 1
    correct_one = 1.0 - BETA_ONE**STEP
    correct_two = 1.0 - BETA_TWO**STEP

    def product(one, two, dims):
        return lax.dot_general(one, two, (dims, ((), ())), preferred_element_type=jnp.float32)

    def kernel(index_ref, *refs):
        sources, refs = refs[: len(grads)], refs[len(grads) :]
        master_ref, first_ref, second_ref, left_ref, right_ref = refs[:5]
        master_out, first_out, second_out, held, sems = refs[5:]
        now = pl.program_id(0)

        @pl.when(now == 0)
        def _():
            def step(i, carry):
                start_copy(sources, index_ref[i], held.at[i], sems.at[i // each])
                return carry

            lax.fori_loop(0, count, step, 0)

        block = held.at[pl.ds(now * each, each)]
        pltpu.make_async_copy(block, block, sems.at[now]).wait()
        lefts, rights, turns = [], [], []
        for i in range(each):
            grad = held[now * each + i]
            lefts.append(split_low(left_ref[i]))
            rights.append(split_low(right_ref[i]))
            half_turned = product(
                jnp.concatenate([grad, grad], axis=1),
                jnp.concatenate(rights[i], axis=0),
                ((1,), (0,)),
            )
            turns.append(split_low(half_turned))
        for i in range(each):
            (left_high, left_low), (high, low) = lefts[i], turns[i]
            turns[i] = product(
                jnp.concatenate([left_high, left_high, left_low], axis=0),
                jnp.concatenate([high, low, high], axis=0),
                ((0,), (0,)),
            )
        for i in range(each):
            right_high, right_low = rights[i]
            first_new = BETA_ONE * first_ref[i] + (1.0 - BETA_ONE) * turns[i]
            second_new = BETA_TWO * second_ref[i] + (1.0 - BETA_TWO) * turns[i] * turns[i]
            first_out[i] = first_new
            second_out[i] = second_new
            high, low = split_low(
                first_new / correct_one / (jnp.sqrt(second_new / correct_two) + ADAM_EPS)
            )
            half_back = product(
                jnp.concatenate([high, low, high], axis=1),
                jnp.concatenate([right_high, right_high, right_low], axis=1),
                ((1,), (1,)),
            )
            turns[i] = split_low(half_back)
        for i in range(each):
            (left_high, left_low), (high, low) = lefts[i], turns[i]
            back = product(
                jnp.concatenate([left_high, left_high, left_low], axis=1),
                jnp.concatenate([high, low, high], axis=0),
                ((1,), (0,)),
            )
            weight = master_ref[i]
            master_out[i] = weight - rate * (back + DECAY * weight)

    spec = pl.BlockSpec((each, tile, tile), lambda i: (i, 0, 0))
    shape = jax.ShapeDtypeStruct(master.shape, jnp.float32)
    total = sum(array.shape[0] for array in grads)
    return pl.pallas_call(
        kernel,
        grid=(count // each,),
        out_shape=(shape, shape, shape),
        cost_estimate=pl.CostEstimate(
            flops=count * 22 * tile**3, transcendentals=0, bytes_accessed=count * tile**2 * 34
        ),
        in_specs=[pl.BlockSpec(memory_space=pltpu.SMEM)]
        + [pl.BlockSpec(memory_space=pl.ANY)] * len(grads)
        + [spec] * 5,
        out_specs=(spec, spec, spec),
        scratch_shapes=[
            pltpu.VMEM((count, tile, tile), jnp.bfloat16),
            pltpu.SemaphoreType.DMA((count // each,)),
        ],
        compiler_params=pltpu.CompilerParams(vmem_limit_bytes=4 * VMEM_BYTES),
    )(jnp.clip(index, 0, total - 1), *grads, master, first, second, left, right)


def seq_swap(value, flip):
    size = lax.axis_size("seq")
    return lax.ppermute(value, "seq", [(i, i ^ flip) for i in range(size)])


def take_blocks(value, order):
    return jnp.stack(
        [lax.dynamic_index_in_dim(value, order[i], 0, False) for i in range(order.shape[0])]
    )


def core_swap(value):
    size = lax.axis_size("fsdp")
    return lax.ppermute(value, "fsdp", [(i, i ^ 1) for i in range(size)])


def chip_shift(value, offset):
    size = lax.axis_size("fsdp")
    chips = size // 2
    return lax.ppermute(
        value, "fsdp", [(i, (i // 2 + offset) % chips * 2 + i % 2) for i in range(size)]
    )


def seq_gather(value):
    size = lax.axis_size("seq")
    return jnp.concatenate([value] + [seq_swap(value, flip) for flip in range(1, size)], axis=0)


def seq_ordered(value):
    size = lax.axis_size("seq")
    parts = jnp.stack([value] + [seq_swap(value, flip) for flip in range(1, size)], axis=0)
    return take_blocks(parts, lax.axis_index("seq") ^ jnp.arange(size))


def seq_exchange(values):
    return [values[0]] + [seq_swap(values[flip], flip) for flip in range(1, len(values))]


def seq_sum(value, wire, ordered=False):
    size = lax.axis_size("seq")
    parts = value.reshape((size, value.shape[0] // size) + value.shape[1:])
    if ordered:
        parts = take_blocks(parts, lax.axis_index("seq") ^ jnp.arange(size))
    total = parts[0]
    for flip in range(1, size):
        total = total + seq_swap(parts[flip].astype(wire), flip).astype(jnp.float32)
    return total


def chip_exchange(values):
    return [values[0]] + [chip_shift(values[offset], offset) for offset in range(1, len(values))]


def core_pair(value):
    other = core_swap(value)
    even = lax.axis_index("fsdp") % 2 == 0
    return jnp.where(even, jnp.stack([value, other]), jnp.stack([other, value]))


def small_sum(value):
    seq_size = lax.axis_size("seq")
    chips = lax.axis_size("fsdp") // 2
    chip = lax.axis_index("fsdp") // 2
    even = lax.axis_index("fsdp") % 2 == 0
    low = value.astype(jnp.bfloat16)
    parts = low.reshape((seq_size, 2, low.shape[0] // (2 * seq_size)) + low.shape[1:])
    kept = jnp.where(even, parts[:, 0], parts[:, 1]).astype(jnp.float32)
    given = jnp.where(even, parts[:, 1], parts[:, 0])
    kept = kept + core_swap(given).astype(jnp.float32)
    kept = seq_sum(kept.reshape((-1,) + low.shape[1:]), jnp.bfloat16, True)
    kept = kept.reshape((chips, kept.shape[0] // chips) + kept.shape[1:])
    kept = take_blocks(kept, (chip + jnp.arange(chips)) % chips)
    total = kept[0]
    for offset in range(1, chips):
        total = total + chip_shift(kept[offset].astype(jnp.bfloat16), offset).astype(jnp.float32)
    total = total.astype(jnp.bfloat16)
    parts = jnp.stack([total] + [chip_shift(total, offset) for offset in range(1, chips)])
    parts = take_blocks(parts, (chip - jnp.arange(chips)) % chips)
    return core_pair(parts).reshape((value.shape[0] // seq_size,) + value.shape[1:])


def turn(value, cosine, sine):
    half = value.shape[-1] // 2
    first, second = value[..., :half], value[..., half:]
    return jnp.concatenate(
        [first * cosine - second * sine, second * cosine + first * sine], axis=-1
    )


def added(one, two):
    return one.astype(jnp.float32) + two.astype(jnp.float32)


def on_device(
    tokens,
    layer_vectors,
    doc_lengths,
    cotangent,
    tile_owner,
    tile_master,
    tile_first,
    tile_second,
    left_basis,
    right_basis,
    small_master,
    small_first,
    small_second,
    small_left,
    small_right,
    gains,
    gain_first,
    gain_second,
):
    bf16 = jnp.bfloat16
    f32 = jnp.float32
    tile = tile_master.shape[1]
    width = tokens.shape[2]
    row_blocks = width // tile
    rows = tokens.shape[1]
    seq_size = lax.axis_size("seq")
    fsdp_size = lax.axis_size("fsdp")
    chips = fsdp_size // 2
    mine = tile_master.shape[0]
    tiles = tile_owner.shape[0]
    length = rows * seq_size
    per_device = HEADS // seq_size
    per_key = seq_size // KV_HEADS
    query_width = HEADS * HEAD_DIM
    key_width = KV_HEADS * HEAD_DIM
    my_seq = lax.axis_index("seq")
    my_fsdp = lax.axis_index("fsdp")
    my_chip = my_fsdp // 2
    my_core = my_fsdp % 2
    flips = jnp.arange(seq_size)
    shifts = jnp.arange(chips)

    query_blocks = query_width // tile
    key_blocks = key_width // tile
    ffn_blocks = FF // tile
    query_each = query_blocks // seq_size
    head_blocks = HEAD_DIM // tile
    ffn_each = ffn_blocks // fsdp_size
    columns = tiles // row_blocks
    attn_first = query_each + head_blocks
    attn_count = row_blocks * (attn_first + query_each)
    ffn_first = 2 * ffn_each
    ffn_count = row_blocks * 3 * ffn_each
    attn_share = (2 * query_blocks + 2 * key_blocks) / columns
    ffn_share = 3 * ffn_blocks / columns
    attn_room = (room(2 * mine, attn_share / seq_size) + 1) // 2
    attn_hold = (room(attn_count, 1.0 / chips) + 1) // 2 + 1
    ffn_room = (room(2 * mine, ffn_share / chips) + 1) // 2
    both_count = row_blocks * ffn_first
    near_hold = (room(2 * mine, ffn_share / fsdp_size) + 3) // 4 * 4
    far_hold = (room(ffn_count * (1.0 - 1.0 / chips), 1.0 / seq_size) + 3) // 4 * 4
    far_half = far_hold * 3 // 7 // 4 * 4
    far_rest = far_hold - far_half

    def tile_places(owner):
        row = owner // columns
        column = owner % columns
        key_at = column - query_blocks
        value_at = key_at - key_blocks
        out_at = value_at - key_blocks
        ffn_at = out_at - query_blocks
        is_attn = ffn_at < 0
        kind = ffn_at // ffn_blocks
        ffn_column = ffn_at % ffn_blocks
        ffn_to = jnp.where(is_attn, -1, ffn_column // ffn_each)
        ffn_local = ffn_column % ffn_each
        ffn_place = jnp.where(
            kind == 2,
            both_count + row * ffn_each + ffn_local,
            row * ffn_first + kind * ffn_each + ffn_local,
        )
        attn_to = jnp.where(
            key_at < 0,
            column // query_each,
            jnp.where(
                value_at < 0,
                key_at // head_blocks * per_key,
                jnp.where(
                    out_at < 0,
                    value_at // head_blocks * per_key + per_key - 1,
                    out_at // query_each,
                ),
            ),
        )
        attn_place = jnp.where(
            key_at < 0,
            row * attn_first + column % query_each,
            jnp.where(
                out_at < 0,
                row * attn_first + query_each + key_at % head_blocks,
                row_blocks * attn_first + row * query_each + out_at % query_each,
            ),
        )
        attn_to = jnp.where(is_attn, attn_to, -1)
        return (ffn_to, ffn_place, attn_to, attn_place)

    owners = tile_owner.reshape(seq_size, fsdp_size, mine)
    slot_seq = jnp.arange(seq_size)[:, None, None]
    slot_fsdp = jnp.arange(fsdp_size)[None, :, None]
    slot_chip = slot_fsdp // 2
    local_slots = jnp.arange(mine)
    both_slots = jnp.arange(2 * mine)
    both_slots = jnp.where(
        both_slots // mine == my_core, both_slots % mine, mine + both_slots % mine
    )

    ffn_to = tile_places(owners)[0]
    ffn_chip = jnp.where(ffn_to < 0, -1, ffn_to // 2)
    chip_view = ffn_chip.reshape(seq_size, chips, 2 * mine)
    chip_rank = count_earlier(chip_view, chip_view >= 0).reshape(owners.shape)
    near_view = jnp.where(slot_chip == ffn_chip, ffn_to, -1).reshape(chip_view.shape)
    near_rank = count_earlier(near_view, near_view >= 0).reshape(owners.shape)
    ffn_slots = lax.dynamic_slice(
        jnp.stack([ffn_chip, chip_rank, near_view.reshape(owners.shape), near_rank]),
        (0, my_seq, 2 * my_chip, 0),
        (4, 1, 2, mine),
    ).reshape(4, 1, 1, 2 * mine)
    near_keep = pick(
        (ffn_slots[2][0] == my_fsdp) & (ffn_slots[3][0] == jnp.arange(near_hold)[:, None]),
        both_slots,
    )
    ffn_pack = pick(
        (ffn_slots[0] == ((my_chip + shifts) % chips)[:, None, None])
        & (ffn_slots[1] == (my_core * ffn_room + jnp.arange(ffn_room))[None, :, None]),
        both_slots,
    )
    master_low = tile_master.astype(bf16)
    masters = [master_low, core_swap(master_low)]
    *ffn_sent, near_kept = gather_tiles(
        masters, [ffn_pack[i] for i in range(1, chips)] + [near_keep]
    )
    small_rows = small_master.shape[0] // 2
    small_half = lax.dynamic_slice_in_dim(small_master, my_core * small_rows, small_rows)
    masters, ffn_sent, near_kept, chip_rank, near_rank, owners, own_tokens, own_gains, small_half = (
        lax.optimization_barrier(
            (
                masters,
                ffn_sent,
                near_kept,
                chip_rank,
                near_rank,
                owners,
                tokens[0],
                gains.astype(bf16),
                small_half.astype(bf16),
            )
        )
    )
    ffn_got = [chip_shift(value, i + 1) for i, value in enumerate(ffn_sent)]
    near_all = lax.all_gather(near_kept, "seq", axis=0, tiled=True)

    ffn_to, ffn_place, attn_to, attn_place = tile_places(owners)
    ffn_chip = jnp.where(ffn_to < 0, -1, ffn_to // 2)
    attn_view = attn_to.reshape(seq_size, chips, 2 * mine)
    attn_rank = count_earlier(attn_view, attn_view >= 0).reshape(owners.shape)
    attn_core = (attn_rank + slot_seq) % 2
    attn_rank = attn_rank // 2
    attn_key = jnp.where(attn_to < 0, -1, 2 * attn_to + attn_core)

    chip_slots = lax.dynamic_slice(
        jnp.stack([attn_key, attn_rank]), (0, my_seq, 2 * my_chip, 0), (2, 1, 2, mine)
    ).reshape(2, 1, 1, 2 * mine)
    attn_message = attn_room + row_blocks * rows // tile + small_rows + -(-own_gains.shape[0] // tile**2)
    attn_pack = pick(
        (chip_slots[0] == (2 * (my_seq ^ flips) + my_core)[:, None, None])
        & (chip_slots[1] == jnp.arange(attn_room)[None, :, None]),
        both_slots,
    )
    attn_sent = gather_tiles(masters, [attn_pack[i] for i in range(seq_size)])
    is_near = slot_chip == ffn_chip
    near_key = jnp.where(is_near, ffn_to, -1)
    far_key = jnp.where(is_near, -1, ffn_to)
    far_rank = count_long(far_key.reshape(seq_size, fsdp_size * mine)).reshape(owners.shape)
    def by_chip(value):
        value = value.reshape(seq_size, chips, 2 * mine).transpose(1, 0, 2)
        return value.reshape(chips, seq_size * 2 * mine)

    attn_key_chip = by_chip(attn_key)
    attn_order_chip = count_long(attn_key_chip)
    attn_order = (
        attn_order_chip.reshape(chips, seq_size, 2 * mine).transpose(1, 0, 2).reshape(owners.shape)
    )
    fits = jnp.all(
        jnp.where(
            ffn_to < 0,
            (attn_rank < attn_room) & (attn_order < attn_hold),
            jnp.where(
                is_near, near_rank < near_hold, (chip_rank < 2 * ffn_room) & (far_rank < far_hold)
            ),
        )
    )
    rank_core = chip_rank // ffn_room
    rank_local = chip_rank % ffn_room
    out_place = (
        jnp.where(rank_core == my_core, 0, (chips - 1) * ffn_room)
        + ((my_chip - slot_chip) % chips - 1) * ffn_room
        + rank_local
    )
    near_start = 2 * (chips - 1) * ffn_room
    back_size = near_start + 2 * near_hold
    back_place = jnp.where(
        is_near,
        near_start + jnp.where(ffn_to == my_fsdp, 0, near_hold) + near_rank,
        jnp.where(rank_core == my_core, 0, (chips - 1) * ffn_room)
        + ((my_chip - ffn_chip) % chips - 1) * ffn_room
        + rank_local,
    )
    attn_back_place = (
        jnp.where(attn_core == my_core, 0, seq_size * attn_room)
        + (attn_to ^ my_seq) * attn_room
        + attn_rank
    )
    my_slots = lax.dynamic_slice(
        jnp.stack([ffn_to, back_place, attn_back_place]), (0, my_seq, my_fsdp, 0), (3, 1, 1, mine)
    ).reshape(3, mine)
    seq_slots = lax.dynamic_slice(
        jnp.stack(
            [
                far_key,
                far_rank,
                ffn_chip,
                out_place,
                chip_rank,
                jnp.broadcast_to(slot_chip, owners.shape),
            ]
        ),
        (0, my_seq, 0, 0),
        (6, 1, fsdp_size, mine),
    ).reshape(6, fsdp_size * mine)
    column_slots = lax.dynamic_slice(
        jnp.stack([attn_key, attn_order, attn_rank, jnp.broadcast_to(slot_seq, owners.shape)]),
        (0, 0, 2 * my_chip, 0),
        (4, seq_size, 2, mine),
    ).reshape(4, 2 * seq_size * mine)
    my_key = 2 * my_seq + my_core

    attn_keep = pick(
        (column_slots[0][None, :] == my_key)
        & (column_slots[1][None, :] == jnp.arange(attn_hold)[:, None]),
        jnp.where(
            column_slots[3] == my_seq,
            0,
            attn_room + ((column_slots[3] ^ my_seq) - 1) * attn_message,
        )
        + column_slots[2],
    )
    attn_join = pick(
        (attn_to.reshape(1, -1) == my_seq)
        & (attn_place.reshape(1, -1) == jnp.arange(attn_count)[:, None]),
        (
            jnp.where(attn_core == my_core, 0, chips * attn_hold)
            + (my_chip - slot_chip) % chips * attn_hold
            + attn_order
        ).reshape(1, -1),
    )
    ffn_keep = pick(
        (seq_slots[0][None, :] == my_fsdp) & (seq_slots[1][None, :] == jnp.arange(far_hold)[:, None]),
        seq_slots[3][None, :],
    )
    ffn_join = pick(
        (ffn_to.reshape(1, -1) == my_fsdp)
        & (ffn_place.reshape(1, -1) == jnp.arange(ffn_count)[:, None]),
        jnp.where(
            is_near,
            slot_seq * near_hold + near_rank,
            seq_size * near_hold
            + jnp.where(
                far_rank < far_half,
                slot_seq * far_half + far_rank,
                seq_size * far_half + slot_seq * far_rest + far_rank - far_half,
            ),
        ).reshape(1, -1),
    )

    def cut_index(key, rank, hold):
        return pick(
            (key.reshape(seq_size, 1, -1) == my_fsdp)
            & (rank.reshape(seq_size, 1, -1) == jnp.arange(hold)[None, :, None]),
            ffn_place.reshape(seq_size, 1, -1),
        )

    far_cut = cut_index(far_key, far_rank, far_hold)
    near_cut = cut_index(near_key, near_rank, near_hold)
    ffn_back = pick(
        (seq_slots[5][None, None, :] == ((my_chip + shifts) % chips)[:, None, None])
        & (seq_slots[2][None, None, :] == my_chip)
        & (seq_slots[4][None, None, :] == (my_core * ffn_room + jnp.arange(ffn_room))[None, :, None]),
        jnp.where(seq_slots[0] == my_fsdp, 0, far_hold) + seq_slots[1],
    )

    token_tiles = own_tokens.reshape(rows, row_blocks, tile).transpose(1, 0, 2)
    token_tiles = token_tiles.reshape(-1, tile, tile)
    gain_rows = own_gains.reshape(-1, tile)
    gain_tiles = jnp.pad(gain_rows, ((0, -gain_rows.shape[0] % tile), (0, 0))).reshape(-1, tile, tile)
    common = jnp.concatenate([token_tiles, small_half, gain_tiles])
    attn_got = [attn_sent[0]] + [
        seq_swap(jnp.concatenate([attn_sent[flip], common]), flip) for flip in range(1, seq_size)
    ]
    segment, position = documents(doc_lengths[0], length)
    places = ((my_seq ^ flips)[:, None] * rows + jnp.arange(rows)[None, :]).reshape(-1)

    def reorder(values):
        blocks = values.reshape(seq_size, rows)
        return jnp.concatenate(
            [lax.dynamic_index_in_dim(blocks, my_seq ^ i, 0, False) for i in range(seq_size)]
        )

    pack_segment = reorder(segment)
    allow = (pack_segment[:, None] == pack_segment[None, :]) & (
        places[None, :] <= places[:, None]
    )
    turns = jnp.arange(HEAD_DIM // 2).astype(f32)
    angle = reorder(position).astype(f32)[:, None] * (THETA ** (-2.0 * turns / HEAD_DIM))[None, :]
    cosine, sine = jnp.cos(angle)[:, None, :], jnp.sin(angle)[:, None, :]
    parts = [common] + [value[attn_room:] for value in attn_got[1:]]
    token_end = token_tiles.shape[0]
    small_end = token_end + small_rows

    def seq_order(value):
        return take_blocks(value, my_seq ^ flips)

    pack_tokens = jnp.concatenate(
        [
            part[:token_end].reshape(row_blocks, rows, tile).transpose(1, 0, 2).reshape(rows, width)
            for part in parts
        ]
    )
    gain_full = seq_order(
        jnp.stack([part[small_end:].reshape(-1, tile)[: gain_rows.shape[0]] for part in parts])
    )
    gain_full = gain_full.reshape(-1).astype(f32)
    gain_in = gain_full[0:width]
    pack_normed = rms_norm(pack_tokens.astype(f32), gain_in).astype(bf16)
    ready = (allow, cosine, sine, ffn_keep, attn_keep, pack_normed, gain_full)
    ffn_got, attn_got, parts, ready, near_all = lax.optimization_barrier(
        (ffn_got, attn_got, parts, ready, near_all)
    )
    allow, cosine, sine, ffn_keep, attn_keep, pack_normed, gain_full = ready
    gain_in = gain_full[0:width]
    small_got = core_pair(seq_order(jnp.stack([part[token_end:small_end] for part in parts])))
    small_got = small_got.transpose(1, 0, 2, 3, 4)
    small_table = assemble(small_got.reshape((-1,) + small_master.shape[1:]), row_blocks)
    (attn_kept,) = gather_tiles(attn_got, [attn_keep])
    ffn_got = ffn_got + [core_swap(value) for value in ffn_got]
    ffn_kept = gather_tiles(ffn_got, [ffn_keep[:far_half], ffn_keep[far_half:]])
    ffn_kept, attn_kept = lax.optimization_barrier((ffn_kept, attn_kept))
    ffn_all = [lax.all_gather(value, "seq", axis=0, tiled=True) for value in ffn_kept]
    attn_all = [attn_kept] + [chip_shift(attn_kept, offset) for offset in range(1, chips)]
    attn_all = attn_all + [core_swap(value) for value in attn_all]

    attn_all, ffn_all[0], attn_join = lax.optimization_barrier((attn_all, ffn_all[0], attn_join))

    def fetch(arrays, index, to, me, place, columns_of):
        def fast():
            return join_tiles(arrays, index, row_blocks, columns_of)

        def slow():
            whole = lax.all_to_all(
                jnp.broadcast_to(master_low[None], (seq_size * fsdp_size,) + master_low.shape),
                ("seq", "fsdp"),
                split_axis=0,
                concat_axis=0,
                tiled=True,
            ).reshape(-1, tile, tile)
            count = row_blocks * sum(columns_of)
            slots = pick(
                (to.reshape(1, -1) == me) & (place.reshape(1, -1) == jnp.arange(count)[:, None]),
                jnp.arange(tiles)[None, :],
            )
            return join_tiles([whole], slots, row_blocks, columns_of)

        return lax.cond(fits, fast, slow)

    w_first, w_out = fetch(
        attn_all, attn_join, attn_to, my_seq, attn_place, (attn_first, query_each)
    )
    gain_attn = gain_full[width : 2 * width]
    gain_laurel = gain_full[2 * width : 3 * width]
    gain_pre = gain_full[3 * width : 4 * width]
    gain_post = gain_full[4 * width : 5 * width]
    gain_vec = gain_full[5 * width : 6 * width]
    gain_query = gain_full[6 * width : 6 * width + HEAD_DIM]
    gain_key = gain_full[6 * width + HEAD_DIM : 6 * width + 2 * HEAD_DIM]
    stream = own_tokens.astype(f32)
    vectors = layer_vectors[0].astype(f32)
    normed, normed_pull = jax.vjp(rms_norm, stream, gain_in)
    normed_low = normed.astype(bf16)
    first_pre = matmul(pack_normed, w_first)
    is_key = my_seq % per_key == 0

    def shape_query(query_in, query_gain):
        value = rms_norm(query_in.reshape(length, per_device, HEAD_DIM), query_gain)
        return turn(value, cosine, sine)

    def shape_key(key_in, key_gain):
        return turn(rms_norm(key_in.reshape(length, 1, HEAD_DIM), key_gain), cosine, sine)

    query_pre = first_pre[:, : per_device * HEAD_DIM]
    other_pre = first_pre[:, per_device * HEAD_DIM :]
    query_rot, query_pull = jax.vjp(shape_query, query_pre, gain_query)
    key_rot, key_pull = jax.vjp(shape_key, other_pre, gain_key)
    query_heads = query_rot.astype(bf16)
    other_low = jnp.where(is_key, key_rot[:, 0, :], other_pre).astype(bf16)
    partner_low = seq_swap(other_low, 1).reshape(seq_size // 2, 2, rows, HEAD_DIM)
    partner_low = partner_low[:, ::-1].reshape(length, HEAD_DIM)
    key_single = jnp.where(is_key, other_low, partner_low)
    value_single = jnp.where(is_key, partner_low, other_low)

    raw = (
        jnp.einsum("qhd,kd->qhk", query_heads, key_single, preferred_element_type=f32) * SCALE
    )
    scores = jnp.where(allow[:, None, :], raw, NEGATIVE)
    powers = jnp.exp(scores - jnp.max(scores, axis=-1, keepdims=True))
    prob = powers / jnp.sum(powers, axis=-1, keepdims=True)
    prob_low = prob.astype(bf16)
    attended_low = (
        jnp.einsum("qhk,kd->qhd", prob_low, value_single, preferred_element_type=f32)
        .astype(bf16)
        .reshape(length, per_device * HEAD_DIM)
    )
    attn_pre = seq_sum(matmul_flip(attended_low, w_out), bf16)
    attn_pre, small_table, ffn_join = lax.optimization_barrier((attn_pre, small_table, ffn_join))
    laurel_left = small_table[:, :RANK]
    laurel_right = small_table[:, RANK : 2 * RANK]
    vector_gate_w = small_table[:, 2 * RANK : 2 * RANK + PLD]
    vector_proj_w = small_table[:, 2 * RANK + PLD :]

    attn_normed, attn_pull = jax.vjp(rms_norm, attn_pre, gain_attn)
    first_sum = stream + attn_normed
    left_pre = matmul(normed_low, laurel_left)
    left_low = left_pre.astype(bf16)
    right_pre = matmul_flip(left_low, laurel_right)
    laurel_normed, laurel_pull = jax.vjp(rms_norm, right_pre, gain_laurel)
    second_sum = (first_sum + normed + laurel_normed) * ROOT_HALF
    feed_normed, feed_pull = jax.vjp(rms_norm, second_sum, gain_pre)
    feed_own = feed_normed.astype(bf16)
    feed_low = lax.all_gather(feed_own, "fsdp", axis=0, tiled=True)
    ffn_all, _ = lax.optimization_barrier((ffn_all, feed_own))
    w_both, w_down = fetch(
        [near_all] + ffn_all, ffn_join, ffn_to, my_fsdp, ffn_place, (ffn_first, ffn_each)
    )
    both_pre = matmul(feed_low, w_both)
    ffn_width = w_down.shape[1]
    hidden, hidden_pull = jax.vjp(gelu_product, both_pre[:, :ffn_width], both_pre[:, ffn_width:])
    hidden_low = hidden.astype(bf16)
    down_pre = lax.psum_scatter(
        matmul_flip(hidden_low, w_down).astype(bf16), "fsdp", scatter_dimension=0, tiled=True
    ).astype(f32)
    down_normed, down_pull = jax.vjp(rms_norm, down_pre, gain_post)
    third_sum = second_sum + down_normed
    third_low = third_sum.astype(bf16)
    vector_pre = matmul(third_low, vector_gate_w)
    vector_gated, vector_pull = jax.vjp(lambda inner: gelu_product(inner, vectors), vector_pre)
    vector_low = vector_gated.astype(bf16)
    proj_pre = matmul_flip(vector_low, vector_proj_w)
    proj_normed, proj_pull = jax.vjp(rms_norm, proj_pre, gain_vec)
    result = third_sum + proj_normed
    output = result.astype(bf16)[None]

    grad_out = cotangent[0].astype(f32)
    grad_proj, grad_gain_vec = proj_pull(grad_out)
    proj_grad_low = grad_proj.astype(bf16)
    (grad_vector_pre,) = vector_pull(matmul(proj_grad_low, vector_proj_w))
    vector_grad_low = grad_vector_pre.astype(bf16)
    grad_third = grad_out + matmul_flip(vector_grad_low, vector_gate_w)
    grad_down, grad_gain_post = down_pull(grad_third)
    down_grad_low = lax.all_gather(grad_down.astype(bf16), "fsdp", axis=0, tiled=True)
    grad_gate, grad_up = hidden_pull(matmul(down_grad_low, w_down))
    both_grad_low = jnp.concatenate([grad_gate, grad_up], axis=1).astype(bf16)

    early_full = jnp.concatenate(
        [matmul_outer(third_low, vector_grad_low), matmul_outer(proj_grad_low, vector_low)], axis=1
    )
    small_early = small_sum(split_tiles(early_full, tile).reshape(-1, tile))
    feed_part = matmul_flip(both_grad_low, w_both).astype(bf16)
    feed_part, small_early = lax.optimization_barrier((feed_part, small_early))
    grad_feed = lax.psum_scatter(feed_part, "fsdp", scatter_dimension=0, tiled=True).astype(f32)
    both_grad_w = matmul_outer(feed_low, both_grad_low).astype(bf16)
    down_grad_w = matmul_outer(down_grad_low, hidden_low).astype(bf16)
    ffn_parts = cut_tiles(
        [both_grad_w, down_grad_w],
        [index.reshape(-1) for index in (far_cut[:, :far_half], far_cut[:, far_half:], near_cut)],
    )
    ffn_parts, grad_feed = lax.optimization_barrier((ffn_parts, grad_feed))
    *ffn_sums, near_sum = [
        lax.psum_scatter(value, "seq", scatter_dimension=0, tiled=True) for value in ffn_parts
    ]

    grad_second_norm, grad_gain_pre = feed_pull(grad_feed)
    half_grad = (grad_third + grad_second_norm) * ROOT_HALF
    grad_right, grad_gain_laurel = laurel_pull(half_grad)
    right_grad_low = grad_right.astype(bf16)
    left_grad_low = matmul(right_grad_low, laurel_right).astype(bf16)
    grad_attn, grad_gain_attn = attn_pull(half_grad)
    attn_grad_low = seq_gather(grad_attn.astype(bf16))
    grad_attended = (
        matmul(attn_grad_low, w_out).astype(bf16).reshape(length, per_device, HEAD_DIM)
    )
    out_grad_w = matmul_outer(attn_grad_low, attended_low).astype(bf16)
    value_grad = jnp.einsum("qhk,qhd->kd", prob_low, grad_attended, preferred_element_type=f32)
    grad_prob = jnp.einsum("qhd,kd->qhk", grad_attended, value_single, preferred_element_type=f32)
    inner = jnp.sum(prob * grad_prob, axis=-1, keepdims=True)
    grad_score = (prob * (grad_prob - inner)).astype(bf16)
    grad_query = (
        jnp.einsum("qhk,kd->qhd", grad_score, key_single, preferred_element_type=f32) * SCALE
    ).astype(bf16)
    key_grad = (
        jnp.einsum("qhk,qhd->kd", grad_score, query_heads, preferred_element_type=f32) * SCALE
    ).astype(bf16)
    value_grad = value_grad.astype(bf16)
    partner_grad = seq_swap(jnp.where(is_key, value_grad, key_grad), 1)
    partner_grad = partner_grad.reshape(seq_size // 2, 2, rows, HEAD_DIM)[:, ::-1]
    other_grad = jnp.where(is_key, key_grad, value_grad).astype(f32) + partner_grad.reshape(
        length, HEAD_DIM
    ).astype(f32)
    grad_query_pre, grad_gain_query = query_pull(grad_query.astype(f32))
    grad_key_pre, grad_gain_key = key_pull(other_grad[:, None, :])
    grad_gain_key = jnp.where(is_key, grad_gain_key, 0.0)
    first_grad_low = jnp.concatenate(
        [grad_query_pre, jnp.where(is_key, grad_key_pre, other_grad)], axis=1
    ).astype(bf16)
    first_grad_w = matmul_outer(pack_normed, first_grad_low).astype(bf16)
    near = (my_chip + shifts) % chips
    near_key = take_blocks(attn_key_chip, near)[:, None, :]
    near_order = take_blocks(attn_order_chip, near)[:, None, :]
    near_place = take_blocks(by_chip(attn_place), near)[:, None, :]

    def attn_cut(core):
        return pick(
            (near_key == 2 * my_seq + core)
            & (near_order == jnp.arange(attn_hold)[None, :, None]),
            near_place,
        ).reshape(-1)

    attn_given, attn_own = cut_tiles(
        [first_grad_w, out_grad_w], [attn_cut(1 - my_core), attn_cut(my_core)]
    )
    attn_given, attn_own, ffn_sums[0] = lax.optimization_barrier(
        (attn_given, attn_own, ffn_sums[0])
    )
    attn_parts = added(attn_own, core_swap(attn_given)).reshape(chips, attn_hold, tile, tile)
    attn_sum = attn_parts[0]
    attn_parts = [attn_parts[offset].astype(bf16) for offset in range(1, chips)]
    normed_pre = matmul_flip(first_grad_low, w_first)
    attn_sum, attn_parts, normed_pre = lax.optimization_barrier((attn_sum, attn_parts, normed_pre))
    normed_sum = seq_sum(normed_pre, bf16)
    for offset in range(1, chips):
        attn_sum = attn_sum + chip_shift(attn_parts[offset - 1], offset).astype(f32)
    attn_sum = attn_sum.astype(bf16)
    attn_back = pick(
        (column_slots[3][None, None, :] == (my_seq ^ flips)[:, None, None])
        & (column_slots[0][None, None, :] == my_key)
        & (column_slots[2][None, None, :] == jnp.arange(attn_room)[None, :, None]),
        column_slots[1],
    )

    grad_normed = half_grad + matmul_flip(left_grad_low, laurel_left) + normed_sum
    grad_stream_norm, grad_gain_in = normed_pull(grad_normed)
    input_grad = (half_grad + grad_stream_norm)[None]
    ffn_sums, attn_sum, grad_gain_in, input_grad = lax.optimization_barrier(
        (ffn_sums, attn_sum, grad_gain_in, input_grad)
    )
    ffn_sums = ffn_sums + [core_swap(value) for value in ffn_sums]
    ffn_return = gather_tiles(ffn_sums, [ffn_back[i] for i in range(1, chips)])
    ffn_return, attn_sum, grad_gain_in = lax.optimization_barrier(
        (ffn_return, attn_sum, grad_gain_in)
    )
    ffn_returned = [chip_shift(value, i + 1) for i, value in enumerate(ffn_return)]
    gain_grad = jnp.concatenate(
        [
            grad_gain_in,
            grad_gain_attn,
            grad_gain_laurel,
            grad_gain_pre,
            grad_gain_post,
            grad_gain_vec,
            grad_gain_query,
            grad_gain_key,
        ]
    )
    late_full = jnp.concatenate(
        [matmul_outer(normed_low, left_grad_low), matmul_outer(right_grad_low, left_low)], axis=1
    )
    late = jnp.concatenate(
        [late_full.reshape(seq_size, -1), gain_grad.reshape(seq_size, -1)], axis=1
    ).reshape(seq_size, -1, tile)
    late = seq_sum(late.reshape(-1, tile), bf16, True)

    late = late.astype(bf16)
    late = added(late, core_swap(late)).astype(bf16)
    attn_returned = seq_exchange(gather_tiles([attn_sum], [attn_back[i] for i in range(seq_size)]))
    attn_returned = attn_returned + [core_swap(value) for value in attn_returned]
    slot_grad = jnp.where(my_slots[0] >= 0, my_slots[1], back_size + my_slots[2])

    def slow_return():
        own_ffn = split_tiles(both_grad_w, tile), split_tiles(down_grad_w, tile)
        own_attn = split_tiles(first_grad_w, tile), split_tiles(out_grad_w, tile)
        parts = jnp.concatenate(own_ffn + own_attn + (jnp.zeros((1, tile, tile), bf16),))
        index = jnp.where(
            ffn_to == my_fsdp,
            ffn_place,
            jnp.where(attn_to == my_seq, ffn_count + attn_place, ffn_count + attn_count),
        )
        spread = jnp.concatenate(
            [gather_tiles([parts], [rows_of])[0] for rows_of in index.reshape(8, -1)]
        )
        spread = lax.all_to_all(
            spread.reshape((seq_size * fsdp_size, mine, tile, tile)),
            ("seq", "fsdp"),
            split_axis=0,
            concat_axis=0,
            tiled=True,
        )
        return jnp.sum(spread.astype(f32), axis=0).astype(bf16)

    slow_start = back_size + 2 * seq_size * attn_room
    slow_grads = lax.cond(fits, lambda: jnp.zeros((mine, tile, tile), bf16), slow_return)
    ffn_returned, slow_grads, near_sum, late = lax.optimization_barrier(
        (ffn_returned, slow_grads, near_sum, late)
    )
    late_parts = [late] + [chip_shift(late, offset) for offset in range(1, chips)]
    ffn_returned = ffn_returned + [core_swap(value) for value in ffn_returned]
    near_sums = [near_sum, core_swap(near_sum)]
    tile_grads = ffn_returned + near_sums + attn_returned + [slow_grads]
    slot_grad = jnp.where(fits, slot_grad, slow_start + local_slots)

    tile_new, tile_first_new, tile_second_new = rotate_update(
        tile_grads, slot_grad, tile_master, tile_first, tile_second, left_basis, right_basis, RATE_TILE
    )
    late_parts, tile_new, tile_first_new, tile_second_new = lax.optimization_barrier(
        (late_parts, tile_new, tile_first_new, tile_second_new)
    )
    late = sum(value.astype(f32) for value in late_parts)
    late_rows = late_full.shape[0] // seq_size
    late_tiles = late[:late_rows].reshape(-1, 1, tile, tile)
    gain_grad_mine = late[late_rows : late_rows + own_gains.shape[0] // tile].reshape(-1)
    small_grad = jnp.concatenate(
        [
            late_tiles.astype(bf16),
            small_early.reshape(late_tiles.shape[0], -1, tile, tile),
        ],
        axis=1,
    ).reshape(small_master.shape)
    small_new, small_first_new, small_second_new = rotate_update(
        [small_grad],
        jnp.arange(small_master.shape[0]),
        small_master,
        small_first,
        small_second,
        small_left,
        small_right,
        RATE_SMALL,
    )
    gain_first_new = BETA_ONE * gain_first + (1.0 - BETA_ONE) * gain_grad_mine
    gain_second_new = BETA_TWO * gain_second + (1.0 - BETA_TWO) * gain_grad_mine * gain_grad_mine
    correct_one = 1.0 - BETA_ONE**STEP
    correct_two = 1.0 - BETA_TWO**STEP
    gain_new = gains - RATE_GAIN * (gain_first_new / correct_one) / (
        jnp.sqrt(gain_second_new / correct_two) + ADAM_EPS
    )
    return (
        output,
        input_grad,
        tile_new,
        tile_first_new,
        tile_second_new,
        small_new,
        small_first_new,
        small_second_new,
        gain_new,
        gain_first_new,
        gain_second_new,
    )


def solution(mesh):
    return jax.shard_map(
        on_device,
        mesh=mesh,
        in_specs=(
            P("fsdp", "seq", None),
            P("fsdp", "seq", None),
            P("fsdp", None),
            P("fsdp", "seq", None),
            P(),
            P(("seq", "fsdp"), None, None),
            P(("seq", "fsdp"), None, None),
            P(("seq", "fsdp"), None, None),
            P(("seq", "fsdp"), None, None),
            P(("seq", "fsdp"), None, None),
            P("seq", None, None),
            P("seq", None, None),
            P("seq", None, None),
            P("seq", None, None),
            P("seq", None, None),
            P("seq"),
            P("seq"),
            P("seq"),
        ),
        out_specs=(
            P("fsdp", "seq", None),
            P("fsdp", "seq", None),
            P(("seq", "fsdp"), None, None),
            P(("seq", "fsdp"), None, None),
            P(("seq", "fsdp"), None, None),
            P("seq", None, None),
            P("seq", None, None),
            P("seq", None, None),
            P("seq"),
            P("seq"),
            P("seq"),
        ),
        check_vma=False,
    )
```

```python
import math

import jax
import jax.numpy as jnp
from jax import lax
from jax.experimental import pallas as pl
from jax.experimental.pallas import tpu as pltpu
from jax.sharding import PartitionSpec as P

HEADS = 8
KV_HEADS = 2
HEAD_DIM = 256
FF = 8192
RANK = 64
PLD = 256
STEP = 5


EPS = 1e-06
SCALE = 0.0625
THETA = 1000000.0
ROOT_HALF = 0.7071067811865476
BETA_ONE = 0.5
BETA_TWO = 0.5
ADAM_EPS = 1e-08
RATE_TILE = 0.02
RATE_SMALL = 0.04
RATE_GAIN = 0.3
DECAY = 0.01
NEGATIVE = -1e30
TILE = 128
VMEM_BYTES = 4 * 1024 * 1024


def rms_norm(value, gain):
    return value * lax.rsqrt(jnp.mean(value * value, axis=-1, keepdims=True) + EPS) * gain


def rotary(value, position):
    half = value.shape[-1] // 2
    freq = THETA ** (-2.0 * jnp.arange(half).astype(jnp.float32) / value.shape[-1])
    angle = position.astype(jnp.float32)[:, None] * freq[None, :]
    cosine = jnp.cos(angle)[:, None, :]
    sine = jnp.sin(angle)[:, None, :]
    first = value[..., :half]
    second = value[..., half:]
    return jnp.concatenate(
        [first * cosine - second * sine, second * cosine + first * sine], axis=-1
    )


def documents(lengths, length):
    places = jnp.arange(length)
    ends = jnp.cumsum(lengths)
    passed = places[:, None] >= ends[None, :]
    segment = jnp.sum(passed.astype(jnp.int32), axis=1)
    before = jnp.sum(jnp.where(passed, lengths[None, :], 0), axis=1)
    return (segment, places - before)


def matmul(left, right):
    return jnp.dot(left, right, preferred_element_type=jnp.float32)


def matmul_flip(left, right):
    return lax.dot_general(
        left, right, (((1,), (1,)), ((), ())), preferred_element_type=jnp.float32
    )


def matmul_outer(left, right):
    return lax.dot_general(
        left, right, (((0,), (0,)), ((), ())), preferred_element_type=jnp.float32
    )


def assemble(tiles, row_blocks):
    size = tiles.shape[1]
    column_blocks = tiles.shape[0] // row_blocks
    return (
        tiles.reshape(row_blocks, column_blocks, size, size)
        .transpose(0, 2, 1, 3)
        .reshape(row_blocks * size, column_blocks * size)
    )


def split_tiles(matrix, size):
    row_blocks = matrix.shape[0] // size
    column_blocks = matrix.shape[1] // size
    return (
        matrix.reshape(row_blocks, size, column_blocks, size)
        .transpose(0, 2, 1, 3)
        .reshape(row_blocks * column_blocks, size, size)
    )


def gelu_product(first, second):
    return jax.nn.gelu(first, approximate=True) * second


def room(count, share):
    mean = count * share
    return math.ceil(mean + 3.6 * math.sqrt(mean * (1.0 - share)) + 3.0)


def count_earlier(group, valid):
    size = group.shape[-1]
    order = jnp.arange(size)
    same = (group[..., :, None] == group[..., None, :]) & valid[..., None, :]
    same = same & (order[None, :] < order[:, None])
    return jnp.sum(same.astype(jnp.int32), axis=-1)


def count_long(keys):
    groups, size = keys.shape

    def kernel(row_ref, column_ref, out_ref):
        row = row_ref[0]
        column = column_ref[0]
        here = lax.broadcasted_iota(jnp.int32, (size, size), 1)
        other = lax.broadcasted_iota(jnp.int32, (size, size), 0)
        earlier = (column == row) & (other < here)
        out_ref[0] = jnp.sum(earlier.astype(jnp.int32), axis=0, keepdims=True)

    return pl.pallas_call(
        kernel,
        grid=(groups,),
        out_shape=jax.ShapeDtypeStruct((groups, 1, size), jnp.int32),
        in_specs=[
            pl.BlockSpec((1, 1, size), lambda i: (i, 0, 0)),
            pl.BlockSpec((1, size, 1), lambda i: (i, 0, 0)),
        ],
        out_specs=pl.BlockSpec((1, 1, size), lambda i: (i, 0, 0)),
        cost_estimate=pl.CostEstimate(flops=0, transcendentals=0, bytes_accessed=0),
        compiler_params=pltpu.CompilerParams(vmem_limit_bytes=4 * VMEM_BYTES),
    )(keys[:, None, :], keys[:, :, None]).reshape(groups, size)


def pick(match, value):
    return jnp.sum(jnp.where(match, value, 0), axis=-1)


def steps_of(counts):
    for steps in (8, 4, 2):
        if all(count % steps == 0 for count in counts) and sum(counts) // steps >= 24:
            return steps
    return 1


def tile_kernel_call(kernel, index, arrays, out_shape, out_specs, steps):
    moved = sum(math.prod(one.shape) * 2 for one in jax.tree.leaves(out_shape))
    return pl.pallas_call(
        kernel,
        grid=(steps,),
        cost_estimate=pl.CostEstimate(flops=0, transcendentals=0, bytes_accessed=2 * moved),
        out_shape=out_shape,
        in_specs=[pl.BlockSpec(memory_space=pltpu.SMEM)]
        + [pl.BlockSpec(memory_space=pl.ANY)] * len(arrays),
        out_specs=out_specs,
        scratch_shapes=[pltpu.SemaphoreType.DMA],
        compiler_params=pltpu.CompilerParams(vmem_limit_bytes=2 * moved // steps + VMEM_BYTES),
    )(index, *arrays)


def start_copy(sources, place, target, sem, start=0):
    if len(sources) == 1:
        pltpu.make_async_copy(sources[0].at[place - start], target, sem).start()
        return
    half = len(sources) // 2
    middle = start + sum(ref.shape[0] for ref in sources[:half])

    @pl.when(place < middle)
    def _():
        start_copy(sources[:half], place, target, sem, start)

    @pl.when(place >= middle)
    def _():
        start_copy(sources[half:], place, target, sem, middle)


def fill_tiles(arrays, indices, total, start):
    tile = arrays[0].shape[-1] if arrays[0].ndim == 3 else TILE
    counts = [index.shape[0] for index in indices]
    steps = steps_of(counts)

    def kernel(index_ref, *refs):
        sources, outs, sem = refs[: len(arrays)], refs[len(arrays) : -1], refs[-1]
        first = 0
        for out, count in zip(outs, counts):
            each = count // steps
            base = first + pl.program_id(0) * each

            def step(i, carry, out=out, base=base):
                start(sources, index_ref[base + i], out.at[i], sem)
                return carry

            lax.fori_loop(0, each, step, 0)
            first = first + count
        for out in outs:
            pltpu.make_async_copy(out, out, sem).wait()

    return tile_kernel_call(
        kernel,
        jnp.clip(jnp.concatenate(indices), 0, total - 1),
        arrays,
        [jax.ShapeDtypeStruct((count, tile, tile), arrays[0].dtype) for count in counts],
        [pl.BlockSpec((count // steps, tile, tile), lambda i: (i, 0, 0)) for count in counts],
        steps,
    )


def gather_tiles(arrays, indices):
    return fill_tiles(arrays, indices, sum(array.shape[0] for array in arrays), start_copy)


def cut_tiles(matrices, indices):
    row_blocks = matrices[0].shape[0] // TILE
    widths = [matrix.shape[1] // TILE for matrix in matrices]

    def start(sources, place, target, sem):
        first = 0
        for ref, width in zip(sources, widths):
            size = row_blocks * width

            @pl.when((place >= first) & (place < first + size))
            def _(ref=ref, first=first, width=width):
                row = (place - first) // width
                column = place - first - row * width
                source = ref.at[
                    pl.ds(pl.multiple_of(row * TILE, TILE), TILE),
                    pl.ds(pl.multiple_of(column * TILE, TILE), TILE),
                ]
                pltpu.make_async_copy(source, target, sem).start()

            first = first + size

    return fill_tiles(matrices, indices, row_blocks * sum(widths), start)


def join_tiles(arrays, index, row_blocks, columns):
    tile = arrays[0].shape[-1]
    steps = 4
    each = row_blocks // steps

    def kernel(index_ref, *refs):
        sources, outs, sem = refs[: len(arrays)], refs[len(arrays) : -1], refs[-1]
        base = pl.program_id(0) * each
        start = 0
        for out, width in zip(outs, columns):

            def step(i, carry, out=out, start=start, width=width):
                row = i // width
                column = i - row * width
                target = out.at[
                    pl.ds(pl.multiple_of(row * tile, tile), tile),
                    pl.ds(pl.multiple_of(column * tile, tile), tile),
                ]
                start_copy(sources, index_ref[start + base * width + i], target, sem)
                return carry

            lax.fori_loop(0, each * width, step, 0)
            start = start + row_blocks * width
        for out in outs:
            pltpu.make_async_copy(out, out, sem).wait()

    total = sum(array.shape[0] for array in arrays)
    out_shape = tuple(
        jax.ShapeDtypeStruct((row_blocks * tile, width * tile), arrays[0].dtype)
        for width in columns
    )
    out_specs = tuple(pl.BlockSpec((each * tile, width * tile), lambda i: (i, 0)) for width in columns)
    return tile_kernel_call(
        kernel, jnp.clip(index, 0, total - 1), arrays, out_shape, out_specs, steps
    )


def split_low(value):
    high = value.astype(jnp.bfloat16)
    return high, (value - high.astype(jnp.float32)).astype(jnp.bfloat16)


def rotate_update(grads, index, master, first, second, left, right, rate):
    count, tile, _ = master.shape
    each = 4 if count % 4 == 0 else 1
    correct_one = 1.0 - BETA_ONE**STEP
    correct_two = 1.0 - BETA_TWO**STEP

    def product(one, two, dims):
        return lax.dot_general(one, two, (dims, ((), ())), preferred_element_type=jnp.float32)

    def kernel(index_ref, *refs):
        sources, refs = refs[: len(grads)], refs[len(grads) :]
        master_ref, first_ref, second_ref, left_ref, right_ref = refs[:5]
        master_out, first_out, second_out, held, sems = refs[5:]
        now = pl.program_id(0)

        @pl.when(now == 0)
        def _():
            def step(i, carry):
                start_copy(sources, index_ref[i], held.at[i], sems.at[i // each])
                return carry

            lax.fori_loop(0, count, step, 0)

        block = held.at[pl.ds(now * each, each)]
        pltpu.make_async_copy(block, block, sems.at[now]).wait()
        lefts, rights, turns = [], [], []
        for i in range(each):
            grad = held[now * each + i]
            lefts.append(split_low(left_ref[i]))
            rights.append(split_low(right_ref[i]))
            half_turned = product(
                jnp.concatenate([grad, grad], axis=1),
                jnp.concatenate(rights[i], axis=0),
                ((1,), (0,)),
            )
            turns.append(split_low(half_turned))
        for i in range(each):
            (left_high, left_low), (high, low) = lefts[i], turns[i]
            turns[i] = product(
                jnp.concatenate([left_high, left_high, left_low], axis=0),
                jnp.concatenate([high, low, high], axis=0),
                ((0,), (0,)),
            )
        for i in range(each):
            right_high, right_low = rights[i]
            first_new = BETA_ONE * first_ref[i] + (1.0 - BETA_ONE) * turns[i]
            second_new = BETA_TWO * second_ref[i] + (1.0 - BETA_TWO) * turns[i] * turns[i]
            first_out[i] = first_new
            second_out[i] = second_new
            high, low = split_low(
                first_new / correct_one / (jnp.sqrt(second_new / correct_two) + ADAM_EPS)
            )
            half_back = product(
                jnp.concatenate([high, low, high], axis=1),
                jnp.concatenate([right_high, right_high, right_low], axis=1),
                ((1,), (1,)),
            )
            turns[i] = split_low(half_back)
        for i in range(each):
            (left_high, left_low), (high, low) = lefts[i], turns[i]
            back = product(
                jnp.concatenate([left_high, left_high, left_low], axis=1),
                jnp.concatenate([high, low, high], axis=0),
                ((1,), (0,)),
            )
            weight = master_ref[i]
            master_out[i] = weight - rate * (back + DECAY * weight)

    spec = pl.BlockSpec((each, tile, tile), lambda i: (i, 0, 0))
    shape = jax.ShapeDtypeStruct(master.shape, jnp.float32)
    total = sum(array.shape[0] for array in grads)
    return pl.pallas_call(
        kernel,
        grid=(count // each,),
        out_shape=(shape, shape, shape),
        cost_estimate=pl.CostEstimate(
            flops=count * 22 * tile**3, transcendentals=0, bytes_accessed=count * tile**2 * 34
        ),
        in_specs=[pl.BlockSpec(memory_space=pltpu.SMEM)]
        + [pl.BlockSpec(memory_space=pl.ANY)] * len(grads)
        + [spec] * 5,
        out_specs=(spec, spec, spec),
        scratch_shapes=[
            pltpu.VMEM((count, tile, tile), jnp.bfloat16),
            pltpu.SemaphoreType.DMA((count // each,)),
        ],
        compiler_params=pltpu.CompilerParams(vmem_limit_bytes=(4 if count < 64 else 10) * VMEM_BYTES),
    )(jnp.clip(index, 0, total - 1), *grads, master, first, second, left, right)


def seq_swap(value, flip):
    size = lax.axis_size("seq")
    return lax.ppermute(value, "seq", [(i, i ^ flip) for i in range(size)])


def take_blocks(value, order):
    return jnp.stack(
        [lax.dynamic_index_in_dim(value, order[i], 0, False) for i in range(order.shape[0])]
    )


def core_swap(value):
    size = lax.axis_size("fsdp")
    return lax.ppermute(value, "fsdp", [(i, i ^ 1) for i in range(size)])


def chip_shift(value, offset):
    size = lax.axis_size("fsdp")
    chips = size // 2
    return lax.ppermute(
        value, "fsdp", [(i, (i // 2 + offset) % chips * 2 + i % 2) for i in range(size)]
    )


def seq_gather(value):
    size = lax.axis_size("seq")
    return jnp.concatenate([value] + [seq_swap(value, flip) for flip in range(1, size)], axis=0)


def seq_ordered(value):
    size = lax.axis_size("seq")
    parts = jnp.stack([value] + [seq_swap(value, flip) for flip in range(1, size)], axis=0)
    return take_blocks(parts, lax.axis_index("seq") ^ jnp.arange(size))


def seq_exchange(values):
    return [values[0]] + [seq_swap(values[flip], flip) for flip in range(1, len(values))]


def seq_sum(value, wire, ordered=False):
    size = lax.axis_size("seq")
    parts = value.reshape((size, value.shape[0] // size) + value.shape[1:])
    if ordered:
        parts = take_blocks(parts, lax.axis_index("seq") ^ jnp.arange(size))
    total = parts[0]
    for flip in range(1, size):
        total = total + seq_swap(parts[flip].astype(wire), flip).astype(jnp.float32)
    return total


def chip_exchange(values):
    return [values[0]] + [chip_shift(values[offset], offset) for offset in range(1, len(values))]


def core_pair(value):
    other = core_swap(value)
    even = lax.axis_index("fsdp") % 2 == 0
    return jnp.where(even, jnp.stack([value, other]), jnp.stack([other, value]))


def small_sum(value):
    seq_size = lax.axis_size("seq")
    chips = lax.axis_size("fsdp") // 2
    chip = lax.axis_index("fsdp") // 2
    even = lax.axis_index("fsdp") % 2 == 0
    low = value.astype(jnp.bfloat16)
    parts = low.reshape((seq_size, 2, low.shape[0] // (2 * seq_size)) + low.shape[1:])
    kept = jnp.where(even, parts[:, 0], parts[:, 1]).astype(jnp.float32)
    given = jnp.where(even, parts[:, 1], parts[:, 0])
    kept = kept + core_swap(given).astype(jnp.float32)
    kept = seq_sum(kept.reshape((-1,) + low.shape[1:]), jnp.bfloat16, True)
    kept = kept.reshape((chips, kept.shape[0] // chips) + kept.shape[1:])
    kept = take_blocks(kept, (chip + jnp.arange(chips)) % chips)
    total = kept[0]
    for offset in range(1, chips):
        total = total + chip_shift(kept[offset].astype(jnp.bfloat16), offset).astype(jnp.float32)
    total = total.astype(jnp.bfloat16)
    parts = jnp.stack([total] + [chip_shift(total, offset) for offset in range(1, chips)])
    parts = take_blocks(parts, (chip - jnp.arange(chips)) % chips)
    return core_pair(parts).reshape((value.shape[0] // seq_size,) + value.shape[1:])


def turn(value, cosine, sine):
    half = value.shape[-1] // 2
    first, second = value[..., :half], value[..., half:]
    return jnp.concatenate(
        [first * cosine - second * sine, second * cosine + first * sine], axis=-1
    )


def added(one, two):
    return one.astype(jnp.float32) + two.astype(jnp.float32)


def on_device(
    tokens,
    layer_vectors,
    doc_lengths,
    cotangent,
    tile_owner,
    tile_master,
    tile_first,
    tile_second,
    left_basis,
    right_basis,
    small_master,
    small_first,
    small_second,
    small_left,
    small_right,
    gains,
    gain_first,
    gain_second,
):
    bf16 = jnp.bfloat16
    f32 = jnp.float32
    tile = tile_master.shape[1]
    width = tokens.shape[2]
    row_blocks = width // tile
    rows = tokens.shape[1]
    seq_size = lax.axis_size("seq")
    fsdp_size = lax.axis_size("fsdp")
    chips = fsdp_size // 2
    mine = tile_master.shape[0]
    tiles = tile_owner.shape[0]
    length = rows * seq_size
    per_device = HEADS // seq_size
    per_key = seq_size // KV_HEADS
    query_width = HEADS * HEAD_DIM
    key_width = KV_HEADS * HEAD_DIM
    my_seq = lax.axis_index("seq")
    my_fsdp = lax.axis_index("fsdp")
    my_chip = my_fsdp // 2
    my_core = my_fsdp % 2
    flips = jnp.arange(seq_size)
    shifts = jnp.arange(chips)

    query_blocks = query_width // tile
    key_blocks = key_width // tile
    ffn_blocks = FF // tile
    query_each = query_blocks // seq_size
    head_blocks = HEAD_DIM // tile
    ffn_each = ffn_blocks // fsdp_size
    columns = tiles // row_blocks
    attn_first = query_each + head_blocks
    attn_count = row_blocks * (attn_first + query_each)
    ffn_first = 2 * ffn_each
    ffn_count = row_blocks * 3 * ffn_each
    attn_share = (2 * query_blocks + 2 * key_blocks) / columns
    ffn_share = 3 * ffn_blocks / columns
    attn_room = (room(2 * mine, attn_share / seq_size) + 1) // 2
    attn_hold = (room(attn_count, 1.0 / chips) + 1) // 2 + 1
    ffn_room = (room(2 * mine, ffn_share / chips) + 1) // 2
    both_count = row_blocks * ffn_first
    near_hold = (room(2 * mine, ffn_share / fsdp_size) + 3) // 4 * 4
    far_hold = (room(ffn_count * (1.0 - 1.0 / chips), 1.0 / seq_size) + 3) // 4 * 4
    far_half = far_hold * 3 // 7 // 4 * 4
    far_rest = far_hold - far_half

    def tile_places(owner):
        row = owner // columns
        column = owner % columns
        key_at = column - query_blocks
        value_at = key_at - key_blocks
        out_at = value_at - key_blocks
        ffn_at = out_at - query_blocks
        is_attn = ffn_at < 0
        kind = ffn_at // ffn_blocks
        ffn_column = ffn_at % ffn_blocks
        ffn_to = jnp.where(is_attn, -1, ffn_column // ffn_each)
        ffn_local = ffn_column % ffn_each
        ffn_place = jnp.where(
            kind == 2,
            both_count + row * ffn_each + ffn_local,
            row * ffn_first + kind * ffn_each + ffn_local,
        )
        attn_to = jnp.where(
            key_at < 0,
            column // query_each,
            jnp.where(
                value_at < 0,
                key_at // head_blocks * per_key,
                jnp.where(
                    out_at < 0,
                    value_at // head_blocks * per_key + per_key - 1,
                    out_at // query_each,
                ),
            ),
        )
        attn_place = jnp.where(
            key_at < 0,
            row * attn_first + column % query_each,
            jnp.where(
                out_at < 0,
                row * attn_first + query_each + key_at % head_blocks,
                row_blocks * attn_first + row * query_each + out_at % query_each,
            ),
        )
        attn_to = jnp.where(is_attn, attn_to, -1)
        return (ffn_to, ffn_place, attn_to, attn_place)

    owners = tile_owner.reshape(seq_size, fsdp_size, mine)
    slot_seq = jnp.arange(seq_size)[:, None, None]
    slot_fsdp = jnp.arange(fsdp_size)[None, :, None]
    slot_chip = slot_fsdp // 2
    local_slots = jnp.arange(mine)
    both_slots = jnp.arange(2 * mine)
    both_slots = jnp.where(
        both_slots // mine == my_core, both_slots % mine, mine + both_slots % mine
    )

    ffn_to = tile_places(owners)[0]
    ffn_chip = jnp.where(ffn_to < 0, -1, ffn_to // 2)
    chip_view = ffn_chip.reshape(seq_size, chips, 2 * mine)
    chip_rank = count_earlier(chip_view, chip_view >= 0).reshape(owners.shape)
    near_view = jnp.where(slot_chip == ffn_chip, ffn_to, -1).reshape(chip_view.shape)
    near_rank = count_earlier(near_view, near_view >= 0).reshape(owners.shape)
    ffn_slots = lax.dynamic_slice(
        jnp.stack([ffn_chip, chip_rank, near_view.reshape(owners.shape), near_rank]),
        (0, my_seq, 2 * my_chip, 0),
        (4, 1, 2, mine),
    ).reshape(4, 1, 1, 2 * mine)
    near_keep = pick(
        (ffn_slots[2][0] == my_fsdp) & (ffn_slots[3][0] == jnp.arange(near_hold)[:, None]),
        both_slots,
    )
    ffn_pack = pick(
        (ffn_slots[0] == ((my_chip + shifts) % chips)[:, None, None])
        & (ffn_slots[1] == (my_core * ffn_room + jnp.arange(ffn_room))[None, :, None]),
        both_slots,
    )
    master_low = tile_master.astype(bf16)
    masters = [master_low, core_swap(master_low)]
    *ffn_sent, near_kept = gather_tiles(
        masters, [ffn_pack[i] for i in range(1, chips)] + [near_keep]
    )
    small_rows = small_master.shape[0] // 2
    small_half = lax.dynamic_slice_in_dim(small_master, my_core * small_rows, small_rows)
    masters, ffn_sent, near_kept, chip_rank, near_rank, owners, own_tokens, own_gains, small_half = (
        lax.optimization_barrier(
            (
                masters,
                ffn_sent,
                near_kept,
                chip_rank,
                near_rank,
                owners,
                tokens[0],
                gains.astype(bf16),
                small_half.astype(bf16),
            )
        )
    )
    ffn_got = [chip_shift(value, i + 1) for i, value in enumerate(ffn_sent)]
    near_all = lax.all_gather(near_kept, "seq", axis=0, tiled=True)

    ffn_to, ffn_place, attn_to, attn_place = tile_places(owners)
    ffn_chip = jnp.where(ffn_to < 0, -1, ffn_to // 2)
    attn_view = attn_to.reshape(seq_size, chips, 2 * mine)
    attn_rank = count_earlier(attn_view, attn_view >= 0).reshape(owners.shape)
    attn_core = (attn_rank + slot_seq) % 2
    attn_rank = attn_rank // 2
    attn_key = jnp.where(attn_to < 0, -1, 2 * attn_to + attn_core)

    chip_slots = lax.dynamic_slice(
        jnp.stack([attn_key, attn_rank]), (0, my_seq, 2 * my_chip, 0), (2, 1, 2, mine)
    ).reshape(2, 1, 1, 2 * mine)
    attn_message = attn_room + row_blocks * rows // tile + small_rows + -(-own_gains.shape[0] // tile**2)
    attn_pack = pick(
        (chip_slots[0] == (2 * (my_seq ^ flips) + my_core)[:, None, None])
        & (chip_slots[1] == jnp.arange(attn_room)[None, :, None]),
        both_slots,
    )
    attn_sent = gather_tiles(masters, [attn_pack[i] for i in range(seq_size)])
    is_near = slot_chip == ffn_chip
    near_key = jnp.where(is_near, ffn_to, -1)
    far_key = jnp.where(is_near, -1, ffn_to)
    far_rank = count_long(far_key.reshape(seq_size, fsdp_size * mine)).reshape(owners.shape)
    def by_chip(value):
        value = value.reshape(seq_size, chips, 2 * mine).transpose(1, 0, 2)
        return value.reshape(chips, seq_size * 2 * mine)

    attn_key_chip = by_chip(attn_key)
    attn_order_chip = count_long(attn_key_chip)
    attn_order = (
        attn_order_chip.reshape(chips, seq_size, 2 * mine).transpose(1, 0, 2).reshape(owners.shape)
    )
    fits = jnp.all(
        jnp.where(
            ffn_to < 0,
            (attn_rank < attn_room) & (attn_order < attn_hold),
            jnp.where(
                is_near, near_rank < near_hold, (chip_rank < 2 * ffn_room) & (far_rank < far_hold)
            ),
        )
    )
    rank_core = chip_rank // ffn_room
    rank_local = chip_rank % ffn_room
    out_place = (
        jnp.where(rank_core == my_core, 0, (chips - 1) * ffn_room)
        + ((my_chip - slot_chip) % chips - 1) * ffn_room
        + rank_local
    )
    near_start = 2 * (chips - 1) * ffn_room
    back_size = near_start + 2 * near_hold
    back_place = jnp.where(
        is_near,
        near_start + jnp.where(ffn_to == my_fsdp, 0, near_hold) + near_rank,
        jnp.where(rank_core == my_core, 0, (chips - 1) * ffn_room)
        + ((my_chip - ffn_chip) % chips - 1) * ffn_room
        + rank_local,
    )
    attn_back_place = (
        jnp.where(attn_core == my_core, 0, seq_size * attn_room)
        + (attn_to ^ my_seq) * attn_room
        + attn_rank
    )
    my_slots = lax.dynamic_slice(
        jnp.stack([ffn_to, back_place, attn_back_place]), (0, my_seq, my_fsdp, 0), (3, 1, 1, mine)
    ).reshape(3, mine)
    seq_slots = lax.dynamic_slice(
        jnp.stack(
            [
                far_key,
                far_rank,
                ffn_chip,
                out_place,
                chip_rank,
                jnp.broadcast_to(slot_chip, owners.shape),
            ]
        ),
        (0, my_seq, 0, 0),
        (6, 1, fsdp_size, mine),
    ).reshape(6, fsdp_size * mine)
    column_slots = lax.dynamic_slice(
        jnp.stack([attn_key, attn_order, attn_rank, jnp.broadcast_to(slot_seq, owners.shape)]),
        (0, 0, 2 * my_chip, 0),
        (4, seq_size, 2, mine),
    ).reshape(4, 2 * seq_size * mine)
    my_key = 2 * my_seq + my_core

    attn_keep = pick(
        (column_slots[0][None, :] == my_key)
        & (column_slots[1][None, :] == jnp.arange(attn_hold)[:, None]),
        jnp.where(
            column_slots[3] == my_seq,
            0,
            attn_room + ((column_slots[3] ^ my_seq) - 1) * attn_message,
        )
        + column_slots[2],
    )
    attn_join = pick(
        (attn_to.reshape(1, -1) == my_seq)
        & (attn_place.reshape(1, -1) == jnp.arange(attn_count)[:, None]),
        (
            jnp.where(attn_core == my_core, 0, chips * attn_hold)
            + (my_chip - slot_chip) % chips * attn_hold
            + attn_order
        ).reshape(1, -1),
    )
    ffn_keep = pick(
        (seq_slots[0][None, :] == my_fsdp) & (seq_slots[1][None, :] == jnp.arange(far_hold)[:, None]),
        seq_slots[3][None, :],
    )
    ffn_join = pick(
        (ffn_to.reshape(1, -1) == my_fsdp)
        & (ffn_place.reshape(1, -1) == jnp.arange(ffn_count)[:, None]),
        jnp.where(
            is_near,
            slot_seq * near_hold + near_rank,
            seq_size * near_hold
            + jnp.where(
                far_rank < far_half,
                slot_seq * far_half + far_rank,
                seq_size * far_half + slot_seq * far_rest + far_rank - far_half,
            ),
        ).reshape(1, -1),
    )

    def cut_index(key, rank, hold):
        return pick(
            (key.reshape(seq_size, 1, -1) == my_fsdp)
            & (rank.reshape(seq_size, 1, -1) == jnp.arange(hold)[None, :, None]),
            ffn_place.reshape(seq_size, 1, -1),
        )

    far_cut = cut_index(far_key, far_rank, far_hold)
    near_cut = cut_index(near_key, near_rank, near_hold)
    ffn_back = pick(
        (seq_slots[5][None, None, :] == ((my_chip + shifts) % chips)[:, None, None])
        & (seq_slots[2][None, None, :] == my_chip)
        & (seq_slots[4][None, None, :] == (my_core * ffn_room + jnp.arange(ffn_room))[None, :, None]),
        jnp.where(seq_slots[0] == my_fsdp, 0, far_hold) + seq_slots[1],
    )

    token_tiles = own_tokens.reshape(rows, row_blocks, tile).transpose(1, 0, 2)
    token_tiles = token_tiles.reshape(-1, tile, tile)
    gain_rows = own_gains.reshape(-1, tile)
    gain_tiles = jnp.pad(gain_rows, ((0, -gain_rows.shape[0] % tile), (0, 0))).reshape(-1, tile, tile)
    common = jnp.concatenate([token_tiles, small_half, gain_tiles])
    attn_got = [attn_sent[0]] + [
        seq_swap(jnp.concatenate([attn_sent[flip], common]), flip) for flip in range(1, seq_size)
    ]
    segment, position = documents(doc_lengths[0], length)
    places = ((my_seq ^ flips)[:, None] * rows + jnp.arange(rows)[None, :]).reshape(-1)

    def reorder(values):
        blocks = values.reshape(seq_size, rows)
        return jnp.concatenate(
            [lax.dynamic_index_in_dim(blocks, my_seq ^ i, 0, False) for i in range(seq_size)]
        )

    pack_segment = reorder(segment)
    allow = (pack_segment[:, None] == pack_segment[None, :]) & (
        places[None, :] <= places[:, None]
    )
    turns = jnp.arange(HEAD_DIM // 2).astype(f32)
    angle = reorder(position).astype(f32)[:, None] * (THETA ** (-2.0 * turns / HEAD_DIM))[None, :]
    cosine, sine = jnp.cos(angle)[:, None, :], jnp.sin(angle)[:, None, :]
    parts = [common] + [value[attn_room:] for value in attn_got[1:]]
    token_end = token_tiles.shape[0]
    small_end = token_end + small_rows

    def seq_order(value):
        return take_blocks(value, my_seq ^ flips)

    pack_tokens = jnp.concatenate(
        [
            part[:token_end].reshape(row_blocks, rows, tile).transpose(1, 0, 2).reshape(rows, width)
            for part in parts
        ]
    )
    gain_full = seq_order(
        jnp.stack([part[small_end:].reshape(-1, tile)[: gain_rows.shape[0]] for part in parts])
    )
    gain_full = gain_full.reshape(-1).astype(f32)
    gain_in = gain_full[0:width]
    pack_normed = rms_norm(pack_tokens.astype(f32), gain_in).astype(bf16)
    ready = (allow, cosine, sine, ffn_keep, attn_keep, pack_normed, gain_full)
    ffn_got, attn_got, parts, ready, near_all = lax.optimization_barrier(
        (ffn_got, attn_got, parts, ready, near_all)
    )
    allow, cosine, sine, ffn_keep, attn_keep, pack_normed, gain_full = ready
    gain_in = gain_full[0:width]
    small_got = core_pair(seq_order(jnp.stack([part[token_end:small_end] for part in parts])))
    small_got = small_got.transpose(1, 0, 2, 3, 4)
    small_table = assemble(small_got.reshape((-1,) + small_master.shape[1:]), row_blocks)
    (attn_kept,) = gather_tiles(attn_got, [attn_keep])
    ffn_got = ffn_got + [core_swap(value) for value in ffn_got]
    ffn_kept = gather_tiles(ffn_got, [ffn_keep[:far_half], ffn_keep[far_half:]])
    ffn_kept, attn_kept = lax.optimization_barrier((ffn_kept, attn_kept))
    ffn_all = [lax.all_gather(value, "seq", axis=0, tiled=True) for value in ffn_kept]
    attn_all = [attn_kept] + [chip_shift(attn_kept, offset) for offset in range(1, chips)]
    attn_all = attn_all + [core_swap(value) for value in attn_all]

    attn_all, ffn_all[0], attn_join = lax.optimization_barrier((attn_all, ffn_all[0], attn_join))

    def fetch(arrays, index, to, me, place, columns_of):
        def fast():
            return join_tiles(arrays, index, row_blocks, columns_of)

        def slow():
            whole = lax.all_to_all(
                jnp.broadcast_to(master_low[None], (seq_size * fsdp_size,) + master_low.shape),
                ("seq", "fsdp"),
                split_axis=0,
                concat_axis=0,
                tiled=True,
            ).reshape(-1, tile, tile)
            count = row_blocks * sum(columns_of)
            slots = pick(
                (to.reshape(1, -1) == me) & (place.reshape(1, -1) == jnp.arange(count)[:, None]),
                jnp.arange(tiles)[None, :],
            )
            return join_tiles([whole], slots, row_blocks, columns_of)

        return lax.cond(fits, fast, slow)

    w_first, w_out = fetch(
        attn_all, attn_join, attn_to, my_seq, attn_place, (attn_first, query_each)
    )
    gain_attn = gain_full[width : 2 * width]
    gain_laurel = gain_full[2 * width : 3 * width]
    gain_pre = gain_full[3 * width : 4 * width]
    gain_post = gain_full[4 * width : 5 * width]
    gain_vec = gain_full[5 * width : 6 * width]
    gain_query = gain_full[6 * width : 6 * width + HEAD_DIM]
    gain_key = gain_full[6 * width + HEAD_DIM : 6 * width + 2 * HEAD_DIM]
    stream = own_tokens.astype(f32)
    vectors = layer_vectors[0].astype(f32)
    normed, normed_pull = jax.vjp(rms_norm, stream, gain_in)
    normed_low = normed.astype(bf16)
    first_pre = matmul(pack_normed, w_first)
    is_key = my_seq % per_key == 0

    def shape_query(query_in, query_gain):
        value = rms_norm(query_in.reshape(length, per_device, HEAD_DIM), query_gain)
        return turn(value, cosine, sine)

    def shape_key(key_in, key_gain):
        return turn(rms_norm(key_in.reshape(length, 1, HEAD_DIM), key_gain), cosine, sine)

    query_pre = first_pre[:, : per_device * HEAD_DIM]
    other_pre = first_pre[:, per_device * HEAD_DIM :]
    query_rot, query_pull = jax.vjp(shape_query, query_pre, gain_query)
    key_rot, key_pull = jax.vjp(shape_key, other_pre, gain_key)
    query_heads = query_rot.astype(bf16)
    other_low = jnp.where(is_key, key_rot[:, 0, :], other_pre).astype(bf16)
    partner_low = seq_swap(other_low, 1).reshape(seq_size // 2, 2, rows, HEAD_DIM)
    partner_low = partner_low[:, ::-1].reshape(length, HEAD_DIM)
    key_single = jnp.where(is_key, other_low, partner_low)
    value_single = jnp.where(is_key, partner_low, other_low)

    raw = (
        jnp.einsum("qhd,kd->qhk", query_heads, key_single, preferred_element_type=f32) * SCALE
    )
    scores = jnp.where(allow[:, None, :], raw, NEGATIVE)
    powers = jnp.exp(scores - jnp.max(scores, axis=-1, keepdims=True))
    prob = powers / jnp.sum(powers, axis=-1, keepdims=True)
    prob_low = prob.astype(bf16)
    attended_low = (
        jnp.einsum("qhk,kd->qhd", prob_low, value_single, preferred_element_type=f32)
        .astype(bf16)
        .reshape(length, per_device * HEAD_DIM)
    )
    attn_pre = seq_sum(matmul_flip(attended_low, w_out), bf16)
    attn_pre, small_table, ffn_join = lax.optimization_barrier((attn_pre, small_table, ffn_join))
    laurel_left = small_table[:, :RANK]
    laurel_right = small_table[:, RANK : 2 * RANK]
    vector_gate_w = small_table[:, 2 * RANK : 2 * RANK + PLD]
    vector_proj_w = small_table[:, 2 * RANK + PLD :]

    attn_normed, attn_pull = jax.vjp(rms_norm, attn_pre, gain_attn)
    first_sum = stream + attn_normed
    left_pre = matmul(normed_low, laurel_left)
    left_low = left_pre.astype(bf16)
    right_pre = matmul_flip(left_low, laurel_right)
    laurel_normed, laurel_pull = jax.vjp(rms_norm, right_pre, gain_laurel)
    second_sum = (first_sum + normed + laurel_normed) * ROOT_HALF
    feed_normed, feed_pull = jax.vjp(rms_norm, second_sum, gain_pre)
    feed_own = feed_normed.astype(bf16)
    feed_low = lax.all_gather(feed_own, "fsdp", axis=0, tiled=True)
    ffn_all, _ = lax.optimization_barrier((ffn_all, feed_own))
    w_both, w_down = fetch(
        [near_all] + ffn_all, ffn_join, ffn_to, my_fsdp, ffn_place, (ffn_first, ffn_each)
    )
    both_pre = matmul(feed_low, w_both)
    ffn_width = w_down.shape[1]
    hidden, hidden_pull = jax.vjp(gelu_product, both_pre[:, :ffn_width], both_pre[:, ffn_width:])
    hidden_low = hidden.astype(bf16)
    down_pre = lax.psum_scatter(
        matmul_flip(hidden_low, w_down).astype(bf16), "fsdp", scatter_dimension=0, tiled=True
    ).astype(f32)
    down_normed, down_pull = jax.vjp(rms_norm, down_pre, gain_post)
    third_sum = second_sum + down_normed
    third_low = third_sum.astype(bf16)
    vector_pre = matmul(third_low, vector_gate_w)
    vector_gated, vector_pull = jax.vjp(lambda inner: gelu_product(inner, vectors), vector_pre)
    vector_low = vector_gated.astype(bf16)
    proj_pre = matmul_flip(vector_low, vector_proj_w)
    proj_normed, proj_pull = jax.vjp(rms_norm, proj_pre, gain_vec)
    result = third_sum + proj_normed
    output = result.astype(bf16)[None]

    grad_out = cotangent[0].astype(f32)
    grad_proj, grad_gain_vec = proj_pull(grad_out)
    proj_grad_low = grad_proj.astype(bf16)
    (grad_vector_pre,) = vector_pull(matmul(proj_grad_low, vector_proj_w))
    vector_grad_low = grad_vector_pre.astype(bf16)
    grad_third = grad_out + matmul_flip(vector_grad_low, vector_gate_w)
    grad_down, grad_gain_post = down_pull(grad_third)
    down_grad_low = lax.all_gather(grad_down.astype(bf16), "fsdp", axis=0, tiled=True)
    grad_gate, grad_up = hidden_pull(matmul(down_grad_low, w_down))
    both_grad_low = jnp.concatenate([grad_gate, grad_up], axis=1).astype(bf16)

    early_full = jnp.concatenate(
        [matmul_outer(third_low, vector_grad_low), matmul_outer(proj_grad_low, vector_low)], axis=1
    )
    small_early = small_sum(split_tiles(early_full, tile).reshape(-1, tile))
    feed_part = matmul_flip(both_grad_low, w_both).astype(bf16)
    feed_part, small_early = lax.optimization_barrier((feed_part, small_early))
    grad_feed = lax.psum_scatter(feed_part, "fsdp", scatter_dimension=0, tiled=True).astype(f32)
    both_grad_w = matmul_outer(feed_low, both_grad_low).astype(bf16)
    down_grad_w = matmul_outer(down_grad_low, hidden_low).astype(bf16)
    ffn_parts = cut_tiles(
        [both_grad_w, down_grad_w],
        [index.reshape(-1) for index in (far_cut[:, :far_half], far_cut[:, far_half:], near_cut)],
    )
    ffn_parts, grad_feed = lax.optimization_barrier((ffn_parts, grad_feed))
    *ffn_sums, near_sum = [
        lax.psum_scatter(value, "seq", scatter_dimension=0, tiled=True) for value in ffn_parts
    ]

    grad_second_norm, grad_gain_pre = feed_pull(grad_feed)
    half_grad = (grad_third + grad_second_norm) * ROOT_HALF
    grad_right, grad_gain_laurel = laurel_pull(half_grad)
    right_grad_low = grad_right.astype(bf16)
    left_grad_low = matmul(right_grad_low, laurel_right).astype(bf16)
    grad_attn, grad_gain_attn = attn_pull(half_grad)
    attn_grad_low = seq_gather(grad_attn.astype(bf16))
    grad_attended = (
        matmul(attn_grad_low, w_out).astype(bf16).reshape(length, per_device, HEAD_DIM)
    )
    out_grad_w = matmul_outer(attn_grad_low, attended_low).astype(bf16)
    value_grad = jnp.einsum("qhk,qhd->kd", prob_low, grad_attended, preferred_element_type=f32)
    grad_prob = jnp.einsum("qhd,kd->qhk", grad_attended, value_single, preferred_element_type=f32)
    inner = jnp.sum(prob * grad_prob, axis=-1, keepdims=True)
    grad_score = (prob * (grad_prob - inner)).astype(bf16)
    grad_query = (
        jnp.einsum("qhk,kd->qhd", grad_score, key_single, preferred_element_type=f32) * SCALE
    ).astype(bf16)
    key_grad = (
        jnp.einsum("qhk,qhd->kd", grad_score, query_heads, preferred_element_type=f32) * SCALE
    ).astype(bf16)
    value_grad = value_grad.astype(bf16)
    partner_grad = seq_swap(jnp.where(is_key, value_grad, key_grad), 1)
    partner_grad = partner_grad.reshape(seq_size // 2, 2, rows, HEAD_DIM)[:, ::-1]
    other_grad = jnp.where(is_key, key_grad, value_grad).astype(f32) + partner_grad.reshape(
        length, HEAD_DIM
    ).astype(f32)
    grad_query_pre, grad_gain_query = query_pull(grad_query.astype(f32))
    grad_key_pre, grad_gain_key = key_pull(other_grad[:, None, :])
    grad_gain_key = jnp.where(is_key, grad_gain_key, 0.0)
    first_grad_low = jnp.concatenate(
        [grad_query_pre, jnp.where(is_key, grad_key_pre, other_grad)], axis=1
    ).astype(bf16)
    first_grad_w = matmul_outer(pack_normed, first_grad_low).astype(bf16)
    near = (my_chip + shifts) % chips
    near_key = take_blocks(attn_key_chip, near)[:, None, :]
    near_order = take_blocks(attn_order_chip, near)[:, None, :]
    near_place = take_blocks(by_chip(attn_place), near)[:, None, :]

    def attn_cut(core):
        return pick(
            (near_key == 2 * my_seq + core)
            & (near_order == jnp.arange(attn_hold)[None, :, None]),
            near_place,
        ).reshape(-1)

    attn_given, attn_own = cut_tiles(
        [first_grad_w, out_grad_w], [attn_cut(1 - my_core), attn_cut(my_core)]
    )
    attn_given, attn_own, ffn_sums[0] = lax.optimization_barrier(
        (attn_given, attn_own, ffn_sums[0])
    )
    attn_parts = added(attn_own, core_swap(attn_given)).reshape(chips, attn_hold, tile, tile)
    attn_sum = attn_parts[0]
    attn_parts = [attn_parts[offset].astype(bf16) for offset in range(1, chips)]
    normed_pre = matmul_flip(first_grad_low, w_first)
    attn_sum, attn_parts, normed_pre = lax.optimization_barrier((attn_sum, attn_parts, normed_pre))
    normed_sum = seq_sum(normed_pre, bf16)
    for offset in range(1, chips):
        attn_sum = attn_sum + chip_shift(attn_parts[offset - 1], offset).astype(f32)
    attn_sum = attn_sum.astype(bf16)
    attn_back = pick(
        (column_slots[3][None, None, :] == (my_seq ^ flips)[:, None, None])
        & (column_slots[0][None, None, :] == my_key)
        & (column_slots[2][None, None, :] == jnp.arange(attn_room)[None, :, None]),
        column_slots[1],
    )

    grad_normed = half_grad + matmul_flip(left_grad_low, laurel_left) + normed_sum
    grad_stream_norm, grad_gain_in = normed_pull(grad_normed)
    input_grad = (half_grad + grad_stream_norm)[None]
    ffn_sums, attn_sum, grad_gain_in, input_grad = lax.optimization_barrier(
        (ffn_sums, attn_sum, grad_gain_in, input_grad)
    )
    ffn_sums = ffn_sums + [core_swap(value) for value in ffn_sums]
    ffn_return = gather_tiles(ffn_sums, [ffn_back[i] for i in range(1, chips)])
    ffn_return, attn_sum, grad_gain_in = lax.optimization_barrier(
        (ffn_return, attn_sum, grad_gain_in)
    )
    ffn_returned = [chip_shift(value, i + 1) for i, value in enumerate(ffn_return)]
    gain_grad = jnp.concatenate(
        [
            grad_gain_in,
            grad_gain_attn,
            grad_gain_laurel,
            grad_gain_pre,
            grad_gain_post,
            grad_gain_vec,
            grad_gain_query,
            grad_gain_key,
        ]
    )
    late_full = jnp.concatenate(
        [matmul_outer(normed_low, left_grad_low), matmul_outer(right_grad_low, left_low)], axis=1
    )
    late = jnp.concatenate(
        [late_full.reshape(seq_size, -1), gain_grad.reshape(seq_size, -1)], axis=1
    ).reshape(seq_size, -1, tile)
    late = seq_sum(late.reshape(-1, tile), bf16, True)

    late = late.astype(bf16)
    late = added(late, core_swap(late)).astype(bf16)
    attn_returned = seq_exchange(gather_tiles([attn_sum], [attn_back[i] for i in range(seq_size)]))
    attn_returned = attn_returned + [core_swap(value) for value in attn_returned]
    slot_grad = jnp.where(my_slots[0] >= 0, my_slots[1], back_size + my_slots[2])

    def slow_return():
        own_ffn = split_tiles(both_grad_w, tile), split_tiles(down_grad_w, tile)
        own_attn = split_tiles(first_grad_w, tile), split_tiles(out_grad_w, tile)
        parts = jnp.concatenate(own_ffn + own_attn + (jnp.zeros((1, tile, tile), bf16),))
        index = jnp.where(
            ffn_to == my_fsdp,
            ffn_place,
            jnp.where(attn_to == my_seq, ffn_count + attn_place, ffn_count + attn_count),
        )
        spread = jnp.concatenate(
            [gather_tiles([parts], [rows_of])[0] for rows_of in index.reshape(8, -1)]
        )
        spread = lax.all_to_all(
            spread.reshape((seq_size * fsdp_size, mine, tile, tile)),
            ("seq", "fsdp"),
            split_axis=0,
            concat_axis=0,
            tiled=True,
        )
        return jnp.sum(spread.astype(f32), axis=0).astype(bf16)

    slow_start = back_size + 2 * seq_size * attn_room
    slow_grads = lax.cond(fits, lambda: jnp.zeros((mine, tile, tile), bf16), slow_return)
    ffn_returned, slow_grads, near_sum, late = lax.optimization_barrier(
        (ffn_returned, slow_grads, near_sum, late)
    )
    late_parts = [late] + [chip_shift(late, offset) for offset in range(1, chips)]
    ffn_returned = ffn_returned + [core_swap(value) for value in ffn_returned]
    near_sums = [near_sum, core_swap(near_sum)]
    tile_grads = ffn_returned + near_sums + attn_returned + [slow_grads]
    slot_grad = jnp.where(fits, slot_grad, slow_start + local_slots)

    tile_new, tile_first_new, tile_second_new = rotate_update(
        tile_grads, slot_grad, tile_master, tile_first, tile_second, left_basis, right_basis, RATE_TILE
    )
    late_parts, tile_new, tile_first_new, tile_second_new = lax.optimization_barrier(
        (late_parts, tile_new, tile_first_new, tile_second_new)
    )
    late = sum(value.astype(f32) for value in late_parts)
    late_rows = late_full.shape[0] // seq_size
    late_tiles = late[:late_rows].reshape(-1, 1, tile, tile)
    gain_grad_mine = late[late_rows : late_rows + own_gains.shape[0] // tile].reshape(-1)
    small_grad = jnp.concatenate(
        [
            late_tiles.astype(bf16),
            small_early.reshape(late_tiles.shape[0], -1, tile, tile),
        ],
        axis=1,
    ).reshape(small_master.shape)
    small_new, small_first_new, small_second_new = rotate_update(
        [small_grad],
        jnp.arange(small_master.shape[0]),
        small_master,
        small_first,
        small_second,
        small_left,
        small_right,
        RATE_SMALL,
    )
    gain_first_new = BETA_ONE * gain_first + (1.0 - BETA_ONE) * gain_grad_mine
    gain_second_new = BETA_TWO * gain_second + (1.0 - BETA_TWO) * gain_grad_mine * gain_grad_mine
    correct_one = 1.0 - BETA_ONE**STEP
    correct_two = 1.0 - BETA_TWO**STEP
    gain_new = gains - RATE_GAIN * (gain_first_new / correct_one) / (
        jnp.sqrt(gain_second_new / correct_two) + ADAM_EPS
    )
    return (
        output,
        input_grad,
        tile_new,
        tile_first_new,
        tile_second_new,
        small_new,
        small_first_new,
        small_second_new,
        gain_new,
        gain_first_new,
        gain_second_new,
    )


def solution(mesh):
    return jax.shard_map(
        on_device,
        mesh=mesh,
        in_specs=(
            P("fsdp", "seq", None),
            P("fsdp", "seq", None),
            P("fsdp", None),
            P("fsdp", "seq", None),
            P(),
            P(("seq", "fsdp"), None, None),
            P(("seq", "fsdp"), None, None),
            P(("seq", "fsdp"), None, None),
            P(("seq", "fsdp"), None, None),
            P(("seq", "fsdp"), None, None),
            P("seq", None, None),
            P("seq", None, None),
            P("seq", None, None),
            P("seq", None, None),
            P("seq", None, None),
            P("seq"),
            P("seq"),
            P("seq"),
        ),
        out_specs=(
            P("fsdp", "seq", None),
            P("fsdp", "seq", None),
            P(("seq", "fsdp"), None, None),
            P(("seq", "fsdp"), None, None),
            P(("seq", "fsdp"), None, None),
            P("seq", None, None),
            P("seq", None, None),
            P("seq", None, None),
            P("seq"),
            P("seq"),
            P("seq"),
        ),
        check_vma=False,
    )
```
